32 devices in a mesh: grp: 2 (over y), blk: 4 (over z), mpo: 2 (over x), rep: 2 (over core).
Axes of the slice: x: 2, y: 2, z: 4, core: 2. Of those that a mesh axis runs over, the one named last changes fastest.
Arguments:
- wavefunction: float32 [64, 64, 1024], P(('grp', 'blk')), parts along dimension 0, may hold values from -4000 to 4000
- environment: float32 [48, 32, 64, 128], P(('grp', 'mpo', 'rep'), None, 'blk'), parts along dimension 0, may hold values from -0.75 to 0.75
- bond_terms: float32 [48, 16, 16], P(('grp', 'mpo', 'rep')), parts along dimension 0, may hold values from -0.3125 to 0.3125
- diagonal: float32 [64, 64, 1024], P(('grp', 'blk'), None, ('mpo', 'rep')), parts along dimension 0, may hold values from 0.5 to 4
- term_slot: int32 [48, 32], P(('grp', 'mpo', 'rep'), 'blk'), parts along dimension 0, may hold values from 0 to 7, as said below
- slot_block: int32 [8, 8], P('grp', 'blk'), parts along dimension 0, may hold values from 0 to 7
Outputs:
- first_image: float32 [64, 64, 1024], P(('grp', 'blk'), None, ('mpo', 'rep')), parts along dimension 0
- second_vector: float32 [64, 64, 1024], P(('grp', 'blk'), None, ('mpo', 'rep')), parts along dimension 0
- second_image: float32 [64, 64, 1024], P(('grp', 'blk'), None, ('mpo', 'rep')), parts along dimension 0
The draws below stay inside these ranges and needn't reach their ends.
There are 2 independent parts, one for each index of `grp`. The reference program is written for one: setup_inputs(seed, part) draws one part's arguments, and reference() takes and returns one part's arrays. A program takes and returns all parts, laid end to end along the dimension named above; each array names one. Nothing has to cross between parts.
Inputs may be any that keep to these rules, and one draw needn't show every extreme that they name: `term_slot`: slot t of the device that owns block j sends to the owner t // 2.
All inputs are finite; a program needn't handle non-finite values.
Results may differ from the reference program's by a relative error of at most 0.00014.
Values sent between devices are 32-bit elements; how exact they have to be, the bound alone decides.
No kernel may reach another device: no remote copies, remote signals or barrier semaphores. Data moves between devices by JAX's collectives and lax.ppermute only.
A program may use at most 128 MiB of HBM per device.

```python
import math
import jax
import jax.numpy as jnp
from jax import lax

B = 64
P_SIZE = 16
NW = 24
CAP = 2
BLK_DEV = 8
NBLK = 32


def draw_wavefunction(key, part):
    key = jax.random.fold_in(key, 13)
    keys = jax.random.split(key, 3)
    row_scale = jnp.exp(jax.random.uniform(keys[1], (NBLK, B, 1), jnp.float32, 0.0, math.log(10.0)))
    col_scale = jnp.exp(jax.random.uniform(keys[2], (1, 1, B * P_SIZE), jnp.float32, 0.0, math.log(10.0)))
    place = jnp.arange(NBLK, dtype=jnp.float32)[:, None, None] / NBLK
    base = jnp.clip(jax.random.normal(keys[0], (NBLK, B, B * P_SIZE), jnp.float32), -6.0, 6.0)
    rising = jnp.exp(math.log(3.0) * place)
    return base * row_scale * col_scale * rising


def draw_term_slot(key, part):
    key = jax.random.fold_in(key, 11)
    keys = jax.random.split(key, 3)
    devices = NBLK // BLK_DEV
    slot_count = devices * CAP
    forced = jax.random.randint(keys[0], (), 0, devices)
    active = jax.random.randint(keys[1], (devices, slot_count), 0, 2)
    owner = jnp.arange(slot_count, dtype=jnp.int32) // CAP
    active = jnp.where(owner[None, :] == forced, 1, active)
    running = jnp.cumsum(active, axis=1)
    live = running[:, -1]
    source = jnp.arange(NBLK, dtype=jnp.int32) // BLK_DEV
    picked = jax.random.randint(keys[2], (NW, NBLK), 0, 1 << 20) % live[source][None, :]
    chosen = jnp.sum((running[source][None, :, :] <= picked[:, :, None]).astype(jnp.int32), axis=-1)
    bond_index = jnp.arange(NW, dtype=jnp.int32)[:, None]
    leading = (jnp.arange(NBLK, dtype=jnp.int32) % BLK_DEV == 0)[None, :]
    forced_slot = forced * CAP + bond_index
    chosen = jnp.where((bond_index < CAP) & leading, forced_slot, chosen)
    return chosen.astype(jnp.int32)


def draw_slot_block(key, part):
    key = jax.random.fold_in(key, 12)
    devices = NBLK // BLK_DEV
    base = jax.random.randint(key, (devices, devices), 0, BLK_DEV)
    base = base.at[0, 0].set(BLK_DEV - CAP)
    base = base.at[0, 1].set(0)
    offsets = jnp.arange(CAP, dtype=jnp.int32)
    table = (base[:, :, None] + offsets[None, None, :]) % BLK_DEV
    return table.reshape(devices, devices * CAP).astype(jnp.int32)


def block_scale(rng, dims, pieces, low, largest):
    def one(axis_at, shards_of):
        draws = jax.random.uniform(jax.random.fold_in(jax.random.fold_in(rng, 6), axis_at), (shards_of,), jnp.float32, low / len(pieces), largest / len(pieces))
        return jnp.repeat(jnp.exp(draws), dims[axis_at] // shards_of).reshape((-1,) + (1,) * (len(dims) - axis_at - 1))

    loudness = one(*pieces[0])
    for cut in pieces[1:]:
        loudness = loudness * one(*cut)
    return loudness


def scatter_about(key, dims, scale, bound, shards=(), held_as=jnp.bfloat16):
    level = block_scale(key, dims, shards, -0.22, 0.18) if shards else 1.0
    array = jax.random.normal(key, dims, jnp.float32) * scale * level
    return jnp.minimum(jnp.maximum(array, -bound), bound).astype(held_as)


def setup_inputs(seed: int = 0, part: int = 0) -> dict:
    arg_keys = jax.random.split(jax.random.key(seed), 7)
    part_keys = jax.random.split(jax.random.fold_in(arg_keys[6], part), 7)
    return {
        "wavefunction": draw_wavefunction(jax.random.fold_in(jax.random.fold_in(arg_keys[6], part), 71), part),
        "environment": scatter_about(part_keys[1], (NW, NBLK, B, 2 * B), B ** -0.5, 0.75, ((0, 4), (2, 4)), jnp.float32),
        "bond_terms": scatter_about(part_keys[2], (NW, P_SIZE, P_SIZE), (P_SIZE * NW) ** -0.5, 0.3125, ((0, 4),), jnp.float32),
        "diagonal": jnp.clip(jnp.exp(math.log(4.0) - 2.0794415 * jax.random.uniform(part_keys[3], (NBLK, B, B * P_SIZE), jnp.float32) ** block_scale(part_keys[3], (NBLK, B, B * P_SIZE), ((0, 4), (2, 4)), -0.2, 0.2)), 0.5, 4.0),
        "term_slot": draw_term_slot(jax.random.fold_in(jax.random.fold_in(arg_keys[6], part), 71), part),
        "slot_block": draw_slot_block(jax.random.fold_in(jax.random.fold_in(arg_keys[6], part), 71), part),
    }


def bond_apply(vector_in, environment, bond_terms, term_slot, slot_block, diagonal):
    blocks = vector_in.reshape(NBLK, B, B, P_SIZE)
    source = jnp.arange(NBLK, dtype=jnp.int32) // BLK_DEV
    targets = (term_slot // CAP * BLK_DEV + slot_block[source[None, :], term_slot]).astype(jnp.int32)

    def one_bond(accumulated, inputs):
        env_block, mixing, target_row = inputs
        left_env = env_block[:, :, :B]
        right_env = env_block[:, :, B:]
        left_done = jnp.einsum('jab,jacs->jbcs', left_env, blocks, precision=lax.Precision.HIGHEST)
        phys_mixed = jnp.einsum('jbcs,st->jbct', left_done, mixing, precision=lax.Precision.HIGHEST)
        bond_term = jnp.einsum('jbct,jcd->jbdt', phys_mixed, right_env, precision=lax.Precision.HIGHEST)
        accumulated = accumulated + jax.ops.segment_sum(bond_term.reshape(NBLK, B, B * P_SIZE), target_row, num_segments=NBLK)
        return (accumulated, None)
    start_value = jnp.zeros((NBLK, B, B * P_SIZE), jnp.float32)
    accumulated, unused = lax.scan(one_bond, start_value, (environment, bond_terms, targets))
    return accumulated + diagonal * vector_in

def reference(wavefunction, environment, bond_terms, diagonal, term_slot, slot_block):
    entries = NBLK * B * B * P_SIZE
    mean_start = jnp.sum(wavefunction * wavefunction) / entries
    first_vector = wavefunction * lax.rsqrt(mean_start + 1e-06)
    first_image = bond_apply(first_vector, environment, bond_terms, term_slot, slot_block, diagonal)
    rayleigh = jnp.sum(first_vector * first_image) / entries
    residual = first_image - rayleigh * first_vector
    mean_resid = jnp.sum(residual * residual) / entries
    second_vector = residual * lax.rsqrt(mean_resid + 1e-06)
    second_image = bond_apply(second_vector, environment, bond_terms, term_slot, slot_block, diagonal)
    return (first_image, second_vector, second_image)
```

```python
import functools
import math

import jax
import jax.numpy as jnp
from jax import lax
from jax.experimental import pallas as pl
from jax.experimental.pallas import tpu as pltpu
from jax.sharding import PartitionSpec as P

LANES = 128
SUB = 8
GROUPS = 3
VMEM_LIMIT = 56 * 1024 * 1024


def plain_apply(vector_full, environment, bond_terms, term_slot, slot_block, diagonal):
    block_count, block_rows, block_width = vector_full.shape
    phys_size = bond_terms.shape[-1]
    right_rows = block_width // phys_size
    slot_count = slot_block.shape[0] * slot_block.shape[1]
    blocks = vector_full.reshape(block_count, block_rows, right_rows, phys_size)
    ordered = jnp.transpose(blocks, (0, 3, 1, 2))
    left_env = environment[:, :, :, :block_rows]
    right_env = environment[:, :, :, block_rows:]
    left_done = jnp.einsum("wjab,jsac->wjsbc", left_env, ordered, precision=lax.Precision.HIGHEST)
    right_done = jnp.einsum(
        "wjsbc,wjcd->wjsbd", left_done, right_env, precision=lax.Precision.HIGHEST
    )
    right_done = right_done.reshape(
        environment.shape[0], block_count, phys_size, block_rows * right_rows
    )
    bond_term = jnp.einsum(
        "wjsx,wst->wjtx", right_done, bond_terms, precision=lax.Precision.HIGHEST
    )
    bond_term = bond_term.reshape(environment.shape[0], block_count, block_rows * block_width)
    slot_table = (
        term_slot[:, None, :] == jnp.arange(slot_count, dtype=jnp.int32)[None, :, None]
    ).astype(jnp.float32)
    slot_buffer = jnp.einsum("wsj,wjx->sx", slot_table, bond_term, precision=lax.Precision.HIGHEST)
    slot_buffer = slot_buffer.reshape(slot_count, phys_size, block_rows, right_rows)
    slot_buffer = jnp.transpose(slot_buffer, (0, 2, 3, 1)).reshape(
        slot_count, block_rows, block_width
    )
    owners = slot_block.reshape(-1)
    selector = (owners[None, :] == jnp.arange(block_count, dtype=jnp.int32)[:, None]).astype(
        jnp.float32
    )
    column_width = block_width // lax.axis_size(("mpo", "rep"))
    column_start = lax.axis_index(("mpo", "rep")) * column_width
    own_part = lax.dynamic_slice_in_dim(vector_full, column_start, column_width, 2)
    shares = lax.psum_scatter(slot_buffer, ("mpo", "rep"), scatter_dimension=2, tiled=True)
    arrived = lax.all_to_all(shares, "blk", split_axis=0, concat_axis=0, tiled=True)
    result = jnp.einsum("ks,sbc->kbc", selector, arrived, precision=lax.Precision.HIGHEST)
    return (result + diagonal * own_part, own_part)


def plain_device(wavefunction, environment, bond_terms, diagonal, term_slot, slot_block):
    arranged = lax.all_to_all(environment, "blk", split_axis=1, concat_axis=2, tiled=True)
    entries = float(
        wavefunction.shape[0] * lax.axis_size("blk") * wavefunction.shape[1] * wavefunction.shape[2]
    )
    square_sum = lax.psum(jnp.sum(wavefunction * wavefunction), "blk")
    first_vector = wavefunction * lax.rsqrt(square_sum / entries + 1e-06)
    first_image, first_part = plain_apply(
        first_vector, arranged, bond_terms, term_slot, slot_block, diagonal
    )
    rayleigh = lax.psum(jnp.sum(first_part * first_image), ("blk", "mpo", "rep")) / entries
    residual = first_image - rayleigh * first_part
    resid_sum = lax.psum(jnp.sum(residual * residual), ("blk", "mpo", "rep"))
    second_vector = residual * lax.rsqrt(resid_sum / entries + 1e-06)
    second_full = lax.all_gather(second_vector, ("mpo", "rep"), axis=2, tiled=True)
    second_image, unused = plain_apply(
        second_full, arranged, bond_terms, term_slot, slot_block, diagonal
    )
    return (first_image, second_vector, second_image)


def split_two(x):
    high = x.astype(jnp.bfloat16)
    low = (x - high.astype(jnp.float32)).astype(jnp.bfloat16)
    return high, low


def prepare_kernel(place_ref, *refs):
    sources = refs[:-3]
    left_high, left_low, right_out = refs[-3:]
    zs, per, blocks, rows, lanes = sources[0].shape
    half = lanes // 2
    lane = lax.broadcasted_iota(jnp.int32, (half, lanes), 1)
    first = place_ref[0]
    pairs = [(s, k) for s in range(len(sources)) for k in range(per)]
    count = lanes // 16
    for j in range(blocks):
        for base in range(0, len(pairs), count):
            group = pairs[base : base + count]
            columns = jnp.zeros((half, lanes), jnp.float32)
            for at, (s, k) in enumerate(group):
                block = jnp.concatenate([sources[s][z, k, j] for z in range(zs)], axis=0)
                turned = pltpu.roll(block, half, 1)
                both = jnp.where(lane < half, block, turned)
                high, low = split_two(both)
                left_high[base + at, j] = high
                left_low[base + at, j] = low
                shift = (16 * at + lanes - half - first) % lanes
                moved = pltpu.roll(block, lax.rem(shift, lanes), 1)
                columns = jnp.where(lane // 16 == at, moved, columns)
            upright = columns.T
            pieces = []
            for at in range(len(group)):
                a = upright[16 * at : 16 * at + 8]
                b = upright[16 * at + 8 : 16 * at + 16]
                pieces.append(jnp.concatenate([a, b], axis=1))
            packed = jnp.concatenate(pieces, axis=0)
            high, low = split_two(packed)
            where = pl.ds(SUB * base, SUB * len(group))
            right_out[j, where, 0:lanes] = high
            right_out[j, where, lanes : 2 * lanes] = high
            right_out[j, where, 2 * lanes : 3 * lanes] = low


def prepare(environments, first_column):
    zs, per, blocks, rows, lanes = environments[0].shape
    total = per * len(environments)
    half = lanes // 2
    step = 2
    return pl.pallas_call(
        prepare_kernel,
        grid_spec=pltpu.PrefetchScalarGridSpec(
            num_scalar_prefetch=1,
            grid=(blocks // step,),
            in_specs=[
                pl.BlockSpec((zs, per, step, rows, lanes), lambda i, p: (0, 0, i, 0, 0))
                for _ in environments
            ],
            out_specs=[
                pl.BlockSpec((total, step, half, lanes), lambda i, p: (0, i, 0, 0)),
                pl.BlockSpec((total, step, half, lanes), lambda i, p: (0, i, 0, 0)),
                pl.BlockSpec((step, total * SUB, 3 * lanes), lambda i, p: (i, 0, 0)),
            ],
        ),
        out_shape=[
            jax.ShapeDtypeStruct((total, blocks, half, lanes), jnp.bfloat16),
            jax.ShapeDtypeStruct((total, blocks, half, lanes), jnp.bfloat16),
            jax.ShapeDtypeStruct((blocks, total * SUB, 3 * lanes), jnp.bfloat16),
        ],
        compiler_params=pltpu.CompilerParams(vmem_limit_bytes=VMEM_LIMIT),
        name="prepare",
    )(first_column.reshape(1), *environments)


def apply_kernel(slot_ref, place_ref, *refs):
    parts = refs[:4]
    left_high, left_low, right_ref, mix_ref, before, out_ref, vec, mid = refs[4:]
    step = parts[0].shape[0]
    total = left_high.shape[0]
    lanes = LANES
    half = lanes // 2
    phys = 16
    lane = lax.broadcasted_iota(jnp.int32, (16, lanes), 1)
    lane64 = lax.broadcasted_iota(jnp.int32, (half, lanes), 1)
    zero16 = jnp.zeros((16, lanes), jnp.float32)
    zero64 = jnp.zeros((half, lanes), jnp.bfloat16)

    @pl.when(pl.program_id(0) == 0)
    def _():
        out_ref[...] = before[...]

    for j in range(step):
        for s in range(phys):
            for g in range(4):
                x = parts[g][j, pl.ds(s, SUB, stride=phys), :]
                y = pltpu.roll(x, half, 1)
                xy = jnp.concatenate([x, y], axis=0)
                yx = jnp.concatenate([y, x], axis=0)
                top_high, top_low = split_two(jnp.where(lane < half, xy, zero16))
                low_high, low_low = split_two(jnp.where(lane < half, zero16, yx))
                row = pl.multiple_of(place_ref[g] * 16, 16)
                columns = slice(s * lanes, (s + 1) * lanes)
                vec[pl.ds(row, 16), columns] = top_high
                vec[pl.ds(row + half, 16), columns] = low_high
                vec[pl.ds(row + lanes, 16), columns] = top_low
                vec[pl.ds(row + lanes + half, 16), columns] = low_low
        mid[j] = jnp.dot(
            right_ref[j, :, 0 : 2 * lanes], vec[...], preferred_element_type=jnp.float32
        ) + jnp.dot(
            right_ref[j, :, 2 * lanes :], vec[0:lanes, :], preferred_element_type=jnp.float32
        )

    def one_bond(w):
        highs, lows = [], []
        for j in range(step):
            rows = pl.ds(pl.multiple_of(w * SUB, SUB), SUB)
            t = jnp.concatenate(
                [mid[j, rows, s * lanes : (s + 1) * lanes] for s in range(phys)], axis=0
            )
            t_high, t_low = split_two(t)
            lh, ll = left_high[w, j], left_low[w, j]
            wide_high = jnp.concatenate(
                [jnp.where(lane64 < half, lh, zero64), jnp.where(lane64 < half, zero64, lh)], axis=0
            )
            wide_low = jnp.concatenate(
                [jnp.where(lane64 < half, ll, zero64), jnp.where(lane64 < half, zero64, ll)], axis=0
            )
            z = jnp.dot(
                jnp.concatenate([t_high, t_low], axis=1),
                jnp.concatenate([wide_high, wide_high], axis=0),
                preferred_element_type=jnp.float32,
            ) + jnp.dot(t_high, wide_low, preferred_element_type=jnp.float32)
            z_high, z_low = split_two(z)
            highs.append(z_high)
            lows.append(z_low)
        z_high = jnp.concatenate(highs, axis=1)
        z_low = jnp.concatenate(lows, axis=1)
        mix_high = mix_ref[w, :, 0:lanes]
        mix_low = mix_ref[w, :, lanes:]
        mixed = jnp.dot(
            jnp.concatenate([mix_high, mix_high], axis=1),
            jnp.concatenate([z_high, z_low], axis=0),
            preferred_element_type=jnp.float32,
        ) + jnp.dot(mix_low, z_high, preferred_element_type=jnp.float32)
        for j in range(step):
            slot = slot_ref[w, pl.program_id(0) * step + j]
            out_ref[slot] += mixed[:, j * lanes : (j + 1) * lanes]

    unroll = 4 if total % 4 == 0 else 1

    def several(i, carry):
        for k in range(unroll):
            one_bond(i * unroll + k)
        return carry

    lax.fori_loop(0, total // unroll, several, 0)


def apply_bonds(parts, places, operands, mixing, slots, before):
    left_high, left_low, right = operands
    total, blocks, half, lanes = left_high.shape
    step = 2
    whole = lambda *shape: pl.BlockSpec(shape, lambda i, *_: (0,) * len(shape))
    flops = 2 * blocks * total * SUB * lanes * (3 * lanes * 16 + 3 * lanes * 16 + 3 * lanes * 16)
    return pl.pallas_call(
        apply_kernel,
        grid_spec=pltpu.PrefetchScalarGridSpec(
            num_scalar_prefetch=2,
            grid=(blocks // step,),
            in_specs=[
                pl.BlockSpec((step, lanes, lanes), lambda i, *_: (i, 0, 0)) for _ in parts
            ]
            + [
                pl.BlockSpec((total, step, half, lanes), lambda i, *_: (0, i, 0, 0)),
                pl.BlockSpec((total, step, half, lanes), lambda i, *_: (0, i, 0, 0)),
                pl.BlockSpec((step, total * SUB, 3 * lanes), lambda i, *_: (i, 0, 0)),
                whole(*mixing.shape),
                whole(*before.shape),
            ],
            out_specs=whole(*before.shape),
            scratch_shapes=[
                pltpu.VMEM((2 * lanes, 16 * lanes), jnp.bfloat16),
                pltpu.VMEM((step, total * SUB, 16 * lanes), jnp.float32),
            ],
        ),
        out_shape=jax.ShapeDtypeStruct(before.shape, jnp.float32),
        compiler_params=pltpu.CompilerParams(vmem_limit_bytes=VMEM_LIMIT),
        cost_estimate=pl.CostEstimate(
            flops=flops, bytes_accessed=12 * 1024 * 1024, transcendentals=0
        ),
        name="apply_bonds",
    )(slots, places, *parts, left_high, left_low, right, mixing, before)


def swap(x, axis):
    return lax.ppermute(x, axis, [(0, 1), (1, 0)])


def gathered(x):
    across = swap(x, "mpo")
    return [x, across, swap(x, "rep"), swap(across, "rep")]


def to_packed(x):
    blocks, rows, width = x.shape
    x = x.reshape(blocks, rows, 2, width // 2)
    return jnp.transpose(x, (0, 3, 2, 1)).reshape(blocks, width // 2, 2 * rows)


def from_packed(x):
    blocks, width, rows = x.shape
    x = x.reshape(blocks, width, 2, rows // 2)
    return jnp.transpose(x, (0, 3, 2, 1)).reshape(blocks, rows // 2, 2 * width)


def mixing_operand(bond_terms):
    count, phys, _ = bond_terms.shape
    eye = jnp.eye(SUB, dtype=jnp.float32)
    wide = jnp.transpose(bond_terms, (0, 2, 1))[:, None, :, :, None] * eye[None, :, None, None, :]
    wide = wide.reshape(count, SUB * phys, phys * SUB)
    high = lax.reduce_precision(wide, 8, 7)
    return jnp.concatenate([high, wide - high], axis=2).astype(jnp.bfloat16)


def owner_sum(slot_sums, slot_block):
    arrived = lax.all_to_all(slot_sums, "blk", split_axis=0, concat_axis=0, tiled=True)
    owners = slot_block.reshape(-1)
    blocks = slot_sums.shape[0]
    total = []
    selector = owners[None, :] == jnp.arange(blocks, dtype=jnp.int32)[:, None]
    return jnp.einsum(
        "ks,sbc->kbc",
        selector.astype(jnp.float32),
        arrived,
        precision=lax.Precision.HIGHEST,
    )


def per_device(wavefunction, environment, bond_terms, diagonal, term_slot, slot_block):
    blocks, rows, width = wavefunction.shape
    zs = lax.axis_size("blk")
    mpo, rep = lax.axis_index("mpo"), lax.axis_index("rep")
    place = lambda m, r: 2 * m + r
    places = jnp.stack(
        [place(mpo, rep), place(1 - mpo, rep), place(mpo, 1 - rep), place(1 - mpo, 1 - rep)]
    ).astype(jnp.int32)
    own = places[0]
    bonds = environment.shape[0]
    per = bonds // GROUPS
    entries = float(blocks * zs * rows * width)

    operands = []
    for group in range(GROUPS):
        piece = environment[group * per : (group + 1) * per]
        piece = piece.reshape(per, zs, blocks, rows // zs, 2 * rows)
        piece = jnp.transpose(piece, (1, 0, 2, 3, 4))
        piece = lax.all_to_all(piece, "blk", split_axis=0, concat_axis=0, tiled=True)
        operands.append(prepare(gathered(piece), 16 * own))

    terms = gathered(bond_terms)
    slots = gathered(term_slot)

    def of_group(items, group):
        return jnp.concatenate([x[group * per : (group + 1) * per] for x in items], axis=0)

    mixings = [mixing_operand(of_group(terms, group)) for group in range(GROUPS)]
    slot_tables = [of_group(slots, group) for group in range(GROUPS)]

    quarters = wavefunction.reshape(blocks, rows, 4, 2, width // 8)
    quarters = jnp.transpose(quarters, (2, 0, 4, 3, 1)).reshape(4, blocks, width // 8, 2 * rows)
    in_order = jnp.arange(4, dtype=jnp.int32)
    own_first = lax.dynamic_index_in_dim(quarters, own, 0, keepdims=False)
    diagonal_packed = to_packed(diagonal)

    def apply(parts, where):
        total = jnp.zeros((zs * slot_block.shape[1], width // 8, 2 * rows), jnp.float32)
        for group in range(GROUPS):
            total = apply_bonds(
                parts, where, operands[group], mixings[group], slot_tables[group], total
            )
        return owner_sum(total, slot_block)

    image = apply([quarters[q] for q in range(4)], in_order) + diagonal_packed * own_first
    second = apply(gathered(image), places) + diagonal_packed * image

    square_sum = lax.psum(jnp.sum(wavefunction * wavefunction), "blk")
    cross_sum = lax.psum(jnp.sum(own_first * image), ("blk", "mpo", "rep"))
    scale = lax.rsqrt(square_sum / entries + 1e-06)
    rayleigh = cross_sum * scale * scale / entries
    residual = scale * (image - rayleigh * own_first)
    resid_sum = lax.psum(jnp.sum(residual * residual), ("blk", "mpo", "rep"))
    second_scale = lax.rsqrt(resid_sum / entries + 1e-06)
    first_image = scale * image
    second_vector = second_scale * residual
    second_image = second_scale * scale * (second - rayleigh * image)
    return tuple(from_packed(x) for x in (first_image, second_vector, second_image))


def solution(mesh):
    packed = mesh.shape["mpo"] == 2 and mesh.shape["rep"] == 2
    return jax.shard_map(
        per_device if packed else plain_device,
        mesh=mesh,
        in_specs=(
            P(("grp", "blk"), None, None),
            P(("grp", "mpo", "rep"), None, "blk", None),
            P(("grp", "mpo", "rep"), None, None),
            P(("grp", "blk"), None, ("mpo", "rep")),
            P(("grp", "mpo", "rep"), "blk"),
            P("grp", "blk"),
        ),
        out_specs=(
            P(("grp", "blk"), None, ("mpo", "rep")),
            P(("grp", "blk"), None, ("mpo", "rep")),
            P(("grp", "blk"), None, ("mpo", "rep")),
        ),
        check_vma=False,
    )
```

```python
import functools

import jax
import jax.numpy as jnp
from jax import lax
from jax.experimental import pallas as pl
from jax.experimental.pallas import tpu as pltpu
from jax.sharding import PartitionSpec as P

LANES = 128
SUB = 8
PHYS = 16
GROUPS = 2
VMEM_LIMIT = 56 * 1024 * 1024


def plain_apply(vector_full, environment, bond_terms, term_slot, slot_block, diagonal):
    block_count, block_rows, block_width = vector_full.shape
    phys_size = bond_terms.shape[-1]
    right_rows = block_width // phys_size
    slot_count = slot_block.shape[0] * slot_block.shape[1]
    blocks = vector_full.reshape(block_count, block_rows, right_rows, phys_size)
    ordered = jnp.transpose(blocks, (0, 3, 1, 2))
    left_env = environment[:, :, :, :block_rows]
    right_env = environment[:, :, :, block_rows:]
    left_done = jnp.einsum("wjab,jsac->wjsbc", left_env, ordered, precision=lax.Precision.HIGHEST)
    right_done = jnp.einsum(
        "wjsbc,wjcd->wjsbd", left_done, right_env, precision=lax.Precision.HIGHEST
    )
    right_done = right_done.reshape(
        environment.shape[0], block_count, phys_size, block_rows * right_rows
    )
    bond_term = jnp.einsum(
        "wjsx,wst->wjtx", right_done, bond_terms, precision=lax.Precision.HIGHEST
    )
    bond_term = bond_term.reshape(environment.shape[0], block_count, block_rows * block_width)
    slot_table = (
        term_slot[:, None, :] == jnp.arange(slot_count, dtype=jnp.int32)[None, :, None]
    ).astype(jnp.float32)
    slot_buffer = jnp.einsum("wsj,wjx->sx", slot_table, bond_term, precision=lax.Precision.HIGHEST)
    slot_buffer = slot_buffer.reshape(slot_count, phys_size, block_rows, right_rows)
    slot_buffer = jnp.transpose(slot_buffer, (0, 2, 3, 1)).reshape(
        slot_count, block_rows, block_width
    )
    owners = slot_block.reshape(-1)
    selector = (owners[None, :] == jnp.arange(block_count, dtype=jnp.int32)[:, None]).astype(
        jnp.float32
    )
    column_width = block_width // lax.axis_size(("mpo", "rep"))
    column_start = lax.axis_index(("mpo", "rep")) * column_width
    own_part = lax.dynamic_slice_in_dim(vector_full, column_start, column_width, 2)
    shares = lax.psum_scatter(slot_buffer, ("mpo", "rep"), scatter_dimension=2, tiled=True)
    arrived = lax.all_to_all(shares, "blk", split_axis=0, concat_axis=0, tiled=True)
    result = jnp.einsum("ks,sbc->kbc", selector, arrived, precision=lax.Precision.HIGHEST)
    return (result + diagonal * own_part, own_part)


def plain_device(wavefunction, environment, bond_terms, diagonal, term_slot, slot_block):
    arranged = lax.all_to_all(environment, "blk", split_axis=1, concat_axis=2, tiled=True)
    entries = float(
        wavefunction.shape[0] * lax.axis_size("blk") * wavefunction.shape[1] * wavefunction.shape[2]
    )
    square_sum = lax.psum(jnp.sum(wavefunction * wavefunction), "blk")
    first_vector = wavefunction * lax.rsqrt(square_sum / entries + 1e-06)
    first_image, first_part = plain_apply(
        first_vector, arranged, bond_terms, term_slot, slot_block, diagonal
    )
    rayleigh = lax.psum(jnp.sum(first_part * first_image), ("blk", "mpo", "rep")) / entries
    residual = first_image - rayleigh * first_part
    resid_sum = lax.psum(jnp.sum(residual * residual), ("blk", "mpo", "rep"))
    second_vector = residual * lax.rsqrt(resid_sum / entries + 1e-06)
    second_full = lax.all_gather(second_vector, ("mpo", "rep"), axis=2, tiled=True)
    second_image, unused = plain_apply(
        second_full, arranged, bond_terms, term_slot, slot_block, diagonal
    )
    return (first_image, second_vector, second_image)


def split_two(x):
    high = x.astype(jnp.bfloat16)
    low = (x - high.astype(jnp.float32)).astype(jnp.bfloat16)
    return high, low


def lane_is_first(rows):
    return lax.broadcasted_iota(jnp.int32, (rows, LANES), 1) < LANES // 2


def whole(*shape):
    return pl.BlockSpec(shape, lambda i, *_: (0,) * len(shape))


def pack_tile(x):
    return jnp.concatenate([x[:, :LANES], x[:, LANES:]], axis=0).T


def unpack_tile(x):
    upright = x.T
    return jnp.concatenate([upright[: LANES // 2], upright[LANES // 2 :]], axis=1)


def store_vector(parts, j, rows_of, put):
    first = lane_is_first(SUB)
    for pair in range(PHYS // 2):
        for part, row in zip(parts, rows_of):
            even = part[j, pl.ds(2 * pair, SUB, stride=PHYS), :]
            odd = part[j, pl.ds(2 * pair + 1, SUB, stride=PHYS), :]
            upper = jnp.where(first, even, pltpu.roll(odd, LANES // 2, 1))
            lower = jnp.where(first, pltpu.roll(even, LANES // 2, 1), odd)
            high, low = split_two(jnp.concatenate([upper, lower], axis=0))
            put(row, pair, high, low)


def pack_kernel(info_ref, wave_ref, own_wave_ref, diag_ref, vec_ref, own_ref, diag_out, tiles):
    half = LANES // 2
    for j in range(wave_ref.shape[0]):
        own_ref[j] = pack_tile(own_wave_ref[j])
        diag_out[j] = pack_tile(diag_ref[j])
        for q in range(4):
            tiles[q, j] = pack_tile(wave_ref[j, :, 2 * LANES * q : 2 * LANES * (q + 1)])

        def put(row, pair, high, low):
            columns = slice(pair * LANES, (pair + 1) * LANES)
            vec_ref[j, row : row + 16, columns] = high
            vec_ref[j, row + half : row + half + 16, columns] = low

        store_vector([tiles.at[q] for q in range(4)], j, [16 * q for q in range(4)], put)


def pack(info, wavefunction, diagonal):
    blocks, rows, width = wavefunction.shape
    step = 2
    tile = pl.BlockSpec((step, LANES, LANES), lambda i, *_: (i, 0, 0))
    return pl.pallas_call(
        pack_kernel,
        grid_spec=pltpu.PrefetchScalarGridSpec(
            num_scalar_prefetch=1,
            grid=(blocks // step,),
            in_specs=[
                pl.BlockSpec((step, rows, width), lambda i, *_: (i, 0, 0)),
                pl.BlockSpec((step, rows, width // 4), lambda i, info: (i, 0, info[0])),
                pl.BlockSpec((step, rows, width // 4), lambda i, *_: (i, 0, 0)),
            ],
            out_specs=[pl.BlockSpec((step, LANES, width), lambda i, *_: (i, 0, 0)), tile, tile],
            scratch_shapes=[pltpu.VMEM((4, step, LANES, LANES), jnp.float32)],
        ),
        out_shape=[
            jax.ShapeDtypeStruct((blocks, LANES, width), jnp.bfloat16),
            jax.ShapeDtypeStruct((blocks, LANES, LANES), jnp.float32),
            jax.ShapeDtypeStruct((blocks, LANES, LANES), jnp.float32),
        ],
        compiler_params=pltpu.CompilerParams(vmem_limit_bytes=VMEM_LIMIT),
        name="pack",
    )(info, wavefunction, wavefunction, diagonal)


def mixing_kernel(*refs):
    sources, out_ref = refs[:-1], refs[-1]
    spread = (
        lax.broadcasted_iota(jnp.int32, (PHYS, LANES), 1) // SUB
        == lax.broadcasted_iota(jnp.int32, (PHYS, LANES), 0)
    ).astype(jnp.bfloat16)
    row = lax.broadcasted_iota(jnp.int32, (LANES, LANES), 0) // PHYS
    column = lax.broadcasted_iota(jnp.int32, (LANES, LANES), 1) % SUB
    same = row == column
    per = sources[0].shape[0] // GROUPS
    at = 0
    for group in range(GROUPS):
        for source in sources:
            for k in range(per):
                for place, term in enumerate(split_two(source[group * per + k].T)):
                    wide = jnp.dot(term, spread, preferred_element_type=jnp.float32)
                    tall = jnp.concatenate([wide] * SUB, axis=0)
                    out_ref[at, :, place * LANES : (place + 1) * LANES] = jnp.where(
                        same, tall, 0.0
                    ).astype(jnp.bfloat16)
                at += 1


def mixing_operand(sources):
    count = sources[0].shape[0] * len(sources)
    return pl.pallas_call(
        mixing_kernel,
        out_shape=jax.ShapeDtypeStruct((count, LANES, 2 * LANES), jnp.bfloat16),
        compiler_params=pltpu.CompilerParams(vmem_limit_bytes=VMEM_LIMIT),
        name="mixing",
    )(*sources)


def prepare_kernel(info_ref, *refs):
    sources, (left_high, left_low, right_out, blocks_ref) = refs[:-4], refs[-4:]
    zs = 4
    per, blocks, rows, lanes = sources[0].shape
    half = lanes // 2
    first = lane_is_first(half)
    lane = lax.broadcasted_iota(jnp.int32, (half, lanes), 1)
    start = info_ref[0] * 16
    count = lanes // 16
    pairs = [(s, k) for s in range(len(sources) // zs) for k in range(per)]
    for j in range(blocks):
        for base in range(0, len(pairs), count):
            group = pairs[base : base + count]
            columns = jnp.zeros((half, lanes), jnp.float32)
            for at, (s, k) in enumerate(group):
                for z in range(zs):
                    row = pl.multiple_of((info_ref[4] ^ z) * rows, rows)
                    blocks_ref[base + at, j, pl.ds(row, rows), :] = sources[s * zs + z][k, j]
                block = blocks_ref[base + at, j]
                high, low = split_two(jnp.where(first, block, pltpu.roll(block, half, 1)))
                left_high[base + at, j] = high
                left_low[base + at, j] = low
                shift = lax.rem(16 * at + lanes + half - start, lanes)
                columns = jnp.where(lane // 16 == at, pltpu.roll(block, shift, 1), columns)
            upright = columns.T[: 16 * len(group)]
            high, low = split_two(upright)
            where = pl.ds(16 * base, 16 * len(group))
            right_out[j, where, 0:lanes] = jnp.concatenate([high, high], axis=1)
            right_out[j, where, lanes : 2 * lanes] = jnp.concatenate([low, low], axis=1)


def prepare(info, sources):
    per, blocks, rows, lanes = sources[0].shape
    total = per * len(sources) // 4
    half = lanes // 2
    step = 2
    return pl.pallas_call(
        prepare_kernel,
        grid_spec=pltpu.PrefetchScalarGridSpec(
            num_scalar_prefetch=1,
            grid=(blocks // step,),
            in_specs=[
                pl.BlockSpec((per, step, rows, lanes), lambda i, *_: (0, i, 0, 0))
                for _ in sources
            ],
            out_specs=[
                pl.BlockSpec((total, step, half, lanes), lambda i, *_: (0, i, 0, 0)),
                pl.BlockSpec((total, step, half, lanes), lambda i, *_: (0, i, 0, 0)),
                pl.BlockSpec((step, total * 16, 2 * lanes), lambda i, *_: (i, 0, 0)),
            ],
            scratch_shapes=[pltpu.VMEM((total, step, half, lanes), jnp.float32)],
        ),
        out_shape=[
            jax.ShapeDtypeStruct((total, blocks, half, lanes), jnp.bfloat16),
            jax.ShapeDtypeStruct((total, blocks, half, lanes), jnp.bfloat16),
            jax.ShapeDtypeStruct((blocks, total * 16, 2 * lanes), jnp.bfloat16),
        ],
        compiler_params=pltpu.CompilerParams(vmem_limit_bytes=VMEM_LIMIT),
        name="prepare",
    )(info, *sources)


def apply_kernel(plan, info_ref, *refs):
    groups, parts_given, before_given, pieces = plan
    refs = list(refs)
    take = lambda n: [refs.pop(0) for _ in range(n)]
    slots = take(4)
    vector = take(4 if parts_given else 1)
    operands = [take(4) for _ in groups]
    before = take(1) if before_given else None
    outs = take(4 if pieces else 1)
    total_ref, vec, mid = refs
    step = vector[0].shape[0]
    lanes, half = LANES, LANES // 2
    first = lane_is_first(SUB)
    first_half = lane_is_first(half)
    keep_first = jnp.where(first_half, 1.0, 0.0).astype(jnp.bfloat16)
    keep_second = jnp.where(first_half, 0.0, 1.0).astype(jnp.bfloat16)
    me = info_ref[4]

    @pl.when(pl.program_id(0) == 0)
    def _():
        total_ref[...] = before[0][...] if before_given else jnp.zeros_like(total_ref)

    for j in range(step):
        if parts_given:

            def put(row, pair, high, low):
                columns = slice(pair * lanes, (pair + 1) * lanes)
                vec[j, pl.ds(row, 16), columns] = high
                vec[j, pl.ds(row + half, 16), columns] = low

            rows_of = [pl.multiple_of(info_ref[g] * 16, 16) for g in range(4)]
            store_vector(vector, j, rows_of, put)
            source = vec[j]
        else:
            source = vector[0][j]
        source = jnp.concatenate([source, source], axis=0)
        at = 0
        for left_high, left_low, right, mix in operands:
            count = right.shape[1]
            mid[j, at : at + count, :] = jnp.dot(
                right[j], source, preferred_element_type=jnp.float32
            )
            at += count

    def one_bond(refs_of, w, slot_of, base):
        left_high, left_low, right, mix = refs_of
        highs, lows = [], []
        for j in range(step):
            row = pl.multiple_of((base + w) * 16, 16)
            tiles = []
            for pair in range(PHYS // 2):
                columns = slice(pair * lanes, (pair + 1) * lanes)
                upper = mid[j, pl.ds(row, SUB), columns]
                lower = mid[j, pl.ds(row + SUB, SUB), columns]
                tiles.append(jnp.where(first, upper, pltpu.roll(lower, half, 1)))
                tiles.append(jnp.where(first, pltpu.roll(upper, half, 1), lower))
            t_high, t_low = split_two(jnp.concatenate(tiles, axis=0))
            lh, ll = left_high[w, j], left_low[w, j]
            wide_high = jnp.concatenate([lh * keep_first, lh * keep_second], axis=0)
            wide_low = jnp.concatenate([ll * keep_first, ll * keep_second], axis=0)
            z = jnp.dot(
                jnp.concatenate([t_high, t_low], axis=1),
                jnp.concatenate([wide_high, wide_high], axis=0),
                preferred_element_type=jnp.float32,
            ) + jnp.dot(t_high, wide_low, preferred_element_type=jnp.float32)
            z_high, z_low = split_two(z)
            highs.append(z_high)
            lows.append(z_low)
        z_high = jnp.concatenate(highs, axis=1)
        z_low = jnp.concatenate(lows, axis=1)
        mix_high = mix[w, :, 0:lanes]
        mix_low = mix[w, :, lanes:]
        mixed = jnp.dot(
            jnp.concatenate([mix_high, mix_high], axis=1),
            jnp.concatenate([z_high, z_low], axis=0),
            preferred_element_type=jnp.float32,
        ) + jnp.dot(mix_low, z_high, preferred_element_type=jnp.float32)
        for j in range(step):
            slot = slot_of(pl.program_id(0) * step + j)
            slot = ((slot >> 1) ^ me) * 2 + (slot & 1)
            total_ref[slot] += mixed[:, j * lanes : (j + 1) * lanes]

    base = 0
    for group, refs_of in zip(groups, operands):
        count = refs_of[0].shape[0]
        per = count // 4
        for s in range(4):
            table = slots[s]

            def some(k, carry):
                one_bond(
                    refs_of, s * per + k, lambda j: table[group * per + k, j], base
                )
                return carry

            for k in range(per):
                some(k, 0)
        base += count

    @pl.when(pl.program_id(0) == pl.num_programs(0) - 1)
    def _():
        if pieces:
            for k in range(4):
                outs[k][...] = total_ref[2 * k : 2 * k + 2]
        else:
            outs[0][...] = total_ref[...]


def apply_bonds(info, slots, vector, groups, operands, mixing, before, pieces):
    blocks, half, lanes = operands[0][0].shape[1:]
    counts = [x[0].shape[0] for x in operands]
    per_group = mixing.shape[0] // GROUPS
    step = 2
    flops = 2 * blocks * sum(counts) * SUB * lanes * (3 * lanes * 16 * 3)
    in_specs = [pl.BlockSpec((step,) + x.shape[1:], lambda i, *_: (i, 0, 0)) for x in vector]
    arguments = list(vector)
    for group, (left_high, left_low, right), count in zip(groups, operands, counts):
        in_specs += [
            pl.BlockSpec((count, step, half, lanes), lambda i, *_: (0, i, 0, 0)),
            pl.BlockSpec((count, step, half, lanes), lambda i, *_: (0, i, 0, 0)),
            pl.BlockSpec((step,) + right.shape[1:], lambda i, *_: (i, 0, 0)),
            pl.BlockSpec((per_group,) + mixing.shape[1:], lambda i, *_, g=group: (g, 0, 0)),
        ]
        arguments += [left_high, left_low, right, mixing]
    if before is not None:
        in_specs.append(whole(*before.shape))
        arguments.append(before)
    shapes = [(2, lanes, lanes)] * 4 if pieces else [(8, lanes, lanes)]
    plan = (tuple(groups), len(vector) == 4, before is not None, pieces)
    return pl.pallas_call(
        functools.partial(apply_kernel, plan),
        grid_spec=pltpu.PrefetchScalarGridSpec(
            num_scalar_prefetch=5,
            grid=(blocks // step,),
            in_specs=in_specs,
            out_specs=[whole(*shape) for shape in shapes],
            scratch_shapes=[
                pltpu.VMEM((8, lanes, lanes), jnp.float32),
                pltpu.VMEM((step, lanes, PHYS * half), jnp.bfloat16),
                pltpu.VMEM((step, sum(counts) * 16, PHYS * half), jnp.float32),
            ],
        ),
        out_shape=[jax.ShapeDtypeStruct(shape, jnp.float32) for shape in shapes],
        compiler_params=pltpu.CompilerParams(vmem_limit_bytes=VMEM_LIMIT),
        cost_estimate=pl.CostEstimate(
            flops=flops, bytes_accessed=12 * 1024 * 1024, transcendentals=0
        ),
        name="apply_bonds",
    )(info, *slots, *arguments)


def folded(x):
    return jnp.sum(x.reshape(-1, SUB, LANES), axis=0)


def add_arrived(info_ref, owner_ref, arrived, total):
    for k in range(4):
        for i in range(2):
            total[owner_ref[info_ref[4] ^ k, i]] += arrived[k][i]


def image_kernel(info_ref, owner_ref, a0, a1, a2, a3, diag_ref, own_ref, image_ref, sums_ref):
    image_ref[...] = diag_ref[...] * own_ref[...]
    add_arrived(info_ref, owner_ref, (a0, a1, a2, a3), image_ref)
    own = own_ref[...]
    sums_ref[0:SUB] = folded(own * image_ref[...])
    sums_ref[SUB:] = folded(own * own)


def owner_image(info, owners, arrived, diagonal, own):
    return pl.pallas_call(
        image_kernel,
        grid_spec=pltpu.PrefetchScalarGridSpec(
            num_scalar_prefetch=2,
            grid=(1,),
            in_specs=[whole(*x.shape) for x in (*arrived, diagonal, own)],
            out_specs=[whole(*own.shape), whole(2 * SUB, LANES)],
        ),
        out_shape=[
            jax.ShapeDtypeStruct(own.shape, jnp.float32),
            jax.ShapeDtypeStruct((2 * SUB, LANES), jnp.float32),
        ],
        compiler_params=pltpu.CompilerParams(vmem_limit_bytes=VMEM_LIMIT),
        name="owner_image",
    )(info, owners, *arrived, diagonal, own)


def scalars_of(sums, entries):
    cross = jnp.sum(sums[0:SUB], keepdims=True) / entries
    square = jnp.sum(sums[SUB:], keepdims=True) / entries
    scale = lax.rsqrt(square + 1e-06)
    return scale, cross * scale * scale


def residual_kernel(entries, sums_ref, image_ref, own_ref, first_ref, resid_ref):
    scale, rayleigh = scalars_of(sums_ref[...], entries)
    total = jnp.zeros((SUB, LANES), jnp.float32)
    for k in range(image_ref.shape[0]):
        image = image_ref[k]
        residual = scale * (image - rayleigh * own_ref[k])
        total += folded(residual * residual)
        first_ref[k] = unpack_tile(scale * image)
    resid_ref[...] = total


def first_outputs(sums, image, own, entries):
    blocks = image.shape[0]
    return pl.pallas_call(
        functools.partial(residual_kernel, entries),
        out_shape=[
            jax.ShapeDtypeStruct((blocks, LANES // 2, 2 * LANES), jnp.float32),
            jax.ShapeDtypeStruct((SUB, LANES), jnp.float32),
        ],
        compiler_params=pltpu.CompilerParams(vmem_limit_bytes=VMEM_LIMIT),
        name="first_outputs",
    )(sums, image, own)


def final_kernel(
    entries, info_ref, owner_ref, a0, a1, a2, a3, diag_ref, own_ref, image_ref, sums_ref, resid_ref,
    vector_ref, second_ref, total,
):
    scale, rayleigh = scalars_of(sums_ref[...], entries)
    mean = jnp.sum(resid_ref[...], keepdims=True) / entries
    scale = scale * lax.rsqrt(mean + 1e-06)
    total[...] = (diag_ref[...] - rayleigh) * image_ref[...]
    add_arrived(info_ref, owner_ref, (a0, a1, a2, a3), total)
    for k in range(image_ref.shape[0]):
        vector_ref[k] = unpack_tile(scale * (image_ref[k] - rayleigh * own_ref[k]))
        second_ref[k] = unpack_tile(scale * total[k])


def second_outputs(info, owners, arrived, diagonal, own, image, sums, resid, entries):
    shape = (own.shape[0], LANES // 2, 2 * LANES)
    arguments = (*arrived, diagonal, own, image, sums, resid)
    return pl.pallas_call(
        functools.partial(final_kernel, entries),
        grid_spec=pltpu.PrefetchScalarGridSpec(
            num_scalar_prefetch=2,
            grid=(1,),
            in_specs=[whole(*x.shape) for x in arguments],
            out_specs=[whole(*shape), whole(*shape)],
            scratch_shapes=[pltpu.VMEM(own.shape, jnp.float32)],
        ),
        out_shape=[jax.ShapeDtypeStruct(shape, jnp.float32)] * 2,
        compiler_params=pltpu.CompilerParams(vmem_limit_bytes=VMEM_LIMIT),
        name="second_outputs",
    )(info, owners, *arguments)


def partner(x, axis, k):
    size = lax.axis_size(axis)
    return lax.ppermute(x, axis, [(i, i ^ k) for i in range(size)])


def gathered(x):
    across = partner(x, "mpo", 1)
    return [x, across, partner(x, "rep", 1), partner(across, "rep", 1)]


def summed(x, axes):
    return x + partner(x, axes, 1) + partner(x, axes, 2) + partner(x, axes, 3)


def exchanged(pieces):
    return [pieces[0]] + [partner(pieces[k], "blk", k) for k in range(1, 4)]


def per_device(wavefunction, environment, bond_terms, diagonal, term_slot, slot_block):
    blocks, rows, width = wavefunction.shape
    zs = lax.axis_size("blk")
    mpo, rep, blk = lax.axis_index("mpo"), lax.axis_index("rep"), lax.axis_index("blk")
    place = 2 * mpo + rep
    info = jnp.stack([place, place ^ 2, place ^ 1, place ^ 3, blk]).astype(jnp.int32)
    bonds = environment.shape[0]
    per = bonds // GROUPS
    entries = float(blocks * zs * rows * width)

    by_owner = environment.reshape(bonds, zs, blocks, rows // zs, 2 * rows)
    operands = []
    for group in range(GROUPS):
        mine = by_owner[group * per : (group + 1) * per]
        pieces = exchanged(
            [lax.dynamic_index_in_dim(mine, blk ^ k, 1, keepdims=False) for k in range(4)]
        )
        by_source = list(zip(*[gathered(piece) for piece in pieces]))
        operands.append(prepare(info, [piece for source in by_source for piece in source]))

    mixing = mixing_operand(gathered(bond_terms))
    slots = gathered(term_slot)
    vector, own, diagonal_packed = pack(info, wavefunction, diagonal)

    total = None
    for group in range(GROUPS):
        last = group == GROUPS - 1
        out = apply_bonds(
            info, slots, [vector], [group], [operands[group]], mixing, total, last
        )
        total = None if last else out[0]
    image, sums = owner_image(info, slot_block, exchanged(out), diagonal_packed, own)

    out = apply_bonds(
        info, slots, gathered(image), list(range(GROUPS)), operands, mixing, None, True
    )
    sums = summed(summed(sums, ("mpo", "rep")), "blk")
    first_image, resid = first_outputs(sums, image, own, entries)
    resid = summed(summed(resid, ("mpo", "rep")), "blk")
    second_vector, second_image = second_outputs(
        info, slot_block, exchanged(out), diagonal_packed, own, image, sums, resid, entries
    )
    return (first_image, second_vector, second_image)


def solution(mesh):
    packed = mesh.shape["mpo"] == 2 and mesh.shape["rep"] == 2 and mesh.shape["blk"] == 4
    return jax.shard_map(
        per_device if packed else plain_device,
        mesh=mesh,
        in_specs=(
            P(("grp", "blk"), None, None),
            P(("grp", "mpo", "rep"), None, "blk", None),
            P(("grp", "mpo", "rep"), None, None),
            P(("grp", "blk"), None, ("mpo", "rep")),
            P(("grp", "mpo", "rep"), "blk"),
            P("grp", "blk"),
        ),
        out_specs=(
            P(("grp", "blk"), None, ("mpo", "rep")),
            P(("grp", "blk"), None, ("mpo", "rep")),
            P(("grp", "blk"), None, ("mpo", "rep")),
        ),
        check_vma=False,
    )
```

```python
import functools

import jax
import jax.numpy as jnp
from jax import lax
from jax.experimental import pallas as pl
from jax.experimental.pallas import tpu as pltpu
from jax.sharding import PartitionSpec as P

LANES = 128
SUB = 8
PHYS = 16
TINY = 1e-30
GROUPS = 3
VMEM_LIMIT = 56 * 1024 * 1024


def plain_apply(vector_full, environment, bond_terms, term_slot, slot_block, diagonal):
    block_count, block_rows, block_width = vector_full.shape
    phys_size = bond_terms.shape[-1]
    right_rows = block_width // phys_size
    slot_count = slot_block.shape[0] * slot_block.shape[1]
    blocks = vector_full.reshape(block_count, block_rows, right_rows, phys_size)
    ordered = jnp.transpose(blocks, (0, 3, 1, 2))
    left_env = environment[:, :, :, :block_rows]
    right_env = environment[:, :, :, block_rows:]
    left_done = jnp.einsum("wjab,jsac->wjsbc", left_env, ordered, precision=lax.Precision.HIGHEST)
    right_done = jnp.einsum(
        "wjsbc,wjcd->wjsbd", left_done, right_env, precision=lax.Precision.HIGHEST
    )
    right_done = right_done.reshape(
        environment.shape[0], block_count, phys_size, block_rows * right_rows
    )
    bond_term = jnp.einsum(
        "wjsx,wst->wjtx", right_done, bond_terms, precision=lax.Precision.HIGHEST
    )
    bond_term = bond_term.reshape(environment.shape[0], block_count, block_rows * block_width)
    slot_table = (
        term_slot[:, None, :] == jnp.arange(slot_count, dtype=jnp.int32)[None, :, None]
    ).astype(jnp.float32)
    slot_buffer = jnp.einsum("wsj,wjx->sx", slot_table, bond_term, precision=lax.Precision.HIGHEST)
    slot_buffer = slot_buffer.reshape(slot_count, phys_size, block_rows, right_rows)
    slot_buffer = jnp.transpose(slot_buffer, (0, 2, 3, 1)).reshape(
        slot_count, block_rows, block_width
    )
    owners = slot_block.reshape(-1)
    selector = (owners[None, :] == jnp.arange(block_count, dtype=jnp.int32)[:, None]).astype(
        jnp.float32
    )
    column_width = block_width // lax.axis_size(("mpo", "rep"))
    column_start = lax.axis_index(("mpo", "rep")) * column_width
    own_part = lax.dynamic_slice_in_dim(vector_full, column_start, column_width, 2)
    shares = lax.psum_scatter(slot_buffer, ("mpo", "rep"), scatter_dimension=2, tiled=True)
    arrived = lax.all_to_all(shares, "blk", split_axis=0, concat_axis=0, tiled=True)
    result = jnp.einsum("ks,sbc->kbc", selector, arrived, precision=lax.Precision.HIGHEST)
    return (result + diagonal * own_part, own_part)


def plain_device(wavefunction, environment, bond_terms, diagonal, term_slot, slot_block):
    arranged = lax.all_to_all(environment, "blk", split_axis=1, concat_axis=2, tiled=True)
    entries = float(
        wavefunction.shape[0] * lax.axis_size("blk") * wavefunction.shape[1] * wavefunction.shape[2]
    )
    square_sum = lax.psum(jnp.sum(wavefunction * wavefunction), "blk")
    first_vector = wavefunction * lax.rsqrt(square_sum / entries + 1e-06)
    first_image, first_part = plain_apply(
        first_vector, arranged, bond_terms, term_slot, slot_block, diagonal
    )
    rayleigh = lax.psum(jnp.sum(first_part * first_image), ("blk", "mpo", "rep")) / entries
    residual = first_image - rayleigh * first_part
    resid_sum = lax.psum(jnp.sum(residual * residual), ("blk", "mpo", "rep"))
    second_vector = residual * lax.rsqrt(resid_sum / entries + 1e-06)
    second_full = lax.all_gather(second_vector, ("mpo", "rep"), axis=2, tiled=True)
    second_image, unused = plain_apply(
        second_full, arranged, bond_terms, term_slot, slot_block, diagonal
    )
    return (first_image, second_vector, second_image)


def split_two(x):
    high = x.astype(jnp.bfloat16)
    low = (x - high.astype(jnp.float32)).astype(jnp.bfloat16)
    return high, low


def lane_is_first(rows):
    return lax.broadcasted_iota(jnp.int32, (rows, LANES), 1) < LANES // 2


def micros(count):
    return pl.CostEstimate(flops=count * 1100000000, bytes_accessed=1 << 20, transcendentals=0)


def whole(*shape):
    return pl.BlockSpec(shape, lambda i, *_: (0,) * len(shape))


def pack_tile(x):
    return jnp.concatenate([x[:, :LANES], x[:, LANES:]], axis=0).T


def unpack_tile(x):
    upright = x.T
    return jnp.concatenate([upright[: LANES // 2], upright[LANES // 2 :]], axis=1)


def store_vector(parts, j, rows_of, put):
    first = lane_is_first(SUB)
    for pair in range(PHYS // 2):
        for part, row in zip(parts, rows_of):
            even = part[j, pl.ds(2 * pair, SUB, stride=PHYS), :]
            odd = part[j, pl.ds(2 * pair + 1, SUB, stride=PHYS), :]
            upper = jnp.where(first, even, pltpu.roll(odd, LANES // 2, 1))
            lower = jnp.where(first, pltpu.roll(even, LANES // 2, 1), odd)
            high, low = split_two(jnp.concatenate([upper, lower], axis=0))
            put(row, pair, high, low)


def pack_kernel(info_ref, wave_ref, own_wave_ref, diag_ref, vec_ref, own_ref, diag_out, tiles):
    half = LANES // 2
    for j in range(wave_ref.shape[0]):
        own_ref[j] = pack_tile(own_wave_ref[j])
        diag_out[j] = pack_tile(diag_ref[j])
        for q in range(4):
            tiles[q, j] = pack_tile(wave_ref[j, :, 2 * LANES * q : 2 * LANES * (q + 1)])

        def put(row, pair, high, low):
            columns = slice(pair * LANES, (pair + 1) * LANES)
            vec_ref[j, row : row + 16, columns] = high
            vec_ref[j, row + half : row + half + 16, columns] = low

        store_vector([tiles.at[q] for q in range(4)], j, [16 * q for q in range(4)], put)


def pack(info, wavefunction, diagonal):
    blocks, rows, width = wavefunction.shape
    step = 2
    tile = pl.BlockSpec((step, LANES, LANES), lambda i, *_: (i, 0, 0))
    return pl.pallas_call(
        pack_kernel,
        grid_spec=pltpu.PrefetchScalarGridSpec(
            num_scalar_prefetch=1,
            grid=(blocks // step,),
            in_specs=[
                pl.BlockSpec((step, rows, width), lambda i, *_: (i, 0, 0)),
                pl.BlockSpec((step, rows, width // 4), lambda i, info: (i, 0, info[0])),
                pl.BlockSpec((step, rows, width // 4), lambda i, *_: (i, 0, 0)),
            ],
            out_specs=[pl.BlockSpec((step, LANES, width), lambda i, *_: (i, 0, 0)), tile, tile],
            scratch_shapes=[pltpu.VMEM((4, step, LANES, LANES), jnp.float32)],
        ),
        out_shape=[
            jax.ShapeDtypeStruct((blocks, LANES, width), jnp.bfloat16),
            jax.ShapeDtypeStruct((blocks, LANES, LANES), jnp.float32),
            jax.ShapeDtypeStruct((blocks, LANES, LANES), jnp.float32),
        ],
        compiler_params=pltpu.CompilerParams(vmem_limit_bytes=VMEM_LIMIT),
        name="pack",
    )(info, wavefunction, wavefunction, diagonal)


def mixing_kernel(*refs):
    sources, out_ref = refs[:-1], refs[-1]
    spread = (
        lax.broadcasted_iota(jnp.int32, (PHYS, LANES), 1) // SUB
        == lax.broadcasted_iota(jnp.int32, (PHYS, LANES), 0)
    ).astype(jnp.bfloat16)
    row = lax.broadcasted_iota(jnp.int32, (LANES, LANES), 0) // PHYS
    column = lax.broadcasted_iota(jnp.int32, (LANES, LANES), 1) % SUB
    same = row == column
    per = sources[0].shape[0] // GROUPS
    at = 0
    for group in range(GROUPS):
        for source in sources:
            for k in range(per):
                for place, term in enumerate(split_two(source[group * per + k].T)):
                    wide = jnp.dot(term, spread, preferred_element_type=jnp.float32)
                    tall = jnp.concatenate([wide] * SUB, axis=0)
                    out_ref[at, :, place * LANES : (place + 1) * LANES] = jnp.where(
                        same, tall, 0.0
                    ).astype(jnp.bfloat16)
                at += 1


def mixing_operand(sources):
    count = sources[0].shape[0] * len(sources)
    return pl.pallas_call(
        mixing_kernel,
        out_shape=jax.ShapeDtypeStruct((count, LANES, 2 * LANES), jnp.bfloat16),
        compiler_params=pltpu.CompilerParams(vmem_limit_bytes=VMEM_LIMIT),
        name="mixing",
    )(*sources)


def prepare_kernel(info_ref, *refs):
    sources, (left_high, left_low, right_out, blocks_ref) = refs[:-4], refs[-4:]
    zs = 4
    per, blocks, rows, lanes = sources[0].shape
    half = lanes // 2
    wide = half // 2
    first = lane_is_first(half)
    lane = lax.broadcasted_iota(jnp.int32, (half, lanes), 1)
    start = info_ref[6] * wide
    count = lanes // wide
    pairs = [(s, k) for s in range(len(sources) // zs) for k in range(per)]
    for j in range(blocks):
        for base in range(0, len(pairs), count):
            group = pairs[base : base + count]
            columns = jnp.zeros((half, lanes), jnp.float32)
            for at, (s, k) in enumerate(group):
                for z in range(zs):
                    row = pl.multiple_of((info_ref[4] ^ z) * rows, rows)
                    blocks_ref[base + at, j, pl.ds(row, rows), :] = sources[s * zs + z][k, j]
                block = blocks_ref[base + at, j]
                high, low = split_two(jnp.where(first, block, pltpu.roll(block, half, 1)))
                left_high[base + at, j] = high
                left_low[base + at, j] = low
                shift = lax.rem(wide * at + lanes + half - start, lanes)
                columns = jnp.where(lane // wide == at, pltpu.roll(block, shift, 1), columns)
            upright = columns.T[: wide * len(group)]
            high, low = split_two(upright)
            where = pl.ds(wide * base, wide * len(group))
            right_out[j, where, 0:lanes] = jnp.concatenate([high, high], axis=1)
            right_out[j, where, lanes : 2 * lanes] = jnp.concatenate([low, low], axis=1)


def prepare(info, sources):
    per, blocks, rows, lanes = sources[0].shape
    total = per * len(sources) // 4
    half = lanes // 2
    step = 2
    return pl.pallas_call(
        prepare_kernel,
        grid_spec=pltpu.PrefetchScalarGridSpec(
            num_scalar_prefetch=1,
            grid=(blocks // step,),
            in_specs=[
                pl.BlockSpec((per, step, rows, lanes), lambda i, *_: (0, i, 0, 0))
                for _ in sources
            ],
            out_specs=[
                pl.BlockSpec((total, step, half, lanes), lambda i, *_: (0, i, 0, 0)),
                pl.BlockSpec((total, step, half, lanes), lambda i, *_: (0, i, 0, 0)),
                pl.BlockSpec((step, total * 32, 2 * lanes), lambda i, *_: (i, 0, 0)),
            ],
            scratch_shapes=[pltpu.VMEM((total, step, half, lanes), jnp.float32)],
        ),
        out_shape=[
            jax.ShapeDtypeStruct((total, blocks, half, lanes), jnp.bfloat16),
            jax.ShapeDtypeStruct((total, blocks, half, lanes), jnp.bfloat16),
            jax.ShapeDtypeStruct((blocks, total * 32, 2 * lanes), jnp.bfloat16),
        ],
        compiler_params=pltpu.CompilerParams(vmem_limit_bytes=VMEM_LIMIT),
        cost_estimate=micros(3),
        name="prepare",
    )(info, *sources)


def apply_kernel(plan, info_ref, *refs):
    groups, parts_given, before_given, pieces = plan
    refs = list(refs)
    take = lambda n: [refs.pop(0) for _ in range(n)]
    slots = take(2)
    vector = take(4 if parts_given else 1)
    operands = [take(4) for _ in groups]
    before = take(1) if before_given else None
    outs = take(2 if pieces else 1)
    total_ref, vec, mid = refs
    step = vector[0].shape[0]
    lanes, half = LANES, LANES // 2
    first = lane_is_first(SUB)
    first_half = lane_is_first(half)
    keep_first = jnp.where(first_half, 1.0, 0.0).astype(jnp.bfloat16)
    keep_second = jnp.where(first_half, 0.0, 1.0).astype(jnp.bfloat16)
    me = info_ref[4]

    @pl.when(pl.program_id(0) == 0)
    def _():
        total_ref[...] = before[0][...] if before_given else jnp.zeros_like(total_ref)

    for j in range(step):
        if parts_given:

            def put(row, pair, high, low):
                columns = slice(pair * lanes, (pair + 1) * lanes)
                vec[j, pl.ds(row, 16), columns] = high
                vec[j, pl.ds(row + half, 16), columns] = low

            rows_of = [pl.multiple_of(info_ref[g] * 16, 16) for g in range(4)]
            store_vector(vector, j, rows_of, put)
            source = vec[j]
        else:
            source = vector[0][j]
        source = jnp.concatenate([source, source], axis=0)
        at = 0
        for left_high, left_low, right, mix in operands:
            count = right.shape[1]
            mid[j, at : at + count, :] = jnp.dot(
                right[j], source, preferred_element_type=jnp.float32
            )
            at += count

    def left_and_right(refs_of, w, base):
        left_high, left_low, right, mix = refs_of
        done = {}
        for j in range(step):
            tiles = []
            for part in range(2):
                row = (base + w) * 32 + part * 16
                for pair in range(PHYS // 2):
                    columns = slice(pair * lanes, (pair + 1) * lanes)
                    upper = mid[j, row : row + SUB, columns]
                    lower = mid[j, row + SUB : row + 2 * SUB, columns]
                    tiles.append(jnp.where(first, upper, pltpu.roll(lower, half, 1)))
                    tiles.append(jnp.where(first, pltpu.roll(upper, half, 1), lower))
            t_high, t_low = split_two(jnp.concatenate(tiles, axis=0))
            lh, ll = left_high[w, j], left_low[w, j]
            wide_high = jnp.concatenate([lh * keep_first, lh * keep_second], axis=0)
            wide_low = jnp.concatenate([ll * keep_first, ll * keep_second], axis=0)
            z = jnp.dot(
                jnp.concatenate([t_high, t_low], axis=1),
                jnp.concatenate([wide_high, wide_high], axis=0),
                preferred_element_type=jnp.float32,
            ) + jnp.dot(t_high, wide_low, preferred_element_type=jnp.float32)
            z_high, z_low = split_two(z)
            for part in range(2):
                rows = slice(part * lanes, (part + 1) * lanes)
                done[part, j] = (z_high[rows], z_low[rows])
        order = [(part, j) for part in range(2) for j in range(step)]
        return [jnp.concatenate([done[at][i] for at in order], axis=1) for i in range(2)]

    def mix_and_add(refs_of, w, z, slot_of):
        z_high, z_low = z
        mix = refs_of[3]
        mix_high = mix[w, :, 0:lanes]
        mix_low = mix[w, :, lanes:]
        mixed = jnp.dot(
            jnp.concatenate([mix_high, mix_high], axis=1),
            jnp.concatenate([z_high, z_low], axis=0),
            preferred_element_type=jnp.float32,
        ) + jnp.dot(mix_low, z_high, preferred_element_type=jnp.float32)
        for j in range(step):
            slot = slot_of(pl.program_id(0) * step + j)
            slot = ((slot >> 1) ^ me) * 2 + (slot & 1)
            for part in range(2):
                at = part * step + j
                total_ref[part, slot] += mixed[:, at * lanes : (at + 1) * lanes]

    base = 0
    waiting = None
    for group, refs_of in zip(groups, operands):
        count = refs_of[0].shape[0]
        per = count // 2
        for w in range(count):
            z = left_and_right(refs_of, w, base)
            if waiting is not None:
                mix_and_add(*waiting)
            table, bond = slots[w // per], group * per + w % per
            waiting = (refs_of, w, z, lambda j, table=table, bond=bond: table[bond, j])
        base += count
    mix_and_add(*waiting)

    @pl.when(pl.program_id(0) == pl.num_programs(0) - 1)
    def _():
        if pieces:
            outs[0][...] = total_ref[info_ref[5]]
            outs[1][...] = total_ref[1 - info_ref[5]]
        else:
            outs[0][...] = total_ref[...]


def apply_bonds(info, slots, vector, groups, operands, mixing, before, pieces):
    blocks, half, lanes = operands[0][0].shape[1:]
    counts = [x[0].shape[0] for x in operands]
    per_group = mixing.shape[0] // GROUPS
    step = 2
    in_specs = [pl.BlockSpec((step,) + x.shape[1:], lambda i, *_: (i, 0, 0)) for x in vector]
    arguments = list(vector)
    for group, (left_high, left_low, right), count in zip(groups, operands, counts):
        in_specs += [
            pl.BlockSpec((count, step, half, lanes), lambda i, *_: (0, i, 0, 0)),
            pl.BlockSpec((count, step, half, lanes), lambda i, *_: (0, i, 0, 0)),
            pl.BlockSpec((step,) + right.shape[1:], lambda i, *_: (i, 0, 0)),
            pl.BlockSpec((per_group,) + mixing.shape[1:], lambda i, *_, g=group: (g, 0, 0)),
        ]
        arguments += [left_high, left_low, right, mixing]
    if before is not None:
        in_specs.append(whole(*before.shape))
        arguments.append(before)
    shapes = [(8, lanes, lanes)] * 2 if pieces else [(2, 8, lanes, lanes)]
    plan = (tuple(groups), len(vector) == 4, before is not None, pieces)
    return pl.pallas_call(
        functools.partial(apply_kernel, plan),
        grid_spec=pltpu.PrefetchScalarGridSpec(
            num_scalar_prefetch=3,
            grid=(blocks // step,),
            in_specs=in_specs,
            out_specs=[whole(*shape) for shape in shapes],
            scratch_shapes=[
                pltpu.VMEM((2, 8, lanes, lanes), jnp.float32),
                pltpu.VMEM((step, lanes, PHYS * half), jnp.bfloat16),
                pltpu.VMEM((step, sum(counts) * 32, PHYS * half), jnp.float32),
            ],
        ),
        out_shape=[jax.ShapeDtypeStruct(shape, jnp.float32) for shape in shapes],
        compiler_params=pltpu.CompilerParams(vmem_limit_bytes=VMEM_LIMIT),
        cost_estimate=micros(2 * sum(counts)),
        name="apply_bonds",
    )(info, *slots, *arguments)


def add_arrived(info_ref, owner_ref, arrived, total):
    for k in range(4):
        for i in range(2):
            total[owner_ref[info_ref[4] ^ k, i]] += arrived[k][i]


def stacked_rows(*rows):
    at = lax.broadcasted_iota(jnp.int32, (SUB, LANES), 0)
    tile = jnp.zeros((SUB, LANES), jnp.float32)
    for i, row in enumerate(rows):
        tile = jnp.where(at == i, row, tile)
    return tile


def merged(tiles):
    rows = [[tile[i : i + 1] for i in range(3)] for tile in tiles]
    cross = sum(row[0] for row in rows)
    square = sum(row[1] for row in rows)
    ratio = cross / jnp.maximum(square, TINY)
    apart = [
        (row[0] / jnp.maximum(row[1], TINY) - ratio) * jnp.sqrt(row[1]) for row in rows
    ]
    rest = sum(row[2] for row in rows) + sum(x * x for x in apart)
    return cross, square, rest


def image_kernel(info_ref, owner_ref, a0, a1, a2, a3, diag_ref, own_ref, image_ref, stats_ref):
    image_ref[...] = diag_ref[...] * own_ref[...]
    add_arrived(info_ref, owner_ref, (a0, a1, a2, a3), image_ref)
    blocks = image_ref.shape[0]
    cross = jnp.zeros((LANES, LANES), jnp.float32)
    square = jnp.zeros((LANES, LANES), jnp.float32)
    for k in range(blocks):
        own = own_ref[k]
        cross += own * image_ref[k]
        square += own * own
    cross = jnp.sum(cross, keepdims=True)
    square = jnp.sum(square, keepdims=True)
    ratio = cross / jnp.maximum(square, TINY)
    rest = jnp.zeros((LANES, LANES), jnp.float32)
    for k in range(blocks):
        apart = image_ref[k] - ratio * own_ref[k]
        rest += apart * apart
    stats_ref[...] = stacked_rows(cross, square, jnp.sum(rest, keepdims=True))


def owner_image(info, owners, arrived, diagonal, own):
    return pl.pallas_call(
        image_kernel,
        grid_spec=pltpu.PrefetchScalarGridSpec(
            num_scalar_prefetch=2,
            grid=(1,),
            in_specs=[whole(*x.shape) for x in (*arrived, diagonal, own)],
            out_specs=[whole(*own.shape), whole(SUB, LANES)],
        ),
        out_shape=[
            jax.ShapeDtypeStruct(own.shape, jnp.float32),
            jax.ShapeDtypeStruct((SUB, LANES), jnp.float32),
        ],
        compiler_params=pltpu.CompilerParams(vmem_limit_bytes=VMEM_LIMIT),
        cost_estimate=micros(3),
        name="owner_image",
    )(info, owners, *arrived, diagonal, own)


def merge_kernel(*refs):
    refs[-1][...] = stacked_rows(*merged([ref[...] for ref in refs[:-1]]))


def merge(tiles):
    return pl.pallas_call(
        merge_kernel,
        out_shape=jax.ShapeDtypeStruct((SUB, LANES), jnp.float32),
        cost_estimate=micros(1),
        name="merge",
    )(*tiles)


def scales_of(tiles, entries):
    cross, square, rest = merged(tiles)
    scale = lax.rsqrt(square / entries + 1e-06)
    rayleigh = scale * scale * (cross / entries)
    apart = (cross / jnp.maximum(square, TINY) - rayleigh) * jnp.sqrt(square)
    mean = scale * scale * ((rest + apart * apart) / entries)
    return scale, rayleigh, scale * lax.rsqrt(mean + 1e-06)


def first_kernel(entries, s0, s1, s2, s3, image_ref, own_ref, first_ref, second_ref):
    tiles = [ref[...] for ref in (s0, s1, s2, s3)]
    scale, rayleigh, second_scale = scales_of(tiles, entries)
    for k in range(image_ref.shape[0]):
        image = image_ref[k]
        first_ref[k] = unpack_tile(scale * image)
        second_ref[k] = unpack_tile(second_scale * (image - rayleigh * own_ref[k]))


def first_outputs(stats, image, own, entries):
    blocks = image.shape[0]
    shape = jax.ShapeDtypeStruct((blocks, LANES // 2, 2 * LANES), jnp.float32)
    return pl.pallas_call(
        functools.partial(first_kernel, entries),
        out_shape=[shape, shape],
        compiler_params=pltpu.CompilerParams(vmem_limit_bytes=VMEM_LIMIT),
        cost_estimate=micros(3),
        name="first_outputs",
    )(*stats, image, own)


def final_kernel(
    entries, info_ref, owner_ref, a0, a1, a2, a3, diag_ref, image_ref, s0, s1, s2, s3,
    second_ref, total,
):
    tiles = [ref[...] for ref in (s0, s1, s2, s3)]
    scale, rayleigh, second_scale = scales_of(tiles, entries)
    for k in range(image_ref.shape[0]):
        total[k] = (diag_ref[k] - rayleigh) * image_ref[k]
    add_arrived(info_ref, owner_ref, (a0, a1, a2, a3), total)
    for k in range(image_ref.shape[0]):
        second_ref[k] = unpack_tile(second_scale * total[k])


def second_output(info, owners, arrived, diagonal, image, stats, entries):
    shape = (image.shape[0], LANES // 2, 2 * LANES)
    arguments = (*arrived, diagonal, image, *stats)
    return pl.pallas_call(
        functools.partial(final_kernel, entries),
        grid_spec=pltpu.PrefetchScalarGridSpec(
            num_scalar_prefetch=2,
            grid=(1,),
            in_specs=[whole(*x.shape) for x in arguments],
            out_specs=whole(*shape),
            scratch_shapes=[pltpu.VMEM(image.shape, jnp.float32)],
        ),
        out_shape=jax.ShapeDtypeStruct(shape, jnp.float32),
        compiler_params=pltpu.CompilerParams(vmem_limit_bytes=VMEM_LIMIT),
        cost_estimate=micros(3),
        name="second_output",
    )(info, owners, *arguments)


def partner(x, axis, k):
    size = lax.axis_size(axis)
    return lax.ppermute(x, axis, [(i, i ^ k) for i in range(size)])


def after(x, *others):
    return lax.optimization_barrier((x, *others))[0]


def gathered(x):
    across = partner(x, "mpo", 1)
    return [x, across, partner(x, "rep", 1), partner(across, "rep", 1)]


def everyone(x, axes):
    return [x] + [partner(x, axes, k) for k in range(1, 4)]


def to_owners(mine, theirs):
    other = partner(theirs, "rep", 1)
    pieces = [mine[2 * k : 2 * k + 2] + other[2 * k : 2 * k + 2] for k in range(4)]
    return [pieces[0]] + [partner(pieces[k], "blk", k) for k in range(1, 4)]


def per_device(wavefunction, environment, bond_terms, diagonal, term_slot, slot_block):
    blocks, rows, width = wavefunction.shape
    zs = lax.axis_size("blk")
    mpo, rep, blk = lax.axis_index("mpo"), lax.axis_index("rep"), lax.axis_index("blk")
    place = 2 * mpo + rep
    info = jnp.stack([place, place ^ 2, place ^ 1, place ^ 3, blk, rep, mpo]).astype(jnp.int32)
    bonds = environment.shape[0]
    per = bonds // GROUPS
    entries = float(blocks * zs * rows * width)

    vector, own, diagonal_packed = pack(info, wavefunction, diagonal)
    mixing = mixing_operand([bond_terms, partner(bond_terms, "mpo", 1)])
    slots = [term_slot, partner(term_slot, "mpo", 1)]

    by_owner = environment.reshape(bonds, zs, blocks, rows // zs, 2 * rows)
    operands = []
    arrived = [None] * 4
    for group in range(GROUPS):
        mine = by_owner[group * per : (group + 1) * per]
        pieces = []
        for k in range(4):
            piece = lax.dynamic_index_in_dim(mine, blk ^ k, 1, keepdims=False)
            if k:
                if arrived[k] is not None:
                    piece = after(piece, arrived[k])
                piece = arrived[k] = partner(piece, "blk", k)
            pieces.append(piece)
        operands.append(prepare(info, pieces + [partner(piece, "mpo", 1) for piece in pieces]))

    total = None
    for group in range(GROUPS):
        last = group == GROUPS - 1
        out = apply_bonds(
            info, slots, [vector], [group], [operands[group]], mixing, total, last
        )
        total = None if last else out[0]
    image, stats = owner_image(info, slot_block, to_owners(*out), diagonal_packed, own)

    stats = everyone(stats, ("mpo", "rep"))
    parts = gathered(image)
    parts[0] = after(parts[0], *stats)
    out = apply_bonds(info, slots, parts, list(range(GROUPS)), operands, mixing, None, True)
    stats = everyone(merge([after(x, out[1]) for x in stats]), "blk")
    first_image, second_vector = first_outputs(stats, image, own, entries)
    second_image = second_output(
        info, slot_block, to_owners(*out), diagonal_packed, image, stats, entries
    )
    return (first_image, second_vector, second_image)


def solution(mesh):
    packed = mesh.shape["mpo"] == 2 and mesh.shape["rep"] == 2 and mesh.shape["blk"] == 4
    return jax.shard_map(
        per_device if packed else plain_device,
        mesh=mesh,
        in_specs=(
            P(("grp", "blk"), None, None),
            P(("grp", "mpo", "rep"), None, "blk", None),
            P(("grp", "mpo", "rep"), None, None),
            P(("grp", "blk"), None, ("mpo", "rep")),
            P(("grp", "mpo", "rep"), "blk"),
            P("grp", "blk"),
        ),
        out_specs=(
            P(("grp", "blk"), None, ("mpo", "rep")),
            P(("grp", "blk"), None, ("mpo", "rep")),
            P(("grp", "blk"), None, ("mpo", "rep")),
        ),
        check_vma=False,
    )
```

```python
import functools

import jax
import jax.numpy as jnp
from jax import lax
from jax.experimental import pallas as pl
from jax.experimental.pallas import tpu as pltpu
from jax.sharding import PartitionSpec as P

LANES = 128
SUB = 8
PHYS = 16
TINY = 1e-30
GROUPS = 2
VMEM_LIMIT = 62 * 1024 * 1024


def plain_apply(vector_full, environment, bond_terms, term_slot, slot_block, diagonal):
    block_count, block_rows, block_width = vector_full.shape
    phys_size = bond_terms.shape[-1]
    right_rows = block_width // phys_size
    slot_count = slot_block.shape[0] * slot_block.shape[1]
    blocks = vector_full.reshape(block_count, block_rows, right_rows, phys_size)
    ordered = jnp.transpose(blocks, (0, 3, 1, 2))
    left_env = environment[:, :, :, :block_rows]
    right_env = environment[:, :, :, block_rows:]
    left_done = jnp.einsum("wjab,jsac->wjsbc", left_env, ordered, precision=lax.Precision.HIGHEST)
    right_done = jnp.einsum(
        "wjsbc,wjcd->wjsbd", left_done, right_env, precision=lax.Precision.HIGHEST
    )
    right_done = right_done.reshape(
        environment.shape[0], block_count, phys_size, block_rows * right_rows
    )
    bond_term = jnp.einsum(
        "wjsx,wst->wjtx", right_done, bond_terms, precision=lax.Precision.HIGHEST
    )
    bond_term = bond_term.reshape(environment.shape[0], block_count, block_rows * block_width)
    slot_table = (
        term_slot[:, None, :] == jnp.arange(slot_count, dtype=jnp.int32)[None, :, None]
    ).astype(jnp.float32)
    slot_buffer = jnp.einsum("wsj,wjx->sx", slot_table, bond_term, precision=lax.Precision.HIGHEST)
    slot_buffer = slot_buffer.reshape(slot_count, phys_size, block_rows, right_rows)
    slot_buffer = jnp.transpose(slot_buffer, (0, 2, 3, 1)).reshape(
        slot_count, block_rows, block_width
    )
    owners = slot_block.reshape(-1)
    selector = (owners[None, :] == jnp.arange(block_count, dtype=jnp.int32)[:, None]).astype(
        jnp.float32
    )
    column_width = block_width // lax.axis_size(("mpo", "rep"))
    column_start = lax.axis_index(("mpo", "rep")) * column_width
    own_part = lax.dynamic_slice_in_dim(vector_full, column_start, column_width, 2)
    shares = lax.psum_scatter(slot_buffer, ("mpo", "rep"), scatter_dimension=2, tiled=True)
    arrived = lax.all_to_all(shares, "blk", split_axis=0, concat_axis=0, tiled=True)
    result = jnp.einsum("ks,sbc->kbc", selector, arrived, precision=lax.Precision.HIGHEST)
    return (result + diagonal * own_part, own_part)


def plain_device(wavefunction, environment, bond_terms, diagonal, term_slot, slot_block):
    arranged = lax.all_to_all(environment, "blk", split_axis=1, concat_axis=2, tiled=True)
    entries = float(
        wavefunction.shape[0] * lax.axis_size("blk") * wavefunction.shape[1] * wavefunction.shape[2]
    )
    square_sum = lax.psum(jnp.sum(wavefunction * wavefunction), "blk")
    first_vector = wavefunction * lax.rsqrt(square_sum / entries + 1e-06)
    first_image, first_part = plain_apply(
        first_vector, arranged, bond_terms, term_slot, slot_block, diagonal
    )
    rayleigh = lax.psum(jnp.sum(first_part * first_image), ("blk", "mpo", "rep")) / entries
    residual = first_image - rayleigh * first_part
    resid_sum = lax.psum(jnp.sum(residual * residual), ("blk", "mpo", "rep"))
    second_vector = residual * lax.rsqrt(resid_sum / entries + 1e-06)
    second_full = lax.all_gather(second_vector, ("mpo", "rep"), axis=2, tiled=True)
    second_image, unused = plain_apply(
        second_full, arranged, bond_terms, term_slot, slot_block, diagonal
    )
    return (first_image, second_vector, second_image)


def split_two(x):
    high = x.astype(jnp.bfloat16)
    low = (x - high.astype(jnp.float32)).astype(jnp.bfloat16)
    return high, low


def lane_is_first(rows):
    return lax.broadcasted_iota(jnp.int32, (rows, LANES), 1) < LANES // 2


def micros(count):
    return pl.CostEstimate(flops=count * 1100000000, bytes_accessed=1 << 20, transcendentals=0)


def whole(*shape):
    return pl.BlockSpec(shape, lambda i, *_: (0,) * len(shape))


def pack_tile(x):
    return jnp.concatenate([x[:, :LANES], x[:, LANES:]], axis=0).T


def unpack_tile(x):
    upright = x.T
    return jnp.concatenate([upright[: LANES // 2], upright[LANES // 2 :]], axis=1)


def store_vector(parts, rows_of, put):
    first = lane_is_first(SUB)
    for pair in range(PHYS // 2):
        for part, row in zip(parts, rows_of):
            even = part[pl.ds(2 * pair, SUB, stride=PHYS), :]
            odd = part[pl.ds(2 * pair + 1, SUB, stride=PHYS), :]
            upper = jnp.where(first, even, pltpu.roll(odd, LANES // 2, 1))
            lower = jnp.where(first, pltpu.roll(even, LANES // 2, 1), odd)
            high, low = split_two(jnp.concatenate([upper, lower], axis=0))
            put(row, pair, high, low)


def pack_kernel(info_ref, wave_ref, own_wave_ref, diag_ref, vec_ref, own_ref, diag_out, tiles):
    half = LANES // 2
    for j in range(wave_ref.shape[0]):
        own_ref[j] = pack_tile(own_wave_ref[j])
        diag_out[j] = pack_tile(diag_ref[j])
        for q in range(4):
            tiles[q, j] = pack_tile(wave_ref[j, :, 2 * LANES * q : 2 * LANES * (q + 1)])

        def put(row, pair, high, low):
            columns = slice(pair * LANES, (pair + 1) * LANES)
            vec_ref[j, row : row + 16, columns] = high
            vec_ref[j, row + half : row + half + 16, columns] = low

        store_vector([tiles.at[q, j] for q in range(4)], [16 * q for q in range(4)], put)


def pack(info, wavefunction, diagonal):
    blocks, rows, width = wavefunction.shape
    step = 2
    tile = pl.BlockSpec((step, LANES, LANES), lambda i, *_: (i, 0, 0))
    return pl.pallas_call(
        pack_kernel,
        grid_spec=pltpu.PrefetchScalarGridSpec(
            num_scalar_prefetch=1,
            grid=(blocks // step,),
            in_specs=[
                pl.BlockSpec((step, rows, width), lambda i, *_: (i, 0, 0)),
                pl.BlockSpec((step, rows, width // 4), lambda i, info: (i, 0, info[0])),
                pl.BlockSpec((step, rows, width // 4), lambda i, *_: (i, 0, 0)),
            ],
            out_specs=[pl.BlockSpec((step, LANES, width), lambda i, *_: (i, 0, 0)), tile, tile],
            scratch_shapes=[pltpu.VMEM((4, step, LANES, LANES), jnp.float32)],
        ),
        out_shape=[
            jax.ShapeDtypeStruct((blocks, LANES, width), jnp.bfloat16),
            jax.ShapeDtypeStruct((blocks, LANES, LANES), jnp.float32),
            jax.ShapeDtypeStruct((blocks, LANES, LANES), jnp.float32),
        ],
        compiler_params=pltpu.CompilerParams(vmem_limit_bytes=VMEM_LIMIT),
        cost_estimate=micros(5),
        name="pack",
    )(info, wavefunction, wavefunction, diagonal)


def mixing_kernel(*refs):
    sources, out_ref = refs[:-1], refs[-1]
    spread = (
        lax.broadcasted_iota(jnp.int32, (PHYS, LANES), 1) // SUB
        == lax.broadcasted_iota(jnp.int32, (PHYS, LANES), 0)
    ).astype(jnp.bfloat16)
    row = lax.broadcasted_iota(jnp.int32, (LANES, LANES), 0) // PHYS
    column = lax.broadcasted_iota(jnp.int32, (LANES, LANES), 1) % SUB
    same = row == column
    at = 0
    for source in sources:
        for k in range(source.shape[0]):
            for place, term in enumerate(split_two(source[k].T)):
                wide = jnp.dot(term, spread, preferred_element_type=jnp.float32)
                tall = jnp.concatenate([wide] * SUB, axis=0)
                out_ref[at, :, place * LANES : (place + 1) * LANES] = jnp.where(
                    same, tall, 0.0
                ).astype(jnp.bfloat16)
            at += 1


def mixing_operand(sources):
    count = sources[0].shape[0] * len(sources)
    return pl.pallas_call(
        mixing_kernel,
        out_shape=jax.ShapeDtypeStruct((count, LANES, 2 * LANES), jnp.bfloat16),
        compiler_params=pltpu.CompilerParams(vmem_limit_bytes=VMEM_LIMIT),
        cost_estimate=micros(2),
        name="mixing",
    )(*sources)


def store_right(columns, count, right_out, j):
    used = 32 * count
    high, low = split_two(columns.T[:used])
    right_out[j, 0:used, 0:LANES] = jnp.concatenate([high, high], axis=1)
    right_out[j, 0:used, LANES:] = jnp.concatenate([low, low], axis=1)


def own_operands_kernel(info_ref, *refs):
    pieces, (left_high, left_low, right_out, send, blocks_ref) = refs[:4], refs[4:]
    per, blocks, half, lanes = left_high.shape
    rows = half // 4
    wide = half // 2
    first = lane_is_first(half)
    first_wide = lane_is_first(wide)
    lane = lax.broadcasted_iota(jnp.int32, (half, lanes), 1) // wide
    lane_rows = lax.broadcasted_iota(jnp.int32, (rows, lanes), 1) // wide
    start = info_ref[6] * wide
    other = wide - start
    for j in range(blocks):
        columns = jnp.zeros((half, lanes), jnp.float32)
        for w in range(per):
            for z in range(4):
                row = pl.multiple_of((info_ref[4] ^ z) * rows, rows)
                piece = pieces[z][w, 0, j] if z == 0 else pieces[z][w, j]
                blocks_ref[w, j, pl.ds(row, rows), :] = piece
            block = blocks_ref[w, j]
            turned = pltpu.roll(block, half, 1)
            high, low = split_two(jnp.where(first, block, turned))
            left_high[w, j] = high
            left_low[w, j] = low
            send[w, j, 0:wide] = jnp.where(first_wide, block[:wide], turned[wide:])
            mine = pltpu.roll(block, lax.rem(wide * w + lanes + half - start, lanes), 1)
            columns = jnp.where(lane == w, mine, columns)
            packed = jnp.zeros((rows, lanes), jnp.float32)
            for g in range(4):
                shift = lax.rem(wide * g + lanes + half - other, lanes)
                theirs = pltpu.roll(block[rows * g : rows * (g + 1)], shift, 1)
                packed = jnp.where(lane_rows == g, theirs, packed)
            send[w, j, wide : wide + rows] = packed
        store_right(columns, per, right_out, j)


def other_operands_kernel(sent, left_high, left_low, right_out):
    per, blocks, half, lanes = left_high.shape
    rows = half // 4
    wide = half // 2
    first = lane_is_first(wide)
    lane_rows = lax.broadcasted_iota(jnp.int32, (rows, lanes), 1) // wide
    for j in range(blocks):
        columns = [jnp.zeros((rows, lanes), jnp.float32) for _ in range(4)]
        for w in range(per):
            both = sent[w, j, 0:wide]
            turned = pltpu.roll(both, half, 1)
            full = jnp.concatenate(
                [jnp.where(first, both, turned), jnp.where(first, turned, both)], axis=0
            )
            high, low = split_two(full)
            left_high[w, j] = high
            left_low[w, j] = low
            packed = sent[w, j, wide : wide + rows]
            for g in range(4):
                shift = (wide * (w - g)) % lanes
                moved = pltpu.roll(packed, shift, 1) if shift else packed
                columns[g] = jnp.where(lane_rows == w, moved, columns[g])
        store_right(jnp.concatenate(columns, axis=0), per, right_out, j)


def operand_specs(per, step, half, lanes):
    return [
        pl.BlockSpec((per, step, half, lanes), lambda i, *_: (0, i, 0, 0)),
        pl.BlockSpec((per, step, half, lanes), lambda i, *_: (0, i, 0, 0)),
        pl.BlockSpec((step, per * 32, 2 * lanes), lambda i, *_: (i, 0, 0)),
    ]


def operand_shapes(per, blocks, half, lanes):
    return [
        jax.ShapeDtypeStruct((per, blocks, half, lanes), jnp.bfloat16),
        jax.ShapeDtypeStruct((per, blocks, half, lanes), jnp.bfloat16),
        jax.ShapeDtypeStruct((blocks, per * 32, 2 * lanes), jnp.bfloat16),
    ]


def own_operands(info, by_owner, group, pieces):
    per, blocks, rows, lanes = pieces[0].shape
    half = lanes // 2
    step = 4
    return pl.pallas_call(
        own_operands_kernel,
        grid_spec=pltpu.PrefetchScalarGridSpec(
            num_scalar_prefetch=1,
            grid=(blocks // step,),
            in_specs=[
                pl.BlockSpec(
                    (per, 1, step, rows, lanes), lambda i, info: (group, info[4], i, 0, 0)
                )
            ]
            + [pl.BlockSpec((per, step, rows, lanes), lambda i, *_: (0, i, 0, 0))] * 3,
            out_specs=operand_specs(per, step, half, lanes)
            + [pl.BlockSpec((per, step, 3 * rows, lanes), lambda i, *_: (0, i, 0, 0))],
            scratch_shapes=[pltpu.VMEM((per, step, half, lanes), jnp.float32)],
        ),
        out_shape=operand_shapes(per, blocks, half, lanes)
        + [jax.ShapeDtypeStruct((per, blocks, 3 * rows, lanes), jnp.float32)],
        compiler_params=pltpu.CompilerParams(vmem_limit_bytes=VMEM_LIMIT),
        cost_estimate=micros(3),
        name="own_operands",
    )(info, by_owner, *pieces)


def other_operands(sent):
    per, blocks, rows, lanes = sent.shape
    half = lanes // 2
    step = 4
    return pl.pallas_call(
        other_operands_kernel,
        grid=(blocks // step,),
        in_specs=[pl.BlockSpec((per, step, rows, lanes), lambda i: (0, i, 0, 0))],
        out_specs=operand_specs(per, step, half, lanes),
        out_shape=operand_shapes(per, blocks, half, lanes),
        compiler_params=pltpu.CompilerParams(vmem_limit_bytes=VMEM_LIMIT),
        cost_estimate=micros(3),
        name="other_operands",
    )(sent)


def apply_kernel(plan, info_ref, *refs):
    chunks, parts_given, before_given, pieces = plan
    refs = list(refs)
    take = lambda n: [refs.pop(0) for _ in range(n)]
    slots = take(2)
    vector = take(4 if parts_given else 1)
    operands = [take(4) for _ in chunks]
    before = take(1) if before_given else None
    outs = take(2 if pieces else 1)
    total_ref, vec, mid = refs
    step = mid.shape[0]
    lanes, half = LANES, LANES // 2
    first = lane_is_first(SUB)
    first_half = lane_is_first(half)
    keep_first = jnp.where(first_half, 1.0, 0.0).astype(jnp.bfloat16)
    keep_second = jnp.where(first_half, 0.0, 1.0).astype(jnp.bfloat16)
    nothing = jnp.zeros((lanes, lanes), jnp.bfloat16)
    me = info_ref[4]

    @pl.when(pl.program_id(0) == 0)
    def _():
        total_ref[...] = before[0][...] if before_given else jnp.zeros_like(total_ref)

    def right_side(j):
        if parts_given:

            def put(row, pair, high, low):
                columns = slice(pair * lanes, (pair + 1) * lanes)
                vec[j, pl.ds(row, 16), columns] = high
                vec[j, pl.ds(row + half, 16), columns] = low

            rows_of = [pl.multiple_of(info_ref[g] * 16, 16) for g in range(4)]
            store_vector([x.at[pl.ds(j * lanes, lanes)] for x in vector], rows_of, put)
            source = vec[j]
        else:
            source = vector[0][j]
        source = jnp.concatenate([source, source], axis=0)
        at = 0
        for left_high, left_low, right, mix in operands:
            count = right.shape[1]
            mid[j, at : at + count, :] = jnp.dot(
                right[j], source, preferred_element_type=jnp.float32
            )
            at += count

    def left_side(js, refs_of, w, row_of):
        left_high, left_low, right, mix = refs_of
        done = {}
        for j in js:
            tiles = []
            for part in range(2):
                row = row_of + part * 16
                for pair in range(PHYS // 2):
                    columns = slice(pair * lanes, (pair + 1) * lanes)
                    upper = mid[j, row : row + SUB, columns]
                    lower = mid[j, row + SUB : row + 2 * SUB, columns]
                    tiles.append(jnp.where(first, upper, pltpu.roll(lower, half, 1)))
                    tiles.append(jnp.where(first, pltpu.roll(upper, half, 1), lower))
            t_high, t_low = split_two(jnp.concatenate(tiles, axis=0))
            lh, ll = left_high[w, j], left_low[w, j]
            wide_high = jnp.concatenate([lh * keep_first, lh * keep_second], axis=0)
            wide_low = jnp.concatenate([ll * keep_first, ll * keep_second], axis=0)
            weights = jnp.concatenate(
                [
                    jnp.concatenate([wide_high, wide_low], axis=1),
                    jnp.concatenate([wide_high, nothing], axis=1),
                ],
                axis=0,
            )
            z = jnp.dot(
                jnp.concatenate([t_high, t_low], axis=1),
                weights,
                preferred_element_type=jnp.float32,
            )
            z_high, z_low = split_two(z[:, :lanes] + z[:, lanes:])
            for part in range(2):
                rows = slice(part * lanes, (part + 1) * lanes)
                done[part, j] = (z_high[rows], z_low[rows])
        order = [(part, j) for part in range(2) for j in js]
        return [jnp.concatenate([done[at][i] for at in order], axis=1) for i in range(2)]

    def mix_and_add(js, refs_of, w, z, table, bond):
        z_high, z_low = z
        mix = refs_of[3]
        mix_high = mix[w, :, 0:lanes]
        mix_low = mix[w, :, lanes:]
        mixed = jnp.dot(
            jnp.concatenate([mix_high, mix_high], axis=1),
            jnp.concatenate([z_high, z_low], axis=0),
            preferred_element_type=jnp.float32,
        ) + jnp.dot(mix_low, z_high, preferred_element_type=jnp.float32)
        for i, j in enumerate(js):
            slot = table[bond, pl.program_id(0) * step + j]
            slot = ((slot >> 1) ^ me) * 2 + (slot & 1)
            for part in range(2):
                at = part * len(js) + i
                total_ref[part, slot] += mixed[:, at * lanes : (at + 1) * lanes]

    bonds = []
    for chunk, refs_of in zip(chunks, operands):
        count = refs_of[0].shape[0]
        source, group = chunk // GROUPS, chunk % GROUPS
        for w in range(count):
            bonds.append((refs_of, w, slots[source], group * count + w))
    right_side(0)
    right_side(1)
    waiting = None
    for start in range(0, step, 2):
        js = (start, start + 1)
        for at, (refs_of, w, table, bond) in enumerate(bonds):
            z = left_side(js, refs_of, w, at * 32)
            if waiting is not None:
                mix_and_add(*waiting)
            waiting = (js, refs_of, w, z, table, bond)
            if start + 2 < step and at in (1, 3):
                right_side(start + 2 + at // 2)
    mix_and_add(*waiting)

    @pl.when(pl.program_id(0) == pl.num_programs(0) - 1)
    def _():
        if pieces:
            outs[0][...] = total_ref[info_ref[5]]
            outs[1][...] = total_ref[1 - info_ref[5]]
        else:
            outs[0][...] = total_ref[...]


def apply_bonds(info, slots, vector, chunks, operands, mixing, before, pieces):
    count, blocks, half, lanes = operands[0][0].shape
    step = 4
    parts_given = len(vector) == 4
    if parts_given:
        in_specs = [pl.BlockSpec((step * lanes, lanes), lambda i, *_: (i, 0))] * 4
    else:
        in_specs = [pl.BlockSpec((step,) + vector[0].shape[1:], lambda i, *_: (i, 0, 0))]
    arguments = list(vector)
    for chunk, (left_high, left_low, right) in zip(chunks, operands):
        in_specs += operand_specs(count, step, half, lanes)
        in_specs.append(
            pl.BlockSpec((count,) + mixing.shape[1:], lambda i, *_, at=chunk: (at, 0, 0))
        )
        arguments += [left_high, left_low, right, mixing]
    if before is not None:
        in_specs.append(whole(*before.shape))
        arguments.append(before)
    shapes = [(8, lanes, lanes)] * 2 if pieces else [(2, 8, lanes, lanes)]
    plan = (tuple(chunks), parts_given, before is not None, pieces)
    total = count * len(chunks)
    return pl.pallas_call(
        functools.partial(apply_kernel, plan),
        grid_spec=pltpu.PrefetchScalarGridSpec(
            num_scalar_prefetch=3,
            grid=(blocks // step,),
            in_specs=in_specs,
            out_specs=[whole(*shape) for shape in shapes],
            scratch_shapes=[
                pltpu.VMEM((2, 8, lanes, lanes), jnp.float32),
                pltpu.VMEM((step, lanes, PHYS * half), jnp.bfloat16),
                pltpu.VMEM((step, total * 32, PHYS * half), jnp.float32),
            ],
        ),
        out_shape=[jax.ShapeDtypeStruct(shape, jnp.float32) for shape in shapes],
        compiler_params=pltpu.CompilerParams(vmem_limit_bytes=VMEM_LIMIT),
        cost_estimate=micros(2 + total),
        name="apply_bonds",
    )(info, *slots, *arguments)


def add_arrived(info_ref, owner_ref, arrived, total):
    for k in range(4):
        for i in range(2):
            total[owner_ref[info_ref[4] ^ k, i]] += arrived[k][i]


def stacked_rows(*rows):
    at = lax.broadcasted_iota(jnp.int32, (SUB, LANES), 0)
    tile = jnp.zeros((SUB, LANES), jnp.float32)
    for i, row in enumerate(rows):
        tile = jnp.where(at == i, row, tile)
    return tile


def merged(tiles):
    rows = [[tile[i : i + 1] for i in range(3)] for tile in tiles]
    cross = sum(row[0] for row in rows)
    square = sum(row[1] for row in rows)
    ratio = cross / jnp.maximum(square, TINY)
    apart = [
        (row[0] / jnp.maximum(row[1], TINY) - ratio) * jnp.sqrt(row[1]) for row in rows
    ]
    rest = sum(row[2] for row in rows) + sum(x * x for x in apart)
    return cross, square, rest


def image_kernel(info_ref, owner_ref, a0, a1, a2, a3, diag_ref, own_ref, image_ref, total):
    total[...] = diag_ref[...] * own_ref[...]
    add_arrived(info_ref, owner_ref, (a0, a1, a2, a3), total)
    blocks = total.shape[0]
    cross = jnp.zeros((LANES, LANES), jnp.float32)
    square = jnp.zeros((LANES, LANES), jnp.float32)
    for k in range(blocks):
        own, image = own_ref[k], total[k]
        image_ref[k * LANES : (k + 1) * LANES] = image
        cross += own * image
        square += own * own
    cross = jnp.sum(cross, keepdims=True)
    square = jnp.sum(square, keepdims=True)
    ratio = cross / jnp.maximum(square, TINY)
    rest = jnp.zeros((LANES, LANES), jnp.float32)
    for k in range(blocks):
        apart = total[k] - ratio * own_ref[k]
        rest += apart * apart
    image_ref[blocks * LANES :] = stacked_rows(cross, square, jnp.sum(rest, keepdims=True))


def owner_image(info, owners, arrived, diagonal, own):
    rows = own.shape[0] * LANES + SUB
    return pl.pallas_call(
        image_kernel,
        grid_spec=pltpu.PrefetchScalarGridSpec(
            num_scalar_prefetch=2,
            grid=(1,),
            in_specs=[whole(*x.shape) for x in (*arrived, diagonal, own)],
            out_specs=whole(rows, LANES),
            scratch_shapes=[pltpu.VMEM(own.shape, jnp.float32)],
        ),
        out_shape=jax.ShapeDtypeStruct((rows, LANES), jnp.float32),
        compiler_params=pltpu.CompilerParams(vmem_limit_bytes=VMEM_LIMIT),
        cost_estimate=micros(3),
        name="owner_image",
    )(info, owners, *arrived, diagonal, own)


def join_kernel(mine, other, *refs):
    tiles = refs[:-4] if len(refs) == 4 else refs[:-5]
    pieces = refs[len(tiles) : len(tiles) + 4]
    for k in range(4):
        for i in range(2):
            pieces[k][i] = mine[2 * k + i] + other[2 * k + i]
    if tiles:
        refs[-1][...] = stacked_rows(*merged([ref[...] for ref in tiles]))


def join(mine, other, images):
    shapes = [jax.ShapeDtypeStruct((2, LANES, LANES), jnp.float32)] * 4
    if images:
        shapes.append(jax.ShapeDtypeStruct((SUB, LANES), jnp.float32))
    last = images[0].shape[0] // SUB - 1 if images else 0
    return pl.pallas_call(
        join_kernel,
        grid=(1,),
        in_specs=[whole(*mine.shape), whole(*other.shape)]
        + [pl.BlockSpec((SUB, LANES), lambda i: (last, 0)) for _ in images],
        out_specs=[whole(*x.shape) for x in shapes],
        out_shape=shapes,
        compiler_params=pltpu.CompilerParams(vmem_limit_bytes=VMEM_LIMIT),
        cost_estimate=micros(1),
        name="join",
    )(mine, other, *images)


def scales_of(tiles, entries):
    cross, square, rest = merged(tiles)
    scale = lax.rsqrt(square / entries + 1e-06)
    rayleigh = scale * scale * (cross / entries)
    apart = (cross / jnp.maximum(square, TINY) - rayleigh) * jnp.sqrt(square)
    mean = scale * scale * ((rest + apart * apart) / entries)
    return scale, rayleigh, scale * lax.rsqrt(mean + 1e-06)


def first_kernel(entries, s0, s1, s2, s3, image_ref, own_ref, first_ref, second_ref):
    tiles = [ref[...] for ref in (s0, s1, s2, s3)]
    scale, rayleigh, second_scale = scales_of(tiles, entries)
    for k in range(own_ref.shape[0]):
        image = image_ref[k * LANES : (k + 1) * LANES]
        first_ref[k] = unpack_tile(scale * image)
        second_ref[k] = unpack_tile(second_scale * (image - rayleigh * own_ref[k]))


def first_outputs(stats, image, own, entries):
    step = 4
    blocks = own.shape[0]
    shape = (step, LANES // 2, 2 * LANES)
    return pl.pallas_call(
        functools.partial(first_kernel, entries),
        grid=(blocks // step,),
        in_specs=[whole(SUB, LANES)] * 4
        + [
            pl.BlockSpec((step * LANES, LANES), lambda i: (i, 0)),
            pl.BlockSpec((step, LANES, LANES), lambda i: (i, 0, 0)),
        ],
        out_specs=[pl.BlockSpec(shape, lambda i: (i, 0, 0))] * 2,
        out_shape=[jax.ShapeDtypeStruct((blocks,) + shape[1:], jnp.float32)] * 2,
        compiler_params=pltpu.CompilerParams(vmem_limit_bytes=VMEM_LIMIT),
        cost_estimate=micros(3),
        name="first_outputs",
    )(*stats, image, own)


def final_kernel(
    entries, info_ref, owner_ref, a0, a1, a2, a3, diag_ref, image_ref, s0, s1, s2, s3,
    second_ref, total,
):
    tiles = [ref[...] for ref in (s0, s1, s2, s3)]
    scale, rayleigh, second_scale = scales_of(tiles, entries)
    for k in range(total.shape[0]):
        total[k] = (diag_ref[k] - rayleigh) * image_ref[k * LANES : (k + 1) * LANES]
    add_arrived(info_ref, owner_ref, (a0, a1, a2, a3), total)
    for k in range(total.shape[0]):
        second_ref[k] = unpack_tile(second_scale * total[k])


def second_output(info, owners, arrived, diagonal, image, stats, entries):
    blocks = diagonal.shape[0]
    shape = (blocks, LANES // 2, 2 * LANES)
    return pl.pallas_call(
        functools.partial(final_kernel, entries),
        grid_spec=pltpu.PrefetchScalarGridSpec(
            num_scalar_prefetch=2,
            grid=(1,),
            in_specs=[whole(*x.shape) for x in (*arrived, diagonal)]
            + [whole(blocks * LANES, LANES)]
            + [whole(SUB, LANES)] * 4,
            out_specs=whole(*shape),
            scratch_shapes=[pltpu.VMEM(diagonal.shape, jnp.float32)],
        ),
        out_shape=jax.ShapeDtypeStruct(shape, jnp.float32),
        compiler_params=pltpu.CompilerParams(vmem_limit_bytes=VMEM_LIMIT),
        cost_estimate=micros(3),
        name="second_output",
    )(info, owners, *arrived, diagonal, image, *stats)


def partner(x, axis, k):
    size = lax.axis_size(axis)
    return lax.ppermute(x, axis, [(i, i ^ k) for i in range(size)])


def after(x, *others):
    return lax.optimization_barrier((x, *others))[0]


def gathered(x):
    across = partner(x, "mpo", 1)
    return [x, across, partner(x, "rep", 1), partner(across, "rep", 1)]


def everyone(x, axes):
    return [x] + [partner(x, axes, k) for k in range(1, 4)]


def to_owners(mine, theirs, images):
    out = join(mine, partner(theirs, "rep", 1), images)
    arrived = [out[0]] + [partner(out[k], "blk", k) for k in range(1, 4)]
    return arrived, everyone(out[4], "blk") if images else None


def per_device(wavefunction, environment, bond_terms, diagonal, term_slot, slot_block):
    blocks, rows, width = wavefunction.shape
    zs = lax.axis_size("blk")
    mpo, rep, blk = lax.axis_index("mpo"), lax.axis_index("rep"), lax.axis_index("blk")
    place = 2 * mpo + rep
    info = jnp.stack([place, place ^ 2, place ^ 1, place ^ 3, blk, rep, mpo]).astype(jnp.int32)
    bonds = environment.shape[0]
    per = bonds // GROUPS
    entries = float(blocks * zs * rows * width)

    vector, own, diagonal_packed = pack(info, wavefunction, diagonal)
    mixing = mixing_operand([bond_terms, partner(bond_terms, "mpo", 1)])
    slots = [term_slot, partner(term_slot, "mpo", 1)]

    by_owner = environment.reshape(bonds, zs, blocks, rows // zs, 2 * rows)
    pieces = [[None] * 4 for _ in range(GROUPS)]
    for group in range(GROUPS):
        mine = by_owner[group * per : (group + 1) * per]
        for k in range(1, 4):
            piece = lax.dynamic_index_in_dim(mine, blk ^ k, 1, keepdims=False)
            if group:
                piece = after(piece, pieces[group - 1][k])
            pieces[group][k] = partner(piece, "blk", k)
    pieces[0][1] = after(pieces[0][1], vector, mixing)
    made, sent = [], []
    for group in range(GROUPS):
        *own_set, send = own_operands(info, by_owner, group, pieces[group][1:])
        made.append(own_set)
        sent.append(send)
    received = [partner(send, "mpo", 1) for send in sent]
    operands = [[made[g], other_operands(received[g])] for g in range(GROUPS)]

    total = None
    for group in range(GROUPS):
        last = group == GROUPS - 1
        given = vector if last else after(vector, *sent)
        out = apply_bonds(
            info, slots, [given], [group, GROUPS + group], operands[group], mixing, total, last
        )
        total = None if last else out[0]
    arrived, _ = to_owners(*out, [])
    image = owner_image(info, slot_block, arrived, diagonal_packed, own)

    parts = gathered(image)
    chunks = [group + GROUPS * source for group in range(GROUPS) for source in range(2)]
    flat = [operands[group][source] for group in range(GROUPS) for source in range(2)]
    out = apply_bonds(info, slots, parts, chunks, flat, mixing, None, True)
    arrived, stats = to_owners(*out, parts)
    first_image, second_vector = first_outputs(stats, image, own, entries)
    second_image = second_output(
        info, slot_block, arrived, diagonal_packed, image, stats, entries
    )
    return (first_image, second_vector, second_image)


def solution(mesh):
    packed = mesh.shape["mpo"] == 2 and mesh.shape["rep"] == 2 and mesh.shape["blk"] == 4
    return jax.shard_map(
        per_device if packed else plain_device,
        mesh=mesh,
        in_specs=(
            P(("grp", "blk"), None, None),
            P(("grp", "mpo", "rep"), None, "blk", None),
            P(("grp", "mpo", "rep"), None, None),
            P(("grp", "blk"), None, ("mpo", "rep")),
            P(("grp", "mpo", "rep"), "blk"),
            P("grp", "blk"),
        ),
        out_specs=(
            P(("grp", "blk"), None, ("mpo", "rep")),
            P(("grp", "blk"), None, ("mpo", "rep")),
            P(("grp", "blk"), None, ("mpo", "rep")),
        ),
        check_vma=False,
    )
```

```python
import functools

import jax
import jax.numpy as jnp
from jax import lax
from jax.experimental import pallas as pl
from jax.experimental.pallas import tpu as pltpu
from jax.sharding import PartitionSpec as P

LANES = 128
SUB = 8
PHYS = 16
TINY = 1e-30
GROUPS = 2
VMEM_LIMIT = 63 * 1024 * 1024 + 512 * 1024


def plain_apply(vector_full, environment, bond_terms, term_slot, slot_block, diagonal):
    block_count, block_rows, block_width = vector_full.shape
    phys_size = bond_terms.shape[-1]
    right_rows = block_width // phys_size
    slot_count = slot_block.shape[0] * slot_block.shape[1]
    blocks = vector_full.reshape(block_count, block_rows, right_rows, phys_size)
    ordered = jnp.transpose(blocks, (0, 3, 1, 2))
    left_env = environment[:, :, :, :block_rows]
    right_env = environment[:, :, :, block_rows:]
    left_done = jnp.einsum("wjab,jsac->wjsbc", left_env, ordered, precision=lax.Precision.HIGHEST)
    right_done = jnp.einsum(
        "wjsbc,wjcd->wjsbd", left_done, right_env, precision=lax.Precision.HIGHEST
    )
    right_done = right_done.reshape(
        environment.shape[0], block_count, phys_size, block_rows * right_rows
    )
    bond_term = jnp.einsum(
        "wjsx,wst->wjtx", right_done, bond_terms, precision=lax.Precision.HIGHEST
    )
    bond_term = bond_term.reshape(environment.shape[0], block_count, block_rows * block_width)
    slot_table = (
        term_slot[:, None, :] == jnp.arange(slot_count, dtype=jnp.int32)[None, :, None]
    ).astype(jnp.float32)
    slot_buffer = jnp.einsum("wsj,wjx->sx", slot_table, bond_term, precision=lax.Precision.HIGHEST)
    slot_buffer = slot_buffer.reshape(slot_count, phys_size, block_rows, right_rows)
    slot_buffer = jnp.transpose(slot_buffer, (0, 2, 3, 1)).reshape(
        slot_count, block_rows, block_width
    )
    owners = slot_block.reshape(-1)
    selector = (owners[None, :] == jnp.arange(block_count, dtype=jnp.int32)[:, None]).astype(
        jnp.float32
    )
    column_width = block_width // lax.axis_size(("mpo", "rep"))
    column_start = lax.axis_index(("mpo", "rep")) * column_width
    own_part = lax.dynamic_slice_in_dim(vector_full, column_start, column_width, 2)
    shares = lax.psum_scatter(slot_buffer, ("mpo", "rep"), scatter_dimension=2, tiled=True)
    arrived = lax.all_to_all(shares, "blk", split_axis=0, concat_axis=0, tiled=True)
    result = jnp.einsum("ks,sbc->kbc", selector, arrived, precision=lax.Precision.HIGHEST)
    return (result + diagonal * own_part, own_part)


def plain_device(wavefunction, environment, bond_terms, diagonal, term_slot, slot_block):
    arranged = lax.all_to_all(environment, "blk", split_axis=1, concat_axis=2, tiled=True)
    entries = float(
        wavefunction.shape[0] * lax.axis_size("blk") * wavefunction.shape[1] * wavefunction.shape[2]
    )
    square_sum = lax.psum(jnp.sum(wavefunction * wavefunction), "blk")
    first_vector = wavefunction * lax.rsqrt(square_sum / entries + 1e-06)
    first_image, first_part = plain_apply(
        first_vector, arranged, bond_terms, term_slot, slot_block, diagonal
    )
    rayleigh = lax.psum(jnp.sum(first_part * first_image), ("blk", "mpo", "rep")) / entries
    residual = first_image - rayleigh * first_part
    resid_sum = lax.psum(jnp.sum(residual * residual), ("blk", "mpo", "rep"))
    second_vector = residual * lax.rsqrt(resid_sum / entries + 1e-06)
    second_full = lax.all_gather(second_vector, ("mpo", "rep"), axis=2, tiled=True)
    second_image, unused = plain_apply(
        second_full, arranged, bond_terms, term_slot, slot_block, diagonal
    )
    return (first_image, second_vector, second_image)


def split_two(x):
    high = x.astype(jnp.bfloat16)
    low = (x - high.astype(jnp.float32)).astype(jnp.bfloat16)
    return high, low


def lane_is_first(rows):
    return lax.broadcasted_iota(jnp.int32, (rows, LANES), 1) < LANES // 2


def micros(count):
    return pl.CostEstimate(flops=count * 1100000000, bytes_accessed=1 << 20, transcendentals=0)


def whole(*shape):
    return pl.BlockSpec(shape, lambda i, *_: (0,) * len(shape))


def pack_tile(x):
    return jnp.concatenate([x[:, :LANES], x[:, LANES:]], axis=0).T


def unpack_tile(x):
    upright = x.T
    return jnp.concatenate([upright[: LANES // 2], upright[LANES // 2 :]], axis=1)


def store_vector(parts, rows_of, put):
    first = lane_is_first(SUB)
    for pair in range(PHYS // 2):
        for part, row in zip(parts, rows_of):
            even = part[pl.ds(2 * pair, SUB, stride=PHYS), :]
            odd = part[pl.ds(2 * pair + 1, SUB, stride=PHYS), :]
            upper = jnp.where(first, even, pltpu.roll(odd, LANES // 2, 1))
            lower = jnp.where(first, pltpu.roll(even, LANES // 2, 1), odd)
            high, low = split_two(jnp.concatenate([upper, lower], axis=0))
            put(row, pair, high, low)


def pack_kernel(info_ref, wave_ref, own_wave_ref, diag_ref, vec_ref, own_ref, diag_out, tiles):
    half = LANES // 2
    for j in range(wave_ref.shape[0]):
        own_ref[j] = pack_tile(own_wave_ref[j])
        diag_out[j] = pack_tile(diag_ref[j])
        for q in range(4):
            tiles[q, j] = pack_tile(wave_ref[j, :, 2 * LANES * q : 2 * LANES * (q + 1)])

        def put(row, pair, high, low):
            columns = slice(pair * LANES, (pair + 1) * LANES)
            vec_ref[j, row : row + 16, columns] = high
            vec_ref[j, row + half : row + half + 16, columns] = low

        store_vector([tiles.at[q, j] for q in range(4)], [16 * q for q in range(4)], put)


def pack(info, wavefunction, diagonal):
    blocks, rows, width = wavefunction.shape
    step = 2
    tile = pl.BlockSpec((step, LANES, LANES), lambda i, *_: (i, 0, 0))
    return pl.pallas_call(
        pack_kernel,
        grid_spec=pltpu.PrefetchScalarGridSpec(
            num_scalar_prefetch=1,
            grid=(blocks // step,),
            in_specs=[
                pl.BlockSpec((step, rows, width), lambda i, *_: (i, 0, 0)),
                pl.BlockSpec((step, rows, width // 4), lambda i, info: (i, 0, info[0])),
                pl.BlockSpec((step, rows, width // 4), lambda i, *_: (i, 0, 0)),
            ],
            out_specs=[pl.BlockSpec((step, LANES, width), lambda i, *_: (i, 0, 0)), tile, tile],
            scratch_shapes=[pltpu.VMEM((4, step, LANES, LANES), jnp.float32)],
        ),
        out_shape=[
            jax.ShapeDtypeStruct((blocks, LANES, width), jnp.bfloat16),
            jax.ShapeDtypeStruct((blocks, LANES, LANES), jnp.float32),
            jax.ShapeDtypeStruct((blocks, LANES, LANES), jnp.float32),
        ],
        compiler_params=pltpu.CompilerParams(vmem_limit_bytes=VMEM_LIMIT),
        cost_estimate=micros(5),
        name="pack",
    )(info, wavefunction, wavefunction, diagonal)


def mixing_kernel(*refs):
    sources, out_ref = refs[:-1], refs[-1]
    spread = (
        lax.broadcasted_iota(jnp.int32, (PHYS, LANES), 1) // SUB
        == lax.broadcasted_iota(jnp.int32, (PHYS, LANES), 0)
    ).astype(jnp.bfloat16)
    row = lax.broadcasted_iota(jnp.int32, (LANES, LANES), 0) // PHYS
    column = lax.broadcasted_iota(jnp.int32, (LANES, LANES), 1) % SUB
    same = row == column
    at = 0
    for source in sources:
        for k in range(source.shape[0]):
            high, low = split_two(source[k].T)
            for term, places in ((high, (0, 1)), (low, (2,))):
                wide = jnp.dot(term, spread, preferred_element_type=jnp.float32)
                tall = jnp.concatenate([wide] * SUB, axis=0)
                tall = jnp.where(same, tall, 0.0).astype(jnp.bfloat16)
                for place in places:
                    out_ref[at, :, place * LANES : (place + 1) * LANES] = tall
            at += 1


def mixing_operand(sources):
    count = sources[0].shape[0] * len(sources)
    return pl.pallas_call(
        mixing_kernel,
        out_shape=jax.ShapeDtypeStruct((count, LANES, 3 * LANES), jnp.bfloat16),
        compiler_params=pltpu.CompilerParams(vmem_limit_bytes=VMEM_LIMIT),
        cost_estimate=micros(2),
        name="mixing",
    )(*sources)


def own_operands_kernel(info_ref, *refs):
    pieces, (left_high, left_low, right_out, send, blocks_ref, upright_ref) = refs[:4], refs[4:]
    per, blocks, half, lanes = left_high.shape
    rows = half // 4
    wide = half // 2
    first = lane_is_first(half)
    first_wide = lane_is_first(wide)
    first_rows = lane_is_first(rows)
    mine_at = pl.multiple_of(half + info_ref[6] * wide, wide)
    theirs_at = pl.multiple_of(lanes - wide - info_ref[6] * wide, wide)
    for j in range(blocks):
        for w in range(per):
            for z in range(4):
                row = pl.multiple_of((info_ref[4] ^ z) * rows, rows)
                piece = pieces[z][w, 0, j] if z == 0 else pieces[z][w, j]
                blocks_ref[w, j, pl.ds(row, rows), :] = piece
        for w in range(per):
            block = blocks_ref[w, j]
            upright_ref[w, j] = jnp.concatenate([block, block], axis=0).T
            turned = pltpu.roll(block, half, 1)
            high, low = split_two(jnp.where(first, block, turned))
            left_high[w, j] = high
            left_low[w, j] = low
            send[w, j, 0:wide] = jnp.where(first_wide, block[:wide], turned[wide:])
        for w in range(per):
            high, low = split_two(upright_ref[w, j, pl.ds(mine_at, wide), :])
            right_out[j, wide * w : wide * (w + 1), 0:lanes] = high
            right_out[j, wide * w : wide * (w + 1), lanes:] = low
            upper = upright_ref[w, j, pl.ds(theirs_at, rows), :]
            lower = upright_ref[w, j, pl.ds(theirs_at + rows, rows), :]
            send[w, j, wide : wide + rows] = jnp.where(first_rows, upper, lower)


def other_operands(sent, left_high, left_low, right_out, j):
    per, blocks, half, lanes = left_high.shape
    rows = half // 4
    wide = half // 2
    first = lane_is_first(wide)
    first_rows = lane_is_first(rows)
    for w in range(per):
        both = sent[w, j, 0:wide]
        turned = pltpu.roll(both, half, 1)
        full = jnp.concatenate(
            [jnp.where(first, both, turned), jnp.where(first, turned, both)], axis=0
        )
        high, low = split_two(full)
        left_high[w, j] = high
        left_low[w, j] = low
        both = sent[w, j, wide : wide + rows]
        turned = pltpu.roll(both, half, 1)
        full = jnp.concatenate(
            [jnp.where(first_rows, both, turned), jnp.where(first_rows, turned, both)], axis=0
        )
        high, low = split_two(full)
        right_out[j, wide * w : wide * (w + 1), 0:lanes] = high
        right_out[j, wide * w : wide * (w + 1), lanes:] = low


def operand_specs(per, step, half, lanes):
    return [
        pl.BlockSpec((per, step, half, lanes), lambda i, *_: (0, i, 0, 0)),
        pl.BlockSpec((per, step, half, lanes), lambda i, *_: (0, i, 0, 0)),
        pl.BlockSpec((step, per * 32, 2 * lanes), lambda i, *_: (i, 0, 0)),
    ]


def operand_shapes(per, blocks, half, lanes):
    return [
        jax.ShapeDtypeStruct((per, blocks, half, lanes), jnp.bfloat16),
        jax.ShapeDtypeStruct((per, blocks, half, lanes), jnp.bfloat16),
        jax.ShapeDtypeStruct((blocks, per * 32, 2 * lanes), jnp.bfloat16),
    ]


def own_operands(info, by_owner, group, pieces):
    per, blocks, rows, lanes = pieces[0].shape
    half = lanes // 2
    step = 4
    return pl.pallas_call(
        own_operands_kernel,
        grid_spec=pltpu.PrefetchScalarGridSpec(
            num_scalar_prefetch=1,
            grid=(blocks // step,),
            in_specs=[
                pl.BlockSpec(
                    (per, 1, step, rows, lanes), lambda i, info: (group, info[4], i, 0, 0)
                )
            ]
            + [pl.BlockSpec((per, step, rows, lanes), lambda i, *_: (0, i, 0, 0))] * 3,
            out_specs=operand_specs(per, step, half, lanes)
            + [pl.BlockSpec((per, step, 3 * rows, lanes), lambda i, *_: (0, i, 0, 0))],
            scratch_shapes=[
                pltpu.VMEM((per, step, half, lanes), jnp.float32),
                pltpu.VMEM((per, step, lanes, lanes), jnp.float32),
            ],
        ),
        out_shape=operand_shapes(per, blocks, half, lanes)
        + [jax.ShapeDtypeStruct((per, blocks, 3 * rows, lanes), jnp.float32)],
        compiler_params=pltpu.CompilerParams(vmem_limit_bytes=VMEM_LIMIT),
        cost_estimate=micros(12),
        name="own_operands",
    )(info, by_owner, *pieces)


def apply_kernel(plan, info_ref, *refs):
    chunks, parts_given, sent_given, before_given, pieces = plan
    refs = list(refs)
    take = lambda n: [refs.pop(0) for _ in range(n)]
    slots = take(2)
    vector = take(4 if parts_given else 1)
    tiles = take(4) if parts_given else []
    operands = [take(3) for _ in chunks[: -1 if sent_given else None]]
    sent = take(1)[0] if sent_given else None
    mixes = take(len(chunks))
    before = take(1)[0] if before_given else None
    outs = take(2 if pieces else 1)
    if sent_given:
        operands.append(take(3))
    total_ref, vec, mid = take(3)
    if before_given:
        prior, arrival = take(2)
    step = mid.shape[0]
    lanes, half = LANES, LANES // 2
    first = lane_is_first(SUB)
    first_half = lane_is_first(half)
    keep_first = jnp.where(first_half, 1.0, 0.0).astype(jnp.bfloat16)
    keep_second = jnp.where(first_half, 0.0, 1.0).astype(jnp.bfloat16)
    nothing = jnp.zeros((lanes, lanes), jnp.bfloat16)
    me = info_ref[4]

    @pl.when(pl.program_id(0) == 0)
    def _():
        if before_given:
            pltpu.make_async_copy(before, prior, arrival).start()
        total_ref[...] = jnp.zeros_like(total_ref)

    def right_side(j):
        if sent_given:
            other_operands(sent, *operands[-1], j)
        if parts_given:

            def put(row, pair, high, low):
                columns = slice(pair * lanes, (pair + 1) * lanes)
                vec[j, pl.ds(row, 16), columns] = high
                vec[j, pl.ds(row + half, 16), columns] = low

            rows_of = [pl.multiple_of(info_ref[g] * 16, 16) for g in range(4)]
            store_vector([x.at[pl.ds(j * lanes, lanes)] for x in vector], rows_of, put)
            source = vec[j]
        else:
            source = vector[0][j]
        source = jnp.concatenate([source, source], axis=0)
        at = 0
        for left_high, left_low, right in operands:
            count = right.shape[1]
            mid[j, at : at + count, :] = jnp.dot(
                right[j], source, preferred_element_type=jnp.float32
            )
            at += count

    def left_side(j, refs_of, w, row_of):
        left_high, left_low, right = refs_of
        tiles = []
        for part in range(2):
            row = row_of + part * 16
            for pair in range(PHYS // 2):
                columns = slice(pair * lanes, (pair + 1) * lanes)
                upper = mid[j, row : row + SUB, columns]
                lower = mid[j, row + SUB : row + 2 * SUB, columns]
                tiles.append(jnp.where(first, upper, pltpu.roll(lower, half, 1)))
                tiles.append(jnp.where(first, pltpu.roll(upper, half, 1), lower))
        t_high, t_low = split_two(jnp.concatenate(tiles, axis=0))
        lh, ll = left_high[w, j], left_low[w, j]
        wide_high = jnp.concatenate([lh * keep_first, lh * keep_second], axis=0)
        wide_low = jnp.concatenate([ll * keep_first, ll * keep_second], axis=0)
        weights = jnp.concatenate(
            [
                jnp.concatenate([wide_high, wide_low], axis=1),
                jnp.concatenate([wide_high, nothing], axis=1),
            ],
            axis=0,
        )
        z = jnp.dot(
            jnp.concatenate([t_high, t_low], axis=1), weights, preferred_element_type=jnp.float32
        )
        return split_two(z[:, :lanes] + z[:, lanes:])

    def mix_and_add(j, mix, w, z, table, bond):
        z_high, z_low = [jnp.concatenate([x[:lanes], x[lanes:]], axis=1) for x in z]
        mixed = jnp.dot(
            mix[w],
            jnp.concatenate([z_high, z_low, z_high], axis=0),
            preferred_element_type=jnp.float32,
        )
        slot = table[bond, pl.program_id(0) * step + j]
        slot = ((slot >> 1) ^ me) * 2 + (slot & 1)
        for part in range(2):
            total_ref[part, slot] += mixed[:, part * lanes : (part + 1) * lanes]

    bonds = []
    for chunk, refs_of, mix in zip(chunks, operands, mixes):
        count = mix.shape[0]
        source, group = chunk // GROUPS, chunk % GROUPS
        for w in range(count):
            bonds.append((refs_of, mix, w, slots[source], group * count + w))
    right_side(0)
    waiting = None
    for j in range(step):
        for at, (refs_of, mix, w, table, bond) in enumerate(bonds):
            z = left_side(j, refs_of, w, at * 32)
            if waiting is not None:
                mix_and_add(*waiting)
            waiting = (j, mix, w, z, table, bond)
            if j + 1 < step and at == len(bonds) // 3:
                right_side(j + 1)
    mix_and_add(*waiting)

    @pl.when(pl.program_id(0) == pl.num_programs(0) - 1)
    def _():
        if before_given:
            pltpu.make_async_copy(before, prior, arrival).wait()
            total_ref[...] += prior[...]
        if pieces:
            stats = jnp.zeros((SUB, lanes), jnp.float32)
            if parts_given:
                stats = stacked_rows(*merged([tile[...] for tile in tiles]))
            for out, part in ((outs[0], info_ref[5]), (outs[1], 1 - info_ref[5])):
                for k in range(4):
                    for i in range(2):
                        out[k, i * lanes : (i + 1) * lanes] = total_ref[part, 2 * k + i]
                    out[k, 2 * lanes :] = stats
                stats = jnp.zeros((SUB, lanes), jnp.float32)
        else:
            outs[0][...] = total_ref[...]


def apply_bonds(info, slots, vector, chunks, operands, sent, mixing, before, pieces):
    count, blocks, half, lanes = operands[0][0].shape
    step = 4
    parts_given = len(vector) == 4
    if parts_given:
        last = vector[0].shape[0] // SUB - 1
        in_specs = [pl.BlockSpec((step * lanes, lanes), lambda i, *_: (i, 0))] * 4
        in_specs += [pl.BlockSpec((SUB, lanes), lambda i, *_: (last, 0))] * 4
    else:
        in_specs = [pl.BlockSpec((step,) + vector[0].shape[1:], lambda i, *_: (i, 0, 0))]
    arguments = list(vector) * (2 if parts_given else 1)
    for made in operands:
        in_specs += operand_specs(count, step, half, lanes)
        arguments += made
    if sent is not None:
        in_specs.append(
            pl.BlockSpec((count, step) + sent.shape[2:], lambda i, *_: (0, i, 0, 0))
        )
        arguments.append(sent)
    for chunk in chunks:
        in_specs.append(
            pl.BlockSpec((count,) + mixing.shape[1:], lambda i, *_, at=chunk: (at, 0, 0))
        )
        arguments.append(mixing)
    total = count * len(chunks)
    scratch = [
        pltpu.VMEM((2, 8, lanes, lanes), jnp.float32),
        pltpu.VMEM((step, lanes, PHYS * half), jnp.bfloat16),
        pltpu.VMEM((step, total * 32, PHYS * half), jnp.float32),
    ]
    if before is not None:
        in_specs.append(pl.BlockSpec(memory_space=pl.ANY))
        arguments.append(before)
        scratch += [pltpu.VMEM(before.shape, jnp.float32), pltpu.SemaphoreType.DMA]
    shapes = [(4, 2 * lanes + SUB, lanes)] * 2 if pieces else [(2, 8, lanes, lanes)]
    out_specs = [whole(*shape) for shape in shapes]
    out_shape = [jax.ShapeDtypeStruct(shape, jnp.float32) for shape in shapes]
    if sent is not None:
        out_specs += operand_specs(count, step, half, lanes)
        out_shape += operand_shapes(count, blocks, half, lanes)
    plan = (tuple(chunks), parts_given, sent is not None, before is not None, pieces)
    out = pl.pallas_call(
        functools.partial(apply_kernel, plan),
        grid_spec=pltpu.PrefetchScalarGridSpec(
            num_scalar_prefetch=3,
            grid=(blocks // step,),
            in_specs=in_specs,
            out_specs=out_specs,
            scratch_shapes=scratch,
        ),
        out_shape=out_shape,
        compiler_params=pltpu.CompilerParams(vmem_limit_bytes=VMEM_LIMIT),
        cost_estimate=micros(2 + total),
        name="apply_bonds",
    )(info, *slots, *arguments)
    return out[: len(shapes)], out[len(shapes) :]


def add_arrived(info_ref, owner_ref, arrived, total):
    for k in range(4):
        for i in range(2):
            rows = slice(i * LANES, (i + 1) * LANES)
            total[owner_ref[info_ref[4] ^ k, i]] += arrived[k][rows]


def stacked_rows(*rows):
    at = lax.broadcasted_iota(jnp.int32, (SUB, LANES), 0)
    tile = jnp.zeros((SUB, LANES), jnp.float32)
    for i, row in enumerate(rows):
        tile = jnp.where(at == i, row, tile)
    return tile


def merged(tiles):
    rows = [[tile[i : i + 1] for i in range(3)] for tile in tiles]
    cross = sum(row[0] for row in rows)
    square = sum(row[1] for row in rows)
    ratio = cross / jnp.maximum(square, TINY)
    apart = [
        (row[0] / jnp.maximum(row[1], TINY) - ratio) * jnp.sqrt(row[1]) for row in rows
    ]
    rest = sum(row[2] for row in rows) + sum(x * x for x in apart)
    return cross, square, rest


def image_kernel(info_ref, owner_ref, a0, a1, a2, a3, diag_ref, own_ref, image_ref, total):
    total[...] = diag_ref[...] * own_ref[...]
    add_arrived(info_ref, owner_ref, (a0, a1, a2, a3), total)
    blocks = total.shape[0]
    cross = jnp.zeros((LANES, LANES), jnp.float32)
    square = jnp.zeros((LANES, LANES), jnp.float32)
    for k in range(blocks):
        own, image = own_ref[k], total[k]
        image_ref[k * LANES : (k + 1) * LANES] = image
        cross += own * image
        square += own * own
    cross = jnp.sum(cross, keepdims=True)
    square = jnp.sum(square, keepdims=True)
    ratio = cross / jnp.maximum(square, TINY)
    rest = jnp.zeros((LANES, LANES), jnp.float32)
    for k in range(blocks):
        apart = total[k] - ratio * own_ref[k]
        rest += apart * apart
    image_ref[blocks * LANES :] = stacked_rows(cross, square, jnp.sum(rest, keepdims=True))


def owner_image(info, owners, arrived, diagonal, own):
    rows = own.shape[0] * LANES + SUB
    return pl.pallas_call(
        image_kernel,
        grid_spec=pltpu.PrefetchScalarGridSpec(
            num_scalar_prefetch=2,
            grid=(1,),
            in_specs=[whole(*x.shape) for x in (*arrived, diagonal, own)],
            out_specs=whole(rows, LANES),
            scratch_shapes=[pltpu.VMEM(own.shape, jnp.float32)],
        ),
        out_shape=jax.ShapeDtypeStruct((rows, LANES), jnp.float32),
        compiler_params=pltpu.CompilerParams(vmem_limit_bytes=VMEM_LIMIT),
        cost_estimate=micros(3),
        name="owner_image",
    )(info, owners, *arrived, diagonal, own)


def final_kernel(
    entries, info_ref, owner_ref, a0, a1, a2, a3, diag_ref, own_ref, image_ref, first_ref,
    vector_ref, second_ref, total,
):
    arrived = (a0, a1, a2, a3)
    cross, square, rest = merged([ref[2 * LANES :] for ref in arrived])
    scale = lax.rsqrt(square / entries + 1e-06)
    rayleigh = scale * scale * (cross / entries)
    apart = (cross / jnp.maximum(square, TINY) - rayleigh) * jnp.sqrt(square)
    mean = scale * scale * ((rest + apart * apart) / entries)
    second_scale = scale * lax.rsqrt(mean + 1e-06)
    for k in range(total.shape[0]):
        image = image_ref[k * LANES : (k + 1) * LANES]
        total[k] = (diag_ref[k] - rayleigh) * image
        first_ref[k] = unpack_tile(scale * image)
        vector_ref[k] = unpack_tile(second_scale * (image - rayleigh * own_ref[k]))
    add_arrived(info_ref, owner_ref, arrived, total)
    for k in range(total.shape[0]):
        second_ref[k] = unpack_tile(second_scale * total[k])


def outputs(info, owners, arrived, diagonal, own, image, entries):
    blocks = diagonal.shape[0]
    shape = (blocks, LANES // 2, 2 * LANES)
    return pl.pallas_call(
        functools.partial(final_kernel, entries),
        grid_spec=pltpu.PrefetchScalarGridSpec(
            num_scalar_prefetch=2,
            grid=(1,),
            in_specs=[whole(*x.shape) for x in (*arrived, diagonal, own)]
            + [whole(blocks * LANES, LANES)],
            out_specs=[whole(*shape)] * 3,
            scratch_shapes=[pltpu.VMEM(diagonal.shape, jnp.float32)],
        ),
        out_shape=[jax.ShapeDtypeStruct(shape, jnp.float32)] * 3,
        compiler_params=pltpu.CompilerParams(vmem_limit_bytes=VMEM_LIMIT),
        cost_estimate=micros(4),
        name="outputs",
    )(info, owners, *arrived, diagonal, own, image)


def partner(x, axis, k):
    size = lax.axis_size(axis)
    return lax.ppermute(x, axis, [(i, i ^ k) for i in range(size)])


def after(x, *others):
    return lax.optimization_barrier((x, *others))[0]


def gathered(x):
    across = partner(x, "mpo", 1)
    return [x, across, partner(x, "rep", 1), partner(across, "rep", 1)]


def everyone_of(pieces, axis):
    return [pieces[0]] + [partner(pieces[k], axis, k) for k in range(1, 4)]


def to_owners(mine, theirs):
    other = partner(theirs, "rep", 1)
    pieces = [mine[k] + other[k] for k in range(4)]
    return everyone_of(pieces, "blk")


def per_device(wavefunction, environment, bond_terms, diagonal, term_slot, slot_block):
    blocks, rows, width = wavefunction.shape
    zs = lax.axis_size("blk")
    mpo, rep, blk = lax.axis_index("mpo"), lax.axis_index("rep"), lax.axis_index("blk")
    place = 2 * mpo + rep
    info = jnp.stack([place, place ^ 2, place ^ 1, place ^ 3, blk, rep, mpo]).astype(jnp.int32)
    bonds = environment.shape[0]
    per = bonds // GROUPS
    entries = float(blocks * zs * rows * width)

    vector, own, diagonal_packed = pack(info, wavefunction, diagonal)
    mixing = mixing_operand([bond_terms, partner(bond_terms, "mpo", 1)])
    slots = [term_slot, partner(term_slot, "mpo", 1)]

    by_owner = environment.reshape(bonds, zs, blocks, rows // zs, 2 * rows)
    pieces = [[None] * 4 for _ in range(GROUPS)]
    for group in range(GROUPS):
        mine = by_owner[group * per : (group + 1) * per]
        for k in range(1, 4):
            piece = lax.dynamic_index_in_dim(mine, blk ^ k, 1, keepdims=False)
            if group:
                piece = after(piece, pieces[group - 1][1])
            pieces[group][k] = partner(piece, "blk", k)
    pieces[0][1] = after(pieces[0][1], vector, mixing)
    made, sent = [], []
    for group in range(GROUPS):
        *own_set, send = own_operands(info, by_owner, group, pieces[group][1:])
        made.append(own_set)
        sent.append(send)
    received = [partner(send, "mpo", 1) for send in sent]

    total = None
    operands = []
    for group in range(GROUPS):
        last = group == GROUPS - 1
        given = vector if last else after(vector, *sent)
        out, other = apply_bonds(
            info, slots, [given], [group, GROUPS + group], [made[group]], received[group], mixing,
            total, last,
        )
        operands += [made[group], other]
        total = None if last else out[0]
    image = owner_image(info, slot_block, to_owners(*out), diagonal_packed, own)

    parts = gathered(image)
    chunks = [group + GROUPS * source for group in range(GROUPS) for source in range(2)]
    out, _ = apply_bonds(info, slots, parts, chunks, operands, None, mixing, None, True)
    return tuple(
        outputs(info, slot_block, to_owners(*out), diagonal_packed, own, image, entries)
    )


def solution(mesh):
    packed = mesh.shape["mpo"] == 2 and mesh.shape["rep"] == 2 and mesh.shape["blk"] == 4
    return jax.shard_map(
        per_device if packed else plain_device,
        mesh=mesh,
        in_specs=(
            P(("grp", "blk"), None, None),
            P(("grp", "mpo", "rep"), None, "blk", None),
            P(("grp", "mpo", "rep"), None, None),
            P(("grp", "blk"), None, ("mpo", "rep")),
            P(("grp", "mpo", "rep"), "blk"),
            P("grp", "blk"),
        ),
        out_specs=(
            P(("grp", "blk"), None, ("mpo", "rep")),
            P(("grp", "blk"), None, ("mpo", "rep")),
            P(("grp", "blk"), None, ("mpo", "rep")),
        ),
        check_vma=False,
    )
```

```python
import functools

import jax
import jax.numpy as jnp
from jax import lax
from jax.experimental import pallas as pl
from jax.experimental.pallas import tpu as pltpu
from jax.sharding import PartitionSpec as P

LANES = 128
SUB = 8
PHYS = 16
TINY = 1e-30
GROUPS = 3
SMALL_VMEM = 16 * 1024 * 1024
APPLY_VMEM = 36 * 1024 * 1024


def plain_apply(vector_full, environment, bond_terms, term_slot, slot_block, diagonal):
    block_count, block_rows, block_width = vector_full.shape
    phys_size = bond_terms.shape[-1]
    right_rows = block_width // phys_size
    slot_count = slot_block.shape[0] * slot_block.shape[1]
    blocks = vector_full.reshape(block_count, block_rows, right_rows, phys_size)
    ordered = jnp.transpose(blocks, (0, 3, 1, 2))
    left_env = environment[:, :, :, :block_rows]
    right_env = environment[:, :, :, block_rows:]
    left_done = jnp.einsum("wjab,jsac->wjsbc", left_env, ordered, precision=lax.Precision.HIGHEST)
    right_done = jnp.einsum(
        "wjsbc,wjcd->wjsbd", left_done, right_env, precision=lax.Precision.HIGHEST
    )
    right_done = right_done.reshape(
        environment.shape[0], block_count, phys_size, block_rows * right_rows
    )
    bond_term = jnp.einsum(
        "wjsx,wst->wjtx", right_done, bond_terms, precision=lax.Precision.HIGHEST
    )
    bond_term = bond_term.reshape(environment.shape[0], block_count, block_rows * block_width)
    slot_table = (
        term_slot[:, None, :] == jnp.arange(slot_count, dtype=jnp.int32)[None, :, None]
    ).astype(jnp.float32)
    slot_buffer = jnp.einsum("wsj,wjx->sx", slot_table, bond_term, precision=lax.Precision.HIGHEST)
    slot_buffer = slot_buffer.reshape(slot_count, phys_size, block_rows, right_rows)
    slot_buffer = jnp.transpose(slot_buffer, (0, 2, 3, 1)).reshape(
        slot_count, block_rows, block_width
    )
    owners = slot_block.reshape(-1)
    selector = (owners[None, :] == jnp.arange(block_count, dtype=jnp.int32)[:, None]).astype(
        jnp.float32
    )
    column_width = block_width // lax.axis_size(("mpo", "rep"))
    column_start = lax.axis_index(("mpo", "rep")) * column_width
    own_part = lax.dynamic_slice_in_dim(vector_full, column_start, column_width, 2)
    shares = lax.psum_scatter(slot_buffer, ("mpo", "rep"), scatter_dimension=2, tiled=True)
    arrived = lax.all_to_all(shares, "blk", split_axis=0, concat_axis=0, tiled=True)
    result = jnp.einsum("ks,sbc->kbc", selector, arrived, precision=lax.Precision.HIGHEST)
    return (result + diagonal * own_part, own_part)


def plain_device(wavefunction, environment, bond_terms, diagonal, term_slot, slot_block):
    arranged = lax.all_to_all(environment, "blk", split_axis=1, concat_axis=2, tiled=True)
    entries = float(
        wavefunction.shape[0] * lax.axis_size("blk") * wavefunction.shape[1] * wavefunction.shape[2]
    )
    square_sum = lax.psum(jnp.sum(wavefunction * wavefunction), "blk")
    first_vector = wavefunction * lax.rsqrt(square_sum / entries + 1e-06)
    first_image, first_part = plain_apply(
        first_vector, arranged, bond_terms, term_slot, slot_block, diagonal
    )
    rayleigh = lax.psum(jnp.sum(first_part * first_image), ("blk", "mpo", "rep")) / entries
    residual = first_image - rayleigh * first_part
    resid_sum = lax.psum(jnp.sum(residual * residual), ("blk", "mpo", "rep"))
    second_vector = residual * lax.rsqrt(resid_sum / entries + 1e-06)
    second_full = lax.all_gather(second_vector, ("mpo", "rep"), axis=2, tiled=True)
    second_image, unused = plain_apply(
        second_full, arranged, bond_terms, term_slot, slot_block, diagonal
    )
    return (first_image, second_vector, second_image)


def split_two(x):
    high = x.astype(jnp.bfloat16)
    low = (x - high.astype(jnp.float32)).astype(jnp.bfloat16)
    return high, low


def lane_is_first(rows):
    return lax.broadcasted_iota(jnp.int32, (rows, LANES), 1) < LANES // 2


def micros(count):
    return pl.CostEstimate(flops=count * 1100000000, bytes_accessed=1 << 20, transcendentals=0)


def whole(*shape):
    return pl.BlockSpec(shape, lambda i, *_: (0,) * len(shape))


def pack_tile(x):
    return jnp.concatenate([x[:, :LANES], x[:, LANES:]], axis=0).T


def unpack_tile(x):
    upright = x.T
    return jnp.concatenate([upright[: LANES // 2], upright[LANES // 2 :]], axis=1)


def store_vector(parts, rows_of, put):
    first = lane_is_first(SUB)
    for pair in range(PHYS // 2):
        for part, row in zip(parts, rows_of):
            even = part[pl.ds(2 * pair, SUB, stride=PHYS), :]
            odd = part[pl.ds(2 * pair + 1, SUB, stride=PHYS), :]
            upper = jnp.where(first, even, pltpu.roll(odd, LANES // 2, 1))
            lower = jnp.where(first, pltpu.roll(even, LANES // 2, 1), odd)
            high, low = split_two(jnp.concatenate([upper, lower], axis=0))
            put(row, pair, high, low)


def pack_kernel(info_ref, wave_ref, own_wave_ref, diag_ref, vec_ref, own_ref, diag_out, tiles):
    half = LANES // 2
    for j in range(wave_ref.shape[0]):
        own_ref[j] = pack_tile(own_wave_ref[j])
        diag_out[j] = pack_tile(diag_ref[j])
        for q in range(4):
            tiles[q, j] = pack_tile(wave_ref[j, :, 2 * LANES * q : 2 * LANES * (q + 1)])

        def put(row, pair, high, low):
            columns = slice(pair * LANES, (pair + 1) * LANES)
            vec_ref[j, row : row + 16, columns] = high
            vec_ref[j, row + half : row + half + 16, columns] = low

        store_vector([tiles.at[q, j] for q in range(4)], [16 * q for q in range(4)], put)


def pack(info, wavefunction, diagonal):
    blocks, rows, width = wavefunction.shape
    step = 2
    tile = pl.BlockSpec((step, LANES, LANES), lambda i, *_: (i, 0, 0))
    return pl.pallas_call(
        pack_kernel,
        grid_spec=pltpu.PrefetchScalarGridSpec(
            num_scalar_prefetch=1,
            grid=(blocks // step,),
            in_specs=[
                pl.BlockSpec((step, rows, width), lambda i, *_: (i, 0, 0)),
                pl.BlockSpec((step, rows, width // 4), lambda i, info: (i, 0, info[0])),
                pl.BlockSpec((step, rows, width // 4), lambda i, *_: (i, 0, 0)),
            ],
            out_specs=[pl.BlockSpec((step, LANES, width), lambda i, *_: (i, 0, 0)), tile, tile],
            scratch_shapes=[pltpu.VMEM((4, step, LANES, LANES), jnp.float32)],
        ),
        out_shape=[
            jax.ShapeDtypeStruct((blocks, LANES, width), jnp.bfloat16),
            jax.ShapeDtypeStruct((blocks, LANES, LANES), jnp.float32),
            jax.ShapeDtypeStruct((blocks, LANES, LANES), jnp.float32),
        ],
        compiler_params=pltpu.CompilerParams(vmem_limit_bytes=SMALL_VMEM),
        cost_estimate=micros(5),
        name="pack",
    )(info, wavefunction, wavefunction, diagonal)


def mixing_kernel(*refs):
    sources, out_ref = refs[:-1], refs[-1]
    spread = (
        lax.broadcasted_iota(jnp.int32, (PHYS, LANES), 1) // SUB
        == lax.broadcasted_iota(jnp.int32, (PHYS, LANES), 0)
    ).astype(jnp.bfloat16)
    row = lax.broadcasted_iota(jnp.int32, (LANES, LANES), 0) // PHYS
    column = lax.broadcasted_iota(jnp.int32, (LANES, LANES), 1) % SUB
    same = row == column
    at = 0
    for source in sources:
        for k in range(source.shape[0]):
            high, low = split_two(source[k].T)
            for term, places in ((high, (0, 1)), (low, (2,))):
                wide = jnp.dot(term, spread, preferred_element_type=jnp.float32)
                tall = jnp.concatenate([wide] * SUB, axis=0)
                tall = jnp.where(same, tall, 0.0).astype(jnp.bfloat16)
                for place in places:
                    out_ref[at, :, place * LANES : (place + 1) * LANES] = tall
            at += 1


def mixing_operand(sources):
    count = sources[0].shape[0] * len(sources)
    return pl.pallas_call(
        mixing_kernel,
        out_shape=jax.ShapeDtypeStruct((count, LANES, 3 * LANES), jnp.bfloat16),
        compiler_params=pltpu.CompilerParams(vmem_limit_bytes=SMALL_VMEM),
        cost_estimate=micros(2),
        name="mixing",
    )(*sources)


def own_operands_kernel(info_ref, *refs):
    pieces, (left_high, left_low, right_out, send, blocks_ref, upright_ref) = refs[:4], refs[4:]
    per, blocks, half, lanes = left_high.shape
    rows = half // 4
    wide = half // 2
    first = lane_is_first(half)
    first_wide = lane_is_first(wide)
    first_rows = lane_is_first(rows)
    mine_at = pl.multiple_of(half + info_ref[6] * wide, wide)
    theirs_at = pl.multiple_of(lanes - wide - info_ref[6] * wide, wide)
    for j in range(blocks):
        for w in range(per):
            for z in range(4):
                row = pl.multiple_of((info_ref[4] ^ z) * rows, rows)
                piece = pieces[z][w, 0, j] if z == 0 else pieces[z][w, j]
                blocks_ref[w, j, pl.ds(row, rows), :] = piece
        for w in range(per):
            block = blocks_ref[w, j]
            upright_ref[w, j] = jnp.concatenate([block, block], axis=0).T
            turned = pltpu.roll(block, half, 1)
            high, low = split_two(jnp.where(first, block, turned))
            left_high[w, j] = high
            left_low[w, j] = low
            send[w, j, 0:wide] = jnp.where(first_wide, block[:wide], turned[wide:])
        for w in range(per):
            high, low = split_two(upright_ref[w, j, pl.ds(mine_at, wide), :])
            right_out[j, wide * w : wide * (w + 1), 0:lanes] = high
            right_out[j, wide * w : wide * (w + 1), lanes:] = low
            upper = upright_ref[w, j, pl.ds(theirs_at, rows), :]
            lower = upright_ref[w, j, pl.ds(theirs_at + rows, rows), :]
            send[w, j, wide : wide + rows] = jnp.where(first_rows, upper, lower)


def other_operands(sent, left_high, left_low, right_out, j):
    per, blocks, half, lanes = left_high.shape
    rows = half // 4
    wide = half // 2
    first = lane_is_first(wide)
    first_rows = lane_is_first(rows)
    for w in range(per):
        both = sent[w, j, 0:wide]
        turned = pltpu.roll(both, half, 1)
        full = jnp.concatenate(
            [jnp.where(first, both, turned), jnp.where(first, turned, both)], axis=0
        )
        high, low = split_two(full)
        left_high[w, j] = high
        left_low[w, j] = low
        both = sent[w, j, wide : wide + rows]
        turned = pltpu.roll(both, half, 1)
        full = jnp.concatenate(
            [jnp.where(first_rows, both, turned), jnp.where(first_rows, turned, both)], axis=0
        )
        high, low = split_two(full)
        right_out[j, wide * w : wide * (w + 1), 0:lanes] = high
        right_out[j, wide * w : wide * (w + 1), lanes:] = low


def operand_specs(per, step, half, lanes):
    return [
        pl.BlockSpec((per, step, half, lanes), lambda i, *_: (0, i, 0, 0)),
        pl.BlockSpec((per, step, half, lanes), lambda i, *_: (0, i, 0, 0)),
        pl.BlockSpec((step, per * 32, 2 * lanes), lambda i, *_: (i, 0, 0)),
    ]


def operand_shapes(per, blocks, half, lanes):
    return [
        jax.ShapeDtypeStruct((per, blocks, half, lanes), jnp.bfloat16),
        jax.ShapeDtypeStruct((per, blocks, half, lanes), jnp.bfloat16),
        jax.ShapeDtypeStruct((blocks, per * 32, 2 * lanes), jnp.bfloat16),
    ]


def own_operands(info, by_owner, group, pieces):
    per, blocks, rows, lanes = pieces[0].shape
    half = lanes // 2
    step = 4
    return pl.pallas_call(
        own_operands_kernel,
        grid_spec=pltpu.PrefetchScalarGridSpec(
            num_scalar_prefetch=1,
            grid=(blocks // step,),
            in_specs=[
                pl.BlockSpec(
                    (per, 1, step, rows, lanes), lambda i, info: (group, info[4], i, 0, 0)
                )
            ]
            + [pl.BlockSpec((per, step, rows, lanes), lambda i, *_: (0, i, 0, 0))] * 3,
            out_specs=operand_specs(per, step, half, lanes)
            + [pl.BlockSpec((per, step, 3 * rows, lanes), lambda i, *_: (0, i, 0, 0))],
            scratch_shapes=[
                pltpu.VMEM((per, step, half, lanes), jnp.float32),
                pltpu.VMEM((per, step, lanes, lanes), jnp.float32),
            ],
        ),
        out_shape=operand_shapes(per, blocks, half, lanes)
        + [jax.ShapeDtypeStruct((per, blocks, 3 * rows, lanes), jnp.float32)],
        compiler_params=pltpu.CompilerParams(vmem_limit_bytes=SMALL_VMEM),
        cost_estimate=micros(6),
        name="own_operands",
    )(info, by_owner, *pieces)


def apply_kernel(plan, info_ref, *refs):
    chunks, parts_given, sent_given, before_given, pieces = plan
    refs = list(refs)
    take = lambda n: [refs.pop(0) for _ in range(n)]
    slots = take(2)
    vector = take(4 if parts_given else 1)
    tiles = take(4) if parts_given else []
    operands = [take(3) for _ in chunks[: -1 if sent_given else None]]
    sent = take(1)[0] if sent_given else None
    mixes = take(len(chunks))
    before = take(1)[0] if before_given else None
    outs = take(2 if pieces else 1)
    if sent_given:
        operands.append(take(3))
    total_ref, vec, mid = take(3)
    if before_given:
        prior, arrival = take(2)
    step = mid.shape[0]
    lanes, half = LANES, LANES // 2
    first = lane_is_first(SUB)
    first_half = lane_is_first(half)
    keep_first = jnp.where(first_half, 1.0, 0.0).astype(jnp.bfloat16)
    keep_second = jnp.where(first_half, 0.0, 1.0).astype(jnp.bfloat16)
    nothing = jnp.zeros((lanes, lanes), jnp.bfloat16)
    me = info_ref[4]

    @pl.when(pl.program_id(0) == 0)
    def _():
        if before_given:
            pltpu.make_async_copy(before, prior, arrival).start()
        total_ref[...] = jnp.zeros_like(total_ref)

    def right_side(j):
        if sent_given:
            other_operands(sent, *operands[-1], j)
        if parts_given:

            def put(row, pair, high, low):
                columns = slice(pair * lanes, (pair + 1) * lanes)
                vec[j, pl.ds(row, 16), columns] = high
                vec[j, pl.ds(row + half, 16), columns] = low

            rows_of = [pl.multiple_of(info_ref[g] * 16, 16) for g in range(4)]
            store_vector([x.at[pl.ds(j * lanes, lanes)] for x in vector], rows_of, put)
            source = vec[j]
        else:
            source = vector[0][j]
        source = jnp.concatenate([source, source], axis=0)
        at = 0
        for left_high, left_low, right in operands:
            count = right.shape[1]
            mid[j, at : at + count, :] = jnp.dot(
                right[j], source, preferred_element_type=jnp.float32
            )
            at += count

    def prepared(j, refs_of, w, row_of):
        left_high, left_low, right = refs_of
        tiles = []
        for part in range(2):
            row = row_of + part * 16
            for pair in range(PHYS // 2):
                columns = slice(pair * lanes, (pair + 1) * lanes)
                upper = mid[j, row : row + SUB, columns]
                lower = mid[j, row + SUB : row + 2 * SUB, columns]
                tiles.append(jnp.where(first, upper, pltpu.roll(lower, half, 1)))
                tiles.append(jnp.where(first, pltpu.roll(upper, half, 1), lower))
        t_high, t_low = split_two(jnp.concatenate(tiles, axis=0))
        lh, ll = left_high[w, j], left_low[w, j]
        wide_high = jnp.concatenate([lh * keep_first, lh * keep_second], axis=0)
        wide_low = jnp.concatenate([ll * keep_first, ll * keep_second], axis=0)
        weights = jnp.concatenate(
            [
                jnp.concatenate([wide_high, wide_low], axis=1),
                jnp.concatenate([wide_high, nothing], axis=1),
            ],
            axis=0,
        )
        return jnp.concatenate([t_high, t_low], axis=1), weights

    def mix_unit(mixing, w, z):
        z_high, z_low = [jnp.concatenate([x[:lanes], x[lanes:]], axis=1) for x in z]
        return jnp.dot(
            mixing[w],
            jnp.concatenate([z_high, z_low, z_high], axis=0),
            preferred_element_type=jnp.float32,
        )

    def add_up(j, table, bond, mixed):
        slot = table[bond, pl.program_id(0) * step + j]
        slot = ((slot >> 1) ^ me) * 2 + (slot & 1)
        for part in range(2):
            total_ref[part, slot] += mixed[:, part * lanes : (part + 1) * lanes]

    bonds = []
    for chunk, refs_of, mix in zip(chunks, operands, mixes):
        count = mix.shape[0]
        source, group = chunk // GROUPS, chunk % GROUPS
        for w in range(count):
            bonds.append((refs_of, mix, w, slots[source], group * count + w))
    right_side(0)
    units = [(j, at) for j in range(step) for at in range(len(bonds))]

    def prepare_unit(n):
        j, at = units[n]
        refs_of, mixing, w, table, bond = bonds[at]
        return prepared(j, refs_of, w, at * 32)

    ready = prepare_unit(0)
    waiting = None
    for n, (j, at) in enumerate(units):
        refs_of, mixing, w, table, bond = bonds[at]
        z = jnp.dot(*ready, preferred_element_type=jnp.float32)
        if j + 1 < step and at == len(bonds) // 3:
            right_side(j + 1)
        if n + 1 < len(units):
            ready = prepare_unit(n + 1)
        if waiting is not None:
            before_j, before_mixing, before_w, before_table, before_bond, before_z = waiting
            mixed = mix_unit(before_mixing, before_w, before_z)
        z = split_two(z[:, :lanes] + z[:, lanes:])
        if waiting is not None:
            add_up(before_j, before_table, before_bond, mixed)
        waiting = (j, mixing, w, table, bond, z)
    j, mixing, w, table, bond, z = waiting
    add_up(j, table, bond, mix_unit(mixing, w, z))

    @pl.when(pl.program_id(0) == pl.num_programs(0) - 1)
    def _():
        if before_given:
            pltpu.make_async_copy(before, prior, arrival).wait()
            total_ref[...] += prior[...]
        if pieces:
            stats = jnp.zeros((SUB, lanes), jnp.float32)
            if parts_given:
                stats = stacked_rows(*merged([tile[...] for tile in tiles]))
            for out, part in ((outs[0], info_ref[5]), (outs[1], 1 - info_ref[5])):
                for k in range(4):
                    for i in range(2):
                        out[k, i * lanes : (i + 1) * lanes] = total_ref[part, 2 * k + i]
                    out[k, 2 * lanes :] = stats
                stats = jnp.zeros((SUB, lanes), jnp.float32)
        else:
            outs[0][...] = total_ref[...]


def apply_bonds(info, slots, vector, chunks, operands, sent, mixing, before, pieces):
    count, blocks, half, lanes = operands[0][0].shape
    step = 4
    parts_given = len(vector) == 4
    if parts_given:
        last = vector[0].shape[0] // SUB - 1
        in_specs = [pl.BlockSpec((step * lanes, lanes), lambda i, *_: (i, 0))] * 4
        in_specs += [pl.BlockSpec((SUB, lanes), lambda i, *_: (last, 0))] * 4
    else:
        in_specs = [pl.BlockSpec((step,) + vector[0].shape[1:], lambda i, *_: (i, 0, 0))]
    arguments = list(vector) * (2 if parts_given else 1)
    for made in operands:
        in_specs += operand_specs(count, step, half, lanes)
        arguments += made
    if sent is not None:
        in_specs.append(
            pl.BlockSpec((count, step) + sent.shape[2:], lambda i, *_: (0, i, 0, 0))
        )
        arguments.append(sent)
    for chunk in chunks:
        in_specs.append(
            pl.BlockSpec((count,) + mixing.shape[1:], lambda i, *_, at=chunk: (at, 0, 0))
        )
        arguments.append(mixing)
    total = count * len(chunks)
    scratch = [
        pltpu.VMEM((2, 8, lanes, lanes), jnp.float32),
        pltpu.VMEM((step, lanes, PHYS * half), jnp.bfloat16),
        pltpu.VMEM((step, total * 32, PHYS * half), jnp.float32),
    ]
    if before is not None:
        in_specs.append(pl.BlockSpec(memory_space=pl.ANY))
        arguments.append(before)
        scratch += [pltpu.VMEM(before.shape, jnp.float32), pltpu.SemaphoreType.DMA]
    shapes = [(4, 2 * lanes + SUB, lanes)] * 2 if pieces else [(2, 8, lanes, lanes)]
    out_specs = [whole(*shape) for shape in shapes]
    out_shape = [jax.ShapeDtypeStruct(shape, jnp.float32) for shape in shapes]
    if sent is not None:
        out_specs += operand_specs(count, step, half, lanes)
        out_shape += operand_shapes(count, blocks, half, lanes)
    plan = (tuple(chunks), parts_given, sent is not None, before is not None, pieces)
    out = pl.pallas_call(
        functools.partial(apply_kernel, plan),
        grid_spec=pltpu.PrefetchScalarGridSpec(
            num_scalar_prefetch=3,
            grid=(blocks // step,),
            in_specs=in_specs,
            out_specs=out_specs,
            scratch_shapes=scratch,
        ),
        out_shape=out_shape,
        compiler_params=pltpu.CompilerParams(vmem_limit_bytes=APPLY_VMEM),
        cost_estimate=micros(1),
        name="apply_bonds",
    )(info, *slots, *arguments)
    return out[: len(shapes)], out[len(shapes) :]


def add_arrived(info_ref, owner_ref, arrived, total):
    for k in range(4):
        for i in range(2):
            rows = slice(i * LANES, (i + 1) * LANES)
            total[owner_ref[info_ref[4] ^ k, i]] += arrived[k][rows]


def stacked_rows(*rows):
    at = lax.broadcasted_iota(jnp.int32, (SUB, LANES), 0)
    tile = jnp.zeros((SUB, LANES), jnp.float32)
    for i, row in enumerate(rows):
        tile = jnp.where(at == i, row, tile)
    return tile


def merged(tiles):
    rows = [[tile[i : i + 1] for i in range(3)] for tile in tiles]
    cross = sum(row[0] for row in rows)
    square = sum(row[1] for row in rows)
    ratio = cross / jnp.maximum(square, TINY)
    apart = [
        (row[0] / jnp.maximum(row[1], TINY) - ratio) * jnp.sqrt(row[1]) for row in rows
    ]
    rest = sum(row[2] for row in rows) + sum(x * x for x in apart)
    return cross, square, rest


def image_kernel(info_ref, owner_ref, a0, a1, a2, a3, diag_ref, own_ref, image_ref, total):
    total[...] = diag_ref[...] * own_ref[...]
    add_arrived(info_ref, owner_ref, (a0, a1, a2, a3), total)
    blocks = total.shape[0]
    cross = jnp.zeros((LANES, LANES), jnp.float32)
    square = jnp.zeros((LANES, LANES), jnp.float32)
    for k in range(blocks):
        own, image = own_ref[k], total[k]
        image_ref[k * LANES : (k + 1) * LANES] = image
        cross += own * image
        square += own * own
    cross = jnp.sum(cross, keepdims=True)
    square = jnp.sum(square, keepdims=True)
    ratio = cross / jnp.maximum(square, TINY)
    rest = jnp.zeros((LANES, LANES), jnp.float32)
    for k in range(blocks):
        apart = total[k] - ratio * own_ref[k]
        rest += apart * apart
    image_ref[blocks * LANES :] = stacked_rows(cross, square, jnp.sum(rest, keepdims=True))


def owner_image(info, owners, arrived, diagonal, own):
    rows = own.shape[0] * LANES + SUB
    return pl.pallas_call(
        image_kernel,
        grid_spec=pltpu.PrefetchScalarGridSpec(
            num_scalar_prefetch=2,
            grid=(1,),
            in_specs=[whole(*x.shape) for x in (*arrived, diagonal, own)],
            out_specs=whole(rows, LANES),
            scratch_shapes=[pltpu.VMEM(own.shape, jnp.float32)],
        ),
        out_shape=jax.ShapeDtypeStruct((rows, LANES), jnp.float32),
        compiler_params=pltpu.CompilerParams(vmem_limit_bytes=SMALL_VMEM),
        cost_estimate=micros(3),
        name="owner_image",
    )(info, owners, *arrived, diagonal, own)


def final_kernel(
    entries, info_ref, owner_ref, a0, a1, a2, a3, diag_ref, own_ref, image_ref, first_ref,
    vector_ref, second_ref, total,
):
    arrived = (a0, a1, a2, a3)
    cross, square, rest = merged([ref[2 * LANES :] for ref in arrived])
    scale = lax.rsqrt(square / entries + 1e-06)
    rayleigh = scale * scale * (cross / entries)
    apart = (cross / jnp.maximum(square, TINY) - rayleigh) * jnp.sqrt(square)
    mean = scale * scale * ((rest + apart * apart) / entries)
    second_scale = scale * lax.rsqrt(mean + 1e-06)
    for k in range(total.shape[0]):
        image = image_ref[k * LANES : (k + 1) * LANES]
        total[k] = (diag_ref[k] - rayleigh) * image
        first_ref[k] = unpack_tile(scale * image)
        vector_ref[k] = unpack_tile(second_scale * (image - rayleigh * own_ref[k]))
    add_arrived(info_ref, owner_ref, arrived, total)
    for k in range(total.shape[0]):
        second_ref[k] = unpack_tile(second_scale * total[k])


def outputs(info, owners, arrived, diagonal, own, image, entries):
    blocks = diagonal.shape[0]
    shape = (blocks, LANES // 2, 2 * LANES)
    return pl.pallas_call(
        functools.partial(final_kernel, entries),
        grid_spec=pltpu.PrefetchScalarGridSpec(
            num_scalar_prefetch=2,
            grid=(1,),
            in_specs=[whole(*x.shape) for x in (*arrived, diagonal, own)]
            + [whole(blocks * LANES, LANES)],
            out_specs=[whole(*shape)] * 3,
            scratch_shapes=[pltpu.VMEM(diagonal.shape, jnp.float32)],
        ),
        out_shape=[jax.ShapeDtypeStruct(shape, jnp.float32)] * 3,
        compiler_params=pltpu.CompilerParams(vmem_limit_bytes=SMALL_VMEM),
        cost_estimate=micros(4),
        name="outputs",
    )(info, owners, *arrived, diagonal, own, image)


def partner(x, axis, k):
    size = lax.axis_size(axis)
    return lax.ppermute(x, axis, [(i, i ^ k) for i in range(size)])


def after(x, *others):
    return lax.optimization_barrier((x, *others))[0]


def gathered(x):
    across = partner(x, "mpo", 1)
    return [x, across, partner(x, "rep", 1), partner(across, "rep", 1)]


def everyone_of(pieces, axis):
    return [pieces[0]] + [partner(pieces[k], axis, k) for k in range(1, 4)]


def to_owners(mine, theirs):
    other = partner(theirs, "rep", 1)
    pieces = [mine[k] + other[k] for k in range(4)]
    return everyone_of(pieces, "blk")


def per_device(wavefunction, environment, bond_terms, diagonal, term_slot, slot_block):
    blocks, rows, width = wavefunction.shape
    zs = lax.axis_size("blk")
    mpo, rep, blk = lax.axis_index("mpo"), lax.axis_index("rep"), lax.axis_index("blk")
    place = 2 * mpo + rep
    info = jnp.stack([place, place ^ 2, place ^ 1, place ^ 3, blk, rep, mpo]).astype(jnp.int32)
    bonds = environment.shape[0]
    per = bonds // GROUPS
    entries = float(blocks * zs * rows * width)

    vector, own, diagonal_packed = pack(info, wavefunction, diagonal)
    mixing = mixing_operand([bond_terms, partner(bond_terms, "mpo", 1)])
    slots = [term_slot, partner(term_slot, "mpo", 1)]

    by_owner = environment.reshape(bonds, zs, blocks, rows // zs, 2 * rows)
    pieces = [[None] * 4 for _ in range(GROUPS)]
    for group in range(GROUPS):
        mine = by_owner[group * per : (group + 1) * per]
        for k in range(1, 4):
            piece = lax.dynamic_index_in_dim(mine, blk ^ k, 1, keepdims=False)
            if group:
                piece = after(piece, pieces[group - 1][1])
            pieces[group][k] = partner(piece, "blk", k)
    pieces[0][1] = after(pieces[0][1], vector, mixing)
    made, sent = [], []
    total = None
    operands = []
    done = 0

    def apply_group(group, vector):
        last = group == GROUPS - 1
        out, other = apply_bonds(
            info, slots, [vector], [group, GROUPS + group], [made[group]],
            partner(sent[group], "mpo", 1), mixing, total, last,
        )
        operands.extend([made[group], other])
        return out

    for group in range(GROUPS):
        if group >= 2:
            total = apply_group(group - 2, after(vector, sent[group - 1]))[0]
            pieces[group][3] = after(pieces[group][3], total)
        *own_set, send = own_operands(info, by_owner, group, pieces[group][1:])
        made.append(own_set)
        sent.append(send)
    total = apply_group(GROUPS - 2, after(vector, sent[-1]))[0]
    out = apply_group(GROUPS - 1, vector)
    image = owner_image(info, slot_block, to_owners(*out), diagonal_packed, own)

    parts = gathered(image)
    chunks = [group + GROUPS * source for group in range(GROUPS) for source in range(2)]
    out, _ = apply_bonds(info, slots, parts, chunks, operands, None, mixing, None, True)
    return tuple(
        outputs(info, slot_block, to_owners(*out), diagonal_packed, own, image, entries)
    )


def solution(mesh):
    packed = mesh.shape["mpo"] == 2 and mesh.shape["rep"] == 2 and mesh.shape["blk"] == 4
    return jax.shard_map(
        per_device if packed else plain_device,
        mesh=mesh,
        in_specs=(
            P(("grp", "blk"), None, None),
            P(("grp", "mpo", "rep"), None, "blk", None),
            P(("grp", "mpo", "rep"), None, None),
            P(("grp", "blk"), None, ("mpo", "rep")),
            P(("grp", "mpo", "rep"), "blk"),
            P("grp", "blk"),
        ),
        out_specs=(
            P(("grp", "blk"), None, ("mpo", "rep")),
            P(("grp", "blk"), None, ("mpo", "rep")),
            P(("grp", "blk"), None, ("mpo", "rep")),
        ),
        check_vma=False,
    )
```

```python
import functools

import jax
import jax.numpy as jnp
from jax import lax
from jax.experimental import pallas as pl
from jax.experimental.pallas import tpu as pltpu
from jax.sharding import PartitionSpec as P

LANES = 128
SUB = 8
PHYS = 16
TINY = 1e-30
GROUPS = 3
SMALL_VMEM = 16 * 1024 * 1024
APPLY_VMEM = 36 * 1024 * 1024


def plain_apply(vector_full, environment, bond_terms, term_slot, slot_block, diagonal):
    block_count, block_rows, block_width = vector_full.shape
    phys_size = bond_terms.shape[-1]
    right_rows = block_width // phys_size
    slot_count = slot_block.shape[0] * slot_block.shape[1]
    blocks = vector_full.reshape(block_count, block_rows, right_rows, phys_size)
    ordered = jnp.transpose(blocks, (0, 3, 1, 2))
    left_env = environment[:, :, :, :block_rows]
    right_env = environment[:, :, :, block_rows:]
    left_done = jnp.einsum("wjab,jsac->wjsbc", left_env, ordered, precision=lax.Precision.HIGHEST)
    right_done = jnp.einsum(
        "wjsbc,wjcd->wjsbd", left_done, right_env, precision=lax.Precision.HIGHEST
    )
    right_done = right_done.reshape(
        environment.shape[0], block_count, phys_size, block_rows * right_rows
    )
    bond_term = jnp.einsum(
        "wjsx,wst->wjtx", right_done, bond_terms, precision=lax.Precision.HIGHEST
    )
    bond_term = bond_term.reshape(environment.shape[0], block_count, block_rows * block_width)
    slot_table = (
        term_slot[:, None, :] == jnp.arange(slot_count, dtype=jnp.int32)[None, :, None]
    ).astype(jnp.float32)
    slot_buffer = jnp.einsum("wsj,wjx->sx", slot_table, bond_term, precision=lax.Precision.HIGHEST)
    slot_buffer = slot_buffer.reshape(slot_count, phys_size, block_rows, right_rows)
    slot_buffer = jnp.transpose(slot_buffer, (0, 2, 3, 1)).reshape(
        slot_count, block_rows, block_width
    )
    owners = slot_block.reshape(-1)
    selector = (owners[None, :] == jnp.arange(block_count, dtype=jnp.int32)[:, None]).astype(
        jnp.float32
    )
    column_width = block_width // lax.axis_size(("mpo", "rep"))
    column_start = lax.axis_index(("mpo", "rep")) * column_width
    own_part = lax.dynamic_slice_in_dim(vector_full, column_start, column_width, 2)
    shares = lax.psum_scatter(slot_buffer, ("mpo", "rep"), scatter_dimension=2, tiled=True)
    arrived = lax.all_to_all(shares, "blk", split_axis=0, concat_axis=0, tiled=True)
    result = jnp.einsum("ks,sbc->kbc", selector, arrived, precision=lax.Precision.HIGHEST)
    return (result + diagonal * own_part, own_part)


def plain_device(wavefunction, environment, bond_terms, diagonal, term_slot, slot_block):
    arranged = lax.all_to_all(environment, "blk", split_axis=1, concat_axis=2, tiled=True)
    entries = float(
        wavefunction.shape[0] * lax.axis_size("blk") * wavefunction.shape[1] * wavefunction.shape[2]
    )
    square_sum = lax.psum(jnp.sum(wavefunction * wavefunction), "blk")
    first_vector = wavefunction * lax.rsqrt(square_sum / entries + 1e-06)
    first_image, first_part = plain_apply(
        first_vector, arranged, bond_terms, term_slot, slot_block, diagonal
    )
    rayleigh = lax.psum(jnp.sum(first_part * first_image), ("blk", "mpo", "rep")) / entries
    residual = first_image - rayleigh * first_part
    resid_sum = lax.psum(jnp.sum(residual * residual), ("blk", "mpo", "rep"))
    second_vector = residual * lax.rsqrt(resid_sum / entries + 1e-06)
    second_full = lax.all_gather(second_vector, ("mpo", "rep"), axis=2, tiled=True)
    second_image, unused = plain_apply(
        second_full, arranged, bond_terms, term_slot, slot_block, diagonal
    )
    return (first_image, second_vector, second_image)


def split_two(x):
    high = x.astype(jnp.bfloat16)
    low = (x - high.astype(jnp.float32)).astype(jnp.bfloat16)
    return high, low


def lane_is_first(rows):
    return lax.broadcasted_iota(jnp.int32, (rows, LANES), 1) < LANES // 2


def micros(count):
    return pl.CostEstimate(flops=count * 1100000000, bytes_accessed=1 << 20, transcendentals=0)


def whole(*shape):
    return pl.BlockSpec(shape, lambda i, *_: (0,) * len(shape))


def pack_tile(x):
    return jnp.concatenate([x[:, :LANES], x[:, LANES:]], axis=0).T


def unpack_tile(x):
    upright = x.T
    return jnp.concatenate([upright[: LANES // 2], upright[LANES // 2 :]], axis=1)


def store_vector(parts, rows_of, put):
    first = lane_is_first(SUB)
    for pair in range(PHYS // 2):
        for part, row in zip(parts, rows_of):
            even = part[pl.ds(2 * pair, SUB, stride=PHYS), :]
            odd = part[pl.ds(2 * pair + 1, SUB, stride=PHYS), :]
            upper = jnp.where(first, even, pltpu.roll(odd, LANES // 2, 1))
            lower = jnp.where(first, pltpu.roll(even, LANES // 2, 1), odd)
            high, low = split_two(jnp.concatenate([upper, lower], axis=0))
            put(row, pair, high, low)


def pack_kernel(info_ref, wave_ref, own_wave_ref, diag_ref, vec_ref, own_ref, diag_out, tiles):
    half = LANES // 2
    for j in range(wave_ref.shape[0]):
        own_ref[j] = pack_tile(own_wave_ref[j])
        diag_out[j] = pack_tile(diag_ref[j])
        for q in range(4):
            tiles[q, j] = pack_tile(wave_ref[j, :, 2 * LANES * q : 2 * LANES * (q + 1)])

        def put(row, pair, high, low):
            columns = slice(pair * LANES, (pair + 1) * LANES)
            vec_ref[j, row : row + 16, columns] = high
            vec_ref[j, row + half : row + half + 16, columns] = low

        store_vector([tiles.at[q, j] for q in range(4)], [16 * q for q in range(4)], put)


def pack(info, wavefunction, diagonal):
    blocks, rows, width = wavefunction.shape
    step = 2
    tile = pl.BlockSpec((step, LANES, LANES), lambda i, *_: (i, 0, 0))
    return pl.pallas_call(
        pack_kernel,
        grid_spec=pltpu.PrefetchScalarGridSpec(
            num_scalar_prefetch=1,
            grid=(blocks // step,),
            in_specs=[
                pl.BlockSpec((step, rows, width), lambda i, *_: (i, 0, 0)),
                pl.BlockSpec((step, rows, width // 4), lambda i, info: (i, 0, info[0])),
                pl.BlockSpec((step, rows, width // 4), lambda i, *_: (i, 0, 0)),
            ],
            out_specs=[pl.BlockSpec((step, LANES, width), lambda i, *_: (i, 0, 0)), tile, tile],
            scratch_shapes=[pltpu.VMEM((4, step, LANES, LANES), jnp.float32)],
        ),
        out_shape=[
            jax.ShapeDtypeStruct((blocks, LANES, width), jnp.bfloat16),
            jax.ShapeDtypeStruct((blocks, LANES, LANES), jnp.float32),
            jax.ShapeDtypeStruct((blocks, LANES, LANES), jnp.float32),
        ],
        compiler_params=pltpu.CompilerParams(vmem_limit_bytes=SMALL_VMEM),
        cost_estimate=micros(5),
        name="pack",
    )(info, wavefunction, wavefunction, diagonal)


def mixing_kernel(*refs):
    sources, out_ref = refs[:-1], refs[-1]
    spread = (
        lax.broadcasted_iota(jnp.int32, (PHYS, LANES), 1) // SUB
        == lax.broadcasted_iota(jnp.int32, (PHYS, LANES), 0)
    ).astype(jnp.bfloat16)
    row = lax.broadcasted_iota(jnp.int32, (LANES, LANES), 0) // PHYS
    column = lax.broadcasted_iota(jnp.int32, (LANES, LANES), 1) % SUB
    same = row == column
    at = 0
    for source in sources:
        for k in range(source.shape[0]):
            high, low = split_two(source[k].T)
            for term, places in ((high, (0, 1)), (low, (2,))):
                wide = jnp.dot(term, spread, preferred_element_type=jnp.float32)
                tall = jnp.concatenate([wide] * SUB, axis=0)
                tall = jnp.where(same, tall, 0.0).astype(jnp.bfloat16)
                for place in places:
                    out_ref[at, :, place * LANES : (place + 1) * LANES] = tall
            at += 1


def mixing_operand(sources):
    count = sources[0].shape[0] * len(sources)
    return pl.pallas_call(
        mixing_kernel,
        out_shape=jax.ShapeDtypeStruct((count, LANES, 3 * LANES), jnp.bfloat16),
        compiler_params=pltpu.CompilerParams(vmem_limit_bytes=SMALL_VMEM),
        cost_estimate=micros(2),
        name="mixing",
    )(*sources)


def own_operands_kernel(info_ref, *refs):
    pieces, (left_high, left_low, right_out, send, blocks_ref, upright_ref) = refs[:4], refs[4:]
    per, blocks, half, lanes = left_high.shape
    rows = half // 4
    wide = half // 2
    first = lane_is_first(half)
    first_wide = lane_is_first(wide)
    first_rows = lane_is_first(rows)
    mine_at = pl.multiple_of(half + info_ref[6] * wide, wide)
    theirs_at = pl.multiple_of(lanes - wide - info_ref[6] * wide, wide)
    for j in range(blocks):
        for w in range(per):
            for z in range(4):
                row = pl.multiple_of((info_ref[4] ^ z) * rows, rows)
                piece = pieces[z][w, 0, j] if z == 0 else pieces[z][w, j]
                blocks_ref[w, j, pl.ds(row, rows), :] = piece
        for w in range(per):
            block = blocks_ref[w, j]
            upright_ref[w, j] = jnp.concatenate([block, block], axis=0).T
            turned = pltpu.roll(block, half, 1)
            high, low = split_two(jnp.where(first, block, turned))
            left_high[w, j] = high
            left_low[w, j] = low
            send[w, j, 0:wide] = jnp.where(first_wide, block[:wide], turned[wide:])
        for w in range(per):
            high, low = split_two(upright_ref[w, j, pl.ds(mine_at, wide), :])
            right_out[j, wide * w : wide * (w + 1), 0:lanes] = high
            right_out[j, wide * w : wide * (w + 1), lanes:] = low
            upper = upright_ref[w, j, pl.ds(theirs_at, rows), :]
            lower = upright_ref[w, j, pl.ds(theirs_at + rows, rows), :]
            send[w, j, wide : wide + rows] = jnp.where(first_rows, upper, lower)


def other_operands(sent, left_high, left_low, right_out, j):
    per, blocks, half, lanes = left_high.shape
    rows = half // 4
    wide = half // 2
    first = lane_is_first(wide)
    first_rows = lane_is_first(rows)
    for w in range(per):
        both = sent[w, j, 0:wide]
        turned = pltpu.roll(both, half, 1)
        full = jnp.concatenate(
            [jnp.where(first, both, turned), jnp.where(first, turned, both)], axis=0
        )
        high, low = split_two(full)
        left_high[w, j] = high
        left_low[w, j] = low
        both = sent[w, j, wide : wide + rows]
        turned = pltpu.roll(both, half, 1)
        full = jnp.concatenate(
            [jnp.where(first_rows, both, turned), jnp.where(first_rows, turned, both)], axis=0
        )
        high, low = split_two(full)
        right_out[j, wide * w : wide * (w + 1), 0:lanes] = high
        right_out[j, wide * w : wide * (w + 1), lanes:] = low


def operand_specs(per, step, half, lanes):
    return [
        pl.BlockSpec((per, step, half, lanes), lambda i, *_: (0, i, 0, 0)),
        pl.BlockSpec((per, step, half, lanes), lambda i, *_: (0, i, 0, 0)),
        pl.BlockSpec((step, per * 32, 2 * lanes), lambda i, *_: (i, 0, 0)),
    ]


def operand_shapes(per, blocks, half, lanes):
    return [
        jax.ShapeDtypeStruct((per, blocks, half, lanes), jnp.bfloat16),
        jax.ShapeDtypeStruct((per, blocks, half, lanes), jnp.bfloat16),
        jax.ShapeDtypeStruct((blocks, per * 32, 2 * lanes), jnp.bfloat16),
    ]


def cut_kernel(group, info_ref, source, *refs):
    outs, sems = refs[:3], refs[3]
    per = outs[0].shape[0]
    copies = []
    for k in range(3):
        part = source.at[pl.ds(group * per, per), info_ref[4] ^ (k + 1)]
        copies.append(pltpu.make_async_copy(part, outs[k], sems.at[k]))
    for copy in copies:
        copy.start()
    for copy in copies:
        copy.wait()


def cut_pieces(info, by_owner, group, per):
    shape = jax.ShapeDtypeStruct((per,) + by_owner.shape[2:], jnp.float32)
    return pl.pallas_call(
        functools.partial(cut_kernel, group),
        grid_spec=pltpu.PrefetchScalarGridSpec(
            num_scalar_prefetch=1,
            grid=(1,),
            in_specs=[pl.BlockSpec(memory_space=pl.ANY)],
            out_specs=[pl.BlockSpec(memory_space=pl.ANY)] * 3,
            scratch_shapes=[pltpu.SemaphoreType.DMA((3,))],
        ),
        out_shape=[shape] * 3,
        compiler_params=pltpu.CompilerParams(vmem_limit_bytes=SMALL_VMEM),
        cost_estimate=micros(1),
        name="cut_pieces",
    )(info, by_owner)


def own_operands(info, by_owner, group, pieces):
    per, blocks, rows, lanes = pieces[0].shape
    half = lanes // 2
    step = 4
    return pl.pallas_call(
        own_operands_kernel,
        grid_spec=pltpu.PrefetchScalarGridSpec(
            num_scalar_prefetch=1,
            grid=(blocks // step,),
            in_specs=[
                pl.BlockSpec(
                    (per, 1, step, rows, lanes), lambda i, info: (group, info[4], i, 0, 0)
                )
            ]
            + [pl.BlockSpec((per, step, rows, lanes), lambda i, *_: (0, i, 0, 0))] * 3,
            out_specs=operand_specs(per, step, half, lanes)
            + [pl.BlockSpec((per, step, 3 * rows, lanes), lambda i, *_: (0, i, 0, 0))],
            scratch_shapes=[
                pltpu.VMEM((per, step, half, lanes), jnp.float32),
                pltpu.VMEM((per, step, lanes, lanes), jnp.float32),
            ],
        ),
        out_shape=operand_shapes(per, blocks, half, lanes)
        + [jax.ShapeDtypeStruct((per, blocks, 3 * rows, lanes), jnp.float32)],
        compiler_params=pltpu.CompilerParams(vmem_limit_bytes=SMALL_VMEM),
        cost_estimate=micros(6),
        name="own_operands",
    )(info, by_owner, *pieces)


def apply_kernel(plan, info_ref, *refs):
    chunks, parts_given, sent_given, before_given, pieces = plan
    refs = list(refs)
    take = lambda n: [refs.pop(0) for _ in range(n)]
    slots = take(2)
    vector = take(4 if parts_given else 1)
    tiles = take(4) if parts_given else []
    operands = [take(3) for _ in chunks[: -1 if sent_given else None]]
    sent = take(1)[0] if sent_given else None
    mixes = take(len(chunks))
    before = take(1)[0] if before_given else None
    outs = take(2 if pieces else 1)
    if sent_given:
        operands.append(take(3))
    total_ref, vec, mid = take(3)
    if before_given:
        prior, arrival = take(2)
    step = mid.shape[0]
    lanes, half = LANES, LANES // 2
    first = lane_is_first(SUB)
    first_half = lane_is_first(half)
    keep_first = jnp.where(first_half, 1.0, 0.0).astype(jnp.bfloat16)
    keep_second = jnp.where(first_half, 0.0, 1.0).astype(jnp.bfloat16)
    nothing = jnp.zeros((lanes, lanes), jnp.bfloat16)
    me = info_ref[4]

    @pl.when(pl.program_id(0) == 0)
    def _():
        if before_given:
            pltpu.make_async_copy(before, prior, arrival).start()
        total_ref[...] = jnp.zeros_like(total_ref)

    def right_side(j):
        if sent_given:
            other_operands(sent, *operands[-1], j)
        if parts_given:

            def put(row, pair, high, low):
                columns = slice(pair * lanes, (pair + 1) * lanes)
                vec[j, pl.ds(row, 16), columns] = high
                vec[j, pl.ds(row + half, 16), columns] = low

            rows_of = [pl.multiple_of(info_ref[g] * 16, 16) for g in range(4)]
            store_vector([x.at[pl.ds(j * lanes, lanes)] for x in vector], rows_of, put)
            source = vec[j]
        else:
            source = vector[0][j]
        source = jnp.concatenate([source, source], axis=0)
        at = 0
        for left_high, left_low, right in operands:
            count = right.shape[1]
            mid[j, at : at + count, :] = jnp.dot(
                right[j], source, preferred_element_type=jnp.float32
            )
            at += count

    def prepared(j, refs_of, w, row_of):
        left_high, left_low, right = refs_of
        tiles = []
        for part in range(2):
            row = row_of + part * 16
            for pair in range(PHYS // 2):
                columns = slice(pair * lanes, (pair + 1) * lanes)
                upper = mid[j, row : row + SUB, columns]
                lower = mid[j, row + SUB : row + 2 * SUB, columns]
                tiles.append(jnp.where(first, upper, pltpu.roll(lower, half, 1)))
                tiles.append(jnp.where(first, pltpu.roll(upper, half, 1), lower))
        t_high, t_low = split_two(jnp.concatenate(tiles, axis=0))
        lh, ll = left_high[w, j], left_low[w, j]
        wide_high = jnp.concatenate([lh * keep_first, lh * keep_second], axis=0)
        wide_low = jnp.concatenate([ll * keep_first, ll * keep_second], axis=0)
        weights = jnp.concatenate(
            [
                jnp.concatenate([wide_high, wide_low], axis=1),
                jnp.concatenate([wide_high, nothing], axis=1),
            ],
            axis=0,
        )
        return jnp.concatenate([t_high, t_low], axis=1), weights

    def mix_unit(mixing, w, z):
        z_high, z_low = [jnp.concatenate([x[:lanes], x[lanes:]], axis=1) for x in z]
        return jnp.dot(
            mixing[w],
            jnp.concatenate([z_high, z_low, z_high], axis=0),
            preferred_element_type=jnp.float32,
        )

    def add_up(j, table, bond, mixed):
        slot = table[bond, pl.program_id(0) * step + j]
        slot = ((slot >> 1) ^ me) * 2 + (slot & 1)
        for part in range(2):
            total_ref[part, slot] += mixed[:, part * lanes : (part + 1) * lanes]

    bonds = []
    for chunk, refs_of, mix in zip(chunks, operands, mixes):
        count = mix.shape[0]
        source, group = chunk // GROUPS, chunk % GROUPS
        for w in range(count):
            bonds.append((refs_of, mix, w, slots[source], group * count + w))
    right_side(0)
    units = [(j, at) for j in range(step) for at in range(len(bonds))]

    def prepare_unit(n):
        j, at = units[n]
        refs_of, mixing, w, table, bond = bonds[at]
        return prepared(j, refs_of, w, at * 32)

    ready = prepare_unit(0)
    waiting = None
    for n, (j, at) in enumerate(units):
        refs_of, mixing, w, table, bond = bonds[at]
        z = jnp.dot(*ready, preferred_element_type=jnp.float32)
        if j + 1 < step and at == len(bonds) // 3:
            right_side(j + 1)
        if n + 1 < len(units):
            ready = prepare_unit(n + 1)
        if waiting is not None:
            before_j, before_mixing, before_w, before_table, before_bond, before_z = waiting
            mixed = mix_unit(before_mixing, before_w, before_z)
        z = split_two(z[:, :lanes] + z[:, lanes:])
        if waiting is not None:
            add_up(before_j, before_table, before_bond, mixed)
        waiting = (j, mixing, w, table, bond, z)
    j, mixing, w, table, bond, z = waiting
    add_up(j, table, bond, mix_unit(mixing, w, z))

    @pl.when(pl.program_id(0) == pl.num_programs(0) - 1)
    def _():
        if before_given:
            pltpu.make_async_copy(before, prior, arrival).wait()
            total_ref[...] += prior[...]
        if pieces:
            stats = jnp.zeros((SUB, lanes), jnp.float32)
            if parts_given:
                stats = stacked_rows(*merged([tile[...] for tile in tiles]))
            for out, part in ((outs[0], info_ref[5]), (outs[1], 1 - info_ref[5])):
                for k in range(4):
                    for i in range(2):
                        out[k, i * lanes : (i + 1) * lanes] = total_ref[part, 2 * k + i]
                    out[k, 2 * lanes :] = stats
                stats = jnp.zeros((SUB, lanes), jnp.float32)
        else:
            outs[0][...] = total_ref[...]


def apply_bonds(info, slots, vector, chunks, operands, sent, mixing, before, pieces):
    count, blocks, half, lanes = operands[0][0].shape
    step = 4
    parts_given = len(vector) == 4
    if parts_given:
        last = vector[0].shape[0] // SUB - 1
        in_specs = [pl.BlockSpec((step * lanes, lanes), lambda i, *_: (i, 0))] * 4
        in_specs += [pl.BlockSpec((SUB, lanes), lambda i, *_: (last, 0))] * 4
    else:
        in_specs = [pl.BlockSpec((step,) + vector[0].shape[1:], lambda i, *_: (i, 0, 0))]
    arguments = list(vector) * (2 if parts_given else 1)
    for made in operands:
        in_specs += operand_specs(count, step, half, lanes)
        arguments += made
    if sent is not None:
        in_specs.append(
            pl.BlockSpec((count, step) + sent.shape[2:], lambda i, *_: (0, i, 0, 0))
        )
        arguments.append(sent)
    for chunk in chunks:
        in_specs.append(
            pl.BlockSpec((count,) + mixing.shape[1:], lambda i, *_, at=chunk: (at, 0, 0))
        )
        arguments.append(mixing)
    total = count * len(chunks)
    scratch = [
        pltpu.VMEM((2, 8, lanes, lanes), jnp.float32),
        pltpu.VMEM((step, lanes, PHYS * half), jnp.bfloat16),
        pltpu.VMEM((step, total * 32, PHYS * half), jnp.float32),
    ]
    if before is not None:
        in_specs.append(pl.BlockSpec(memory_space=pl.ANY))
        arguments.append(before)
        scratch += [pltpu.VMEM(before.shape, jnp.float32), pltpu.SemaphoreType.DMA]
    shapes = [(4, 2 * lanes + SUB, lanes)] * 2 if pieces else [(2, 8, lanes, lanes)]
    out_specs = [whole(*shape) for shape in shapes]
    out_shape = [jax.ShapeDtypeStruct(shape, jnp.float32) for shape in shapes]
    if sent is not None:
        out_specs += operand_specs(count, step, half, lanes)
        out_shape += operand_shapes(count, blocks, half, lanes)
    plan = (tuple(chunks), parts_given, sent is not None, before is not None, pieces)
    out = pl.pallas_call(
        functools.partial(apply_kernel, plan),
        grid_spec=pltpu.PrefetchScalarGridSpec(
            num_scalar_prefetch=3,
            grid=(blocks // step,),
            in_specs=in_specs,
            out_specs=out_specs,
            scratch_shapes=scratch,
        ),
        out_shape=out_shape,
        compiler_params=pltpu.CompilerParams(vmem_limit_bytes=APPLY_VMEM),
        cost_estimate=micros(1),
        name="apply_bonds",
    )(info, *slots, *arguments)
    return out[: len(shapes)], out[len(shapes) :]


def add_arrived(info_ref, owner_ref, arrived, total):
    for k in range(4):
        for i in range(2):
            rows = slice(i * LANES, (i + 1) * LANES)
            total[owner_ref[info_ref[4] ^ k, i]] += arrived[k][rows]


def stacked_rows(*rows):
    at = lax.broadcasted_iota(jnp.int32, (SUB, LANES), 0)
    tile = jnp.zeros((SUB, LANES), jnp.float32)
    for i, row in enumerate(rows):
        tile = jnp.where(at == i, row, tile)
    return tile


def merged(tiles):
    rows = [[tile[i : i + 1] for i in range(3)] for tile in tiles]
    cross = sum(row[0] for row in rows)
    square = sum(row[1] for row in rows)
    ratio = cross / jnp.maximum(square, TINY)
    apart = [
        (row[0] / jnp.maximum(row[1], TINY) - ratio) * jnp.sqrt(row[1]) for row in rows
    ]
    rest = sum(row[2] for row in rows) + sum(x * x for x in apart)
    return cross, square, rest


def image_kernel(info_ref, owner_ref, a0, a1, a2, a3, diag_ref, own_ref, image_ref, total):
    total[...] = diag_ref[...] * own_ref[...]
    add_arrived(info_ref, owner_ref, (a0, a1, a2, a3), total)
    blocks = total.shape[0]
    cross = jnp.zeros((LANES, LANES), jnp.float32)
    square = jnp.zeros((LANES, LANES), jnp.float32)
    for k in range(blocks):
        own, image = own_ref[k], total[k]
        image_ref[k * LANES : (k + 1) * LANES] = image
        cross += own * image
        square += own * own
    cross = jnp.sum(cross, keepdims=True)
    square = jnp.sum(square, keepdims=True)
    ratio = cross / jnp.maximum(square, TINY)
    rest = jnp.zeros((LANES, LANES), jnp.float32)
    for k in range(blocks):
        apart = total[k] - ratio * own_ref[k]
        rest += apart * apart
    image_ref[blocks * LANES :] = stacked_rows(cross, square, jnp.sum(rest, keepdims=True))


def owner_image(info, owners, arrived, diagonal, own):
    rows = own.shape[0] * LANES + SUB
    return pl.pallas_call(
        image_kernel,
        grid_spec=pltpu.PrefetchScalarGridSpec(
            num_scalar_prefetch=2,
            grid=(1,),
            in_specs=[whole(*x.shape) for x in (*arrived, diagonal, own)],
            out_specs=whole(rows, LANES),
            scratch_shapes=[pltpu.VMEM(own.shape, jnp.float32)],
        ),
        out_shape=jax.ShapeDtypeStruct((rows, LANES), jnp.float32),
        compiler_params=pltpu.CompilerParams(vmem_limit_bytes=SMALL_VMEM),
        cost_estimate=micros(3),
        name="owner_image",
    )(info, owners, *in_hbm(arrived[0]), *arrived[1:], *in_hbm(diagonal, own))


def final_kernel(
    entries, info_ref, owner_ref, a0, a1, a2, a3, diag_ref, own_ref, image_ref, first_ref,
    vector_ref, second_ref, total,
):
    arrived = (a0, a1, a2, a3)
    cross, square, rest = merged([ref[2 * LANES :] for ref in arrived])
    scale = lax.rsqrt(square / entries + 1e-06)
    rayleigh = scale * scale * (cross / entries)
    apart = (cross / jnp.maximum(square, TINY) - rayleigh) * jnp.sqrt(square)
    mean = scale * scale * ((rest + apart * apart) / entries)
    second_scale = scale * lax.rsqrt(mean + 1e-06)
    for k in range(total.shape[0]):
        image = image_ref[k * LANES : (k + 1) * LANES]
        total[k] = (diag_ref[k] - rayleigh) * image
        first_ref[k] = unpack_tile(scale * image)
        vector_ref[k] = unpack_tile(second_scale * (image - rayleigh * own_ref[k]))
    add_arrived(info_ref, owner_ref, arrived, total)
    for k in range(total.shape[0]):
        second_ref[k] = unpack_tile(second_scale * total[k])


def outputs(info, owners, arrived, diagonal, own, image, entries):
    blocks = diagonal.shape[0]
    shape = (blocks, LANES // 2, 2 * LANES)
    return pl.pallas_call(
        functools.partial(final_kernel, entries),
        grid_spec=pltpu.PrefetchScalarGridSpec(
            num_scalar_prefetch=2,
            grid=(1,),
            in_specs=[whole(*x.shape) for x in (*arrived, diagonal, own)]
            + [whole(blocks * LANES, LANES)],
            out_specs=[whole(*shape)] * 3,
            scratch_shapes=[pltpu.VMEM(diagonal.shape, jnp.float32)],
        ),
        out_shape=[jax.ShapeDtypeStruct(shape, jnp.float32)] * 3,
        compiler_params=pltpu.CompilerParams(vmem_limit_bytes=SMALL_VMEM),
        cost_estimate=micros(4),
        name="outputs",
    )(info, owners, *arrived, diagonal, own, image)


def in_hbm(*arrays):
    return [pltpu.with_memory_space_constraint(x, pltpu.HBM) for x in arrays]


def partner(x, axis, k):
    size = lax.axis_size(axis)
    return lax.ppermute(x, axis, [(i, i ^ k) for i in range(size)])


def after(x, *others):
    return lax.optimization_barrier((x, *others))[0]


def gathered(x):
    across = partner(x, "mpo", 1)
    return [x, across, partner(x, "rep", 1), partner(across, "rep", 1)]


def everyone_of(pieces, axis):
    return [pieces[0]] + [partner(pieces[k], axis, k) for k in range(1, 4)]


def to_owners(mine, theirs):
    other = partner(theirs, "rep", 1)
    pieces = [mine[k] + other[k] for k in range(4)]
    return everyone_of(pieces, "blk")


def per_device(wavefunction, environment, bond_terms, diagonal, term_slot, slot_block):
    blocks, rows, width = wavefunction.shape
    zs = lax.axis_size("blk")
    mpo, rep, blk = lax.axis_index("mpo"), lax.axis_index("rep"), lax.axis_index("blk")
    place = 2 * mpo + rep
    info = jnp.stack([place, place ^ 2, place ^ 1, place ^ 3, blk, rep, mpo]).astype(jnp.int32)
    bonds = environment.shape[0]
    per = bonds // GROUPS
    entries = float(blocks * zs * rows * width)

    vector, own, diagonal_packed = pack(info, wavefunction, diagonal)

    by_owner = environment.reshape(bonds, zs, blocks, rows // zs, 2 * rows)
    pieces = []
    for group in range(GROUPS):
        cuts = cut_pieces(info, by_owner, group, per)
        if group:
            cuts = [after(x, y) for x, y in zip(cuts, pieces[-1][1:])]
        pieces.append([None] + [partner(x, "blk", k + 1) for k, x in enumerate(cuts)])
    pieces[0][1] = after(pieces[0][1], vector)
    other_terms = partner(after(bond_terms, pieces[0][1]), "mpo", 1)
    mixing = mixing_operand([bond_terms, other_terms])
    slots = [term_slot, partner(after(term_slot, pieces[0][1]), "mpo", 1)]

    made, sent = [], []
    total = None
    operands = []
    done = 0

    def apply_group(group, vector):
        last = group == GROUPS - 1
        out, other = apply_bonds(
            info, slots, [vector], [group, GROUPS + group], [made[group]],
            partner(sent[group], "mpo", 1), mixing, total, last,
        )
        operands.extend([made[group], other])
        return out

    for group in range(GROUPS):
        if group >= 2:
            total = apply_group(group - 2, after(vector, sent[group - 1]))[0]
            pieces[group][3] = after(pieces[group][3], total)
        *own_set, send = own_operands(info, by_owner, group, pieces[group][1:])
        made.append(own_set)
        sent.append(send)
    total = apply_group(GROUPS - 2, after(vector, sent[-1]))[0]
    out = apply_group(GROUPS - 1, vector)
    image = owner_image(info, slot_block, to_owners(*out), diagonal_packed, own)

    parts = gathered(image)
    chunks = [group + GROUPS * source for group in range(GROUPS) for source in range(2)]
    out, _ = apply_bonds(info, slots, parts, chunks, operands, None, mixing, None, True)
    return tuple(
        outputs(info, slot_block, to_owners(*out), diagonal_packed, own, image, entries)
    )


def solution(mesh):
    packed = mesh.shape["mpo"] == 2 and mesh.shape["rep"] == 2 and mesh.shape["blk"] == 4
    return jax.shard_map(
        per_device if packed else plain_device,
        mesh=mesh,
        in_specs=(
            P(("grp", "blk"), None, None),
            P(("grp", "mpo", "rep"), None, "blk", None),
            P(("grp", "mpo", "rep"), None, None),
            P(("grp", "blk"), None, ("mpo", "rep")),
            P(("grp", "mpo", "rep"), "blk"),
            P("grp", "blk"),
        ),
        out_specs=(
            P(("grp", "blk"), None, ("mpo", "rep")),
            P(("grp", "blk"), None, ("mpo", "rep")),
            P(("grp", "blk"), None, ("mpo", "rep")),
        ),
        check_vma=False,
    )
```

```python
import functools

import jax
import jax.numpy as jnp
from jax import lax
from jax.experimental import pallas as pl
from jax.experimental.pallas import tpu as pltpu
from jax.sharding import PartitionSpec as P

LANES = 128
SUB = 8
PHYS = 16
TINY = 1e-30
GROUPS = 3
SMALL_VMEM = 16 * 1024 * 1024
APPLY_VMEM = 26 * 1024 * 1024


def plain_apply(vector_full, environment, bond_terms, term_slot, slot_block, diagonal):
    block_count, block_rows, block_width = vector_full.shape
    phys_size = bond_terms.shape[-1]
    right_rows = block_width // phys_size
    slot_count = slot_block.shape[0] * slot_block.shape[1]
    blocks = vector_full.reshape(block_count, block_rows, right_rows, phys_size)
    ordered = jnp.transpose(blocks, (0, 3, 1, 2))
    left_env = environment[:, :, :, :block_rows]
    right_env = environment[:, :, :, block_rows:]
    left_done = jnp.einsum("wjab,jsac->wjsbc", left_env, ordered, precision=lax.Precision.HIGHEST)
    right_done = jnp.einsum(
        "wjsbc,wjcd->wjsbd", left_done, right_env, precision=lax.Precision.HIGHEST
    )
    right_done = right_done.reshape(
        environment.shape[0], block_count, phys_size, block_rows * right_rows
    )
    bond_term = jnp.einsum(
        "wjsx,wst->wjtx", right_done, bond_terms, precision=lax.Precision.HIGHEST
    )
    bond_term = bond_term.reshape(environment.shape[0], block_count, block_rows * block_width)
    slot_table = (
        term_slot[:, None, :] == jnp.arange(slot_count, dtype=jnp.int32)[None, :, None]
    ).astype(jnp.float32)
    slot_buffer = jnp.einsum("wsj,wjx->sx", slot_table, bond_term, precision=lax.Precision.HIGHEST)
    slot_buffer = slot_buffer.reshape(slot_count, phys_size, block_rows, right_rows)
    slot_buffer = jnp.transpose(slot_buffer, (0, 2, 3, 1)).reshape(
        slot_count, block_rows, block_width
    )
    owners = slot_block.reshape(-1)
    selector = (owners[None, :] == jnp.arange(block_count, dtype=jnp.int32)[:, None]).astype(
        jnp.float32
    )
    column_width = block_width // lax.axis_size(("mpo", "rep"))
    column_start = lax.axis_index(("mpo", "rep")) * column_width
    own_part = lax.dynamic_slice_in_dim(vector_full, column_start, column_width, 2)
    shares = lax.psum_scatter(slot_buffer, ("mpo", "rep"), scatter_dimension=2, tiled=True)
    arrived = lax.all_to_all(shares, "blk", split_axis=0, concat_axis=0, tiled=True)
    result = jnp.einsum("ks,sbc->kbc", selector, arrived, precision=lax.Precision.HIGHEST)
    return (result + diagonal * own_part, own_part)


def plain_device(wavefunction, environment, bond_terms, diagonal, term_slot, slot_block):
    arranged = lax.all_to_all(environment, "blk", split_axis=1, concat_axis=2, tiled=True)
    entries = float(
        wavefunction.shape[0] * lax.axis_size("blk") * wavefunction.shape[1] * wavefunction.shape[2]
    )
    square_sum = lax.psum(jnp.sum(wavefunction * wavefunction), "blk")
    first_vector = wavefunction * lax.rsqrt(square_sum / entries + 1e-06)
    first_image, first_part = plain_apply(
        first_vector, arranged, bond_terms, term_slot, slot_block, diagonal
    )
    rayleigh = lax.psum(jnp.sum(first_part * first_image), ("blk", "mpo", "rep")) / entries
    residual = first_image - rayleigh * first_part
    resid_sum = lax.psum(jnp.sum(residual * residual), ("blk", "mpo", "rep"))
    second_vector = residual * lax.rsqrt(resid_sum / entries + 1e-06)
    second_full = lax.all_gather(second_vector, ("mpo", "rep"), axis=2, tiled=True)
    second_image, unused = plain_apply(
        second_full, arranged, bond_terms, term_slot, slot_block, diagonal
    )
    return (first_image, second_vector, second_image)


def split_two(x):
    high = x.astype(jnp.bfloat16)
    low = (x - high.astype(jnp.float32)).astype(jnp.bfloat16)
    return high, low


def lane_is_first(rows):
    return lax.broadcasted_iota(jnp.int32, (rows, LANES), 1) < LANES // 2


def micros(count):
    return pl.CostEstimate(flops=count * 1100000000, bytes_accessed=1 << 20, transcendentals=0)


def whole(*shape):
    return pl.BlockSpec(shape, lambda i, *_: (0,) * len(shape))


def pack_tile(x):
    return jnp.concatenate([x[:, :LANES], x[:, LANES:]], axis=0).T


def unpack_tile(x):
    upright = x.T
    return jnp.concatenate([upright[: LANES // 2], upright[LANES // 2 :]], axis=1)


def store_vector(parts, rows_of, put):
    first = lane_is_first(SUB)
    for pair in range(PHYS // 2):
        for part, row in zip(parts, rows_of):
            even = part[pl.ds(2 * pair, SUB, stride=PHYS), :]
            odd = part[pl.ds(2 * pair + 1, SUB, stride=PHYS), :]
            upper = jnp.where(first, even, pltpu.roll(odd, LANES // 2, 1))
            lower = jnp.where(first, pltpu.roll(even, LANES // 2, 1), odd)
            high, low = split_two(jnp.concatenate([upper, lower], axis=0))
            put(row, pair, high, low)


def pack_kernel(info_ref, wave_ref, diag_ref, vec_ref, wave_out, diag_out, start_ref):
    half = LANES // 2
    for j in range(wave_ref.shape[0]):
        for q in range(4):
            wave_out[q, j] = pack_tile(wave_ref[j, :, 2 * LANES * q : 2 * LANES * (q + 1)])
        diagonal = pack_tile(diag_ref[j])
        diag_out[j] = diagonal
        start_ref[j] = diagonal * wave_out[info_ref[0], j]

        def put(row, pair, high, low):
            columns = slice(pair * LANES, (pair + 1) * LANES)
            vec_ref[j, row : row + 16, columns] = high
            vec_ref[j, row + half : row + half + 16, columns] = low

        store_vector([wave_out.at[q, j] for q in range(4)], [16 * q for q in range(4)], put)


def pack(info, wavefunction, diagonal):
    blocks, rows, width = wavefunction.shape
    step = 2
    tile = pl.BlockSpec((step, LANES, LANES), lambda i, *_: (i, 0, 0))
    tiles = jax.ShapeDtypeStruct((blocks, LANES, LANES), jnp.float32)
    return pl.pallas_call(
        pack_kernel,
        grid_spec=pltpu.PrefetchScalarGridSpec(
            num_scalar_prefetch=1,
            grid=(blocks // step,),
            in_specs=[
                pl.BlockSpec((step, rows, width), lambda i, *_: (i, 0, 0)),
                pl.BlockSpec((step, rows, width // 4), lambda i, *_: (i, 0, 0)),
            ],
            out_specs=[
                pl.BlockSpec((step, LANES, width), lambda i, *_: (i, 0, 0)),
                pl.BlockSpec((4, step, LANES, LANES), lambda i, *_: (0, i, 0, 0)),
                tile,
                tile,
            ],
        ),
        out_shape=[
            jax.ShapeDtypeStruct((blocks, LANES, width), jnp.bfloat16),
            jax.ShapeDtypeStruct((4, blocks, LANES, LANES), jnp.float32),
            tiles,
            tiles,
        ],
        compiler_params=pltpu.CompilerParams(vmem_limit_bytes=SMALL_VMEM),
        cost_estimate=micros(5),
        name="pack",
    )(info, wavefunction, diagonal)


def mixing_kernel(*refs):
    sources, out_ref = refs[:-1], refs[-1]
    spread = (
        lax.broadcasted_iota(jnp.int32, (PHYS, LANES), 1) // SUB
        == lax.broadcasted_iota(jnp.int32, (PHYS, LANES), 0)
    ).astype(jnp.bfloat16)
    row = lax.broadcasted_iota(jnp.int32, (LANES, LANES), 0) // PHYS
    column = lax.broadcasted_iota(jnp.int32, (LANES, LANES), 1) % SUB
    same = row == column
    at = 0
    for source in sources:
        for k in range(source.shape[0]):
            high, low = split_two(source[k].T)
            for term, places in ((high, (0, 1)), (low, (2,))):
                wide = jnp.dot(term, spread, preferred_element_type=jnp.float32)
                tall = jnp.concatenate([wide] * SUB, axis=0)
                tall = jnp.where(same, tall, 0.0).astype(jnp.bfloat16)
                for place in places:
                    out_ref[at, :, place * LANES : (place + 1) * LANES] = tall
            at += 1


def mixing_operand(sources):
    count = sources[0].shape[0] * len(sources)
    return pl.pallas_call(
        mixing_kernel,
        out_shape=jax.ShapeDtypeStruct((count, LANES, 3 * LANES), jnp.bfloat16),
        compiler_params=pltpu.CompilerParams(vmem_limit_bytes=SMALL_VMEM),
        cost_estimate=micros(2),
        name="mixing",
    )(*sources)


def own_operands_kernel(info_ref, *refs):
    pieces, (left_high, left_low, right_out, send, blocks_ref, upright_ref) = refs[:4], refs[4:]
    per, blocks, half, lanes = left_high.shape
    rows = half // 4
    wide = half // 2
    first = lane_is_first(half)
    first_wide = lane_is_first(wide)
    first_rows = lane_is_first(rows)
    mine_at = pl.multiple_of(half + info_ref[6] * wide, wide)
    theirs_at = pl.multiple_of(lanes - wide - info_ref[6] * wide, wide)
    for j in range(blocks):
        for w in range(per):
            for z in range(4):
                row = pl.multiple_of((info_ref[4] ^ z) * rows, rows)
                piece = pieces[z][w, 0, j] if z == 0 else pieces[z][w, j]
                blocks_ref[w, j, pl.ds(row, rows), :] = piece
        for w in range(per):
            block = blocks_ref[w, j]
            upright_ref[w, j] = jnp.concatenate([block, block], axis=0).T
            turned = pltpu.roll(block, half, 1)
            high, low = split_two(jnp.where(first, block, turned))
            left_high[w, j] = high
            left_low[w, j] = low
            send[w, j, 0:wide] = jnp.where(first_wide, block[:wide], turned[wide:])
        for w in range(per):
            high, low = split_two(upright_ref[w, j, pl.ds(mine_at, wide), :])
            right_out[j, wide * w : wide * (w + 1), 0:lanes] = high
            right_out[j, wide * w : wide * (w + 1), lanes:] = low
            upper = upright_ref[w, j, pl.ds(theirs_at, rows), :]
            lower = upright_ref[w, j, pl.ds(theirs_at + rows, rows), :]
            send[w, j, wide : wide + rows] = jnp.where(first_rows, upper, lower)


def other_operands(sent, left_high, left_low, right_out, j):
    per, blocks, half, lanes = left_high.shape
    rows = half // 4
    wide = half // 2
    first = lane_is_first(wide)
    first_rows = lane_is_first(rows)
    for w in range(per):
        both = sent[w, j, 0:wide]
        turned = pltpu.roll(both, half, 1)
        full = jnp.concatenate(
            [jnp.where(first, both, turned), jnp.where(first, turned, both)], axis=0
        )
        high, low = split_two(full)
        left_high[w, j] = high
        left_low[w, j] = low
        both = sent[w, j, wide : wide + rows]
        turned = pltpu.roll(both, half, 1)
        full = jnp.concatenate(
            [jnp.where(first_rows, both, turned), jnp.where(first_rows, turned, both)], axis=0
        )
        high, low = split_two(full)
        right_out[j, wide * w : wide * (w + 1), 0:lanes] = high
        right_out[j, wide * w : wide * (w + 1), lanes:] = low


def operand_specs(per, step, half, lanes):
    return [
        pl.BlockSpec((per, step, half, lanes), lambda i, *_: (0, i, 0, 0)),
        pl.BlockSpec((per, step, half, lanes), lambda i, *_: (0, i, 0, 0)),
        pl.BlockSpec((step, per * 32, 2 * lanes), lambda i, *_: (i, 0, 0)),
    ]


def operand_shapes(per, blocks, half, lanes):
    return [
        jax.ShapeDtypeStruct((per, blocks, half, lanes), jnp.bfloat16),
        jax.ShapeDtypeStruct((per, blocks, half, lanes), jnp.bfloat16),
        jax.ShapeDtypeStruct((blocks, per * 32, 2 * lanes), jnp.bfloat16),
    ]


def cut_kernel(group, info_ref, source, *refs):
    outs, sems = refs[:3], refs[3]
    per = outs[0].shape[0]
    copies = []
    for k in range(3):
        part = source.at[pl.ds(group * per, per), info_ref[4] ^ (k + 1)]
        copies.append(pltpu.make_async_copy(part, outs[k], sems.at[k]))
    for copy in copies:
        copy.start()
    for copy in copies:
        copy.wait()


def cut_pieces(info, by_owner, group, per):
    shape = jax.ShapeDtypeStruct((per,) + by_owner.shape[2:], jnp.float32)
    return pl.pallas_call(
        functools.partial(cut_kernel, group),
        grid_spec=pltpu.PrefetchScalarGridSpec(
            num_scalar_prefetch=1,
            grid=(1,),
            in_specs=[pl.BlockSpec(memory_space=pl.ANY)],
            out_specs=[pl.BlockSpec(memory_space=pl.ANY)] * 3,
            scratch_shapes=[pltpu.SemaphoreType.DMA((3,))],
        ),
        out_shape=[shape] * 3,
        compiler_params=pltpu.CompilerParams(vmem_limit_bytes=SMALL_VMEM),
        cost_estimate=micros(1),
        name="cut_pieces",
    )(info, *in_hbm(by_owner))


def own_operands(info, by_owner, group, pieces):
    per, blocks, rows, lanes = pieces[0].shape
    half = lanes // 2
    step = 4
    return pl.pallas_call(
        own_operands_kernel,
        grid_spec=pltpu.PrefetchScalarGridSpec(
            num_scalar_prefetch=1,
            grid=(blocks // step,),
            in_specs=[
                pl.BlockSpec(
                    (per, 1, step, rows, lanes), lambda i, info: (group, info[4], i, 0, 0)
                )
            ]
            + [pl.BlockSpec((per, step, rows, lanes), lambda i, *_: (0, i, 0, 0))] * 3,
            out_specs=operand_specs(per, step, half, lanes)
            + [pl.BlockSpec((per, step, 3 * rows, lanes), lambda i, *_: (0, i, 0, 0))],
            scratch_shapes=[
                pltpu.VMEM((per, step, half, lanes), jnp.float32),
                pltpu.VMEM((per, step, lanes, lanes), jnp.float32),
            ],
        ),
        out_shape=operand_shapes(per, blocks, half, lanes)
        + [jax.ShapeDtypeStruct((per, blocks, 3 * rows, lanes), jnp.float32)],
        compiler_params=pltpu.CompilerParams(vmem_limit_bytes=SMALL_VMEM),
        cost_estimate=micros(6),
        name="own_operands",
    )(info, *in_hbm(by_owner), *pieces)


def apply_kernel(plan, info_ref, *refs):
    chunks, sent_given, before_given, stats_given, pieces = plan
    refs = list(refs)
    take = lambda n: [refs.pop(0) for _ in range(n)]
    slots = take(2)
    vector = take(1)[0]
    stats = take(1)[0] if stats_given else None
    operands = [take(3) for _ in chunks[: -1 if sent_given else None]]
    sent = take(1)[0] if sent_given else None
    mixes = take(len(chunks))
    before = take(1)[0] if before_given else None
    outs = take(2 if pieces else 1)
    if sent_given:
        operands.append(take(3))
    total_ref, mid = take(2)
    if before_given:
        prior, arrival = take(2)
    step = mid.shape[0]
    lanes, half = LANES, LANES // 2
    first = lane_is_first(SUB)
    first_half = lane_is_first(half)
    keep_first = jnp.where(first_half, 1.0, 0.0).astype(jnp.bfloat16)
    keep_second = jnp.where(first_half, 0.0, 1.0).astype(jnp.bfloat16)
    me = info_ref[4]

    @pl.when(pl.program_id(0) == 0)
    def _():
        if before_given:
            pltpu.make_async_copy(before, prior, arrival).start()
        total_ref[...] = jnp.zeros_like(total_ref)

    def right_side(j):
        if sent_given:
            other_operands(sent, *operands[-1], j)
        source = vector[j]
        source = jnp.concatenate([source, source], axis=0)
        at = 0
        for left_high, left_low, right in operands:
            count = right.shape[1]
            mid[j, at : at + count, :] = jnp.dot(
                right[j], source, preferred_element_type=jnp.float32
            )
            at += count

    def prepared(j, refs_of, w, row_of):
        left_high, left_low, right = refs_of
        tiles = []
        for part in range(2):
            row = row_of + part * 16
            for pair in range(PHYS // 2):
                columns = slice(pair * lanes, (pair + 1) * lanes)
                upper = mid[j, row : row + SUB, columns]
                lower = mid[j, row + SUB : row + 2 * SUB, columns]
                tiles.append(jnp.where(first, upper, pltpu.roll(lower, half, 1)))
                tiles.append(jnp.where(first, pltpu.roll(upper, half, 1), lower))
        t_high, t_low = split_two(jnp.concatenate(tiles, axis=0))
        lh, ll = left_high[w, j], left_low[w, j]
        wide_high = jnp.concatenate([lh * keep_first, lh * keep_second], axis=0)
        wide_low = jnp.concatenate([ll * keep_first, ll * keep_second], axis=0)
        weights = jnp.concatenate([wide_high, wide_high, wide_low], axis=0)
        return jnp.concatenate([t_high, t_low, t_high], axis=1), weights

    def mix_unit(mixing, w, z):
        z_high, z_low = [jnp.concatenate([x[:lanes], x[lanes:]], axis=1) for x in z]
        return jnp.dot(
            mixing[w],
            jnp.concatenate([z_high, z_low, z_high], axis=0),
            preferred_element_type=jnp.float32,
        )

    def add_up(j, table, bond, mixed):
        slot = table[bond, pl.program_id(0) * step + j]
        slot = ((slot >> 1) ^ me) * 2 + (slot & 1)
        for part in range(2):
            total_ref[part, slot] += mixed[:, part * lanes : (part + 1) * lanes]

    bonds = []
    for chunk, refs_of, mix in zip(chunks, operands, mixes):
        count = mix.shape[0]
        source, group = chunk // GROUPS, chunk % GROUPS
        for w in range(count):
            bonds.append((refs_of, mix, w, slots[source], group * count + w))
    right_side(0)
    units = [(j, at) for j in range(step) for at in range(len(bonds))]

    def prepare_unit(n):
        j, at = units[n]
        refs_of, mixing, w, table, bond = bonds[at]
        return prepared(j, refs_of, w, at * 32)

    ready = prepare_unit(0)
    waiting = None
    for n, (j, at) in enumerate(units):
        refs_of, mixing, w, table, bond = bonds[at]
        z = jnp.dot(*ready, preferred_element_type=jnp.float32)
        if j + 1 < step and at == len(bonds) // 3:
            right_side(j + 1)
        if n + 1 < len(units):
            ready = prepare_unit(n + 1)
        if waiting is not None:
            before_j, before_mixing, before_w, before_table, before_bond, before_z = waiting
            mixed = mix_unit(before_mixing, before_w, before_z)
        z = split_two(z)
        if waiting is not None:
            add_up(before_j, before_table, before_bond, mixed)
        waiting = (j, mixing, w, table, bond, z)
    j, mixing, w, table, bond, z = waiting
    add_up(j, table, bond, mix_unit(mixing, w, z))

    @pl.when(pl.program_id(0) == pl.num_programs(0) - 1)
    def _():
        if before_given:
            pltpu.make_async_copy(before, prior, arrival).wait()
            total_ref[...] += prior[...]
        if pieces:
            nil = jnp.zeros((SUB, lanes), jnp.float32)
            row = stats[...] if stats_given else nil
            for out, part in ((outs[0], info_ref[5]), (outs[1], 1 - info_ref[5])):
                for k in range(4):
                    for i in range(2):
                        out[k, i * lanes : (i + 1) * lanes] = total_ref[part, 2 * k + i]
                    out[k, 2 * lanes :] = row
                row = nil
        else:
            outs[0][...] = total_ref[...]


def apply_bonds(info, slots, vector, stats, chunks, operands, sent, mixing, before, pieces):
    count, blocks, half, lanes = operands[0][0].shape
    step = 4
    in_specs = [pl.BlockSpec((step,) + vector.shape[1:], lambda i, *_: (i, 0, 0))]
    arguments = [vector]
    if stats is not None:
        in_specs.append(whole(*stats.shape))
        arguments.append(stats)
    for made in operands:
        in_specs += operand_specs(count, step, half, lanes)
        arguments += made
    if sent is not None:
        in_specs.append(
            pl.BlockSpec((count, step) + sent.shape[2:], lambda i, *_: (0, i, 0, 0))
        )
        arguments.append(sent)
    for chunk in chunks:
        in_specs.append(
            pl.BlockSpec((count,) + mixing.shape[1:], lambda i, *_, at=chunk: (at, 0, 0))
        )
        arguments.append(mixing)
    total = count * len(chunks)
    scratch = [
        pltpu.VMEM((2, 8, lanes, lanes), jnp.float32),
        pltpu.VMEM((step, total * 32, PHYS * half), jnp.float32),
    ]
    if before is not None:
        in_specs.append(pl.BlockSpec(memory_space=pl.ANY))
        arguments.append(before)
        scratch += [pltpu.VMEM(before.shape, jnp.float32), pltpu.SemaphoreType.DMA]
    shapes = [(4, 2 * lanes + SUB, lanes)] * 2 if pieces else [(2, 8, lanes, lanes)]
    out_specs = [whole(*shape) for shape in shapes]
    out_shape = [jax.ShapeDtypeStruct(shape, jnp.float32) for shape in shapes]
    if sent is not None:
        out_specs += operand_specs(count, step, half, lanes)
        out_shape += operand_shapes(count, blocks, half, lanes)
    plan = (tuple(chunks), sent is not None, before is not None, stats is not None, pieces)
    out = pl.pallas_call(
        functools.partial(apply_kernel, plan),
        grid_spec=pltpu.PrefetchScalarGridSpec(
            num_scalar_prefetch=3,
            grid=(blocks // step,),
            in_specs=in_specs,
            out_specs=out_specs,
            scratch_shapes=scratch,
        ),
        out_shape=out_shape,
        compiler_params=pltpu.CompilerParams(vmem_limit_bytes=APPLY_VMEM),
        cost_estimate=micros(1),
        name="apply_bonds",
    )(info, *slots, *arguments)
    return out[: len(shapes)], out[len(shapes) :]


def add_arrived(info_ref, owner_ref, arrived, total):
    for k in range(4):
        for i in range(2):
            rows = slice(i * LANES, (i + 1) * LANES)
            total[owner_ref[info_ref[4] ^ k, i]] += arrived[k][rows]


def stacked_rows(*rows):
    at = lax.broadcasted_iota(jnp.int32, (SUB, LANES), 0)
    tile = jnp.zeros((SUB, LANES), jnp.float32)
    for i, row in enumerate(rows):
        tile = jnp.where(at == i, row, tile)
    return tile


def merged(tiles):
    rows = [[tile[i : i + 1] for i in range(3)] for tile in tiles]
    cross = sum(row[0] for row in rows)
    square = sum(row[1] for row in rows)
    ratio = cross / jnp.maximum(square, TINY)
    apart = [
        (row[0] / jnp.maximum(row[1], TINY) - ratio) * jnp.sqrt(row[1]) for row in rows
    ]
    rest = sum(row[2] for row in rows) + sum(x * x for x in apart)
    return cross, square, rest


def image_kernel(info_ref, owner_ref, *refs):
    arrived = [refs[4 * g : 4 * g + 4][::-1] for g in range(4)]
    starts, wave_ref, image_ref, vec_ref, stats_ref, total = refs[16:20], *refs[20:]
    half = LANES // 2
    blocks = image_ref.shape[0]
    cross = jnp.zeros((LANES, LANES), jnp.float32)
    square = jnp.zeros((LANES, LANES), jnp.float32)
    for g in range(4):
        total[g] = starts[g][...]
        add_arrived(info_ref, owner_ref, arrived[g], total.at[g])
        for k in range(blocks):
            wave = wave_ref[info_ref[g], k]
            cross += wave * total[g, k]
            square += wave * wave
    image_ref[...] = total[0]
    cross = jnp.sum(cross, keepdims=True)
    square = jnp.sum(square, keepdims=True)
    ratio = cross / jnp.maximum(square, TINY)
    rest = jnp.zeros((LANES, LANES), jnp.float32)
    for g in range(4):
        for k in range(blocks):
            apart = total[g, k] - ratio * wave_ref[info_ref[g], k]
            rest += apart * apart
    stats_ref[...] = stacked_rows(cross, square, jnp.sum(rest, keepdims=True))
    rows_of = [pl.multiple_of(info_ref[g] * 16, 16) for g in range(4)]
    for j in range(blocks):

        def put(row, pair, high, low):
            columns = slice(pair * LANES, (pair + 1) * LANES)
            vec_ref[j, pl.ds(row, 16), columns] = high
            vec_ref[j, pl.ds(row + half, 16), columns] = low

        store_vector([total.at[g, j] for g in range(4)], rows_of, put)


def whole_image(info, owners, arrived, starts, waves):
    blocks = waves.shape[1]
    pieces = [piece for part in arrived for piece in part]
    arguments = (*pieces, *starts, waves)
    shapes = [
        jax.ShapeDtypeStruct((blocks, LANES, LANES), jnp.float32),
        jax.ShapeDtypeStruct((blocks, LANES, 8 * LANES), jnp.bfloat16),
        jax.ShapeDtypeStruct((SUB, LANES), jnp.float32),
    ]
    return pl.pallas_call(
        image_kernel,
        grid_spec=pltpu.PrefetchScalarGridSpec(
            num_scalar_prefetch=2,
            grid=(1,),
            in_specs=[whole(*x.shape) for x in arguments],
            out_specs=[whole(*x.shape) for x in shapes],
            scratch_shapes=[pltpu.VMEM(waves.shape, jnp.float32)],
        ),
        out_shape=shapes,
        compiler_params=pltpu.CompilerParams(vmem_limit_bytes=APPLY_VMEM),
        cost_estimate=micros(3),
        name="whole_image",
    )(info, owners, *arguments)


def final_kernel(
    entries, info_ref, owner_ref, a0, a1, a2, a3, diag_ref, wave_ref, image_ref, first_ref,
    vector_ref, second_ref, total,
):
    arrived = (a0, a1, a2, a3)
    cross, square, rest = merged([ref[2 * LANES :] for ref in arrived])
    scale = lax.rsqrt(square / entries + 1e-06)
    rayleigh = scale * scale * (cross / entries)
    apart = (cross / jnp.maximum(square, TINY) - rayleigh) * jnp.sqrt(square)
    mean = scale * scale * ((rest + apart * apart) / entries)
    second_scale = scale * lax.rsqrt(mean + 1e-06)
    for k in range(total.shape[0]):
        image = image_ref[k]
        total[k] = (diag_ref[k] - rayleigh) * image
        first_ref[k] = unpack_tile(scale * image)
        vector_ref[k] = unpack_tile(second_scale * (image - rayleigh * wave_ref[0, k]))
    add_arrived(info_ref, owner_ref, arrived, total)
    for k in range(total.shape[0]):
        second_ref[k] = unpack_tile(second_scale * total[k])


def outputs(info, owners, arrived, diagonal, waves, image, entries):
    blocks = diagonal.shape[0]
    shape = (blocks, LANES // 2, 2 * LANES)
    return pl.pallas_call(
        functools.partial(final_kernel, entries),
        grid_spec=pltpu.PrefetchScalarGridSpec(
            num_scalar_prefetch=2,
            grid=(1,),
            in_specs=[whole(*x.shape) for x in (*arrived, diagonal)]
            + [pl.BlockSpec((1,) + waves.shape[1:], lambda i, info, _: (info[0], 0, 0, 0))]
            + [whole(*image.shape)],
            out_specs=[whole(*shape)] * 3,
            scratch_shapes=[pltpu.VMEM(diagonal.shape, jnp.float32)],
        ),
        out_shape=[jax.ShapeDtypeStruct(shape, jnp.float32)] * 3,
        compiler_params=pltpu.CompilerParams(vmem_limit_bytes=SMALL_VMEM),
        cost_estimate=micros(4),
        name="outputs",
    )(info, owners, *arrived, diagonal, waves, image)


def in_hbm(*arrays):
    return [pltpu.with_memory_space_constraint(x, pltpu.HBM) for x in arrays]


def partner(x, axis, k):
    size = lax.axis_size(axis)
    return lax.ppermute(x, axis, [(i, i ^ k) for i in range(size)])


def after(x, *others):
    return lax.optimization_barrier((x, *others))[0]


def gathered(x):
    across = partner(x, "mpo", 1)
    return [x, across, partner(x, "rep", 1), partner(across, "rep", 1)]


def everyone_of(pieces, axis):
    sent = {k: partner(pieces[k], axis, k) for k in (3, 2, 1)}
    return [pieces[0], sent[1], sent[2], sent[3]]


def to_owners(mine, theirs):
    other = partner(theirs, "rep", 1)
    pieces = [mine[k] + other[k] for k in range(4)]
    return everyone_of(pieces, "blk")


def per_device(wavefunction, environment, bond_terms, diagonal, term_slot, slot_block):
    blocks, rows, width = wavefunction.shape
    zs = lax.axis_size("blk")
    mpo, rep, blk = lax.axis_index("mpo"), lax.axis_index("rep"), lax.axis_index("blk")
    place = 2 * mpo + rep
    info = jnp.stack([place, place ^ 2, place ^ 1, place ^ 3, blk, rep, mpo]).astype(jnp.int32)
    bonds = environment.shape[0]
    per = bonds // GROUPS
    entries = float(blocks * zs * rows * width)


    by_owner = environment.reshape(bonds, zs, blocks, rows // zs, 2 * rows)
    pieces = []
    for group in range(GROUPS):
        cuts = cut_pieces(info, by_owner, group, per)
        if group == 0:
            first_cut = cuts[0]
        else:
            cuts = [after(x, y) for x, y in zip(cuts, pieces[-1][1:])]
        pieces.append([None] + [partner(x, "blk", k + 1) for k, x in enumerate(cuts)])
    vector, waves, diagonal_packed, start = pack(after(info, pieces[0][1]), wavefunction, diagonal)
    pieces[0][1] = after(pieces[0][1], vector)
    other_terms = partner(after(bond_terms, pieces[0][1]), "mpo", 1)
    mixing = mixing_operand([bond_terms, other_terms])
    slots = [term_slot, partner(after(term_slot, pieces[0][1]), "mpo", 1)]
    starts = gathered(start)
    vector = after(vector, *starts[1:])

    made, sent = [], []
    total = None
    operands = []
    done = 0

    def apply_group(group, vector):
        last = group == GROUPS - 1
        out, other = apply_bonds(
            info, slots, vector, None, [group, GROUPS + group], [made[group]],
            partner(sent[group], "mpo", 1), mixing, total, last,
        )
        operands.extend([made[group], other])
        return out

    for group in range(GROUPS):
        if group >= 2:
            total = apply_group(group - 2, after(vector, sent[group - 1]))[0]
            pieces[group][3] = after(pieces[group][3], total)
        *own_set, send = own_operands(info, by_owner, group, pieces[group][1:])
        made.append(own_set)
        sent.append(send)
    total = apply_group(GROUPS - 2, after(vector, sent[-1]))[0]
    out = apply_group(GROUPS - 1, vector)
    arrived = to_owners(*out)
    by_part = list(zip(*[gathered(piece) for piece in arrived[::-1]]))
    image, vector, stats = whole_image(info, slot_block, by_part, starts, waves)

    chunks = [group + GROUPS * source for group in range(GROUPS) for source in range(2)]
    out, _ = apply_bonds(info, slots, vector, stats, chunks, operands, None, mixing, None, True)
    return tuple(
        outputs(info, slot_block, to_owners(*out), diagonal_packed, waves, image, entries)
    )


def solution(mesh):
    packed = mesh.shape["mpo"] == 2 and mesh.shape["rep"] == 2 and mesh.shape["blk"] == 4
    return jax.shard_map(
        per_device if packed else plain_device,
        mesh=mesh,
        in_specs=(
            P(("grp", "blk"), None, None),
            P(("grp", "mpo", "rep"), None, "blk", None),
            P(("grp", "mpo", "rep"), None, None),
            P(("grp", "blk"), None, ("mpo", "rep")),
            P(("grp", "mpo", "rep"), "blk"),
            P("grp", "blk"),
        ),
        out_specs=(
            P(("grp", "blk"), None, ("mpo", "rep")),
            P(("grp", "blk"), None, ("mpo", "rep")),
            P(("grp", "blk"), None, ("mpo", "rep")),
        ),
        check_vma=False,
    )
```

```python
import functools

import jax
import jax.numpy as jnp
from jax import lax
from jax.experimental import pallas as pl
from jax.experimental.pallas import tpu as pltpu
from jax.sharding import PartitionSpec as P

LANES = 128
SUB = 8
PHYS = 16
TINY = 1e-30
GROUPS = 3
SMALL_VMEM = 16 * 1024 * 1024
APPLY_VMEM = 26 * 1024 * 1024


def plain_apply(vector_full, environment, bond_terms, term_slot, slot_block, diagonal):
    block_count, block_rows, block_width = vector_full.shape
    phys_size = bond_terms.shape[-1]
    right_rows = block_width // phys_size
    slot_count = slot_block.shape[0] * slot_block.shape[1]
    blocks = vector_full.reshape(block_count, block_rows, right_rows, phys_size)
    ordered = jnp.transpose(blocks, (0, 3, 1, 2))
    left_env = environment[:, :, :, :block_rows]
    right_env = environment[:, :, :, block_rows:]
    left_done = jnp.einsum("wjab,jsac->wjsbc", left_env, ordered, precision=lax.Precision.HIGHEST)
    right_done = jnp.einsum(
        "wjsbc,wjcd->wjsbd", left_done, right_env, precision=lax.Precision.HIGHEST
    )
    right_done = right_done.reshape(
        environment.shape[0], block_count, phys_size, block_rows * right_rows
    )
    bond_term = jnp.einsum(
        "wjsx,wst->wjtx", right_done, bond_terms, precision=lax.Precision.HIGHEST
    )
    bond_term = bond_term.reshape(environment.shape[0], block_count, block_rows * block_width)
    slot_table = (
        term_slot[:, None, :] == jnp.arange(slot_count, dtype=jnp.int32)[None, :, None]
    ).astype(jnp.float32)
    slot_buffer = jnp.einsum("wsj,wjx->sx", slot_table, bond_term, precision=lax.Precision.HIGHEST)
    slot_buffer = slot_buffer.reshape(slot_count, phys_size, block_rows, right_rows)
    slot_buffer = jnp.transpose(slot_buffer, (0, 2, 3, 1)).reshape(
        slot_count, block_rows, block_width
    )
    owners = slot_block.reshape(-1)
    selector = (owners[None, :] == jnp.arange(block_count, dtype=jnp.int32)[:, None]).astype(
        jnp.float32
    )
    column_width = block_width // lax.axis_size(("mpo", "rep"))
    column_start = lax.axis_index(("mpo", "rep")) * column_width
    own_part = lax.dynamic_slice_in_dim(vector_full, column_start, column_width, 2)
    shares = lax.psum_scatter(slot_buffer, ("mpo", "rep"), scatter_dimension=2, tiled=True)
    arrived = lax.all_to_all(shares, "blk", split_axis=0, concat_axis=0, tiled=True)
    result = jnp.einsum("ks,sbc->kbc", selector, arrived, precision=lax.Precision.HIGHEST)
    return (result + diagonal * own_part, own_part)


def plain_device(wavefunction, environment, bond_terms, diagonal, term_slot, slot_block):
    arranged = lax.all_to_all(environment, "blk", split_axis=1, concat_axis=2, tiled=True)
    entries = float(
        wavefunction.shape[0] * lax.axis_size("blk") * wavefunction.shape[1] * wavefunction.shape[2]
    )
    square_sum = lax.psum(jnp.sum(wavefunction * wavefunction), "blk")
    first_vector = wavefunction * lax.rsqrt(square_sum / entries + 1e-06)
    first_image, first_part = plain_apply(
        first_vector, arranged, bond_terms, term_slot, slot_block, diagonal
    )
    rayleigh = lax.psum(jnp.sum(first_part * first_image), ("blk", "mpo", "rep")) / entries
    residual = first_image - rayleigh * first_part
    resid_sum = lax.psum(jnp.sum(residual * residual), ("blk", "mpo", "rep"))
    second_vector = residual * lax.rsqrt(resid_sum / entries + 1e-06)
    second_full = lax.all_gather(second_vector, ("mpo", "rep"), axis=2, tiled=True)
    second_image, unused = plain_apply(
        second_full, arranged, bond_terms, term_slot, slot_block, diagonal
    )
    return (first_image, second_vector, second_image)


def split_two(x):
    high = x.astype(jnp.bfloat16)
    low = (x - high.astype(jnp.float32)).astype(jnp.bfloat16)
    return high, low


def lane_is_first(rows):
    return lax.broadcasted_iota(jnp.int32, (rows, LANES), 1) < LANES // 2


def micros(count):
    return pl.CostEstimate(flops=count * 1100000000, bytes_accessed=1 << 20, transcendentals=0)


def whole(*shape):
    return pl.BlockSpec(shape, lambda i, *_: (0,) * len(shape))


def pack_tile(x):
    return jnp.concatenate([x[:, :LANES], x[:, LANES:]], axis=0).T


def unpack_tile(x):
    upright = x.T
    return jnp.concatenate([upright[: LANES // 2], upright[LANES // 2 :]], axis=1)


def store_vector(parts, rows_of, put):
    first = lane_is_first(SUB)
    for pair in range(PHYS // 2):
        for part, row in zip(parts, rows_of):
            even = part[pl.ds(2 * pair, SUB, stride=PHYS), :]
            odd = part[pl.ds(2 * pair + 1, SUB, stride=PHYS), :]
            upper = jnp.where(first, even, pltpu.roll(odd, LANES // 2, 1))
            lower = jnp.where(first, pltpu.roll(even, LANES // 2, 1), odd)
            high, low = split_two(jnp.concatenate([upper, lower], axis=0))
            put(row, pair, high, low)


def pack_kernel(info_ref, wave_ref, own_wave_ref, diag_ref, vec_ref, own_ref, diag_out, tiles):
    half = LANES // 2
    for j in range(wave_ref.shape[0]):
        own_ref[j] = pack_tile(own_wave_ref[j])
        diag_out[j] = pack_tile(diag_ref[j])
        for q in range(4):
            tiles[q, j] = pack_tile(wave_ref[j, :, 2 * LANES * q : 2 * LANES * (q + 1)])

        def put(row, pair, high, low):
            columns = slice(pair * LANES, (pair + 1) * LANES)
            vec_ref[j, row : row + 16, columns] = high
            vec_ref[j, row + half : row + half + 16, columns] = low

        store_vector([tiles.at[q, j] for q in range(4)], [16 * q for q in range(4)], put)


def pack(info, wavefunction, diagonal):
    blocks, rows, width = wavefunction.shape
    step = 2
    tile = pl.BlockSpec((step, LANES, LANES), lambda i, *_: (i, 0, 0))
    return pl.pallas_call(
        pack_kernel,
        grid_spec=pltpu.PrefetchScalarGridSpec(
            num_scalar_prefetch=1,
            grid=(blocks // step,),
            in_specs=[
                pl.BlockSpec((step, rows, width), lambda i, *_: (i, 0, 0)),
                pl.BlockSpec((step, rows, width // 4), lambda i, info: (i, 0, info[0])),
                pl.BlockSpec((step, rows, width // 4), lambda i, *_: (i, 0, 0)),
            ],
            out_specs=[pl.BlockSpec((step, LANES, width), lambda i, *_: (i, 0, 0)), tile, tile],
            scratch_shapes=[pltpu.VMEM((4, step, LANES, LANES), jnp.float32)],
        ),
        out_shape=[
            jax.ShapeDtypeStruct((blocks, LANES, width), jnp.bfloat16),
            jax.ShapeDtypeStruct((blocks, LANES, LANES), jnp.float32),
            jax.ShapeDtypeStruct((blocks, LANES, LANES), jnp.float32),
        ],
        compiler_params=pltpu.CompilerParams(vmem_limit_bytes=SMALL_VMEM),
        cost_estimate=micros(5),
        name="pack",
    )(info, wavefunction, wavefunction, diagonal)


def mixing_kernel(*refs):
    sources, out_ref = refs[:-1], refs[-1]
    spread = (
        lax.broadcasted_iota(jnp.int32, (PHYS, LANES), 1) // SUB
        == lax.broadcasted_iota(jnp.int32, (PHYS, LANES), 0)
    ).astype(jnp.bfloat16)
    row = lax.broadcasted_iota(jnp.int32, (LANES, LANES), 0) // PHYS
    column = lax.broadcasted_iota(jnp.int32, (LANES, LANES), 1) % SUB
    same = row == column
    at = 0
    for source in sources:
        for k in range(source.shape[0]):
            high, low = split_two(source[k].T)
            for place, term in enumerate((high, low)):
                wide = jnp.dot(term, spread, preferred_element_type=jnp.float32)
                tall = jnp.concatenate([wide] * SUB, axis=0)
                tall = jnp.where(same, tall, 0.0).astype(jnp.bfloat16)
                rows = slice(place * LANES, (place + 1) * LANES)
                out_ref[at, rows] = jnp.concatenate([tall, tall], axis=1)
            at += 1


def mixing_operand(sources):
    count = sources[0].shape[0] * len(sources)
    return pl.pallas_call(
        mixing_kernel,
        out_shape=jax.ShapeDtypeStruct((count, 2 * LANES, 2 * LANES), jnp.bfloat16),
        compiler_params=pltpu.CompilerParams(vmem_limit_bytes=SMALL_VMEM),
        cost_estimate=micros(2),
        name="mixing",
    )(*sources)


def own_operands_kernel(info_ref, *refs):
    pieces, (left_high, left_low, right_out, send, blocks_ref, upright_ref) = refs[:4], refs[4:]
    per, blocks, half, lanes = left_high.shape
    rows = half // 4
    wide = half // 2
    first = lane_is_first(half)
    first_wide = lane_is_first(wide)
    first_rows = lane_is_first(rows)
    mine_at = pl.multiple_of(half + info_ref[6] * wide, wide)
    theirs_at = pl.multiple_of(lanes - wide - info_ref[6] * wide, wide)
    for j in range(blocks):
        for w in range(per):
            for z in range(4):
                row = pl.multiple_of((info_ref[4] ^ z) * rows, rows)
                piece = pieces[z][w, 0, j] if z == 0 else pieces[z][w, j]
                blocks_ref[w, j, pl.ds(row, rows), :] = piece
        for w in range(per):
            block = blocks_ref[w, j]
            upright_ref[w, j] = jnp.concatenate([block, block], axis=0).T
            turned = pltpu.roll(block, half, 1)
            high, low = split_two(jnp.where(first, block, turned))
            left_high[w, j] = high
            left_low[w, j] = low
            send[w, j, 0:wide] = jnp.where(first_wide, block[:wide], turned[wide:])
        for w in range(per):
            high, low = split_two(upright_ref[w, j, pl.ds(mine_at, wide), :])
            right_out[j, wide * w : wide * (w + 1), 0:lanes] = high
            right_out[j, wide * w : wide * (w + 1), lanes:] = low
            upper = upright_ref[w, j, pl.ds(theirs_at, rows), :]
            lower = upright_ref[w, j, pl.ds(theirs_at + rows, rows), :]
            send[w, j, wide : wide + rows] = jnp.where(first_rows, upper, lower)


def other_operands(sent, left_high, left_low, right_out, j):
    per, blocks, half, lanes = left_high.shape
    rows = half // 4
    wide = half // 2
    first = lane_is_first(wide)
    first_rows = lane_is_first(rows)
    for w in range(per):
        both = sent[w, j, 0:wide]
        turned = pltpu.roll(both, half, 1)
        full = jnp.concatenate(
            [jnp.where(first, both, turned), jnp.where(first, turned, both)], axis=0
        )
        high, low = split_two(full)
        left_high[w, j] = high
        left_low[w, j] = low
        both = sent[w, j, wide : wide + rows]
        turned = pltpu.roll(both, half, 1)
        full = jnp.concatenate(
            [jnp.where(first_rows, both, turned), jnp.where(first_rows, turned, both)], axis=0
        )
        high, low = split_two(full)
        right_out[j, wide * w : wide * (w + 1), 0:lanes] = high
        right_out[j, wide * w : wide * (w + 1), lanes:] = low


def operand_specs(per, step, half, lanes):
    return [
        pl.BlockSpec((per, step, half, lanes), lambda i, *_: (0, i, 0, 0)),
        pl.BlockSpec((per, step, half, lanes), lambda i, *_: (0, i, 0, 0)),
        pl.BlockSpec((step, per * 32, 2 * lanes), lambda i, *_: (i, 0, 0)),
    ]


def operand_shapes(per, blocks, half, lanes):
    return [
        jax.ShapeDtypeStruct((per, blocks, half, lanes), jnp.bfloat16),
        jax.ShapeDtypeStruct((per, blocks, half, lanes), jnp.bfloat16),
        jax.ShapeDtypeStruct((blocks, per * 32, 2 * lanes), jnp.bfloat16),
    ]


def cut_kernel(group, info_ref, source, *refs):
    outs, sems = refs[:3], refs[3]
    per = outs[0].shape[0]
    copies = []
    for k in range(3):
        part = source.at[pl.ds(group * per, per), info_ref[4] ^ (k + 1)]
        copies.append(pltpu.make_async_copy(part, outs[k], sems.at[k]))
    for copy in copies:
        copy.start()
    for copy in copies:
        copy.wait()


def cut_pieces(info, by_owner, group, per):
    shape = jax.ShapeDtypeStruct((per,) + by_owner.shape[2:], jnp.float32)
    return pl.pallas_call(
        functools.partial(cut_kernel, group),
        grid_spec=pltpu.PrefetchScalarGridSpec(
            num_scalar_prefetch=1,
            grid=(1,),
            in_specs=[pl.BlockSpec(memory_space=pl.ANY)],
            out_specs=[pl.BlockSpec(memory_space=pl.ANY)] * 3,
            scratch_shapes=[pltpu.SemaphoreType.DMA((3,))],
        ),
        out_shape=[shape] * 3,
        compiler_params=pltpu.CompilerParams(vmem_limit_bytes=SMALL_VMEM),
        cost_estimate=micros(1),
        name="cut_pieces",
    )(info, *(in_hbm(by_owner) if group == 0 else [by_owner]))


def own_operands(info, by_owner, group, pieces):
    per, blocks, rows, lanes = pieces[0].shape
    half = lanes // 2
    step = 4
    return pl.pallas_call(
        own_operands_kernel,
        grid_spec=pltpu.PrefetchScalarGridSpec(
            num_scalar_prefetch=1,
            grid=(blocks // step,),
            in_specs=[
                pl.BlockSpec(
                    (per, 1, step, rows, lanes), lambda i, info: (group, info[4], i, 0, 0)
                )
            ]
            + [pl.BlockSpec((per, step, rows, lanes), lambda i, *_: (0, i, 0, 0))] * 3,
            out_specs=operand_specs(per, step, half, lanes)
            + [pl.BlockSpec((per, step, 3 * rows, lanes), lambda i, *_: (0, i, 0, 0))],
            scratch_shapes=[
                pltpu.VMEM((per, step, half, lanes), jnp.float32),
                pltpu.VMEM((per, step, lanes, lanes), jnp.float32),
            ],
        ),
        out_shape=operand_shapes(per, blocks, half, lanes)
        + [jax.ShapeDtypeStruct((per, blocks, 3 * rows, lanes), jnp.float32)],
        compiler_params=pltpu.CompilerParams(vmem_limit_bytes=SMALL_VMEM),
        cost_estimate=micros(6),
        name="own_operands",
    )(info, by_owner, *pieces)


def apply_kernel(plan, info_ref, *refs):
    chunks, parts_given, sent_given, before_given, pieces = plan
    refs = list(refs)
    take = lambda n: [refs.pop(0) for _ in range(n)]
    slots = take(2)
    vector = take(4 if parts_given else 1)
    tiles = take(4) if parts_given else []
    operands = [take(3) for _ in chunks[: -1 if sent_given else None]]
    sent = take(1)[0] if sent_given else None
    mixes = take(len(chunks))
    before = take(1)[0] if before_given else None
    outs = take(2 if pieces else 1)
    if sent_given:
        operands.append(take(3))
    total_ref, vec, mid = take(3)
    if before_given:
        prior, arrival = take(2)
    step = mid.shape[0]
    lanes, half = LANES, LANES // 2
    first = lane_is_first(SUB)
    first_half = lane_is_first(half)
    keep_first = jnp.where(first_half, 1.0, 0.0).astype(jnp.bfloat16)
    keep_second = jnp.where(first_half, 0.0, 1.0).astype(jnp.bfloat16)
    me = info_ref[4]

    @pl.when(pl.program_id(0) == 0)
    def _():
        if before_given:
            pltpu.make_async_copy(before, prior, arrival).start()
        total_ref[...] = jnp.zeros_like(total_ref)

    def right_side(j):
        if sent_given:
            other_operands(sent, *operands[-1], j)
        if parts_given:

            def put(row, pair, high, low):
                columns = slice(pair * lanes, (pair + 1) * lanes)
                vec[j, pl.ds(row, 16), columns] = high
                vec[j, pl.ds(row + half, 16), columns] = low

            rows_of = [pl.multiple_of(info_ref[g] * 16, 16) for g in range(4)]
            store_vector([x.at[pl.ds(j * lanes, lanes)] for x in vector], rows_of, put)
            source = vec[j]
        else:
            source = vector[0][j]
        source = jnp.concatenate([source, source], axis=0)
        at = 0
        for left_high, left_low, right in operands:
            count = right.shape[1]
            mid[j, at : at + count, :] = jnp.dot(
                right[j], source, preferred_element_type=jnp.float32
            )
            at += count

    def prepared(j, refs_of, w, row_of):
        left_high, left_low, right = refs_of
        tiles = []
        for part in range(2):
            row = row_of + part * 16
            for pair in range(PHYS // 2):
                columns = slice(pair * lanes, (pair + 1) * lanes)
                upper = mid[j, row : row + SUB, columns]
                lower = mid[j, row + SUB : row + 2 * SUB, columns]
                tiles.append(jnp.where(first, upper, pltpu.roll(lower, half, 1)))
                tiles.append(jnp.where(first, pltpu.roll(upper, half, 1), lower))
        t_high, t_low = split_two(jnp.concatenate(tiles, axis=0))
        lh, ll = left_high[w, j], left_low[w, j]
        wide_high = jnp.concatenate([lh * keep_first, lh * keep_second], axis=0)
        wide_low = jnp.concatenate([ll * keep_first, ll * keep_second], axis=0)
        weights = jnp.concatenate([wide_high, wide_low], axis=1)
        weights = jnp.concatenate([weights, weights], axis=0)
        return jnp.concatenate([t_high, t_low], axis=1), weights

    def mix_unit(mixing, w, z):
        z_high, z_low = [jnp.concatenate([x[:lanes], x[lanes:]], axis=1) for x in z]
        return jnp.dot(
            mixing[w],
            jnp.concatenate([z_high, z_low], axis=0),
            preferred_element_type=jnp.float32,
        )

    def add_up(j, table, bond, mixed):
        slot = table[bond, pl.program_id(0) * step + j]
        slot = ((slot >> 1) ^ me) * 2 + (slot & 1)
        for part in range(2):
            columns = slice(part * lanes, (part + 1) * lanes)
            total_ref[part, slot] += mixed[:lanes, columns] + mixed[lanes:, columns]

    bonds = []
    for chunk, refs_of, mix in zip(chunks, operands, mixes):
        count = mix.shape[0]
        source, group = chunk // GROUPS, chunk % GROUPS
        for w in range(count):
            bonds.append((refs_of, mix, w, slots[source], group * count + w))
    right_side(0)
    units = [(j, at) for j in range(step) for at in range(len(bonds))]

    def prepare_unit(n):
        j, at = units[n]
        refs_of, mixing, w, table, bond = bonds[at]
        return prepared(j, refs_of, w, at * 32)

    ready = prepare_unit(0)
    waiting = None
    for n, (j, at) in enumerate(units):
        refs_of, mixing, w, table, bond = bonds[at]
        z = jnp.dot(*ready, preferred_element_type=jnp.float32)
        if j + 1 < step and at == len(bonds) // 3:
            right_side(j + 1)
        if n + 1 < len(units):
            ready = prepare_unit(n + 1)
        if waiting is not None:
            before_j, before_mixing, before_w, before_table, before_bond, before_z = waiting
            mixed = mix_unit(before_mixing, before_w, before_z)
        z = split_two(z[:, :lanes] + z[:, lanes:])
        if waiting is not None:
            add_up(before_j, before_table, before_bond, mixed)
        waiting = (j, mixing, w, table, bond, z)
    j, mixing, w, table, bond, z = waiting
    add_up(j, table, bond, mix_unit(mixing, w, z))

    @pl.when(pl.program_id(0) == pl.num_programs(0) - 1)
    def _():
        if before_given:
            pltpu.make_async_copy(before, prior, arrival).wait()
            total_ref[...] += prior[...]
        if pieces:
            stats = jnp.zeros((SUB, lanes), jnp.float32)
            if parts_given:
                stats = stacked_rows(*merged([tile[...] for tile in tiles]))
            for out, part in ((outs[0], info_ref[5]), (outs[1], 1 - info_ref[5])):
                for k in range(4):
                    for i in range(2):
                        out[k, i * lanes : (i + 1) * lanes] = total_ref[part, 2 * k + i]
                    out[k, 2 * lanes :] = stats
                stats = jnp.zeros((SUB, lanes), jnp.float32)
        else:
            outs[0][...] = total_ref[...]


def apply_bonds(info, slots, vector, chunks, operands, sent, mixing, before, pieces):
    count, blocks, half, lanes = operands[0][0].shape
    step = 4
    parts_given = len(vector) == 4
    if parts_given:
        last = vector[0].shape[0] // SUB - 1
        in_specs = [pl.BlockSpec((step * lanes, lanes), lambda i, *_: (i, 0))] * 4
        in_specs += [pl.BlockSpec((SUB, lanes), lambda i, *_: (last, 0))] * 4
    else:
        in_specs = [pl.BlockSpec((step,) + vector[0].shape[1:], lambda i, *_: (i, 0, 0))]
    arguments = list(vector) * (2 if parts_given else 1)
    for made in operands:
        in_specs += operand_specs(count, step, half, lanes)
        arguments += made
    if sent is not None:
        in_specs.append(
            pl.BlockSpec((count, step) + sent.shape[2:], lambda i, *_: (0, i, 0, 0))
        )
        arguments.append(sent)
    for chunk in chunks:
        in_specs.append(
            pl.BlockSpec((count,) + mixing.shape[1:], lambda i, *_, at=chunk: (at, 0, 0))
        )
        arguments.append(mixing)
    total = count * len(chunks)
    scratch = [
        pltpu.VMEM((2, 8, lanes, lanes), jnp.float32),
        pltpu.VMEM((step, lanes, PHYS * half), jnp.bfloat16),
        pltpu.VMEM((step, total * 32, PHYS * half), jnp.float32),
    ]
    if before is not None:
        in_specs.append(pl.BlockSpec(memory_space=pl.ANY))
        arguments.append(before)
        scratch += [pltpu.VMEM(before.shape, jnp.float32), pltpu.SemaphoreType.DMA]
    shapes = [(4, 2 * lanes + SUB, lanes)] * 2 if pieces else [(2, 8, lanes, lanes)]
    out_specs = [whole(*shape) for shape in shapes]
    out_shape = [jax.ShapeDtypeStruct(shape, jnp.float32) for shape in shapes]
    if sent is not None:
        out_specs += operand_specs(count, step, half, lanes)
        out_shape += operand_shapes(count, blocks, half, lanes)
    plan = (tuple(chunks), parts_given, sent is not None, before is not None, pieces)
    out = pl.pallas_call(
        functools.partial(apply_kernel, plan),
        grid_spec=pltpu.PrefetchScalarGridSpec(
            num_scalar_prefetch=3,
            grid=(blocks // step,),
            in_specs=in_specs,
            out_specs=out_specs,
            scratch_shapes=scratch,
        ),
        out_shape=out_shape,
        compiler_params=pltpu.CompilerParams(vmem_limit_bytes=APPLY_VMEM),
        cost_estimate=micros(1),
        name="apply_bonds",
    )(info, *slots, *arguments)
    return out[: len(shapes)], out[len(shapes) :]


def add_arrived(info_ref, owner_ref, arrived, total):
    for k in range(4):
        for i in range(2):
            rows = slice(i * LANES, (i + 1) * LANES)
            total[owner_ref[info_ref[4] ^ k, i]] += arrived[k][rows]


def stacked_rows(*rows):
    at = lax.broadcasted_iota(jnp.int32, (SUB, LANES), 0)
    tile = jnp.zeros((SUB, LANES), jnp.float32)
    for i, row in enumerate(rows):
        tile = jnp.where(at == i, row, tile)
    return tile


def merged(tiles):
    rows = [[tile[i : i + 1] for i in range(3)] for tile in tiles]
    cross = sum(row[0] for row in rows)
    square = sum(row[1] for row in rows)
    ratio = cross / jnp.maximum(square, TINY)
    apart = [
        (row[0] / jnp.maximum(row[1], TINY) - ratio) * jnp.sqrt(row[1]) for row in rows
    ]
    rest = sum(row[2] for row in rows) + sum(x * x for x in apart)
    return cross, square, rest


def image_kernel(info_ref, owner_ref, a0, a1, a2, a3, diag_ref, own_ref, image_ref, total):
    total[...] = diag_ref[...] * own_ref[...]
    add_arrived(info_ref, owner_ref, (a0, a1, a2, a3), total)
    blocks = total.shape[0]
    cross = jnp.zeros((LANES, LANES), jnp.float32)
    square = jnp.zeros((LANES, LANES), jnp.float32)
    for k in range(blocks):
        own, image = own_ref[k], total[k]
        image_ref[k * LANES : (k + 1) * LANES] = image
        cross += own * image
        square += own * own
    cross = jnp.sum(cross, keepdims=True)
    square = jnp.sum(square, keepdims=True)
    ratio = cross / jnp.maximum(square, TINY)
    rest = jnp.zeros((LANES, LANES), jnp.float32)
    for k in range(blocks):
        apart = total[k] - ratio * own_ref[k]
        rest += apart * apart
    image_ref[blocks * LANES :] = stacked_rows(cross, square, jnp.sum(rest, keepdims=True))


def owner_image(info, owners, arrived, diagonal, own):
    rows = own.shape[0] * LANES + SUB
    return pl.pallas_call(
        image_kernel,
        grid_spec=pltpu.PrefetchScalarGridSpec(
            num_scalar_prefetch=2,
            grid=(1,),
            in_specs=[whole(*x.shape) for x in (*arrived, diagonal, own)],
            out_specs=whole(rows, LANES),
            scratch_shapes=[pltpu.VMEM(own.shape, jnp.float32)],
        ),
        out_shape=jax.ShapeDtypeStruct((rows, LANES), jnp.float32),
        compiler_params=pltpu.CompilerParams(vmem_limit_bytes=SMALL_VMEM),
        cost_estimate=micros(3),
        name="owner_image",
    )(info, owners, *in_hbm(arrived[0]), *arrived[1:], *in_hbm(diagonal, own))


def final_kernel(
    entries, info_ref, owner_ref, a0, a1, a2, a3, diag_ref, own_ref, image_ref, first_ref,
    vector_ref, second_ref, total,
):
    arrived = (a0, a1, a2, a3)
    cross, square, rest = merged([ref[2 * LANES :] for ref in arrived])
    scale = lax.rsqrt(square / entries + 1e-06)
    rayleigh = scale * scale * (cross / entries)
    apart = (cross / jnp.maximum(square, TINY) - rayleigh) * jnp.sqrt(square)
    mean = scale * scale * ((rest + apart * apart) / entries)
    second_scale = scale * lax.rsqrt(mean + 1e-06)
    for k in range(total.shape[0]):
        image = image_ref[k * LANES : (k + 1) * LANES]
        total[k] = (diag_ref[k] - rayleigh) * image
        first_ref[k] = unpack_tile(scale * image)
        vector_ref[k] = unpack_tile(second_scale * (image - rayleigh * own_ref[k]))
    add_arrived(info_ref, owner_ref, arrived, total)
    for k in range(total.shape[0]):
        second_ref[k] = unpack_tile(second_scale * total[k])


def outputs(info, owners, arrived, diagonal, own, image, entries):
    blocks = diagonal.shape[0]
    shape = (blocks, LANES // 2, 2 * LANES)
    return pl.pallas_call(
        functools.partial(final_kernel, entries),
        grid_spec=pltpu.PrefetchScalarGridSpec(
            num_scalar_prefetch=2,
            grid=(1,),
            in_specs=[whole(*x.shape) for x in (*arrived, diagonal, own)]
            + [whole(blocks * LANES, LANES)],
            out_specs=[whole(*shape)] * 3,
            scratch_shapes=[pltpu.VMEM(diagonal.shape, jnp.float32)],
        ),
        out_shape=[jax.ShapeDtypeStruct(shape, jnp.float32)] * 3,
        compiler_params=pltpu.CompilerParams(vmem_limit_bytes=SMALL_VMEM),
        cost_estimate=micros(4),
        name="outputs",
    )(info, owners, *arrived, diagonal, own, image)


def in_hbm(*arrays):
    return [pltpu.with_memory_space_constraint(x, pltpu.HBM) for x in arrays]


def partner(x, axis, k):
    size = lax.axis_size(axis)
    return lax.ppermute(x, axis, [(i, i ^ k) for i in range(size)])


def after(x, *others):
    return lax.optimization_barrier((x, *others))[0]


def gathered(x):
    across = partner(x, "mpo", 1)
    return [x, across, partner(x, "rep", 1), partner(across, "rep", 1)]


def everyone_of(pieces, axis):
    return [pieces[0]] + [partner(pieces[k], axis, k) for k in range(1, 4)]


def to_owners(mine, theirs):
    other = partner(theirs, "rep", 1)
    pieces = [mine[k] + other[k] for k in range(4)]
    return everyone_of(pieces, "blk")


def per_device(wavefunction, environment, bond_terms, diagonal, term_slot, slot_block):
    blocks, rows, width = wavefunction.shape
    zs = lax.axis_size("blk")
    mpo, rep, blk = lax.axis_index("mpo"), lax.axis_index("rep"), lax.axis_index("blk")
    place = 2 * mpo + rep
    info = jnp.stack([place, place ^ 2, place ^ 1, place ^ 3, blk, rep, mpo]).astype(jnp.int32)
    bonds = environment.shape[0]
    per = bonds // GROUPS
    entries = float(blocks * zs * rows * width)

    vector, own, diagonal_packed = pack(info, wavefunction, diagonal)

    by_owner = environment.reshape(bonds, zs, blocks, rows // zs, 2 * rows)
    pieces = []
    for group in range(GROUPS):
        cuts = cut_pieces(info, by_owner, group, per)
        if group:
            cuts = [after(x, y) for x, y in zip(cuts, pieces[-1][1:])]
        pieces.append([None] + [partner(x, "blk", k + 1) for k, x in enumerate(cuts)])
    pieces[0][1] = after(pieces[0][1], vector)
    other_terms = partner(after(bond_terms, pieces[0][1]), "mpo", 1)
    mixing = mixing_operand([bond_terms, other_terms])
    slots = [term_slot, partner(after(term_slot, pieces[0][1]), "mpo", 1)]

    made, sent = [], []
    total = None
    operands = []
    done = 0

    def apply_group(group, vector):
        last = group == GROUPS - 1
        out, other = apply_bonds(
            info, slots, [vector], [group, GROUPS + group], [made[group]],
            partner(sent[group], "mpo", 1), mixing, total, last,
        )
        operands.extend([made[group], other])
        return out

    for group in range(GROUPS):
        if group >= 2:
            total = apply_group(group - 2, after(vector, sent[group - 1]))[0]
            pieces[group][3] = after(pieces[group][3], total)
        *own_set, send = own_operands(info, by_owner, group, pieces[group][1:])
        made.append(own_set)
        sent.append(send)
    total = apply_group(GROUPS - 2, after(vector, sent[-1]))[0]
    out = apply_group(GROUPS - 1, vector)
    image = owner_image(info, slot_block, to_owners(*out), diagonal_packed, own)

    parts = gathered(image)
    chunks = [group + GROUPS * source for group in range(GROUPS) for source in range(2)]
    out, _ = apply_bonds(info, slots, parts, chunks, operands, None, mixing, None, True)
    return tuple(
        outputs(info, slot_block, to_owners(*out), diagonal_packed, own, image, entries)
    )


def solution(mesh):
    packed = mesh.shape["mpo"] == 2 and mesh.shape["rep"] == 2 and mesh.shape["blk"] == 4
    return jax.shard_map(
        per_device if packed else plain_device,
        mesh=mesh,
        in_specs=(
            P(("grp", "blk"), None, None),
            P(("grp", "mpo", "rep"), None, "blk", None),
            P(("grp", "mpo", "rep"), None, None),
            P(("grp", "blk"), None, ("mpo", "rep")),
            P(("grp", "mpo", "rep"), "blk"),
            P("grp", "blk"),
        ),
        out_specs=(
            P(("grp", "blk"), None, ("mpo", "rep")),
            P(("grp", "blk"), None, ("mpo", "rep")),
            P(("grp", "blk"), None, ("mpo", "rep")),
        ),
        check_vma=False,
    )
```

```python
import functools

import jax
import jax.numpy as jnp
from jax import lax
from jax.experimental import pallas as pl
from jax.experimental.pallas import tpu as pltpu
from jax.sharding import PartitionSpec as P

LANES = 128
SUB = 8
PHYS = 16
TINY = 1e-30
SMALL_VMEM = 16 * 1024 * 1024
APPLY_VMEM = 26 * 1024 * 1024


def plain_apply(vector_full, environment, bond_terms, term_slot, slot_block, diagonal):
    block_count, block_rows, block_width = vector_full.shape
    phys_size = bond_terms.shape[-1]
    right_rows = block_width // phys_size
    slot_count = slot_block.shape[0] * slot_block.shape[1]
    blocks = vector_full.reshape(block_count, block_rows, right_rows, phys_size)
    ordered = jnp.transpose(blocks, (0, 3, 1, 2))
    left_env = environment[:, :, :, :block_rows]
    right_env = environment[:, :, :, block_rows:]
    left_done = jnp.einsum("wjab,jsac->wjsbc", left_env, ordered, precision=lax.Precision.HIGHEST)
    right_done = jnp.einsum(
        "wjsbc,wjcd->wjsbd", left_done, right_env, precision=lax.Precision.HIGHEST
    )
    right_done = right_done.reshape(
        environment.shape[0], block_count, phys_size, block_rows * right_rows
    )
    bond_term = jnp.einsum(
        "wjsx,wst->wjtx", right_done, bond_terms, precision=lax.Precision.HIGHEST
    )
    bond_term = bond_term.reshape(environment.shape[0], block_count, block_rows * block_width)
    slot_table = (
        term_slot[:, None, :] == jnp.arange(slot_count, dtype=jnp.int32)[None, :, None]
    ).astype(jnp.float32)
    slot_buffer = jnp.einsum("wsj,wjx->sx", slot_table, bond_term, precision=lax.Precision.HIGHEST)
    slot_buffer = slot_buffer.reshape(slot_count, phys_size, block_rows, right_rows)
    slot_buffer = jnp.transpose(slot_buffer, (0, 2, 3, 1)).reshape(
        slot_count, block_rows, block_width
    )
    owners = slot_block.reshape(-1)
    selector = (owners[None, :] == jnp.arange(block_count, dtype=jnp.int32)[:, None]).astype(
        jnp.float32
    )
    column_width = block_width // lax.axis_size(("mpo", "rep"))
    column_start = lax.axis_index(("mpo", "rep")) * column_width
    own_part = lax.dynamic_slice_in_dim(vector_full, column_start, column_width, 2)
    shares = lax.psum_scatter(slot_buffer, ("mpo", "rep"), scatter_dimension=2, tiled=True)
    arrived = lax.all_to_all(shares, "blk", split_axis=0, concat_axis=0, tiled=True)
    result = jnp.einsum("ks,sbc->kbc", selector, arrived, precision=lax.Precision.HIGHEST)
    return (result + diagonal * own_part, own_part)


def plain_device(wavefunction, environment, bond_terms, diagonal, term_slot, slot_block):
    arranged = lax.all_to_all(environment, "blk", split_axis=1, concat_axis=2, tiled=True)
    entries = float(
        wavefunction.shape[0] * lax.axis_size("blk") * wavefunction.shape[1] * wavefunction.shape[2]
    )
    square_sum = lax.psum(jnp.sum(wavefunction * wavefunction), "blk")
    first_vector = wavefunction * lax.rsqrt(square_sum / entries + 1e-06)
    first_image, first_part = plain_apply(
        first_vector, arranged, bond_terms, term_slot, slot_block, diagonal
    )
    rayleigh = lax.psum(jnp.sum(first_part * first_image), ("blk", "mpo", "rep")) / entries
    residual = first_image - rayleigh * first_part
    resid_sum = lax.psum(jnp.sum(residual * residual), ("blk", "mpo", "rep"))
    second_vector = residual * lax.rsqrt(resid_sum / entries + 1e-06)
    second_full = lax.all_gather(second_vector, ("mpo", "rep"), axis=2, tiled=True)
    second_image, unused = plain_apply(
        second_full, arranged, bond_terms, term_slot, slot_block, diagonal
    )
    return (first_image, second_vector, second_image)


def split_two(x):
    high = x.astype(jnp.bfloat16)
    low = (x - high.astype(jnp.float32)).astype(jnp.bfloat16)
    return high, low


def lane_is_first(rows):
    return lax.broadcasted_iota(jnp.int32, (rows, LANES), 1) < LANES // 2


def micros(count):
    return pl.CostEstimate(flops=count * 1100000000, bytes_accessed=1 << 20, transcendentals=0)


def whole(*shape):
    return pl.BlockSpec(shape, lambda i, *_: (0,) * len(shape))


def pack_tile(x):
    return jnp.concatenate([x[:, :LANES], x[:, LANES:]], axis=0).T


def unpack_tile(x):
    upright = x.T
    return jnp.concatenate([upright[: LANES // 2], upright[LANES // 2 :]], axis=1)


def store_vector(parts, rows_of, put):
    first = lane_is_first(SUB)
    for pair in range(PHYS // 2):
        for part, row in zip(parts, rows_of):
            even = part[pl.ds(2 * pair, SUB, stride=PHYS), :]
            odd = part[pl.ds(2 * pair + 1, SUB, stride=PHYS), :]
            upper = jnp.where(first, even, pltpu.roll(odd, LANES // 2, 1))
            lower = jnp.where(first, pltpu.roll(even, LANES // 2, 1), odd)
            high, low = split_two(jnp.concatenate([upper, lower], axis=0))
            put(row, pair, high, low)


def pack_kernel(info_ref, wave_ref, own_wave_ref, diag_ref, vec_ref, own_ref, diag_out, tiles):
    half = LANES // 2
    for j in range(wave_ref.shape[0]):
        own_ref[j] = pack_tile(own_wave_ref[j])
        diag_out[j] = pack_tile(diag_ref[j])
        for q in range(4):
            tiles[q, j] = pack_tile(wave_ref[j, :, 2 * LANES * q : 2 * LANES * (q + 1)])

        def put(row, pair, high, low):
            columns = slice(pair * LANES, (pair + 1) * LANES)
            vec_ref[j, row : row + 16, columns] = high
            vec_ref[j, row + half : row + half + 16, columns] = low

        store_vector([tiles.at[q, j] for q in range(4)], [16 * q for q in range(4)], put)


def pack(info, wavefunction, diagonal):
    blocks, rows, width = wavefunction.shape
    step = 2
    tile = pl.BlockSpec((step, LANES, LANES), lambda i, *_: (i, 0, 0))
    return pl.pallas_call(
        pack_kernel,
        grid_spec=pltpu.PrefetchScalarGridSpec(
            num_scalar_prefetch=1,
            grid=(blocks // step,),
            in_specs=[
                pl.BlockSpec((step, rows, width), lambda i, *_: (i, 0, 0)),
                pl.BlockSpec((step, rows, width // 4), lambda i, info: (i, 0, info[0])),
                pl.BlockSpec((step, rows, width // 4), lambda i, *_: (i, 0, 0)),
            ],
            out_specs=[pl.BlockSpec((step, LANES, width), lambda i, *_: (i, 0, 0)), tile, tile],
            scratch_shapes=[pltpu.VMEM((4, step, LANES, LANES), jnp.float32)],
        ),
        out_shape=[
            jax.ShapeDtypeStruct((blocks, LANES, width), jnp.bfloat16),
            jax.ShapeDtypeStruct((blocks, LANES, LANES), jnp.float32),
            jax.ShapeDtypeStruct((blocks, LANES, LANES), jnp.float32),
        ],
        compiler_params=pltpu.CompilerParams(vmem_limit_bytes=SMALL_VMEM),
        cost_estimate=micros(5),
        name="pack",
    )(info, wavefunction, wavefunction, diagonal)


def mixing_kernel(sizes, *refs):
    sources, outs = refs[:2], refs[2:]
    spread = (
        lax.broadcasted_iota(jnp.int32, (PHYS, LANES), 1) // SUB
        == lax.broadcasted_iota(jnp.int32, (PHYS, LANES), 0)
    ).astype(jnp.bfloat16)
    row = lax.broadcasted_iota(jnp.int32, (LANES, LANES), 0) // PHYS
    column = lax.broadcasted_iota(jnp.int32, (LANES, LANES), 1) % SUB
    same = row == column
    for n, source in enumerate(sources):
        start = 0
        for group, size in enumerate(sizes):
            out_ref = outs[n * len(sizes) + group]
            for at in range(size):
                for place, term in enumerate(split_two(source[start + at].T)):
                    wide = jnp.dot(term, spread, preferred_element_type=jnp.float32)
                    tall = jnp.concatenate([wide] * SUB, axis=0)
                    tall = jnp.where(same, tall, 0.0).astype(jnp.bfloat16)
                    rows = slice(place * LANES, (place + 1) * LANES)
                    out_ref[at, rows] = jnp.concatenate([tall, tall], axis=1)
            start += size


def mixing_operands(sources, sizes):
    out = pl.pallas_call(
        functools.partial(mixing_kernel, sizes),
        out_shape=[
            jax.ShapeDtypeStruct((size, 2 * LANES, 2 * LANES), jnp.bfloat16)
            for _ in sources
            for size in sizes
        ],
        compiler_params=pltpu.CompilerParams(vmem_limit_bytes=SMALL_VMEM),
        cost_estimate=micros(2),
        name="mixing",
    )(*sources)
    return [out[: len(sizes)], out[len(sizes) :]]


def own_operands_kernel(info_ref, *refs):
    pieces, (left_high, left_low, right_out, send, blocks_ref, upright_ref) = refs[:4], refs[4:]
    per, blocks, half, lanes = left_high.shape
    rows = half // 4
    wide = half // 2
    first = lane_is_first(half)
    first_wide = lane_is_first(wide)
    first_rows = lane_is_first(rows)
    mine_at = pl.multiple_of(half + info_ref[6] * wide, wide)
    theirs_at = pl.multiple_of(lanes - wide - info_ref[6] * wide, wide)
    for j in range(blocks):
        for w in range(per):
            for z in range(4):
                row = pl.multiple_of((info_ref[4] ^ z) * rows, rows)
                blocks_ref[w, j, pl.ds(row, rows), :] = pieces[z][w, j]
        for w in range(per):
            block = blocks_ref[w, j]
            upright_ref[w, j] = jnp.concatenate([block, block], axis=0).T
            turned = pltpu.roll(block, half, 1)
            high, low = split_two(jnp.where(first, block, turned))
            left_high[w, j] = high
            left_low[w, j] = low
            send[w, j, 0:wide] = jnp.where(first_wide, block[:wide], turned[wide:])
        for w in range(per):
            high, low = split_two(upright_ref[w, j, pl.ds(mine_at, wide), :])
            right_out[j, wide * w : wide * (w + 1), 0:lanes] = high
            right_out[j, wide * w : wide * (w + 1), lanes:] = low
            upper = upright_ref[w, j, pl.ds(theirs_at, rows), :]
            lower = upright_ref[w, j, pl.ds(theirs_at + rows, rows), :]
            send[w, j, wide : wide + rows] = jnp.where(first_rows, upper, lower)


def other_operands(sent, left_high, left_low, right_out, j):
    per, blocks, half, lanes = left_high.shape
    rows = half // 4
    wide = half // 2
    first = lane_is_first(wide)
    first_rows = lane_is_first(rows)
    for w in range(per):
        both = sent[w, j, 0:wide]
        turned = pltpu.roll(both, half, 1)
        full = jnp.concatenate(
            [jnp.where(first, both, turned), jnp.where(first, turned, both)], axis=0
        )
        high, low = split_two(full)
        left_high[w, j] = high
        left_low[w, j] = low
        both = sent[w, j, wide : wide + rows]
        turned = pltpu.roll(both, half, 1)
        full = jnp.concatenate(
            [jnp.where(first_rows, both, turned), jnp.where(first_rows, turned, both)], axis=0
        )
        high, low = split_two(full)
        right_out[j, wide * w : wide * (w + 1), 0:lanes] = high
        right_out[j, wide * w : wide * (w + 1), lanes:] = low


def operand_specs(per, step, half, lanes, at=0):
    return [
        pl.BlockSpec((per, step, half, lanes), lambda i, *_: (0, at + i, 0, 0)),
        pl.BlockSpec((per, step, half, lanes), lambda i, *_: (0, at + i, 0, 0)),
        pl.BlockSpec((step, per * 32, 2 * lanes), lambda i, *_: (at + i, 0, 0)),
    ]


def operand_shapes(per, blocks, half, lanes):
    return [
        jax.ShapeDtypeStruct((per, blocks, half, lanes), jnp.bfloat16),
        jax.ShapeDtypeStruct((per, blocks, half, lanes), jnp.bfloat16),
        jax.ShapeDtypeStruct((blocks, per * 32, 2 * lanes), jnp.bfloat16),
    ]


def cut_kernel(first, info_ref, source, *refs):
    outs, sems = refs[:4], refs[4]
    per = outs[0].shape[0]
    copies = []
    for k in range(4):
        part = source.at[pl.ds(first, per), info_ref[4] ^ k]
        copies.append(pltpu.make_async_copy(part, outs[k], sems.at[k]))
    for copy in copies:
        copy.start()
    for copy in copies:
        copy.wait()


def cut_pieces(info, by_owner, first, per):
    shape = jax.ShapeDtypeStruct((per,) + by_owner.shape[2:], jnp.float32)
    return pl.pallas_call(
        functools.partial(cut_kernel, first),
        grid_spec=pltpu.PrefetchScalarGridSpec(
            num_scalar_prefetch=1,
            grid=(1,),
            in_specs=[pl.BlockSpec(memory_space=pl.ANY)],
            out_specs=[pl.BlockSpec(memory_space=pl.ANY)] * 4,
            scratch_shapes=[pltpu.SemaphoreType.DMA((4,))],
        ),
        out_shape=[shape] * 4,
        compiler_params=pltpu.CompilerParams(vmem_limit_bytes=SMALL_VMEM),
        cost_estimate=micros(1),
        name="cut_pieces",
    )(info, *(in_hbm(by_owner) if first == 0 else [by_owner]))


def own_operands(info, pieces):
    per, blocks, rows, lanes = pieces[0].shape
    half = lanes // 2
    step = 4
    return pl.pallas_call(
        own_operands_kernel,
        grid_spec=pltpu.PrefetchScalarGridSpec(
            num_scalar_prefetch=1,
            grid=(blocks // step,),
            in_specs=[pl.BlockSpec((per, step, rows, lanes), lambda i, *_: (0, i, 0, 0))] * 4,
            out_specs=operand_specs(per, step, half, lanes)
            + [pl.BlockSpec((per, step, 3 * rows, lanes), lambda i, *_: (0, i, 0, 0))],
            scratch_shapes=[
                pltpu.VMEM((per, step, half, lanes), jnp.float32),
                pltpu.VMEM((per, step, lanes, lanes), jnp.float32),
            ],
        ),
        out_shape=operand_shapes(per, blocks, half, lanes)
        + [jax.ShapeDtypeStruct((per, blocks, 3 * rows, lanes), jnp.float32)],
        compiler_params=pltpu.CompilerParams(vmem_limit_bytes=SMALL_VMEM),
        cost_estimate=micros(12),
        name="own_operands",
    )(info, *pieces)


def apply_kernel(plan, info_ref, *refs):
    chunks, first_block, parts_given, sent_given, before_given, pieces = plan
    refs = list(refs)
    take = lambda n: [refs.pop(0) for _ in range(n)]
    slots = take(2)
    vector = take(4 if parts_given else 1)
    tiles = take(4) if parts_given and pieces else []
    operands = [take(3) for _ in chunks[: -1 if sent_given else None]]
    sent = take(1)[0] if sent_given else None
    mixes = take(len(chunks))
    before = take(1)[0] if before_given else None
    outs = take(2 if pieces else 1)
    if sent_given:
        operands.append(take(3))
    total_ref, vec, mid = take(3)
    if before_given:
        prior, arrival = take(2)
    step = mid.shape[0]
    lanes, half = LANES, LANES // 2
    first = lane_is_first(SUB)
    first_half = lane_is_first(half)
    keep_first = jnp.where(first_half, 1.0, 0.0).astype(jnp.bfloat16)
    keep_second = jnp.where(first_half, 0.0, 1.0).astype(jnp.bfloat16)
    me = info_ref[4]

    @pl.when(pl.program_id(0) == 0)
    def _():
        if before_given:
            pltpu.make_async_copy(before, prior, arrival).start()
        total_ref[...] = jnp.zeros_like(total_ref)

    def right_side(j):
        if sent_given:
            other_operands(sent, *operands[-1], j)
        if parts_given:

            def put(row, pair, high, low):
                columns = slice(pair * lanes, (pair + 1) * lanes)
                vec[j, pl.ds(row, 16), columns] = high
                vec[j, pl.ds(row + half, 16), columns] = low

            rows_of = [pl.multiple_of(info_ref[g] * 16, 16) for g in range(4)]
            store_vector([x.at[pl.ds(j * lanes, lanes)] for x in vector], rows_of, put)
            source = vec[j]
        else:
            source = vector[0][j]
        source = jnp.concatenate([source, source], axis=0)
        at = 0
        for left_high, left_low, right in operands:
            count = right.shape[1]
            mid[j, at : at + count, :] = jnp.dot(
                right[j], source, preferred_element_type=jnp.float32
            )
            at += count

    def prepared(j, refs_of, w, row_of):
        left_high, left_low, right = refs_of
        tiles = []
        for part in range(2):
            row = row_of + part * 16
            for pair in range(PHYS // 2):
                columns = slice(pair * lanes, (pair + 1) * lanes)
                upper = mid[j, row : row + SUB, columns]
                lower = mid[j, row + SUB : row + 2 * SUB, columns]
                tiles.append(jnp.where(first, upper, pltpu.roll(lower, half, 1)))
                tiles.append(jnp.where(first, pltpu.roll(upper, half, 1), lower))
        t_high, t_low = split_two(jnp.concatenate(tiles, axis=0))
        lh, ll = left_high[w, j], left_low[w, j]
        wide_high = jnp.concatenate([lh * keep_first, lh * keep_second], axis=0)
        wide_low = jnp.concatenate([ll * keep_first, ll * keep_second], axis=0)
        weights = jnp.concatenate([wide_high, wide_low], axis=1)
        weights = jnp.concatenate([weights, weights], axis=0)
        return jnp.concatenate([t_high, t_low], axis=1), weights

    def mix_unit(mixing, w, z):
        z_high, z_low = [jnp.concatenate([x[:lanes], x[lanes:]], axis=1) for x in z]
        return jnp.dot(
            mixing[w],
            jnp.concatenate([z_high, z_low], axis=0),
            preferred_element_type=jnp.float32,
        )

    def add_up(j, table, bond, mixed):
        slot = table[bond, first_block + pl.program_id(0) * step + j]
        slot = ((slot >> 1) ^ me) * 2 + (slot & 1)
        for part in range(2):
            columns = slice(part * lanes, (part + 1) * lanes)
            total_ref[part, slot] += mixed[:lanes, columns] + mixed[lanes:, columns]

    bonds = []
    for (source, start), refs_of, mix in zip(chunks, operands, mixes):
        for w in range(mix.shape[0]):
            bonds.append((refs_of, mix, w, slots[source], start + w))
    right_side(0)
    units = [(j, at) for j in range(step) for at in range(len(bonds))]

    def prepare_unit(n):
        j, at = units[n]
        refs_of, mixing, w, table, bond = bonds[at]
        return prepared(j, refs_of, w, at * 32)

    ready = prepare_unit(0)
    waiting = None
    for n, (j, at) in enumerate(units):
        refs_of, mixing, w, table, bond = bonds[at]
        z = jnp.dot(*ready, preferred_element_type=jnp.float32)
        if j + 1 < step and at == len(bonds) // 3:
            right_side(j + 1)
        if n + 1 < len(units):
            ready = prepare_unit(n + 1)
        if waiting is not None:
            before_j, before_mixing, before_w, before_table, before_bond, before_z = waiting
            mixed = mix_unit(before_mixing, before_w, before_z)
        z = split_two(z[:, :lanes] + z[:, lanes:])
        if waiting is not None:
            add_up(before_j, before_table, before_bond, mixed)
        waiting = (j, mixing, w, table, bond, z)
    j, mixing, w, table, bond, z = waiting
    add_up(j, table, bond, mix_unit(mixing, w, z))

    @pl.when(pl.program_id(0) == pl.num_programs(0) - 1)
    def _():
        if before_given:
            pltpu.make_async_copy(before, prior, arrival).wait()
            total_ref[...] += prior[...]
        if pieces:
            stats = jnp.zeros((SUB, lanes), jnp.float32)
            if tiles:
                stats = stacked_rows(*merged([tile[...] for tile in tiles]))
            for out, part in ((outs[0], info_ref[5]), (outs[1], 1 - info_ref[5])):
                for k in range(4):
                    for i in range(2):
                        out[k, i * lanes : (i + 1) * lanes] = total_ref[part, 2 * k + i]
                    out[k, 2 * lanes :] = stats
                stats = jnp.zeros((SUB, lanes), jnp.float32)
        else:
            outs[0][...] = total_ref[...]


def apply_bonds(info, slots, vector, chunks, operands, sent, mixes, before, pieces, half_of=None):
    blocks, half, lanes = operands[0][0].shape[1:]
    step = 4
    parts_given = half_of is not None
    at = half_of or 0
    if parts_given:
        in_specs = [whole(step * lanes, lanes)] * 4
        arguments = list(vector)
        if pieces:
            last = vector[0].shape[0] // SUB - 1
            in_specs += [pl.BlockSpec((SUB, lanes), lambda i, *_: (last, 0))] * 4
            arguments += list(vector)
    else:
        in_specs = [pl.BlockSpec((step,) + vector.shape[1:], lambda i, *_: (i, 0, 0))]
        arguments = [vector]
    for made in operands:
        in_specs += operand_specs(made[0].shape[0], step, half, lanes, at)
        arguments += made
    counts = [mix.shape[0] for mix in mixes]
    if sent is not None:
        in_specs.append(
            pl.BlockSpec((counts[-1], step) + sent.shape[2:], lambda i, *_: (0, i, 0, 0))
        )
        arguments.append(sent)
    for mix in mixes:
        in_specs.append(whole(*mix.shape))
        arguments.append(mix)
    scratch = [
        pltpu.VMEM((2, 8, lanes, lanes), jnp.float32),
        pltpu.VMEM((step, lanes, PHYS * half), jnp.bfloat16),
        pltpu.VMEM((step, sum(counts) * 32, PHYS * half), jnp.float32),
    ]
    if before is not None:
        in_specs.append(pl.BlockSpec(memory_space=pl.ANY))
        arguments.append(before)
        scratch += [pltpu.VMEM(before.shape, jnp.float32), pltpu.SemaphoreType.DMA]
    shapes = [(4, 2 * lanes + SUB, lanes)] * 2 if pieces else [(2, 8, lanes, lanes)]
    out_specs = [whole(*shape) for shape in shapes]
    out_shape = [jax.ShapeDtypeStruct(shape, jnp.float32) for shape in shapes]
    if sent is not None:
        out_specs += operand_specs(counts[-1], step, half, lanes)
        out_shape += operand_shapes(counts[-1], blocks, half, lanes)
    plan = (
        tuple(chunks), at * step, parts_given, sent is not None, before is not None, pieces,
    )
    out = pl.pallas_call(
        functools.partial(apply_kernel, plan),
        grid_spec=pltpu.PrefetchScalarGridSpec(
            num_scalar_prefetch=3,
            grid=(1 if parts_given else blocks // step,),
            in_specs=in_specs,
            out_specs=out_specs,
            scratch_shapes=scratch,
        ),
        out_shape=out_shape,
        compiler_params=pltpu.CompilerParams(vmem_limit_bytes=APPLY_VMEM),
        cost_estimate=micros(10 if parts_given else 1),
        name="apply_bonds",
    )(info, *slots, *arguments)
    return out[: len(shapes)], out[len(shapes) :]


def add_arrived(info_ref, owner_ref, arrived, total):
    for k in range(4):
        for i in range(2):
            rows = slice(i * LANES, (i + 1) * LANES)
            total[owner_ref[info_ref[4] ^ k, i]] += arrived[k][rows]


def stacked_rows(*rows):
    at = lax.broadcasted_iota(jnp.int32, (SUB, LANES), 0)
    tile = jnp.zeros((SUB, LANES), jnp.float32)
    for i, row in enumerate(rows):
        tile = jnp.where(at == i, row, tile)
    return tile


def merged(tiles):
    rows = [[tile[i : i + 1] for i in range(3)] for tile in tiles]
    cross = sum(row[0] for row in rows)
    square = sum(row[1] for row in rows)
    ratio = cross / jnp.maximum(square, TINY)
    apart = [
        (row[0] / jnp.maximum(row[1], TINY) - ratio) * jnp.sqrt(row[1]) for row in rows
    ]
    rest = sum(row[2] for row in rows) + sum(x * x for x in apart)
    return cross, square, rest


def image_kernel(
    info_ref, owner_ref, a0, a1, a2, a3, diag_ref, own_ref, lower_ref, upper_ref, total
):
    total[...] = diag_ref[...] * own_ref[...]
    add_arrived(info_ref, owner_ref, (a0, a1, a2, a3), total)
    blocks = total.shape[0]
    cross = jnp.zeros((LANES, LANES), jnp.float32)
    square = jnp.zeros((LANES, LANES), jnp.float32)
    for k in range(blocks):
        own, image = own_ref[k], total[k]
        half = lower_ref if k < blocks // 2 else upper_ref
        at = k % (blocks // 2) * LANES
        half[at : at + LANES] = image
        cross += own * image
        square += own * own
    cross = jnp.sum(cross, keepdims=True)
    square = jnp.sum(square, keepdims=True)
    ratio = cross / jnp.maximum(square, TINY)
    rest = jnp.zeros((LANES, LANES), jnp.float32)
    for k in range(blocks):
        apart = total[k] - ratio * own_ref[k]
        rest += apart * apart
    upper_ref[blocks // 2 * LANES :] = stacked_rows(cross, square, jnp.sum(rest, keepdims=True))


def owner_image(info, owners, arrived, diagonal, own):
    rows = own.shape[0] // 2 * LANES
    shapes = [jax.ShapeDtypeStruct((n, LANES), jnp.float32) for n in (rows, rows + SUB)]
    return pl.pallas_call(
        image_kernel,
        grid_spec=pltpu.PrefetchScalarGridSpec(
            num_scalar_prefetch=2,
            grid=(1,),
            in_specs=[whole(*x.shape) for x in (*arrived, diagonal, own)],
            out_specs=[whole(*x.shape) for x in shapes],
            scratch_shapes=[pltpu.VMEM(own.shape, jnp.float32)],
        ),
        out_shape=shapes,
        compiler_params=pltpu.CompilerParams(vmem_limit_bytes=SMALL_VMEM),
        cost_estimate=micros(3),
        name="owner_image",
    )(info, owners, *in_hbm(arrived[0]), *arrived[1:], *in_hbm(diagonal, own))


def final_kernel(
    entries, info_ref, owner_ref, a0, a1, a2, a3, diag_ref, own_ref, lower_ref, upper_ref,
    first_ref, vector_ref, second_ref, total,
):
    arrived = (a0, a1, a2, a3)
    cross, square, rest = merged([ref[2 * LANES :] for ref in arrived])
    scale = lax.rsqrt(square / entries + 1e-06)
    rayleigh = scale * scale * (cross / entries)
    apart = (cross / jnp.maximum(square, TINY) - rayleigh) * jnp.sqrt(square)
    mean = scale * scale * ((rest + apart * apart) / entries)
    second_scale = scale * lax.rsqrt(mean + 1e-06)
    for k in range(total.shape[0]):
        at = k % (total.shape[0] // 2) * LANES
        image = (lower_ref if k < total.shape[0] // 2 else upper_ref)[at : at + LANES]
        total[k] = (diag_ref[k] - rayleigh) * image
        first_ref[k] = unpack_tile(scale * image)
        vector_ref[k] = unpack_tile(second_scale * (image - rayleigh * own_ref[k]))
    add_arrived(info_ref, owner_ref, arrived, total)
    for k in range(total.shape[0]):
        second_ref[k] = unpack_tile(second_scale * total[k])


def outputs(info, owners, arrived, diagonal, own, images, entries):
    blocks = diagonal.shape[0]
    shape = (blocks, LANES // 2, 2 * LANES)
    return pl.pallas_call(
        functools.partial(final_kernel, entries),
        grid_spec=pltpu.PrefetchScalarGridSpec(
            num_scalar_prefetch=2,
            grid=(1,),
            in_specs=[whole(*x.shape) for x in (*arrived, diagonal, own)]
            + [whole(blocks // 2 * LANES, LANES)] * 2,
            out_specs=[whole(*shape)] * 3,
            scratch_shapes=[pltpu.VMEM(diagonal.shape, jnp.float32)],
        ),
        out_shape=[jax.ShapeDtypeStruct(shape, jnp.float32)] * 3,
        compiler_params=pltpu.CompilerParams(vmem_limit_bytes=SMALL_VMEM),
        cost_estimate=micros(4),
        name="outputs",
    )(info, owners, *arrived, diagonal, own, *images)


def in_hbm(*arrays):
    return [pltpu.with_memory_space_constraint(x, pltpu.HBM) for x in arrays]


def partner(x, axis, k):
    size = lax.axis_size(axis)
    return lax.ppermute(x, axis, [(i, i ^ k) for i in range(size)])


def after(x, *others):
    return lax.optimization_barrier((x, *others))[0]


def gathered(x):
    across = partner(x, "mpo", 1)
    return [x, across, partner(x, "rep", 1), partner(across, "rep", 1)]


def everyone_of(pieces, axis):
    return [pieces[0]] + [partner(pieces[k], axis, k) for k in range(1, 4)]


def to_owners(mine, theirs):
    other = partner(theirs, "rep", 1)
    pieces = [mine[k] + other[k] for k in range(4)]
    return everyone_of(pieces, "blk")


def per_device(wavefunction, environment, bond_terms, diagonal, term_slot, slot_block):
    blocks, rows, width = wavefunction.shape
    zs = lax.axis_size("blk")
    mpo, rep, blk = lax.axis_index("mpo"), lax.axis_index("rep"), lax.axis_index("blk")
    place = 2 * mpo + rep
    info = jnp.stack([place, place ^ 2, place ^ 1, place ^ 3, blk, rep, mpo]).astype(jnp.int32)
    bonds = environment.shape[0]
    sizes = tuple(bonds * part // 6 for part in (2, 2, 1, 1))
    firsts = tuple(sum(sizes[:group]) for group in range(len(sizes)))
    entries = float(blocks * zs * rows * width)

    vector, own, diagonal_packed = pack(info, wavefunction, diagonal)

    by_owner = environment.reshape(bonds, zs, blocks, rows // zs, 2 * rows)
    pieces = []
    for group in range(len(sizes)):
        cuts = list(cut_pieces(info, by_owner, firsts[group], sizes[group]))
        if group:
            cuts[1:] = [after(x, y) for x, y in zip(cuts[1:], pieces[-1][1:])]
        pieces.append(cuts[:1] + [partner(cuts[k], "blk", k) for k in range(1, 4)])
    pieces[0][1] = after(pieces[0][1], vector)
    other_terms = partner(after(bond_terms, pieces[0][1]), "mpo", 1)
    mixing = mixing_operands([bond_terms, other_terms], sizes)
    slots = [term_slot, partner(after(term_slot, pieces[0][1]), "mpo", 1)]

    made, sent = [], []
    total = None
    operands = []
    done = 0

    def apply_group(group, vector):
        out, other = apply_bonds(
            info, slots, vector, [(0, firsts[group]), (1, firsts[group])], [made[group]],
            partner(sent[group], "mpo", 1), [terms[group] for terms in mixing], total,
            group == len(sizes) - 1,
        )
        operands.extend([made[group], other])
        return out

    for group in range(len(sizes)):
        if group >= 2:
            total = apply_group(group - 2, after(vector, sent[group - 1]))[0]
            pieces[group][3] = after(pieces[group][3], total)
        if group + 1 < len(sizes):
            pieces[group][1] = after(pieces[group][1], pieces[group + 1][1])
        *own_set, send = own_operands(info, pieces[group])
        made.append(own_set)
        sent.append(send)
    total = apply_group(len(sizes) - 2, after(vector, sent[-1]))[0]
    out = apply_group(len(sizes) - 1, vector)
    lower, upper = owner_image(info, slot_block, to_owners(*out), diagonal_packed, own)

    chunks = [(source, first) for first in firsts for source in range(2)]
    mixes = [mixing[source][group] for group in range(len(sizes)) for source in range(2)]
    lower_parts = gathered(lower)
    across = partner(after(upper, lower_parts[1]), "mpo", 1)
    out, _ = apply_bonds(
        info, slots, lower_parts, chunks, operands, None, mixes, None, False, 0
    )
    upper_parts = [upper, across, partner(upper, "rep", 1)]
    upper_parts.append(partner(after(across, out[0]), "rep", 1))
    out, _ = apply_bonds(
        info, slots, upper_parts, chunks, operands, None, mixes, out[0], True, 1
    )
    return tuple(
        outputs(
            info, slot_block, to_owners(*out), diagonal_packed, own, (lower, upper), entries
        )
    )


def solution(mesh):
    packed = mesh.shape["mpo"] == 2 and mesh.shape["rep"] == 2 and mesh.shape["blk"] == 4
    return jax.shard_map(
        per_device if packed else plain_device,
        mesh=mesh,
        in_specs=(
            P(("grp", "blk"), None, None),
            P(("grp", "mpo", "rep"), None, "blk", None),
            P(("grp", "mpo", "rep"), None, None),
            P(("grp", "blk"), None, ("mpo", "rep")),
            P(("grp", "mpo", "rep"), "blk"),
            P("grp", "blk"),
        ),
        out_specs=(
            P(("grp", "blk"), None, ("mpo", "rep")),
            P(("grp", "blk"), None, ("mpo", "rep")),
            P(("grp", "blk"), None, ("mpo", "rep")),
        ),
        check_vma=False,
    )
```

```python
import functools

import jax
import jax.numpy as jnp
from jax import lax
from jax.experimental import pallas as pl
from jax.experimental.pallas import tpu as pltpu
from jax.sharding import PartitionSpec as P

LANES = 128
SUB = 8
PHYS = 16
TINY = 1e-30
SMALL_VMEM = 16 * 1024 * 1024
APPLY_VMEM = 16 * 1024 * 1024


def plain_apply(vector_full, environment, bond_terms, term_slot, slot_block, diagonal):
    block_count, block_rows, block_width = vector_full.shape
    phys_size = bond_terms.shape[-1]
    right_rows = block_width // phys_size
    slot_count = slot_block.shape[0] * slot_block.shape[1]
    blocks = vector_full.reshape(block_count, block_rows, right_rows, phys_size)
    ordered = jnp.transpose(blocks, (0, 3, 1, 2))
    left_env = environment[:, :, :, :block_rows]
    right_env = environment[:, :, :, block_rows:]
    left_done = jnp.einsum("wjab,jsac->wjsbc", left_env, ordered, precision=lax.Precision.HIGHEST)
    right_done = jnp.einsum(
        "wjsbc,wjcd->wjsbd", left_done, right_env, precision=lax.Precision.HIGHEST
    )
    right_done = right_done.reshape(
        environment.shape[0], block_count, phys_size, block_rows * right_rows
    )
    bond_term = jnp.einsum(
        "wjsx,wst->wjtx", right_done, bond_terms, precision=lax.Precision.HIGHEST
    )
    bond_term = bond_term.reshape(environment.shape[0], block_count, block_rows * block_width)
    slot_table = (
        term_slot[:, None, :] == jnp.arange(slot_count, dtype=jnp.int32)[None, :, None]
    ).astype(jnp.float32)
    slot_buffer = jnp.einsum("wsj,wjx->sx", slot_table, bond_term, precision=lax.Precision.HIGHEST)
    slot_buffer = slot_buffer.reshape(slot_count, phys_size, block_rows, right_rows)
    slot_buffer = jnp.transpose(slot_buffer, (0, 2, 3, 1)).reshape(
        slot_count, block_rows, block_width
    )
    owners = slot_block.reshape(-1)
    selector = (owners[None, :] == jnp.arange(block_count, dtype=jnp.int32)[:, None]).astype(
        jnp.float32
    )
    column_width = block_width // lax.axis_size(("mpo", "rep"))
    column_start = lax.axis_index(("mpo", "rep")) * column_width
    own_part = lax.dynamic_slice_in_dim(vector_full, column_start, column_width, 2)
    shares = lax.psum_scatter(slot_buffer, ("mpo", "rep"), scatter_dimension=2, tiled=True)
    arrived = lax.all_to_all(shares, "blk", split_axis=0, concat_axis=0, tiled=True)
    result = jnp.einsum("ks,sbc->kbc", selector, arrived, precision=lax.Precision.HIGHEST)
    return (result + diagonal * own_part, own_part)


def plain_device(wavefunction, environment, bond_terms, diagonal, term_slot, slot_block):
    arranged = lax.all_to_all(environment, "blk", split_axis=1, concat_axis=2, tiled=True)
    entries = float(
        wavefunction.shape[0] * lax.axis_size("blk") * wavefunction.shape[1] * wavefunction.shape[2]
    )
    square_sum = lax.psum(jnp.sum(wavefunction * wavefunction), "blk")
    first_vector = wavefunction * lax.rsqrt(square_sum / entries + 1e-06)
    first_image, first_part = plain_apply(
        first_vector, arranged, bond_terms, term_slot, slot_block, diagonal
    )
    rayleigh = lax.psum(jnp.sum(first_part * first_image), ("blk", "mpo", "rep")) / entries
    residual = first_image - rayleigh * first_part
    resid_sum = lax.psum(jnp.sum(residual * residual), ("blk", "mpo", "rep"))
    second_vector = residual * lax.rsqrt(resid_sum / entries + 1e-06)
    second_full = lax.all_gather(second_vector, ("mpo", "rep"), axis=2, tiled=True)
    second_image, unused = plain_apply(
        second_full, arranged, bond_terms, term_slot, slot_block, diagonal
    )
    return (first_image, second_vector, second_image)


def split_two(x):
    high = x.astype(jnp.bfloat16)
    low = (x - high.astype(jnp.float32)).astype(jnp.bfloat16)
    return high, low


def lane_is_first(rows):
    return lax.broadcasted_iota(jnp.int32, (rows, LANES), 1) < LANES // 2


def micros(count):
    return pl.CostEstimate(flops=count * 1100000000, bytes_accessed=1 << 20, transcendentals=0)


def whole(*shape):
    return pl.BlockSpec(shape, lambda i, *_: (0,) * len(shape))


def pack_tile(x):
    return jnp.concatenate([x[:, :LANES], x[:, LANES:]], axis=0).T


def unpack_tile(x):
    upright = x.T
    return jnp.concatenate([upright[: LANES // 2], upright[LANES // 2 :]], axis=1)


def store_vector(parts, rows_of, put):
    first = lane_is_first(SUB)
    for pair in range(PHYS // 2):
        for part, row in zip(parts, rows_of):
            even = part[pl.ds(2 * pair, SUB, stride=PHYS), :]
            odd = part[pl.ds(2 * pair + 1, SUB, stride=PHYS), :]
            upper = jnp.where(first, even, pltpu.roll(odd, LANES // 2, 1))
            lower = jnp.where(first, pltpu.roll(even, LANES // 2, 1), odd)
            high, low = split_two(jnp.concatenate([upper, lower], axis=0))
            put(row, pair, high, low)


def pack_kernel(info_ref, wave_ref, own_wave_ref, diag_ref, vec_ref, own_ref, diag_out, tiles):
    half = LANES // 2
    for j in range(wave_ref.shape[0]):
        own_ref[j] = pack_tile(own_wave_ref[j])
        diag_out[j] = pack_tile(diag_ref[j])
        for q in range(4):
            tiles[q, j] = pack_tile(wave_ref[j, :, 2 * LANES * q : 2 * LANES * (q + 1)])

        def put(row, pair, high, low):
            columns = slice(pair * LANES, (pair + 1) * LANES)
            vec_ref[j, row : row + 16, columns] = high
            vec_ref[j, row + half : row + half + 16, columns] = low

        store_vector([tiles.at[q, j] for q in range(4)], [16 * q for q in range(4)], put)


def pack(info, wavefunction, diagonal):
    blocks, rows, width = wavefunction.shape
    step = 2
    tile = pl.BlockSpec((step, LANES, LANES), lambda i, *_: (i, 0, 0))
    return pl.pallas_call(
        pack_kernel,
        grid_spec=pltpu.PrefetchScalarGridSpec(
            num_scalar_prefetch=1,
            grid=(blocks // step,),
            in_specs=[
                pl.BlockSpec((step, rows, width), lambda i, *_: (i, 0, 0)),
                pl.BlockSpec((step, rows, width // 4), lambda i, info: (i, 0, info[0])),
                pl.BlockSpec((step, rows, width // 4), lambda i, *_: (i, 0, 0)),
            ],
            out_specs=[pl.BlockSpec((step, LANES, width), lambda i, *_: (i, 0, 0)), tile, tile],
            scratch_shapes=[pltpu.VMEM((4, step, LANES, LANES), jnp.float32)],
        ),
        out_shape=[
            jax.ShapeDtypeStruct((blocks, LANES, width), jnp.bfloat16),
            jax.ShapeDtypeStruct((blocks, LANES, LANES), jnp.float32),
            jax.ShapeDtypeStruct((blocks, LANES, LANES), jnp.float32),
        ],
        compiler_params=pltpu.CompilerParams(vmem_limit_bytes=SMALL_VMEM),
        cost_estimate=micros(5),
        name="pack",
    )(info, wavefunction, wavefunction, diagonal)


def mixing_kernel(sizes, *refs):
    sources, outs = refs[:2], refs[2:]
    spread = (
        lax.broadcasted_iota(jnp.int32, (PHYS, LANES), 1) // SUB
        == lax.broadcasted_iota(jnp.int32, (PHYS, LANES), 0)
    ).astype(jnp.bfloat16)
    row = lax.broadcasted_iota(jnp.int32, (LANES, LANES), 0) // PHYS
    column = lax.broadcasted_iota(jnp.int32, (LANES, LANES), 1) % SUB
    same = row == column
    for n, source in enumerate(sources):
        start = 0
        for group, size in enumerate(sizes):
            out_ref = outs[n * len(sizes) + group]
            for at in range(size):
                for place, term in enumerate(split_two(source[start + at].T)):
                    wide = jnp.dot(term, spread, preferred_element_type=jnp.float32)
                    tall = jnp.concatenate([wide] * SUB, axis=0)
                    tall = jnp.where(same, tall, 0.0).astype(jnp.bfloat16)
                    rows = slice(place * LANES, (place + 1) * LANES)
                    out_ref[at, rows] = jnp.concatenate([tall, tall], axis=1)
            start += size


def mixing_operands(sources, sizes):
    out = pl.pallas_call(
        functools.partial(mixing_kernel, sizes),
        out_shape=[
            jax.ShapeDtypeStruct((size, 2 * LANES, 2 * LANES), jnp.bfloat16)
            for _ in sources
            for size in sizes
        ],
        compiler_params=pltpu.CompilerParams(vmem_limit_bytes=SMALL_VMEM),
        cost_estimate=micros(2),
        name="mixing",
    )(*sources)
    return [out[: len(sizes)], out[len(sizes) :]]


def own_operands_kernel(info_ref, *refs):
    pieces, (left_high, left_low, right_out, send, blocks_ref, upright_ref) = refs[:4], refs[4:]
    per, blocks, half, lanes = left_high.shape
    rows = half // 4
    wide = half // 2
    first = lane_is_first(half)
    first_wide = lane_is_first(wide)
    first_rows = lane_is_first(rows)
    mine_at = pl.multiple_of(half + info_ref[6] * wide, wide)
    theirs_at = pl.multiple_of(lanes - wide - info_ref[6] * wide, wide)
    for j in range(blocks):
        for w in range(per):
            for z in range(4):
                row = pl.multiple_of((info_ref[4] ^ z) * rows, rows)
                blocks_ref[w, j, pl.ds(row, rows), :] = pieces[z][w, j]
        for w in range(per):
            block = blocks_ref[w, j]
            upright_ref[w, j] = jnp.concatenate([block, block], axis=0).T
            turned = pltpu.roll(block, half, 1)
            high, low = split_two(jnp.where(first, block, turned))
            left_high[w, j] = high
            left_low[w, j] = low
            send[w, j, 0:wide] = jnp.where(first_wide, block[:wide], turned[wide:])
        for w in range(per):
            high, low = split_two(upright_ref[w, j, pl.ds(mine_at, wide), :])
            right_out[j, wide * w : wide * (w + 1), 0:lanes] = high
            right_out[j, wide * w : wide * (w + 1), lanes:] = low
            upper = upright_ref[w, j, pl.ds(theirs_at, rows), :]
            lower = upright_ref[w, j, pl.ds(theirs_at + rows, rows), :]
            send[w, j, wide : wide + rows] = jnp.where(first_rows, upper, lower)


def other_operands(sent, left_high, left_low, right_out, j):
    per, blocks, half, lanes = left_high.shape
    rows = half // 4
    wide = half // 2
    first = lane_is_first(wide)
    first_rows = lane_is_first(rows)
    for w in range(per):
        both = sent[w, j, 0:wide]
        turned = pltpu.roll(both, half, 1)
        full = jnp.concatenate(
            [jnp.where(first, both, turned), jnp.where(first, turned, both)], axis=0
        )
        high, low = split_two(full)
        left_high[w, j] = high
        left_low[w, j] = low
        both = sent[w, j, wide : wide + rows]
        turned = pltpu.roll(both, half, 1)
        full = jnp.concatenate(
            [jnp.where(first_rows, both, turned), jnp.where(first_rows, turned, both)], axis=0
        )
        high, low = split_two(full)
        right_out[j, wide * w : wide * (w + 1), 0:lanes] = high
        right_out[j, wide * w : wide * (w + 1), lanes:] = low


def operand_specs(per, step, half, lanes, at=0):
    return [
        pl.BlockSpec((per, step, half, lanes), lambda i, *_: (0, at + i, 0, 0)),
        pl.BlockSpec((per, step, half, lanes), lambda i, *_: (0, at + i, 0, 0)),
        pl.BlockSpec((step, per * 32, 2 * lanes), lambda i, *_: (at + i, 0, 0)),
    ]


def operand_shapes(per, blocks, half, lanes):
    return [
        jax.ShapeDtypeStruct((per, blocks, half, lanes), jnp.bfloat16),
        jax.ShapeDtypeStruct((per, blocks, half, lanes), jnp.bfloat16),
        jax.ShapeDtypeStruct((blocks, per * 32, 2 * lanes), jnp.bfloat16),
    ]


def cut_kernel(first, info_ref, source, *refs):
    outs, sems = refs[:4], refs[4]
    per = outs[0].shape[0]
    copies = []
    for k in range(4):
        part = source.at[pl.ds(first, per), info_ref[4] ^ k]
        copies.append(pltpu.make_async_copy(part, outs[k], sems.at[k]))
    for copy in copies:
        copy.start()
    for copy in copies:
        copy.wait()


def cut_pieces(info, by_owner, first, per):
    shape = jax.ShapeDtypeStruct((per,) + by_owner.shape[2:], jnp.float32)
    return pl.pallas_call(
        functools.partial(cut_kernel, first),
        grid_spec=pltpu.PrefetchScalarGridSpec(
            num_scalar_prefetch=1,
            grid=(1,),
            in_specs=[pl.BlockSpec(memory_space=pl.ANY)],
            out_specs=[pl.BlockSpec(memory_space=pl.ANY)] * 4,
            scratch_shapes=[pltpu.SemaphoreType.DMA((4,))],
        ),
        out_shape=[shape] * 4,
        compiler_params=pltpu.CompilerParams(vmem_limit_bytes=SMALL_VMEM),
        cost_estimate=micros(1),
        name="cut_pieces",
    )(info, *(in_hbm(by_owner) if first == 0 else [by_owner]))


def own_operands(info, pieces):
    per, blocks, rows, lanes = pieces[0].shape
    half = lanes // 2
    step = 4
    return pl.pallas_call(
        own_operands_kernel,
        grid_spec=pltpu.PrefetchScalarGridSpec(
            num_scalar_prefetch=1,
            grid=(blocks // step,),
            in_specs=[pl.BlockSpec((per, step, rows, lanes), lambda i, *_: (0, i, 0, 0))] * 4,
            out_specs=operand_specs(per, step, half, lanes)
            + [pl.BlockSpec((per, step, 3 * rows, lanes), lambda i, *_: (0, i, 0, 0))],
            scratch_shapes=[
                pltpu.VMEM((per, step, half, lanes), jnp.float32),
                pltpu.VMEM((per, step, lanes, lanes), jnp.float32),
            ],
        ),
        out_shape=operand_shapes(per, blocks, half, lanes)
        + [jax.ShapeDtypeStruct((per, blocks, 3 * rows, lanes), jnp.float32)],
        compiler_params=pltpu.CompilerParams(vmem_limit_bytes=SMALL_VMEM),
        cost_estimate=micros(12),
        name="own_operands",
    )(info, *pieces)


def apply_kernel(plan, info_ref, *refs):
    chunks, first_block, parts_given, sent_given, before_given, pieces = plan
    refs = list(refs)
    take = lambda n: [refs.pop(0) for _ in range(n)]
    slots = take(2)
    vector = take(4 if parts_given else 1)
    operands = [take(3) for _ in chunks[: -1 if sent_given else None]]
    sent = take(1)[0] if sent_given else None
    mixes = take(len(chunks))
    before = take(1)[0] if before_given else None
    outs = take(2 if pieces else 1)
    if sent_given:
        operands.append(take(3))
    scratch = take(2)
    vec, mid = scratch
    total_ref = take(1)[0] if pieces else outs[0]
    step = mid.shape[0]
    lanes, half = LANES, LANES // 2
    first = lane_is_first(SUB)
    first_half = lane_is_first(half)
    keep_first = jnp.where(first_half, 1.0, 0.0).astype(jnp.bfloat16)
    keep_second = jnp.where(first_half, 0.0, 1.0).astype(jnp.bfloat16)
    me = info_ref[4]

    if not before_given:
        total_ref[...] = jnp.zeros_like(total_ref)
    else:
        total_ref[...] = before[...]

    def right_side(j):
        if sent_given:
            other_operands(sent, *operands[-1], first_block + j)
        if parts_given:

            def put(row, pair, high, low):
                columns = slice(pair * lanes, (pair + 1) * lanes)
                vec[j, pl.ds(row, 16), columns] = high
                vec[j, pl.ds(row + half, 16), columns] = low

            rows_of = [pl.multiple_of(info_ref[g] * 16, 16) for g in range(4)]
            store_vector([x.at[pl.ds(j * lanes, lanes)] for x in vector], rows_of, put)
            source = vec[j]
        else:
            source = vector[0][first_block + j]
        source = jnp.concatenate([source, source], axis=0)
        at = 0
        for left_high, left_low, right in operands:
            count = right.shape[1]
            mid[j, at : at + count, :] = jnp.dot(
                right[first_block + j], source, preferred_element_type=jnp.float32
            )
            at += count

    def prepared(j, refs_of, w, row_of):
        left_high, left_low, right = refs_of
        tiles = []
        for part in range(2):
            row = row_of + part * 16
            for pair in range(PHYS // 2):
                columns = slice(pair * lanes, (pair + 1) * lanes)
                upper = mid[j, row : row + SUB, columns]
                lower = mid[j, row + SUB : row + 2 * SUB, columns]
                tiles.append(jnp.where(first, upper, pltpu.roll(lower, half, 1)))
                tiles.append(jnp.where(first, pltpu.roll(upper, half, 1), lower))
        t_high, t_low = split_two(jnp.concatenate(tiles, axis=0))
        lh, ll = left_high[w, first_block + j], left_low[w, first_block + j]
        wide_high = jnp.concatenate([lh * keep_first, lh * keep_second], axis=0)
        wide_low = jnp.concatenate([ll * keep_first, ll * keep_second], axis=0)
        weights = jnp.concatenate([wide_high, wide_low], axis=1)
        weights = jnp.concatenate([weights, weights], axis=0)
        return jnp.concatenate([t_high, t_low], axis=1), weights

    def mix_unit(mixing, w, z):
        z_high, z_low = [jnp.concatenate([x[:lanes], x[lanes:]], axis=1) for x in z]
        return jnp.dot(
            mixing[w],
            jnp.concatenate([z_high, z_low], axis=0),
            preferred_element_type=jnp.float32,
        )

    def add_up(j, table, bond, mixed):
        slot = table[bond, first_block + j]
        slot = ((slot >> 1) ^ me) * 2 + (slot & 1)
        for part in range(2):
            columns = slice(part * lanes, (part + 1) * lanes)
            total_ref[part, slot] += mixed[:lanes, columns] + mixed[lanes:, columns]

    bonds = []
    for (source, start), refs_of, mix in zip(chunks, operands, mixes):
        for w in range(mix.shape[0]):
            bonds.append((refs_of, mix, w, slots[source], start + w))
    right_side(0)
    units = [(j, at) for j in range(step) for at in range(len(bonds))]

    def prepare_unit(n):
        j, at = units[n]
        refs_of, mixing, w, table, bond = bonds[at]
        return prepared(j, refs_of, w, at * 32)

    ready = prepare_unit(0)
    waiting = None
    for n, (j, at) in enumerate(units):
        refs_of, mixing, w, table, bond = bonds[at]
        z = jnp.dot(*ready, preferred_element_type=jnp.float32)
        if j + 1 < step and at == len(bonds) // 3:
            right_side(j + 1)
        if n + 1 < len(units):
            ready = prepare_unit(n + 1)
        if waiting is not None:
            before_j, before_mixing, before_w, before_table, before_bond, before_z = waiting
            mixed = mix_unit(before_mixing, before_w, before_z)
        z = split_two(z[:, :lanes] + z[:, lanes:])
        if waiting is not None:
            add_up(before_j, before_table, before_bond, mixed)
        waiting = (j, mixing, w, table, bond, z)
    j, mixing, w, table, bond, z = waiting
    add_up(j, table, bond, mix_unit(mixing, w, z))

    if pieces:
        stats = jnp.zeros((SUB, lanes), jnp.float32)
        if parts_given:
            tail = vector[0].shape[0] - SUB
            stats = stacked_rows(*merged([x[tail:] for x in vector]))
        for out, part in ((outs[0], info_ref[5]), (outs[1], 1 - info_ref[5])):
            for k in range(4):
                for i in range(2):
                    out[k, i * lanes : (i + 1) * lanes] = total_ref[part, 2 * k + i]
                out[k, 2 * lanes :] = stats
            stats = jnp.zeros((SUB, lanes), jnp.float32)


def apply_bonds(info, slots, vector, chunks, operands, sent, mixes, before, pieces, half_of=None):
    blocks, half, lanes = operands[0][0].shape[1:]
    parts_given = half_of is not None
    step = 4 if parts_given else blocks
    arguments = list(vector) if parts_given else [vector]
    for made in operands:
        arguments += made
    if sent is not None:
        arguments.append(sent)
    arguments += mixes
    aliases = {}
    if before is not None:
        if not pieces:
            aliases[3 + len(arguments)] = 0
        arguments.append(before)
    counts = [mix.shape[0] for mix in mixes]
    shapes = [(4, 2 * lanes + SUB, lanes)] * 2 if pieces else [(2, 8, lanes, lanes)]
    out_shape = [jax.ShapeDtypeStruct(shape, jnp.float32) for shape in shapes]
    if sent is not None:
        out_shape += operand_shapes(counts[-1], blocks, half, lanes)
    scratch = [
        pltpu.VMEM((step if parts_given else 1, lanes, PHYS * half), jnp.bfloat16),
        pltpu.VMEM((step, sum(counts) * 32, PHYS * half), jnp.float32),
    ]
    if pieces:
        scratch.append(pltpu.VMEM((2, 8, lanes, lanes), jnp.float32))
    plan = (
        tuple(chunks), (half_of or 0) * step, parts_given, sent is not None, before is not None,
        pieces,
    )
    out = pl.pallas_call(
        functools.partial(apply_kernel, plan),
        in_specs=[pl.BlockSpec(memory_space=pltpu.SMEM)] * 3
        + [pl.BlockSpec(memory_space=pltpu.VMEM)] * len(arguments),
        out_specs=[pl.BlockSpec(memory_space=pltpu.VMEM)] * len(out_shape),
        scratch_shapes=scratch,
        out_shape=out_shape,
        input_output_aliases=aliases,
        compiler_params=pltpu.CompilerParams(vmem_limit_bytes=APPLY_VMEM),
        cost_estimate=micros(10 if parts_given else 1),
        name="apply_bonds",
    )(info, *slots, *arguments)
    return out[: len(shapes)], out[len(shapes) :]


def add_arrived(info_ref, owner_ref, arrived, total):
    for k in range(4):
        for i in range(2):
            rows = slice(i * LANES, (i + 1) * LANES)
            total[owner_ref[info_ref[4] ^ k, i]] += arrived[k][rows]


def stacked_rows(*rows):
    at = lax.broadcasted_iota(jnp.int32, (SUB, LANES), 0)
    tile = jnp.zeros((SUB, LANES), jnp.float32)
    for i, row in enumerate(rows):
        tile = jnp.where(at == i, row, tile)
    return tile


def merged(tiles):
    rows = [[tile[i : i + 1] for i in range(3)] for tile in tiles]
    cross = sum(row[0] for row in rows)
    square = sum(row[1] for row in rows)
    ratio = cross / jnp.maximum(square, TINY)
    apart = [
        (row[0] / jnp.maximum(row[1], TINY) - ratio) * jnp.sqrt(row[1]) for row in rows
    ]
    rest = sum(row[2] for row in rows) + sum(x * x for x in apart)
    return cross, square, rest


def image_kernel(
    info_ref, owner_ref, a0, a1, a2, a3, diag_ref, own_ref, lower_ref, upper_ref, total
):
    total[...] = diag_ref[...] * own_ref[...]
    add_arrived(info_ref, owner_ref, (a0, a1, a2, a3), total)
    blocks = total.shape[0]
    cross = jnp.zeros((LANES, LANES), jnp.float32)
    square = jnp.zeros((LANES, LANES), jnp.float32)
    for k in range(blocks):
        own, image = own_ref[k], total[k]
        half = lower_ref if k < blocks // 2 else upper_ref
        at = k % (blocks // 2) * LANES
        half[at : at + LANES] = image
        cross += own * image
        square += own * own
    cross = jnp.sum(cross, keepdims=True)
    square = jnp.sum(square, keepdims=True)
    ratio = cross / jnp.maximum(square, TINY)
    rest = jnp.zeros((LANES, LANES), jnp.float32)
    for k in range(blocks):
        apart = total[k] - ratio * own_ref[k]
        rest += apart * apart
    upper_ref[blocks // 2 * LANES :] = stacked_rows(cross, square, jnp.sum(rest, keepdims=True))


def owner_image(info, owners, arrived, diagonal, own):
    rows = own.shape[0] // 2 * LANES
    shapes = [jax.ShapeDtypeStruct((n, LANES), jnp.float32) for n in (rows, rows + SUB)]
    return pl.pallas_call(
        image_kernel,
        in_specs=[pl.BlockSpec(memory_space=pltpu.SMEM)] * 2
        + [pl.BlockSpec(memory_space=pltpu.VMEM)] * 6,
        out_specs=[pl.BlockSpec(memory_space=pltpu.VMEM)] * 2,
        scratch_shapes=[pltpu.VMEM(own.shape, jnp.float32)],
        out_shape=shapes,
        compiler_params=pltpu.CompilerParams(vmem_limit_bytes=SMALL_VMEM),
        cost_estimate=micros(3),
        name="owner_image",
    )(info, owners, *arrived, diagonal, own)


def final_kernel(
    entries, info_ref, owner_ref, a0, a1, a2, a3, diag_ref, own_ref, lower_ref, upper_ref,
    first_ref, vector_ref, second_ref, total,
):
    arrived = (a0, a1, a2, a3)
    cross, square, rest = merged([ref[2 * LANES :] for ref in arrived])
    scale = lax.rsqrt(square / entries + 1e-06)
    rayleigh = scale * scale * (cross / entries)
    apart = (cross / jnp.maximum(square, TINY) - rayleigh) * jnp.sqrt(square)
    mean = scale * scale * ((rest + apart * apart) / entries)
    second_scale = scale * lax.rsqrt(mean + 1e-06)
    for k in range(total.shape[0]):
        at = k % (total.shape[0] // 2) * LANES
        image = (lower_ref if k < total.shape[0] // 2 else upper_ref)[at : at + LANES]
        total[k] = (diag_ref[k] - rayleigh) * image
        first_ref[k] = unpack_tile(scale * image)
        vector_ref[k] = unpack_tile(second_scale * (image - rayleigh * own_ref[k]))
    add_arrived(info_ref, owner_ref, arrived, total)
    for k in range(total.shape[0]):
        second_ref[k] = unpack_tile(second_scale * total[k])


def outputs(info, owners, arrived, diagonal, own, images, entries):
    blocks = diagonal.shape[0]
    shape = (blocks, LANES // 2, 2 * LANES)
    return pl.pallas_call(
        functools.partial(final_kernel, entries),
        grid_spec=pltpu.PrefetchScalarGridSpec(
            num_scalar_prefetch=2,
            grid=(1,),
            in_specs=[whole(*x.shape) for x in (*arrived, diagonal, own)]
            + [whole(blocks // 2 * LANES, LANES)] * 2,
            out_specs=[whole(*shape)] * 3,
            scratch_shapes=[pltpu.VMEM(diagonal.shape, jnp.float32)],
        ),
        out_shape=[jax.ShapeDtypeStruct(shape, jnp.float32)] * 3,
        compiler_params=pltpu.CompilerParams(vmem_limit_bytes=SMALL_VMEM),
        cost_estimate=micros(4),
        name="outputs",
    )(info, owners, *arrived, diagonal, own, *images)


def in_hbm(*arrays):
    return [pltpu.with_memory_space_constraint(x, pltpu.HBM) for x in arrays]


def partner(x, axis, k):
    size = lax.axis_size(axis)
    return lax.ppermute(x, axis, [(i, i ^ k) for i in range(size)])


def after(x, *others):
    return lax.optimization_barrier((x, *others))[0]


def gathered(x):
    across = partner(x, "mpo", 1)
    return [x, across, partner(x, "rep", 1), partner(across, "rep", 1)]


def everyone_of(pieces, axis):
    return [pieces[0]] + [partner(pieces[k], axis, k) for k in range(1, 4)]


def to_owners(mine, theirs):
    other = partner(theirs, "rep", 1)
    pieces = [mine[k] + other[k] for k in range(4)]
    return everyone_of(pieces, "blk")


def per_device(wavefunction, environment, bond_terms, diagonal, term_slot, slot_block):
    blocks, rows, width = wavefunction.shape
    zs = lax.axis_size("blk")
    mpo, rep, blk = lax.axis_index("mpo"), lax.axis_index("rep"), lax.axis_index("blk")
    place = 2 * mpo + rep
    info = jnp.stack([place, place ^ 2, place ^ 1, place ^ 3, blk, rep, mpo]).astype(jnp.int32)
    bonds = environment.shape[0]
    sizes = tuple(bonds * part // 6 for part in (2, 2, 1, 1))
    firsts = tuple(sum(sizes[:group]) for group in range(len(sizes)))
    entries = float(blocks * zs * rows * width)

    vector, own, diagonal_packed = pack(info, wavefunction, diagonal)

    by_owner = environment.reshape(bonds, zs, blocks, rows // zs, 2 * rows)
    pieces = []
    for group in range(len(sizes)):
        cuts = list(cut_pieces(info, by_owner, firsts[group], sizes[group]))
        if group:
            cuts[1:] = [after(x, y) for x, y in zip(cuts[1:], pieces[-1][1:])]
        pieces.append(cuts[:1] + [partner(cuts[k], "blk", k) for k in range(1, 4)])
    pieces[0][1] = after(pieces[0][1], vector)
    other_terms = partner(after(bond_terms, pieces[0][1]), "mpo", 1)
    mixing = mixing_operands([bond_terms, other_terms], sizes)
    slots = [term_slot, partner(after(term_slot, pieces[0][1]), "mpo", 1)]

    made, sent = [], []
    total = None
    operands = []
    done = 0

    def apply_group(group, vector):
        out, other = apply_bonds(
            info, slots, vector, [(0, firsts[group]), (1, firsts[group])], [made[group]],
            partner(sent[group], "mpo", 1), [terms[group] for terms in mixing], total,
            group == len(sizes) - 1,
        )
        operands.extend([made[group], other])
        return out

    for group in range(len(sizes)):
        if group >= 2:
            total = apply_group(group - 2, after(vector, sent[group - 1]))[0]
            pieces[group][3] = after(pieces[group][3], total)
        if group + 1 < len(sizes):
            pieces[group][1] = after(pieces[group][1], pieces[group + 1][1])
        *own_set, send = own_operands(info, pieces[group])
        made.append(own_set)
        sent.append(send)
    total = apply_group(len(sizes) - 2, after(vector, sent[-1]))[0]
    out = apply_group(len(sizes) - 1, vector)
    lower, upper = owner_image(info, slot_block, to_owners(*out), diagonal_packed, own)

    chunks = [(source, first) for first in firsts for source in range(2)]
    mixes = [mixing[source][group] for group in range(len(sizes)) for source in range(2)]
    lower_parts = gathered(lower)
    across = partner(after(upper, lower_parts[1]), "mpo", 1)
    out, _ = apply_bonds(
        info, slots, lower_parts, chunks, operands, None, mixes, None, False, 0
    )
    upper_parts = [upper, across, partner(upper, "rep", 1)]
    upper_parts.append(partner(after(across, out[0]), "rep", 1))
    out, _ = apply_bonds(
        info, slots, upper_parts, chunks, operands, None, mixes, out[0], True, 1
    )
    return tuple(
        outputs(
            info, slot_block, to_owners(*out), diagonal_packed, own, (lower, upper), entries
        )
    )


def solution(mesh):
    packed = mesh.shape["mpo"] == 2 and mesh.shape["rep"] == 2 and mesh.shape["blk"] == 4
    return jax.shard_map(
        per_device if packed else plain_device,
        mesh=mesh,
        in_specs=(
            P(("grp", "blk"), None, None),
            P(("grp", "mpo", "rep"), None, "blk", None),
            P(("grp", "mpo", "rep"), None, None),
            P(("grp", "blk"), None, ("mpo", "rep")),
            P(("grp", "mpo", "rep"), "blk"),
            P("grp", "blk"),
        ),
        out_specs=(
            P(("grp", "blk"), None, ("mpo", "rep")),
            P(("grp", "blk"), None, ("mpo", "rep")),
            P(("grp", "blk"), None, ("mpo", "rep")),
        ),
        check_vma=False,
    )
```

```python
import functools

import jax
import jax.numpy as jnp
from jax import lax
from jax.experimental import pallas as pl
from jax.experimental.pallas import tpu as pltpu
from jax.sharding import PartitionSpec as P

LANES = 128
SUB = 8
PHYS = 16
TINY = 1e-30
SMALL_VMEM = 16 * 1024 * 1024
APPLY_VMEM = 16 * 1024 * 1024


def plain_apply(vector_full, environment, bond_terms, term_slot, slot_block, diagonal):
    block_count, block_rows, block_width = vector_full.shape
    phys_size = bond_terms.shape[-1]
    right_rows = block_width // phys_size
    slot_count = slot_block.shape[0] * slot_block.shape[1]
    blocks = vector_full.reshape(block_count, block_rows, right_rows, phys_size)
    ordered = jnp.transpose(blocks, (0, 3, 1, 2))
    left_env = environment[:, :, :, :block_rows]
    right_env = environment[:, :, :, block_rows:]
    left_done = jnp.einsum("wjab,jsac->wjsbc", left_env, ordered, precision=lax.Precision.HIGHEST)
    right_done = jnp.einsum(
        "wjsbc,wjcd->wjsbd", left_done, right_env, precision=lax.Precision.HIGHEST
    )
    right_done = right_done.reshape(
        environment.shape[0], block_count, phys_size, block_rows * right_rows
    )
    bond_term = jnp.einsum(
        "wjsx,wst->wjtx", right_done, bond_terms, precision=lax.Precision.HIGHEST
    )
    bond_term = bond_term.reshape(environment.shape[0], block_count, block_rows * block_width)
    slot_table = (
        term_slot[:, None, :] == jnp.arange(slot_count, dtype=jnp.int32)[None, :, None]
    ).astype(jnp.float32)
    slot_buffer = jnp.einsum("wsj,wjx->sx", slot_table, bond_term, precision=lax.Precision.HIGHEST)
    slot_buffer = slot_buffer.reshape(slot_count, phys_size, block_rows, right_rows)
    slot_buffer = jnp.transpose(slot_buffer, (0, 2, 3, 1)).reshape(
        slot_count, block_rows, block_width
    )
    owners = slot_block.reshape(-1)
    selector = (owners[None, :] == jnp.arange(block_count, dtype=jnp.int32)[:, None]).astype(
        jnp.float32
    )
    column_width = block_width // lax.axis_size(("mpo", "rep"))
    column_start = lax.axis_index(("mpo", "rep")) * column_width
    own_part = lax.dynamic_slice_in_dim(vector_full, column_start, column_width, 2)
    shares = lax.psum_scatter(slot_buffer, ("mpo", "rep"), scatter_dimension=2, tiled=True)
    arrived = lax.all_to_all(shares, "blk", split_axis=0, concat_axis=0, tiled=True)
    result = jnp.einsum("ks,sbc->kbc", selector, arrived, precision=lax.Precision.HIGHEST)
    return (result + diagonal * own_part, own_part)


def plain_device(wavefunction, environment, bond_terms, diagonal, term_slot, slot_block):
    arranged = lax.all_to_all(environment, "blk", split_axis=1, concat_axis=2, tiled=True)
    entries = float(
        wavefunction.shape[0] * lax.axis_size("blk") * wavefunction.shape[1] * wavefunction.shape[2]
    )
    square_sum = lax.psum(jnp.sum(wavefunction * wavefunction), "blk")
    first_vector = wavefunction * lax.rsqrt(square_sum / entries + 1e-06)
    first_image, first_part = plain_apply(
        first_vector, arranged, bond_terms, term_slot, slot_block, diagonal
    )
    rayleigh = lax.psum(jnp.sum(first_part * first_image), ("blk", "mpo", "rep")) / entries
    residual = first_image - rayleigh * first_part
    resid_sum = lax.psum(jnp.sum(residual * residual), ("blk", "mpo", "rep"))
    second_vector = residual * lax.rsqrt(resid_sum / entries + 1e-06)
    second_full = lax.all_gather(second_vector, ("mpo", "rep"), axis=2, tiled=True)
    second_image, unused = plain_apply(
        second_full, arranged, bond_terms, term_slot, slot_block, diagonal
    )
    return (first_image, second_vector, second_image)


def split_two(x):
    high = x.astype(jnp.bfloat16)
    low = (x - high.astype(jnp.float32)).astype(jnp.bfloat16)
    return high, low


def lane_is_first(rows):
    return lax.broadcasted_iota(jnp.int32, (rows, LANES), 1) < LANES // 2


def micros(count):
    return pl.CostEstimate(flops=count * 1100000000, bytes_accessed=1 << 20, transcendentals=0)


def whole(*shape):
    return pl.BlockSpec(shape, lambda i, *_: (0,) * len(shape))


def pack_tile(x):
    return jnp.concatenate([x[:, :LANES], x[:, LANES:]], axis=0).T


def unpack_tile(x):
    upright = x.T
    return jnp.concatenate([upright[: LANES // 2], upright[LANES // 2 :]], axis=1)


def store_vector(parts, rows_of, put):
    first = lane_is_first(SUB)
    for pair in range(PHYS // 2):
        for part, row in zip(parts, rows_of):
            even = part[pl.ds(2 * pair, SUB, stride=PHYS), :]
            odd = part[pl.ds(2 * pair + 1, SUB, stride=PHYS), :]
            upper = jnp.where(first, even, pltpu.roll(odd, LANES // 2, 1))
            lower = jnp.where(first, pltpu.roll(even, LANES // 2, 1), odd)
            high, low = split_two(jnp.concatenate([upper, lower], axis=0))
            put(row, pair, high, low)


def pack_kernel(info_ref, wave_ref, own_wave_ref, diag_ref, vec_ref, own_ref, diag_out, tiles):
    half = LANES // 2
    for j in range(wave_ref.shape[0]):
        own_ref[j] = pack_tile(own_wave_ref[j])
        diag_out[j] = pack_tile(diag_ref[j])
        for q in range(4):
            tiles[q, j] = pack_tile(wave_ref[j, :, 2 * LANES * q : 2 * LANES * (q + 1)])

        def put(row, pair, high, low):
            columns = slice(pair * LANES, (pair + 1) * LANES)
            vec_ref[j, row : row + 16, columns] = high
            vec_ref[j, row + half : row + half + 16, columns] = low

        store_vector([tiles.at[q, j] for q in range(4)], [16 * q for q in range(4)], put)


def pack(info, wavefunction, diagonal):
    blocks, rows, width = wavefunction.shape
    step = 2
    tile = pl.BlockSpec((step, LANES, LANES), lambda i, *_: (i, 0, 0))
    return pl.pallas_call(
        pack_kernel,
        grid_spec=pltpu.PrefetchScalarGridSpec(
            num_scalar_prefetch=1,
            grid=(blocks // step,),
            in_specs=[
                pl.BlockSpec((step, rows, width), lambda i, *_: (i, 0, 0)),
                pl.BlockSpec((step, rows, width // 4), lambda i, info: (i, 0, info[0])),
                pl.BlockSpec((step, rows, width // 4), lambda i, *_: (i, 0, 0)),
            ],
            out_specs=[pl.BlockSpec((step, LANES, width), lambda i, *_: (i, 0, 0)), tile, tile],
            scratch_shapes=[pltpu.VMEM((4, step, LANES, LANES), jnp.float32)],
        ),
        out_shape=[
            jax.ShapeDtypeStruct((blocks, LANES, width), jnp.bfloat16),
            jax.ShapeDtypeStruct((blocks, LANES, LANES), jnp.float32),
            jax.ShapeDtypeStruct((blocks, LANES, LANES), jnp.float32),
        ],
        compiler_params=pltpu.CompilerParams(vmem_limit_bytes=SMALL_VMEM),
        cost_estimate=micros(5),
        name="pack",
    )(info, wavefunction, wavefunction, diagonal)


def mixing_kernel(sizes, *refs):
    sources, outs = refs[:2], refs[2:]
    spread = (
        lax.broadcasted_iota(jnp.int32, (PHYS, LANES), 1) // SUB
        == lax.broadcasted_iota(jnp.int32, (PHYS, LANES), 0)
    ).astype(jnp.bfloat16)
    row = lax.broadcasted_iota(jnp.int32, (LANES, LANES), 0) // PHYS
    column = lax.broadcasted_iota(jnp.int32, (LANES, LANES), 1) % SUB
    same = row == column
    for n, source in enumerate(sources):
        start = 0
        for group, size in enumerate(sizes):
            out_ref = outs[n * len(sizes) + group]
            for at in range(size):
                for place, term in enumerate(split_two(source[start + at].T)):
                    wide = jnp.dot(term, spread, preferred_element_type=jnp.float32)
                    tall = jnp.concatenate([wide] * SUB, axis=0)
                    tall = jnp.where(same, tall, 0.0).astype(jnp.bfloat16)
                    rows = slice(place * LANES, (place + 1) * LANES)
                    out_ref[at, rows] = jnp.concatenate([tall, tall], axis=1)
            start += size


def mixing_operands(sources, sizes):
    out = pl.pallas_call(
        functools.partial(mixing_kernel, sizes),
        out_shape=[
            jax.ShapeDtypeStruct((size, 2 * LANES, 2 * LANES), jnp.bfloat16)
            for _ in sources
            for size in sizes
        ],
        compiler_params=pltpu.CompilerParams(vmem_limit_bytes=SMALL_VMEM),
        cost_estimate=micros(2),
        name="mixing",
    )(*sources)
    return [out[: len(sizes)], out[len(sizes) :]]


def own_operands_kernel(info_ref, *refs):
    pieces, (left_high, left_low, right_out, send, blocks_ref, upright_ref) = refs[:4], refs[4:]
    per, blocks, half, lanes = left_high.shape
    rows = half // 4
    wide = half // 2
    first = lane_is_first(half)
    first_wide = lane_is_first(wide)
    first_rows = lane_is_first(rows)
    mine_at = pl.multiple_of(half + info_ref[6] * wide, wide)
    theirs_at = pl.multiple_of(lanes - wide - info_ref[6] * wide, wide)
    for j in range(blocks):
        for w in range(per):
            for z in range(4):
                row = pl.multiple_of((info_ref[4] ^ z) * rows, rows)
                blocks_ref[w, j, pl.ds(row, rows), :] = pieces[z][w, j]
        for w in range(per):
            block = blocks_ref[w, j]
            upright_ref[w, j] = jnp.concatenate([block, block], axis=0).T
            turned = pltpu.roll(block, half, 1)
            high, low = split_two(jnp.where(first, block, turned))
            left_high[w, j] = high
            left_low[w, j] = low
            send[w, j, 0:wide] = jnp.where(first_wide, block[:wide], turned[wide:])
        for w in range(per):
            high, low = split_two(upright_ref[w, j, pl.ds(mine_at, wide), :])
            right_out[j, wide * w : wide * (w + 1), 0:lanes] = high
            right_out[j, wide * w : wide * (w + 1), lanes:] = low
            upper = upright_ref[w, j, pl.ds(theirs_at, rows), :]
            lower = upright_ref[w, j, pl.ds(theirs_at + rows, rows), :]
            send[w, j, wide : wide + rows] = jnp.where(first_rows, upper, lower)


def other_operands(sent, left_high, left_low, right_out, j):
    per, blocks, half, lanes = left_high.shape
    rows = half // 4
    wide = half // 2
    first = lane_is_first(wide)
    first_rows = lane_is_first(rows)
    for w in range(per):
        both = sent[w, j, 0:wide]
        turned = pltpu.roll(both, half, 1)
        full = jnp.concatenate(
            [jnp.where(first, both, turned), jnp.where(first, turned, both)], axis=0
        )
        high, low = split_two(full)
        left_high[w, j] = high
        left_low[w, j] = low
        both = sent[w, j, wide : wide + rows]
        turned = pltpu.roll(both, half, 1)
        full = jnp.concatenate(
            [jnp.where(first_rows, both, turned), jnp.where(first_rows, turned, both)], axis=0
        )
        high, low = split_two(full)
        right_out[j, wide * w : wide * (w + 1), 0:lanes] = high
        right_out[j, wide * w : wide * (w + 1), lanes:] = low


def operand_specs(per, step, half, lanes, at=0):
    return [
        pl.BlockSpec((per, step, half, lanes), lambda i, *_: (0, at + i, 0, 0)),
        pl.BlockSpec((per, step, half, lanes), lambda i, *_: (0, at + i, 0, 0)),
        pl.BlockSpec((step, per * 32, 2 * lanes), lambda i, *_: (at + i, 0, 0)),
    ]


def operand_shapes(per, blocks, half, lanes):
    return [
        jax.ShapeDtypeStruct((per, blocks, half, lanes), jnp.bfloat16),
        jax.ShapeDtypeStruct((per, blocks, half, lanes), jnp.bfloat16),
        jax.ShapeDtypeStruct((blocks, per * 32, 2 * lanes), jnp.bfloat16),
    ]


def cut_kernel(first, info_ref, source, *refs):
    outs, sems = refs[:4], refs[4]
    per = outs[0].shape[0]
    copies = []
    for k in range(4):
        part = source.at[pl.ds(first, per), info_ref[4] ^ k]
        copies.append(pltpu.make_async_copy(part, outs[k], sems.at[k]))
    for copy in copies:
        copy.start()
    for copy in copies:
        copy.wait()


def cut_pieces(info, by_owner, first, per):
    shape = jax.ShapeDtypeStruct((per,) + by_owner.shape[2:], jnp.float32)
    return pl.pallas_call(
        functools.partial(cut_kernel, first),
        grid_spec=pltpu.PrefetchScalarGridSpec(
            num_scalar_prefetch=1,
            grid=(1,),
            in_specs=[pl.BlockSpec(memory_space=pl.ANY)],
            out_specs=[pl.BlockSpec(memory_space=pl.ANY)] * 4,
            scratch_shapes=[pltpu.SemaphoreType.DMA((4,))],
        ),
        out_shape=[shape] * 4,
        compiler_params=pltpu.CompilerParams(vmem_limit_bytes=SMALL_VMEM),
        cost_estimate=micros(1),
        name="cut_pieces",
    )(info, *(in_hbm(by_owner) if first == 0 else [by_owner]))


def own_operands(info, pieces):
    per, blocks, rows, lanes = pieces[0].shape
    half = lanes // 2
    step = 4
    return pl.pallas_call(
        own_operands_kernel,
        grid_spec=pltpu.PrefetchScalarGridSpec(
            num_scalar_prefetch=1,
            grid=(blocks // step,),
            in_specs=[pl.BlockSpec((per, step, rows, lanes), lambda i, *_: (0, i, 0, 0))] * 4,
            out_specs=operand_specs(per, step, half, lanes)
            + [pl.BlockSpec((per, step, 3 * rows, lanes), lambda i, *_: (0, i, 0, 0))],
            scratch_shapes=[
                pltpu.VMEM((per, step, half, lanes), jnp.float32),
                pltpu.VMEM((per, step, lanes, lanes), jnp.float32),
            ],
        ),
        out_shape=operand_shapes(per, blocks, half, lanes)
        + [jax.ShapeDtypeStruct((per, blocks, 3 * rows, lanes), jnp.float32)],
        compiler_params=pltpu.CompilerParams(vmem_limit_bytes=SMALL_VMEM),
        cost_estimate=micros(12),
        name="own_operands",
    )(info, *pieces)


def apply_kernel(plan, info_ref, *refs):
    chunks, first_block, parts_given, sent_given, before_given, pieces = plan
    refs = list(refs)
    take = lambda n: [refs.pop(0) for _ in range(n)]
    slots = take(2)
    vector = take(4 if parts_given else 1)
    operands = [take(3) for _ in chunks[: -1 if sent_given else None]]
    sent = take(1)[0] if sent_given else None
    mixes = take(len(chunks))
    before = take(1)[0] if before_given else None
    outs = take(2 if pieces else 1)
    if sent_given:
        operands.append(take(3))
    scratch = take(2)
    vec, mid = scratch
    total_ref = take(1)[0] if pieces else outs[0]
    step = mid.shape[0]
    lanes, half = LANES, LANES // 2
    first = lane_is_first(SUB)
    first_half = lane_is_first(half)
    keep_first = jnp.where(first_half, 1.0, 0.0).astype(jnp.bfloat16)
    keep_second = jnp.where(first_half, 0.0, 1.0).astype(jnp.bfloat16)
    me = info_ref[4]

    if not before_given:
        total_ref[...] = jnp.zeros_like(total_ref)
    else:
        total_ref[...] = before[...]

    def right_side(j):
        if sent_given:
            other_operands(sent, *operands[-1], first_block + j)
        if parts_given:

            def put(row, pair, high, low):
                columns = slice(pair * lanes, (pair + 1) * lanes)
                vec[j, pl.ds(row, 16), columns] = high
                vec[j, pl.ds(row + half, 16), columns] = low

            rows_of = [pl.multiple_of(info_ref[g] * 16, 16) for g in range(4)]
            store_vector([x.at[pl.ds(j * lanes, lanes)] for x in vector], rows_of, put)
            source = vec[j]
        else:
            source = vector[0][first_block + j]
        source = jnp.concatenate([source, source], axis=0)
        at = 0
        for left_high, left_low, right in operands:
            count = right.shape[1]
            mid[j, at : at + count, :] = jnp.dot(
                right[first_block + j], source, preferred_element_type=jnp.float32
            )
            at += count

    def prepared(j, refs_of, w, row_of):
        left_high, left_low, right = refs_of
        tiles = []
        for part in range(2):
            row = row_of + part * 16
            for pair in range(PHYS // 2):
                columns = slice(pair * lanes, (pair + 1) * lanes)
                upper = mid[j, row : row + SUB, columns]
                lower = mid[j, row + SUB : row + 2 * SUB, columns]
                tiles.append(jnp.where(first, upper, pltpu.roll(lower, half, 1)))
                tiles.append(jnp.where(first, pltpu.roll(upper, half, 1), lower))
        t_high, t_low = split_two(jnp.concatenate(tiles, axis=0))
        lh, ll = left_high[w, first_block + j], left_low[w, first_block + j]
        wide_high = jnp.concatenate([lh * keep_first, lh * keep_second], axis=0)
        wide_low = jnp.concatenate([ll * keep_first, ll * keep_second], axis=0)
        weights = jnp.concatenate([wide_high, wide_low], axis=1)
        weights = jnp.concatenate([weights, weights], axis=0)
        return jnp.concatenate([t_high, t_low], axis=1), weights

    def mix_unit(mixing, w, z):
        z_high, z_low = [jnp.concatenate([x[:lanes], x[lanes:]], axis=1) for x in z]
        return jnp.dot(
            mixing[w],
            jnp.concatenate([z_high, z_low], axis=0),
            preferred_element_type=jnp.float32,
        )

    def add_up(j, table, bond, mixed):
        slot = table[bond, first_block + j]
        slot = ((slot >> 1) ^ me) * 2 + (slot & 1)
        for part in range(2):
            columns = slice(part * lanes, (part + 1) * lanes)
            total_ref[part, slot] += mixed[:lanes, columns] + mixed[lanes:, columns]

    bonds = []
    for (source, start), refs_of, mix in zip(chunks, operands, mixes):
        for w in range(mix.shape[0]):
            bonds.append((refs_of, mix, w, slots[source], start + w))
    right_side(0)
    units = [(j, at) for j in range(step) for at in range(len(bonds))]

    def prepare_unit(n):
        j, at = units[n]
        refs_of, mixing, w, table, bond = bonds[at]
        return prepared(j, refs_of, w, at * 32)

    ready = prepare_unit(0)
    waiting = None
    for n, (j, at) in enumerate(units):
        refs_of, mixing, w, table, bond = bonds[at]
        z = jnp.dot(*ready, preferred_element_type=jnp.float32)
        if j + 1 < step and at == len(bonds) // 3:
            right_side(j + 1)
        if n + 1 < len(units):
            ready = prepare_unit(n + 1)
        if waiting is not None:
            before_j, before_mixing, before_w, before_table, before_bond, before_z = waiting
            mixed = mix_unit(before_mixing, before_w, before_z)
        z = split_two(z[:, :lanes] + z[:, lanes:])
        if waiting is not None:
            add_up(before_j, before_table, before_bond, mixed)
        waiting = (j, mixing, w, table, bond, z)
    j, mixing, w, table, bond, z = waiting
    add_up(j, table, bond, mix_unit(mixing, w, z))

    if pieces:
        stats = jnp.zeros((SUB, lanes), jnp.float32)
        if parts_given:
            tail = vector[0].shape[0] - SUB
            stats = stacked_rows(*merged([x[tail:] for x in vector]))
        for out, part in ((outs[0], info_ref[5]), (outs[1], 1 - info_ref[5])):
            for k in range(4):
                for i in range(2):
                    out[k, i * lanes : (i + 1) * lanes] = total_ref[part, 2 * k + i]
                out[k, 2 * lanes :] = stats
            stats = jnp.zeros((SUB, lanes), jnp.float32)


def apply_bonds(info, slots, vector, chunks, operands, sent, mixes, before, pieces, half_of=None):
    blocks, half, lanes = operands[0][0].shape[1:]
    parts_given = half_of is not None
    step = 4 if parts_given else blocks
    arguments = list(vector) if parts_given else [vector]
    for made in operands:
        arguments += made
    if sent is not None:
        arguments.append(sent)
    arguments += mixes
    aliases = {}
    if before is not None:
        if not pieces:
            aliases[3 + len(arguments)] = 0
        arguments.append(before)
    counts = [mix.shape[0] for mix in mixes]
    shapes = [(4, 2 * lanes + SUB, lanes)] * 2 if pieces else [(2, 8, lanes, lanes)]
    out_shape = [jax.ShapeDtypeStruct(shape, jnp.float32) for shape in shapes]
    if sent is not None:
        out_shape += operand_shapes(counts[-1], blocks, half, lanes)
    scratch = [
        pltpu.VMEM((step if parts_given else 1, lanes, PHYS * half), jnp.bfloat16),
        pltpu.VMEM((step, sum(counts) * 32, PHYS * half), jnp.float32),
    ]
    if pieces:
        scratch.append(pltpu.VMEM((2, 8, lanes, lanes), jnp.float32))
    plan = (
        tuple(chunks), (half_of or 0) * step, parts_given, sent is not None, before is not None,
        pieces,
    )
    out = pl.pallas_call(
        functools.partial(apply_kernel, plan),
        in_specs=[pl.BlockSpec(memory_space=pltpu.SMEM)] * 3
        + [pl.BlockSpec(memory_space=pltpu.VMEM)] * len(arguments),
        out_specs=[pl.BlockSpec(memory_space=pltpu.VMEM)] * len(out_shape),
        scratch_shapes=scratch,
        out_shape=out_shape,
        input_output_aliases=aliases,
        compiler_params=pltpu.CompilerParams(vmem_limit_bytes=APPLY_VMEM),
        cost_estimate=micros(10 if parts_given else 1),
        name="apply_bonds",
    )(info, *slots, *arguments)
    return out[: len(shapes)], out[len(shapes) :]


def add_arrived(info_ref, owner_ref, arrived, total):
    for k in range(4):
        for i in range(2):
            rows = slice(i * LANES, (i + 1) * LANES)
            total[owner_ref[info_ref[4] ^ k, i]] += arrived[k][rows]


def stacked_rows(*rows):
    at = lax.broadcasted_iota(jnp.int32, (SUB, LANES), 0)
    tile = jnp.zeros((SUB, LANES), jnp.float32)
    for i, row in enumerate(rows):
        tile = jnp.where(at == i, row, tile)
    return tile


def merged(tiles):
    rows = [[tile[i : i + 1] for i in range(3)] for tile in tiles]
    cross = sum(row[0] for row in rows)
    square = sum(row[1] for row in rows)
    ratio = cross / jnp.maximum(square, TINY)
    apart = [
        (row[0] / jnp.maximum(row[1], TINY) - ratio) * jnp.sqrt(row[1]) for row in rows
    ]
    rest = sum(row[2] for row in rows) + sum(x * x for x in apart)
    return cross, square, rest


def image_kernel(
    info_ref, owner_ref, a0, a1, a2, a3, diag_hbm, own_hbm, lower_ref, upper_ref, total,
    diag_ref, own_ref, sems,
):
    copies = [
        pltpu.make_async_copy(diag_hbm, diag_ref, sems.at[0]),
        pltpu.make_async_copy(own_hbm, own_ref, sems.at[1]),
    ]
    for copy in copies:
        copy.start()
    total[...] = jnp.zeros_like(total)
    add_arrived(info_ref, owner_ref, (a0, a1, a2, a3), total)
    for copy in copies:
        copy.wait()
    total[...] += diag_ref[...] * own_ref[...]
    blocks = total.shape[0]
    cross = jnp.zeros((LANES, LANES), jnp.float32)
    square = jnp.zeros((LANES, LANES), jnp.float32)
    for k in range(blocks):
        own, image = own_ref[k], total[k]
        half = lower_ref if k < blocks // 2 else upper_ref
        at = k % (blocks // 2) * LANES
        half[at : at + LANES] = image
        cross += own * image
        square += own * own
    cross = jnp.sum(cross, keepdims=True)
    square = jnp.sum(square, keepdims=True)
    ratio = cross / jnp.maximum(square, TINY)
    rest = jnp.zeros((LANES, LANES), jnp.float32)
    for k in range(blocks):
        apart = total[k] - ratio * own_ref[k]
        rest += apart * apart
    upper_ref[blocks // 2 * LANES :] = stacked_rows(cross, square, jnp.sum(rest, keepdims=True))


def owner_image(info, owners, arrived, diagonal, own):
    rows = own.shape[0] // 2 * LANES
    shapes = [jax.ShapeDtypeStruct((n, LANES), jnp.float32) for n in (rows, rows + SUB)]
    return pl.pallas_call(
        image_kernel,
        in_specs=[pl.BlockSpec(memory_space=pltpu.SMEM)] * 2
        + [pl.BlockSpec(memory_space=pltpu.VMEM)] * 4
        + [pl.BlockSpec(memory_space=pl.ANY)] * 2,
        out_specs=[pl.BlockSpec(memory_space=pltpu.VMEM)] * 2,
        scratch_shapes=[pltpu.VMEM(own.shape, jnp.float32)] * 3 + [pltpu.SemaphoreType.DMA((2,))],
        out_shape=shapes,
        compiler_params=pltpu.CompilerParams(vmem_limit_bytes=SMALL_VMEM),
        cost_estimate=micros(3),
        name="owner_image",
    )(info, owners, *arrived, *in_hbm(diagonal, own))


def final_kernel(
    entries, info_ref, owner_ref, a0, a1, a2, a3, diag_ref, own_ref, lower_ref, upper_ref,
    first_ref, vector_ref, second_ref, total,
):
    arrived = (a0, a1, a2, a3)
    cross, square, rest = merged([ref[2 * LANES :] for ref in arrived])
    scale = lax.rsqrt(square / entries + 1e-06)
    rayleigh = scale * scale * (cross / entries)
    apart = (cross / jnp.maximum(square, TINY) - rayleigh) * jnp.sqrt(square)
    mean = scale * scale * ((rest + apart * apart) / entries)
    second_scale = scale * lax.rsqrt(mean + 1e-06)
    for k in range(total.shape[0]):
        at = k % (total.shape[0] // 2) * LANES
        image = (lower_ref if k < total.shape[0] // 2 else upper_ref)[at : at + LANES]
        total[k] = (diag_ref[k] - rayleigh) * image
        first_ref[k] = unpack_tile(scale * image)
        vector_ref[k] = unpack_tile(second_scale * (image - rayleigh * own_ref[k]))
    add_arrived(info_ref, owner_ref, arrived, total)
    for k in range(total.shape[0]):
        second_ref[k] = unpack_tile(second_scale * total[k])


def outputs(info, owners, arrived, diagonal, own, images, entries):
    blocks = diagonal.shape[0]
    shape = (blocks, LANES // 2, 2 * LANES)
    return pl.pallas_call(
        functools.partial(final_kernel, entries),
        grid_spec=pltpu.PrefetchScalarGridSpec(
            num_scalar_prefetch=2,
            grid=(1,),
            in_specs=[whole(*x.shape) for x in (*arrived, diagonal, own)]
            + [whole(blocks // 2 * LANES, LANES)] * 2,
            out_specs=[whole(*shape)] * 3,
            scratch_shapes=[pltpu.VMEM(diagonal.shape, jnp.float32)],
        ),
        out_shape=[jax.ShapeDtypeStruct(shape, jnp.float32)] * 3,
        compiler_params=pltpu.CompilerParams(vmem_limit_bytes=SMALL_VMEM),
        cost_estimate=micros(4),
        name="outputs",
    )(info, owners, *arrived, diagonal, own, *images)


def in_hbm(*arrays):
    return [pltpu.with_memory_space_constraint(x, pltpu.HBM) for x in arrays]


def partner(x, axis, k):
    size = lax.axis_size(axis)
    return lax.ppermute(x, axis, [(i, i ^ k) for i in range(size)])


def after(x, *others):
    return lax.optimization_barrier((x, *others))[0]


def gathered(x):
    across = partner(x, "mpo", 1)
    return [x, across, partner(x, "rep", 1), partner(across, "rep", 1)]


def everyone_of(pieces, axis):
    return [pieces[0]] + [partner(pieces[k], axis, k) for k in range(1, 4)]


def to_owners(mine, theirs):
    other = partner(theirs, "rep", 1)
    pieces = [mine[k] + other[k] for k in range(4)]
    return everyone_of(pieces, "blk")


def per_device(wavefunction, environment, bond_terms, diagonal, term_slot, slot_block):
    blocks, rows, width = wavefunction.shape
    zs = lax.axis_size("blk")
    mpo, rep, blk = lax.axis_index("mpo"), lax.axis_index("rep"), lax.axis_index("blk")
    place = 2 * mpo + rep
    info = jnp.stack([place, place ^ 2, place ^ 1, place ^ 3, blk, rep, mpo]).astype(jnp.int32)
    bonds = environment.shape[0]
    sizes = tuple(bonds * part // 6 for part in (2, 2, 2))
    firsts = tuple(sum(sizes[:group]) for group in range(len(sizes)))
    entries = float(blocks * zs * rows * width)

    vector, own, diagonal_packed = pack(info, wavefunction, diagonal)

    by_owner = environment.reshape(bonds, zs, blocks, rows // zs, 2 * rows)
    pieces = []
    for group in range(len(sizes)):
        cuts = list(cut_pieces(info, by_owner, firsts[group], sizes[group]))
        if group:
            cuts[1:] = [after(x, y) for x, y in zip(cuts[1:], pieces[-1][1:])]
        pieces.append(cuts[:1] + [partner(cuts[k], "blk", k) for k in range(1, 4)])
    pieces[0][1] = after(pieces[0][1], vector)
    other_terms = partner(after(bond_terms, pieces[0][1]), "mpo", 1)
    mixing = mixing_operands([bond_terms, other_terms], sizes)
    slots = [term_slot, partner(after(term_slot, pieces[0][1]), "mpo", 1)]

    made, sent = [], []
    total = None
    operands = []
    done = 0

    def apply_group(group, vector):
        out, other = apply_bonds(
            info, slots, vector, [(0, firsts[group]), (1, firsts[group])], [made[group]],
            partner(sent[group], "mpo", 1), [terms[group] for terms in mixing], total,
            group == len(sizes) - 1,
        )
        operands.extend([made[group], other])
        return out

    for group in range(len(sizes)):
        if group >= 2:
            total = apply_group(group - 2, after(vector, sent[group - 1]))[0]
            pieces[group][3] = after(pieces[group][3], total)
        if group < 1:
            pieces[group][1] = after(pieces[group][1], pieces[group + 1][1])
        *own_set, send = own_operands(info, pieces[group])
        made.append(own_set)
        sent.append(send)
    total = apply_group(len(sizes) - 2, after(vector, sent[-1]))[0]
    out = apply_group(len(sizes) - 1, vector)
    lower, upper = owner_image(info, slot_block, to_owners(*out), diagonal_packed, own)

    chunks = [(source, first) for first in firsts for source in range(2)]
    mixes = [mixing[source][group] for group in range(len(sizes)) for source in range(2)]
    lower_parts = gathered(lower)
    across = partner(after(upper, lower_parts[1]), "mpo", 1)
    out, _ = apply_bonds(
        info, slots, lower_parts, chunks, operands, None, mixes, None, False, 0
    )
    upper_parts = [upper, across, partner(upper, "rep", 1)]
    upper_parts.append(partner(after(across, out[0]), "rep", 1))
    out, _ = apply_bonds(
        info, slots, upper_parts, chunks, operands, None, mixes, out[0], True, 1
    )
    return tuple(
        outputs(
            info, slot_block, to_owners(*out), diagonal_packed, own, (lower, upper), entries
        )
    )


def solution(mesh):
    packed = mesh.shape["mpo"] == 2 and mesh.shape["rep"] == 2 and mesh.shape["blk"] == 4
    return jax.shard_map(
        per_device if packed else plain_device,
        mesh=mesh,
        in_specs=(
            P(("grp", "blk"), None, None),
            P(("grp", "mpo", "rep"), None, "blk", None),
            P(("grp", "mpo", "rep"), None, None),
            P(("grp", "blk"), None, ("mpo", "rep")),
            P(("grp", "mpo", "rep"), "blk"),
            P("grp", "blk"),
        ),
        out_specs=(
            P(("grp", "blk"), None, ("mpo", "rep")),
            P(("grp", "blk"), None, ("mpo", "rep")),
            P(("grp", "blk"), None, ("mpo", "rep")),
        ),
        check_vma=False,
    )
```

```python
import functools

import jax
import jax.numpy as jnp
from jax import lax
from jax.experimental import pallas as pl
from jax.experimental.pallas import tpu as pltpu
from jax.sharding import PartitionSpec as P

LANES = 128
SUB = 8
PHYS = 16
TINY = 1e-30
SMALL_VMEM = 16 * 1024 * 1024
APPLY_VMEM = 16 * 1024 * 1024


def plain_apply(vector_full, environment, bond_terms, term_slot, slot_block, diagonal):
    block_count, block_rows, block_width = vector_full.shape
    phys_size = bond_terms.shape[-1]
    right_rows = block_width // phys_size
    slot_count = slot_block.shape[0] * slot_block.shape[1]
    blocks = vector_full.reshape(block_count, block_rows, right_rows, phys_size)
    ordered = jnp.transpose(blocks, (0, 3, 1, 2))
    left_env = environment[:, :, :, :block_rows]
    right_env = environment[:, :, :, block_rows:]
    left_done = jnp.einsum("wjab,jsac->wjsbc", left_env, ordered, precision=lax.Precision.HIGHEST)
    right_done = jnp.einsum(
        "wjsbc,wjcd->wjsbd", left_done, right_env, precision=lax.Precision.HIGHEST
    )
    right_done = right_done.reshape(
        environment.shape[0], block_count, phys_size, block_rows * right_rows
    )
    bond_term = jnp.einsum(
        "wjsx,wst->wjtx", right_done, bond_terms, precision=lax.Precision.HIGHEST
    )
    bond_term = bond_term.reshape(environment.shape[0], block_count, block_rows * block_width)
    slot_table = (
        term_slot[:, None, :] == jnp.arange(slot_count, dtype=jnp.int32)[None, :, None]
    ).astype(jnp.float32)
    slot_buffer = jnp.einsum("wsj,wjx->sx", slot_table, bond_term, precision=lax.Precision.HIGHEST)
    slot_buffer = slot_buffer.reshape(slot_count, phys_size, block_rows, right_rows)
    slot_buffer = jnp.transpose(slot_buffer, (0, 2, 3, 1)).reshape(
        slot_count, block_rows, block_width
    )
    owners = slot_block.reshape(-1)
    selector = (owners[None, :] == jnp.arange(block_count, dtype=jnp.int32)[:, None]).astype(
        jnp.float32
    )
    column_width = block_width // lax.axis_size(("mpo", "rep"))
    column_start = lax.axis_index(("mpo", "rep")) * column_width
    own_part = lax.dynamic_slice_in_dim(vector_full, column_start, column_width, 2)
    shares = lax.psum_scatter(slot_buffer, ("mpo", "rep"), scatter_dimension=2, tiled=True)
    arrived = lax.all_to_all(shares, "blk", split_axis=0, concat_axis=0, tiled=True)
    result = jnp.einsum("ks,sbc->kbc", selector, arrived, precision=lax.Precision.HIGHEST)
    return (result + diagonal * own_part, own_part)


def plain_device(wavefunction, environment, bond_terms, diagonal, term_slot, slot_block):
    arranged = lax.all_to_all(environment, "blk", split_axis=1, concat_axis=2, tiled=True)
    entries = float(
        wavefunction.shape[0] * lax.axis_size("blk") * wavefunction.shape[1] * wavefunction.shape[2]
    )
    square_sum = lax.psum(jnp.sum(wavefunction * wavefunction), "blk")
    first_vector = wavefunction * lax.rsqrt(square_sum / entries + 1e-06)
    first_image, first_part = plain_apply(
        first_vector, arranged, bond_terms, term_slot, slot_block, diagonal
    )
    rayleigh = lax.psum(jnp.sum(first_part * first_image), ("blk", "mpo", "rep")) / entries
    residual = first_image - rayleigh * first_part
    resid_sum = lax.psum(jnp.sum(residual * residual), ("blk", "mpo", "rep"))
    second_vector = residual * lax.rsqrt(resid_sum / entries + 1e-06)
    second_full = lax.all_gather(second_vector, ("mpo", "rep"), axis=2, tiled=True)
    second_image, unused = plain_apply(
        second_full, arranged, bond_terms, term_slot, slot_block, diagonal
    )
    return (first_image, second_vector, second_image)


def split_two(x):
    high = x.astype(jnp.bfloat16)
    low = (x - high.astype(jnp.float32)).astype(jnp.bfloat16)
    return high, low


def lane_is_first(rows):
    return lax.broadcasted_iota(jnp.int32, (rows, LANES), 1) < LANES // 2


def micros(count):
    return pl.CostEstimate(flops=count * 1100000000, bytes_accessed=1 << 20, transcendentals=0)


def whole(*shape):
    return pl.BlockSpec(shape, lambda i, *_: (0,) * len(shape))


def pack_tile(x):
    return jnp.concatenate([x[:, :LANES], x[:, LANES:]], axis=0).T


def unpack_tile(x):
    upright = x.T
    return jnp.concatenate([upright[: LANES // 2], upright[LANES // 2 :]], axis=1)


def store_vector(parts, rows_of, put):
    first = lane_is_first(SUB)
    for pair in range(PHYS // 2):
        for part, row in zip(parts, rows_of):
            even = part[pl.ds(2 * pair, SUB, stride=PHYS), :]
            odd = part[pl.ds(2 * pair + 1, SUB, stride=PHYS), :]
            upper = jnp.where(first, even, pltpu.roll(odd, LANES // 2, 1))
            lower = jnp.where(first, pltpu.roll(even, LANES // 2, 1), odd)
            high, low = split_two(jnp.concatenate([upper, lower], axis=0))
            put(row, pair, high, low)


def pack_kernel(
    info_ref, wave_ref, own_wave_ref, diag_ref, vec_ref, own_ref, diag_out, start_ref, tiles
):
    half = LANES // 2
    for j in range(wave_ref.shape[0]):
        own_ref[j] = pack_tile(own_wave_ref[j])
        diag_out[j] = pack_tile(diag_ref[j])
        start_ref[j] = diag_out[j] * own_ref[j]
        for q in range(4):
            tiles[q, j] = pack_tile(wave_ref[j, :, 2 * LANES * q : 2 * LANES * (q + 1)])

        def put(row, pair, high, low):
            columns = slice(pair * LANES, (pair + 1) * LANES)
            vec_ref[j, row : row + 16, columns] = high
            vec_ref[j, row + half : row + half + 16, columns] = low

        store_vector([tiles.at[q, j] for q in range(4)], [16 * q for q in range(4)], put)


def pack(info, wavefunction, diagonal):
    blocks, rows, width = wavefunction.shape
    step = 2
    tile = pl.BlockSpec((step, LANES, LANES), lambda i, *_: (i, 0, 0))
    return pl.pallas_call(
        pack_kernel,
        grid_spec=pltpu.PrefetchScalarGridSpec(
            num_scalar_prefetch=1,
            grid=(blocks // step,),
            in_specs=[
                pl.BlockSpec((step, rows, width), lambda i, *_: (i, 0, 0)),
                pl.BlockSpec((step, rows, width // 4), lambda i, info: (i, 0, info[0])),
                pl.BlockSpec((step, rows, width // 4), lambda i, *_: (i, 0, 0)),
            ],
            out_specs=[pl.BlockSpec((step, LANES, width), lambda i, *_: (i, 0, 0))] + [tile] * 3,
            scratch_shapes=[pltpu.VMEM((4, step, LANES, LANES), jnp.float32)],
        ),
        out_shape=[
            jax.ShapeDtypeStruct((blocks, LANES, width), jnp.bfloat16),
        ]
        + [jax.ShapeDtypeStruct((blocks, LANES, LANES), jnp.float32)] * 3,
        compiler_params=pltpu.CompilerParams(vmem_limit_bytes=SMALL_VMEM),
        cost_estimate=micros(5),
        name="pack",
    )(info, wavefunction, wavefunction, diagonal)


def mixing_kernel(sizes, *refs):
    sources, outs = refs[:2], refs[2:]
    spread = (
        lax.broadcasted_iota(jnp.int32, (PHYS, LANES), 1) // SUB
        == lax.broadcasted_iota(jnp.int32, (PHYS, LANES), 0)
    ).astype(jnp.bfloat16)
    row = lax.broadcasted_iota(jnp.int32, (LANES, LANES), 0) // PHYS
    column = lax.broadcasted_iota(jnp.int32, (LANES, LANES), 1) % SUB
    same = row == column
    for n, source in enumerate(sources):
        start = 0
        for group, size in enumerate(sizes):
            out_ref = outs[n * len(sizes) + group]
            for at in range(size):
                for place, term in enumerate(split_two(source[start + at].T)):
                    wide = jnp.dot(term, spread, preferred_element_type=jnp.float32)
                    tall = jnp.concatenate([wide] * SUB, axis=0)
                    tall = jnp.where(same, tall, 0.0).astype(jnp.bfloat16)
                    rows = slice(place * LANES, (place + 1) * LANES)
                    out_ref[at, rows] = jnp.concatenate([tall, tall], axis=1)
            start += size


def mixing_operands(sources, sizes):
    out = pl.pallas_call(
        functools.partial(mixing_kernel, sizes),
        out_shape=[
            jax.ShapeDtypeStruct((size, 2 * LANES, 2 * LANES), jnp.bfloat16)
            for _ in sources
            for size in sizes
        ],
        compiler_params=pltpu.CompilerParams(vmem_limit_bytes=SMALL_VMEM),
        cost_estimate=micros(2),
        name="mixing",
    )(*sources)
    return [out[: len(sizes)], out[len(sizes) :]]


def own_operands_kernel(info_ref, *refs):
    pieces, (left_high, left_low, right_out, send, blocks_ref, upright_ref) = refs[:4], refs[4:]
    per, blocks, half, lanes = left_high.shape
    rows = half // 4
    wide = half // 2
    first = lane_is_first(half)
    first_wide = lane_is_first(wide)
    first_rows = lane_is_first(rows)
    mine_at = pl.multiple_of(half + info_ref[6] * wide, wide)
    theirs_at = pl.multiple_of(lanes - wide - info_ref[6] * wide, wide)
    for j in range(blocks):
        for w in range(per):
            for z in range(4):
                row = pl.multiple_of((info_ref[4] ^ z) * rows, rows)
                blocks_ref[w, j, pl.ds(row, rows), :] = pieces[z][w, j]
        for w in range(per):
            block = blocks_ref[w, j]
            upright_ref[w, j] = jnp.concatenate([block, block], axis=0).T
            turned = pltpu.roll(block, half, 1)
            high, low = split_two(jnp.where(first, block, turned))
            left_high[w, j] = high
            left_low[w, j] = low
            send[w, j, 0:wide] = jnp.where(first_wide, block[:wide], turned[wide:])
        for w in range(per):
            high, low = split_two(upright_ref[w, j, pl.ds(mine_at, wide), :])
            right_out[j, wide * w : wide * (w + 1), 0:lanes] = high
            right_out[j, wide * w : wide * (w + 1), lanes:] = low
            upper = upright_ref[w, j, pl.ds(theirs_at, rows), :]
            lower = upright_ref[w, j, pl.ds(theirs_at + rows, rows), :]
            send[w, j, wide : wide + rows] = jnp.where(first_rows, upper, lower)


def other_operands(sent, left_high, left_low, right_out, j):
    per, blocks, half, lanes = left_high.shape
    rows = half // 4
    wide = half // 2
    first = lane_is_first(wide)
    first_rows = lane_is_first(rows)
    for w in range(per):
        both = sent[w, j, 0:wide]
        turned = pltpu.roll(both, half, 1)
        full = jnp.concatenate(
            [jnp.where(first, both, turned), jnp.where(first, turned, both)], axis=0
        )
        high, low = split_two(full)
        left_high[w, j] = high
        left_low[w, j] = low
        both = sent[w, j, wide : wide + rows]
        turned = pltpu.roll(both, half, 1)
        full = jnp.concatenate(
            [jnp.where(first_rows, both, turned), jnp.where(first_rows, turned, both)], axis=0
        )
        high, low = split_two(full)
        right_out[j, wide * w : wide * (w + 1), 0:lanes] = high
        right_out[j, wide * w : wide * (w + 1), lanes:] = low


def operand_specs(per, step, half, lanes, at=0):
    return [
        pl.BlockSpec((per, step, half, lanes), lambda i, *_: (0, at + i, 0, 0)),
        pl.BlockSpec((per, step, half, lanes), lambda i, *_: (0, at + i, 0, 0)),
        pl.BlockSpec((step, per * 32, 2 * lanes), lambda i, *_: (at + i, 0, 0)),
    ]


def operand_shapes(per, blocks, half, lanes):
    return [
        jax.ShapeDtypeStruct((per, blocks, half, lanes), jnp.bfloat16),
        jax.ShapeDtypeStruct((per, blocks, half, lanes), jnp.bfloat16),
        jax.ShapeDtypeStruct((blocks, per * 32, 2 * lanes), jnp.bfloat16),
    ]


def cut_kernel(first, info_ref, source, *refs):
    outs, sems = refs[:4], refs[4]
    per = outs[0].shape[0]
    copies = []
    for k in range(4):
        part = source.at[pl.ds(first, per), info_ref[4] ^ k]
        copies.append(pltpu.make_async_copy(part, outs[k], sems.at[k]))
    for copy in copies:
        copy.start()
    for copy in copies:
        copy.wait()


def cut_pieces(info, by_owner, first, per):
    shape = jax.ShapeDtypeStruct((per,) + by_owner.shape[2:], jnp.float32)
    return pl.pallas_call(
        functools.partial(cut_kernel, first),
        grid_spec=pltpu.PrefetchScalarGridSpec(
            num_scalar_prefetch=1,
            grid=(1,),
            in_specs=[pl.BlockSpec(memory_space=pl.ANY)],
            out_specs=[pl.BlockSpec(memory_space=pl.ANY)] * 4,
            scratch_shapes=[pltpu.SemaphoreType.DMA((4,))],
        ),
        out_shape=[shape] * 4,
        compiler_params=pltpu.CompilerParams(vmem_limit_bytes=SMALL_VMEM),
        cost_estimate=micros(1),
        name="cut_pieces",
    )(info, *(in_hbm(by_owner) if first == 0 else [by_owner]))


def own_operands(info, pieces):
    per, blocks, rows, lanes = pieces[0].shape
    half = lanes // 2
    step = 4
    return pl.pallas_call(
        own_operands_kernel,
        grid_spec=pltpu.PrefetchScalarGridSpec(
            num_scalar_prefetch=1,
            grid=(blocks // step,),
            in_specs=[pl.BlockSpec((per, step, rows, lanes), lambda i, *_: (0, i, 0, 0))] * 4,
            out_specs=operand_specs(per, step, half, lanes)
            + [pl.BlockSpec((per, step, 3 * rows, lanes), lambda i, *_: (0, i, 0, 0))],
            scratch_shapes=[
                pltpu.VMEM((per, step, half, lanes), jnp.float32),
                pltpu.VMEM((per, step, lanes, lanes), jnp.float32),
            ],
        ),
        out_shape=operand_shapes(per, blocks, half, lanes)
        + [jax.ShapeDtypeStruct((per, blocks, 3 * rows, lanes), jnp.float32)],
        compiler_params=pltpu.CompilerParams(vmem_limit_bytes=SMALL_VMEM),
        cost_estimate=micros(12),
        name="own_operands",
    )(info, *pieces)


def apply_kernel(plan, info_ref, *refs):
    chunks, first_block, parts_given, sent_given, before_given, pieces = plan
    refs = list(refs)
    take = lambda n: [refs.pop(0) for _ in range(n)]
    slots = take(2)
    vector = take(4 if parts_given else 1)
    operands = [take(3) for _ in chunks[: -1 if sent_given else None]]
    sent = take(1)[0] if sent_given else None
    mixes = take(len(chunks))
    before = take(1)[0] if before_given else None
    outs = take(2 if pieces else 1)
    if sent_given:
        operands.append(take(3))
    scratch = take(2)
    vec, mid = scratch
    total_ref = take(1)[0] if pieces else outs[0]
    step = mid.shape[0]
    lanes, half = LANES, LANES // 2
    first = lane_is_first(SUB)
    first_half = lane_is_first(half)
    keep_first = jnp.where(first_half, 1.0, 0.0).astype(jnp.bfloat16)
    keep_second = jnp.where(first_half, 0.0, 1.0).astype(jnp.bfloat16)
    me = info_ref[4]

    if not before_given:
        total_ref[...] = jnp.zeros_like(total_ref)
    else:
        total_ref[...] = before[...]

    def right_side(j):
        if sent_given:
            other_operands(sent, *operands[-1], first_block + j)
        if parts_given:

            def put(row, pair, high, low):
                columns = slice(pair * lanes, (pair + 1) * lanes)
                vec[j, pl.ds(row, 16), columns] = high
                vec[j, pl.ds(row + half, 16), columns] = low

            rows_of = [pl.multiple_of(info_ref[g] * 16, 16) for g in range(4)]
            store_vector([x.at[pl.ds(j * lanes, lanes)] for x in vector], rows_of, put)
            source = vec[j]
        else:
            source = vector[0][first_block + j]
        source = jnp.concatenate([source, source], axis=0)
        at = 0
        for left_high, left_low, right in operands:
            count = right.shape[1]
            mid[j, at : at + count, :] = jnp.dot(
                right[first_block + j], source, preferred_element_type=jnp.float32
            )
            at += count

    def prepared(j, refs_of, w, row_of):
        left_high, left_low, right = refs_of
        tiles = []
        for part in range(2):
            row = row_of + part * 16
            for pair in range(PHYS // 2):
                columns = slice(pair * lanes, (pair + 1) * lanes)
                upper = mid[j, row : row + SUB, columns]
                lower = mid[j, row + SUB : row + 2 * SUB, columns]
                tiles.append(jnp.where(first, upper, pltpu.roll(lower, half, 1)))
                tiles.append(jnp.where(first, pltpu.roll(upper, half, 1), lower))
        t_high, t_low = split_two(jnp.concatenate(tiles, axis=0))
        lh, ll = left_high[w, first_block + j], left_low[w, first_block + j]
        wide_high = jnp.concatenate([lh * keep_first, lh * keep_second], axis=0)
        wide_low = jnp.concatenate([ll * keep_first, ll * keep_second], axis=0)
        weights = jnp.concatenate([wide_high, wide_low], axis=1)
        weights = jnp.concatenate([weights, weights], axis=0)
        return jnp.concatenate([t_high, t_low], axis=1), weights

    def mix_unit(mixing, w, z):
        z_high, z_low = [jnp.concatenate([x[:lanes], x[lanes:]], axis=1) for x in z]
        return jnp.dot(
            mixing[w],
            jnp.concatenate([z_high, z_low], axis=0),
            preferred_element_type=jnp.float32,
        )

    def add_up(j, table, bond, mixed):
        slot = table[bond, first_block + j]
        slot = ((slot >> 1) ^ me) * 2 + (slot & 1)
        for part in range(2):
            columns = slice(part * lanes, (part + 1) * lanes)
            total_ref[part, slot] += mixed[:lanes, columns] + mixed[lanes:, columns]

    bonds = []
    for (source, start), refs_of, mix in zip(chunks, operands, mixes):
        for w in range(mix.shape[0]):
            bonds.append((refs_of, mix, w, slots[source], start + w))
    right_side(0)
    units = [(j, at) for j in range(step) for at in range(len(bonds))]

    def prepare_unit(n):
        j, at = units[n]
        refs_of, mixing, w, table, bond = bonds[at]
        return prepared(j, refs_of, w, at * 32)

    ready = prepare_unit(0)
    waiting = None
    for n, (j, at) in enumerate(units):
        refs_of, mixing, w, table, bond = bonds[at]
        z = jnp.dot(*ready, preferred_element_type=jnp.float32)
        if j + 1 < step and at == len(bonds) // 3:
            right_side(j + 1)
        if n + 1 < len(units):
            ready = prepare_unit(n + 1)
        if waiting is not None:
            before_j, before_mixing, before_w, before_table, before_bond, before_z = waiting
            mixed = mix_unit(before_mixing, before_w, before_z)
        z = split_two(z[:, :lanes] + z[:, lanes:])
        if waiting is not None:
            add_up(before_j, before_table, before_bond, mixed)
        waiting = (j, mixing, w, table, bond, z)
    j, mixing, w, table, bond, z = waiting
    add_up(j, table, bond, mix_unit(mixing, w, z))

    if pieces:
        stats = jnp.zeros((SUB, lanes), jnp.float32)
        if parts_given:
            tail = vector[0].shape[0] - SUB
            stats = stacked_rows(*merged([x[tail:] for x in vector]))
        for out, part in ((outs[0], info_ref[5]), (outs[1], 1 - info_ref[5])):
            for k in range(4):
                for i in range(2):
                    out[k, i * lanes : (i + 1) * lanes] = total_ref[part, 2 * k + i]
                out[k, 2 * lanes :] = stats
            stats = jnp.zeros((SUB, lanes), jnp.float32)


def apply_bonds(info, slots, vector, chunks, operands, sent, mixes, before, pieces, half_of=None):
    blocks, half, lanes = operands[0][0].shape[1:]
    parts_given = half_of is not None
    step = 4 if parts_given else blocks
    arguments = list(vector) if parts_given else [vector]
    for made in operands:
        arguments += made
    if sent is not None:
        arguments.append(sent)
    arguments += mixes
    aliases = {}
    if before is not None:
        if not pieces:
            aliases[3 + len(arguments)] = 0
        arguments.append(before)
    counts = [mix.shape[0] for mix in mixes]
    shapes = [(4, 2 * lanes + SUB, lanes)] * 2 if pieces else [(2, 8, lanes, lanes)]
    out_shape = [jax.ShapeDtypeStruct(shape, jnp.float32) for shape in shapes]
    if sent is not None:
        out_shape += operand_shapes(counts[-1], blocks, half, lanes)
    scratch = [
        pltpu.VMEM((step if parts_given else 1, lanes, PHYS * half), jnp.bfloat16),
        pltpu.VMEM((step, sum(counts) * 32, PHYS * half), jnp.float32),
    ]
    if pieces:
        scratch.append(pltpu.VMEM((2, 8, lanes, lanes), jnp.float32))
    plan = (
        tuple(chunks), (half_of or 0) * step, parts_given, sent is not None, before is not None,
        pieces,
    )
    out = pl.pallas_call(
        functools.partial(apply_kernel, plan),
        in_specs=[pl.BlockSpec(memory_space=pltpu.SMEM)] * 3
        + [pl.BlockSpec(memory_space=pltpu.VMEM)] * len(arguments),
        out_specs=[pl.BlockSpec(memory_space=pltpu.VMEM)] * len(out_shape),
        scratch_shapes=scratch,
        out_shape=out_shape,
        input_output_aliases=aliases,
        compiler_params=pltpu.CompilerParams(vmem_limit_bytes=APPLY_VMEM),
        cost_estimate=micros(10 if parts_given else 1),
        name="apply_bonds",
    )(info, *slots, *arguments)
    return out[: len(shapes)], out[len(shapes) :]


def add_arrived(info_ref, owner_ref, arrived, total):
    for k in range(4):
        for i in range(2):
            rows = slice(i * LANES, (i + 1) * LANES)
            total[owner_ref[info_ref[4] ^ k, i]] += arrived[k][rows]


def stacked_rows(*rows):
    at = lax.broadcasted_iota(jnp.int32, (SUB, LANES), 0)
    tile = jnp.zeros((SUB, LANES), jnp.float32)
    for i, row in enumerate(rows):
        tile = jnp.where(at == i, row, tile)
    return tile


def merged(tiles):
    rows = [[tile[i : i + 1] for i in range(3)] for tile in tiles]
    cross = sum(row[0] for row in rows)
    square = sum(row[1] for row in rows)
    ratio = cross / jnp.maximum(square, TINY)
    apart = [
        (row[0] / jnp.maximum(row[1], TINY) - ratio) * jnp.sqrt(row[1]) for row in rows
    ]
    rest = sum(row[2] for row in rows) + sum(x * x for x in apart)
    return cross, square, rest


def image_kernel(
    info_ref, owner_ref, a3, a2, a1, a0, start_hbm, lower_ref, upper_ref, total, start_ref, sems
):
    blocks = total.shape[0]
    copies = [
        pltpu.make_async_copy(start_hbm.at[k], start_ref.at[k], sems.at[k]) for k in range(blocks)
    ]
    for copy in copies:
        copy.start()
    total[...] = jnp.zeros_like(total)
    add_arrived(info_ref, owner_ref, (a0, a1, a2, a3), total)
    for k in range(blocks):
        copies[k].wait()
        half = lower_ref if k < blocks // 2 else upper_ref
        at = k % (blocks // 2) * LANES
        half[at : at + LANES] = total[k] + start_ref[k]


def owner_image(info, owners, arrived, start):
    blocks = start.shape[0]
    shape = jax.ShapeDtypeStruct((blocks // 2 * LANES, LANES), jnp.float32)
    return pl.pallas_call(
        image_kernel,
        in_specs=[pl.BlockSpec(memory_space=pltpu.SMEM)] * 2
        + [pl.BlockSpec(memory_space=pltpu.VMEM)] * 4
        + [pl.BlockSpec(memory_space=pl.ANY)],
        out_specs=[pl.BlockSpec(memory_space=pltpu.VMEM)] * 2,
        scratch_shapes=[pltpu.VMEM(start.shape, jnp.float32)] * 2
        + [pltpu.SemaphoreType.DMA((blocks,))],
        out_shape=[shape, shape],
        compiler_params=pltpu.CompilerParams(vmem_limit_bytes=SMALL_VMEM),
        cost_estimate=micros(1),
        name="owner_image",
    )(info, owners, *arrived[::-1], *in_hbm(start))


def statistics_kernel(own_hbm, lower_ref, upper_ref, out_ref, own_ref, sem):
    copy = pltpu.make_async_copy(own_hbm, own_ref, sem)
    copy.start()
    rows = upper_ref.shape[0]
    out_ref[0:rows] = upper_ref[...]
    copy.wait()
    blocks = own_ref.shape[0]
    images = []
    for half in (lower_ref, upper_ref):
        images += [half.at[pl.ds(k * LANES, LANES)] for k in range(blocks // 2)]
    cross = jnp.zeros((LANES, LANES), jnp.float32)
    square = jnp.zeros((LANES, LANES), jnp.float32)
    for k in range(blocks):
        own = own_ref[k]
        cross += own * images[k][...]
        square += own * own
    cross = jnp.sum(cross, keepdims=True)
    square = jnp.sum(square, keepdims=True)
    ratio = cross / jnp.maximum(square, TINY)
    rest = jnp.zeros((LANES, LANES), jnp.float32)
    for k in range(blocks):
        apart = images[k][...] - ratio * own_ref[k]
        rest += apart * apart
    out_ref[rows:] = stacked_rows(cross, square, jnp.sum(rest, keepdims=True))


def with_statistics(own, lower, upper):
    return pl.pallas_call(
        statistics_kernel,
        in_specs=[pl.BlockSpec(memory_space=pl.ANY)]
        + [pl.BlockSpec(memory_space=pltpu.VMEM)] * 2,
        out_specs=pl.BlockSpec(memory_space=pltpu.VMEM),
        scratch_shapes=[pltpu.VMEM(own.shape, jnp.float32), pltpu.SemaphoreType.DMA],
        out_shape=jax.ShapeDtypeStruct((upper.shape[0] + SUB, LANES), jnp.float32),
        compiler_params=pltpu.CompilerParams(vmem_limit_bytes=SMALL_VMEM),
        cost_estimate=micros(3),
        name="statistics",
    )(*in_hbm(own), lower, upper)


def final_kernel(
    entries, info_ref, owner_ref, a3, a2, a1, a0, diag_ref, own_ref, lower_ref, upper_ref,
    first_ref, vector_ref, second_ref, total,
):
    arrived = (a0, a1, a2, a3)
    cross, square, rest = merged([ref[2 * LANES :] for ref in arrived])
    scale = lax.rsqrt(square / entries + 1e-06)
    rayleigh = scale * scale * (cross / entries)
    apart = (cross / jnp.maximum(square, TINY) - rayleigh) * jnp.sqrt(square)
    mean = scale * scale * ((rest + apart * apart) / entries)
    second_scale = scale * lax.rsqrt(mean + 1e-06)
    for k in range(total.shape[0]):
        at = k % (total.shape[0] // 2) * LANES
        image = (lower_ref if k < total.shape[0] // 2 else upper_ref)[at : at + LANES]
        total[k] = (diag_ref[k] - rayleigh) * image
        first_ref[k] = unpack_tile(scale * image)
        vector_ref[k] = unpack_tile(second_scale * (image - rayleigh * own_ref[k]))
    add_arrived(info_ref, owner_ref, arrived, total)
    for k in range(total.shape[0]):
        second_ref[k] = unpack_tile(second_scale * total[k])


def outputs(info, owners, arrived, diagonal, own, images, entries):
    blocks = diagonal.shape[0]
    shape = (blocks, LANES // 2, 2 * LANES)
    return pl.pallas_call(
        functools.partial(final_kernel, entries),
        grid_spec=pltpu.PrefetchScalarGridSpec(
            num_scalar_prefetch=2,
            grid=(1,),
            in_specs=[whole(*x.shape) for x in (*arrived, diagonal, own)]
            + [whole(blocks // 2 * LANES, LANES)] * 2,
            out_specs=[whole(*shape)] * 3,
            scratch_shapes=[pltpu.VMEM(diagonal.shape, jnp.float32)],
        ),
        out_shape=[jax.ShapeDtypeStruct(shape, jnp.float32)] * 3,
        compiler_params=pltpu.CompilerParams(vmem_limit_bytes=SMALL_VMEM),
        cost_estimate=micros(4),
        name="outputs",
    )(info, owners, *arrived[::-1], diagonal, own, *images)


def in_hbm(*arrays):
    return [pltpu.with_memory_space_constraint(x, pltpu.HBM) for x in arrays]


def partner(x, axis, k):
    size = lax.axis_size(axis)
    return lax.ppermute(x, axis, [(i, i ^ k) for i in range(size)])


def after(x, *others):
    return lax.optimization_barrier((x, *others))[0]


def gathered(x):
    across = partner(x, "mpo", 1)
    return [x, across, partner(x, "rep", 1), partner(across, "rep", 1)]


def everyone_of(pieces, axis):
    return [pieces[0]] + [partner(pieces[k], axis, k) for k in range(1, 4)]


def to_owners(mine, theirs):
    other = partner(theirs, "rep", 1)
    pieces = [mine[k] + other[k] for k in range(4)]
    return everyone_of(pieces, "blk")


def per_device(wavefunction, environment, bond_terms, diagonal, term_slot, slot_block):
    blocks, rows, width = wavefunction.shape
    zs = lax.axis_size("blk")
    mpo, rep, blk = lax.axis_index("mpo"), lax.axis_index("rep"), lax.axis_index("blk")
    place = 2 * mpo + rep
    info = jnp.stack([place, place ^ 2, place ^ 1, place ^ 3, blk, rep, mpo]).astype(jnp.int32)
    bonds = environment.shape[0]
    sizes = tuple(bonds * part // 6 for part in (2, 2, 2))
    firsts = tuple(sum(sizes[:group]) for group in range(len(sizes)))
    entries = float(blocks * zs * rows * width)

    vector, own, diagonal_packed, start = pack(info, wavefunction, diagonal)

    by_owner = environment.reshape(bonds, zs, blocks, rows // zs, 2 * rows)
    pieces = []
    for group in range(len(sizes)):
        cuts = list(cut_pieces(info, by_owner, firsts[group], sizes[group]))
        if group:
            cuts[1:] = [after(x, y) for x, y in zip(cuts[1:], pieces[-1][1:])]
        pieces.append(cuts[:1] + [partner(cuts[k], "blk", k) for k in range(1, 4)])
    pieces[0][1] = after(pieces[0][1], vector)
    other_terms = partner(after(bond_terms, pieces[0][1]), "mpo", 1)
    mixing = mixing_operands([bond_terms, other_terms], sizes)
    slots = [term_slot, partner(after(term_slot, pieces[0][1]), "mpo", 1)]

    made, sent = [], []
    total = None
    operands = []
    done = 0

    def apply_group(group, vector):
        out, other = apply_bonds(
            info, slots, vector, [(0, firsts[group]), (1, firsts[group])], [made[group]],
            partner(sent[group], "mpo", 1), [terms[group] for terms in mixing], total,
            group == len(sizes) - 1,
        )
        operands.extend([made[group], other])
        return out

    for group in range(len(sizes)):
        if group >= 2:
            total = apply_group(group - 2, after(vector, sent[group - 1]))[0]
            pieces[group][3] = after(pieces[group][3], total)
        if group < 1:
            pieces[group][1] = after(pieces[group][1], pieces[group + 1][1])
        *own_set, send = own_operands(info, pieces[group])
        made.append(own_set)
        sent.append(send)
    total = apply_group(len(sizes) - 2, after(vector, sent[-1]))[0]
    out = apply_group(len(sizes) - 1, vector)
    lower, upper = owner_image(info, slot_block, to_owners(*out), start)
    upper = with_statistics(own, lower, upper)

    chunks = [(source, first) for first in firsts for source in range(2)]
    mixes = [mixing[source][group] for group in range(len(sizes)) for source in range(2)]
    lower_parts = [lower, partner(lower, "mpo", 1), partner(lower, "rep", 1)]
    lower_parts.append(partner(after(lower_parts[1], upper), "rep", 1))
    across = partner(after(upper, lower_parts[1]), "mpo", 1)
    out, _ = apply_bonds(
        info, slots, lower_parts, chunks, operands, None, mixes, None, False, 0
    )
    upper_parts = [upper, across, partner(upper, "rep", 1)]
    upper_parts.append(partner(after(across, out[0]), "rep", 1))
    out, _ = apply_bonds(
        info, slots, upper_parts, chunks, operands, None, mixes, out[0], True, 1
    )
    return tuple(
        outputs(
            info, slot_block, to_owners(*out), diagonal_packed, own, (lower, upper), entries
        )
    )


def solution(mesh):
    packed = mesh.shape["mpo"] == 2 and mesh.shape["rep"] == 2 and mesh.shape["blk"] == 4
    return jax.shard_map(
        per_device if packed else plain_device,
        mesh=mesh,
        in_specs=(
            P(("grp", "blk"), None, None),
            P(("grp", "mpo", "rep"), None, "blk", None),
            P(("grp", "mpo", "rep"), None, None),
            P(("grp", "blk"), None, ("mpo", "rep")),
            P(("grp", "mpo", "rep"), "blk"),
            P("grp", "blk"),
        ),
        out_specs=(
            P(("grp", "blk"), None, ("mpo", "rep")),
            P(("grp", "blk"), None, ("mpo", "rep")),
            P(("grp", "blk"), None, ("mpo", "rep")),
        ),
        check_vma=False,
    )
```

```python
import functools

import jax
import jax.numpy as jnp
from jax import lax
from jax.experimental import pallas as pl
from jax.experimental.pallas import tpu as pltpu
from jax.sharding import PartitionSpec as P

LANES = 128
SUB = 8
PHYS = 16
TINY = 1e-30
SMALL_VMEM = 16 * 1024 * 1024
APPLY_VMEM = 16 * 1024 * 1024


def plain_apply(vector_full, environment, bond_terms, term_slot, slot_block, diagonal):
    block_count, block_rows, block_width = vector_full.shape
    phys_size = bond_terms.shape[-1]
    right_rows = block_width // phys_size
    slot_count = slot_block.shape[0] * slot_block.shape[1]
    blocks = vector_full.reshape(block_count, block_rows, right_rows, phys_size)
    ordered = jnp.transpose(blocks, (0, 3, 1, 2))
    left_env = environment[:, :, :, :block_rows]
    right_env = environment[:, :, :, block_rows:]
    left_done = jnp.einsum("wjab,jsac->wjsbc", left_env, ordered, precision=lax.Precision.HIGHEST)
    right_done = jnp.einsum(
        "wjsbc,wjcd->wjsbd", left_done, right_env, precision=lax.Precision.HIGHEST
    )
    right_done = right_done.reshape(
        environment.shape[0], block_count, phys_size, block_rows * right_rows
    )
    bond_term = jnp.einsum(
        "wjsx,wst->wjtx", right_done, bond_terms, precision=lax.Precision.HIGHEST
    )
    bond_term = bond_term.reshape(environment.shape[0], block_count, block_rows * block_width)
    slot_table = (
        term_slot[:, None, :] == jnp.arange(slot_count, dtype=jnp.int32)[None, :, None]
    ).astype(jnp.float32)
    slot_buffer = jnp.einsum("wsj,wjx->sx", slot_table, bond_term, precision=lax.Precision.HIGHEST)
    slot_buffer = slot_buffer.reshape(slot_count, phys_size, block_rows, right_rows)
    slot_buffer = jnp.transpose(slot_buffer, (0, 2, 3, 1)).reshape(
        slot_count, block_rows, block_width
    )
    owners = slot_block.reshape(-1)
    selector = (owners[None, :] == jnp.arange(block_count, dtype=jnp.int32)[:, None]).astype(
        jnp.float32
    )
    column_width = block_width // lax.axis_size(("mpo", "rep"))
    column_start = lax.axis_index(("mpo", "rep")) * column_width
    own_part = lax.dynamic_slice_in_dim(vector_full, column_start, column_width, 2)
    shares = lax.psum_scatter(slot_buffer, ("mpo", "rep"), scatter_dimension=2, tiled=True)
    arrived = lax.all_to_all(shares, "blk", split_axis=0, concat_axis=0, tiled=True)
    result = jnp.einsum("ks,sbc->kbc", selector, arrived, precision=lax.Precision.HIGHEST)
    return (result + diagonal * own_part, own_part)


def plain_device(wavefunction, environment, bond_terms, diagonal, term_slot, slot_block):
    arranged = lax.all_to_all(environment, "blk", split_axis=1, concat_axis=2, tiled=True)
    entries = float(
        wavefunction.shape[0] * lax.axis_size("blk") * wavefunction.shape[1] * wavefunction.shape[2]
    )
    square_sum = lax.psum(jnp.sum(wavefunction * wavefunction), "blk")
    first_vector = wavefunction * lax.rsqrt(square_sum / entries + 1e-06)
    first_image, first_part = plain_apply(
        first_vector, arranged, bond_terms, term_slot, slot_block, diagonal
    )
    rayleigh = lax.psum(jnp.sum(first_part * first_image), ("blk", "mpo", "rep")) / entries
    residual = first_image - rayleigh * first_part
    resid_sum = lax.psum(jnp.sum(residual * residual), ("blk", "mpo", "rep"))
    second_vector = residual * lax.rsqrt(resid_sum / entries + 1e-06)
    second_full = lax.all_gather(second_vector, ("mpo", "rep"), axis=2, tiled=True)
    second_image, unused = plain_apply(
        second_full, arranged, bond_terms, term_slot, slot_block, diagonal
    )
    return (first_image, second_vector, second_image)


def split_two(x):
    high = x.astype(jnp.bfloat16)
    low = (x - high.astype(jnp.float32)).astype(jnp.bfloat16)
    return high, low


def lane_is_first(rows):
    return lax.broadcasted_iota(jnp.int32, (rows, LANES), 1) < LANES // 2


def micros(count):
    return pl.CostEstimate(flops=count * 1100000000, bytes_accessed=1 << 20, transcendentals=0)


def whole(*shape):
    return pl.BlockSpec(shape, lambda i, *_: (0,) * len(shape))


def pack_tile(x):
    return jnp.concatenate([x[:, :LANES], x[:, LANES:]], axis=0).T


def unpack_tile(x):
    upright = x.T
    return jnp.concatenate([upright[: LANES // 2], upright[LANES // 2 :]], axis=1)


def store_vector(parts, rows_of, put):
    first = lane_is_first(SUB)
    for pair in range(PHYS // 2):
        for part, row in zip(parts, rows_of):
            even = part[pl.ds(2 * pair, SUB, stride=PHYS), :]
            odd = part[pl.ds(2 * pair + 1, SUB, stride=PHYS), :]
            upper = jnp.where(first, even, pltpu.roll(odd, LANES // 2, 1))
            lower = jnp.where(first, pltpu.roll(even, LANES // 2, 1), odd)
            high, low = split_two(jnp.concatenate([upper, lower], axis=0))
            put(row, pair, high, low)


def pack_kernel(info_ref, wave_ref, own_wave_ref, diag_ref, vec_ref, own_ref, diag_out, tiles):
    half = LANES // 2
    for j in range(wave_ref.shape[0]):
        own_ref[j] = pack_tile(own_wave_ref[j])
        diag_out[j] = pack_tile(diag_ref[j])
        for q in range(4):
            tiles[q, j] = pack_tile(wave_ref[j, :, 2 * LANES * q : 2 * LANES * (q + 1)])

        def put(row, pair, high, low):
            columns = slice(pair * LANES, (pair + 1) * LANES)
            vec_ref[j, row : row + 16, columns] = high
            vec_ref[j, row + half : row + half + 16, columns] = low

        store_vector([tiles.at[q, j] for q in range(4)], [16 * q for q in range(4)], put)


def pack(info, wavefunction, diagonal):
    blocks, rows, width = wavefunction.shape
    step = 2
    tile = pl.BlockSpec((step, LANES, LANES), lambda i, *_: (i, 0, 0))
    return pl.pallas_call(
        pack_kernel,
        grid_spec=pltpu.PrefetchScalarGridSpec(
            num_scalar_prefetch=1,
            grid=(blocks // step,),
            in_specs=[
                pl.BlockSpec((step, rows, width), lambda i, *_: (i, 0, 0)),
                pl.BlockSpec((step, rows, width // 4), lambda i, info: (i, 0, info[0])),
                pl.BlockSpec((step, rows, width // 4), lambda i, *_: (i, 0, 0)),
            ],
            out_specs=[pl.BlockSpec((step, LANES, width), lambda i, *_: (i, 0, 0))] + [tile] * 2,
            scratch_shapes=[pltpu.VMEM((4, step, LANES, LANES), jnp.float32)],
        ),
        out_shape=[
            jax.ShapeDtypeStruct((blocks, LANES, width), jnp.bfloat16),
        ]
        + [jax.ShapeDtypeStruct((blocks, LANES, LANES), jnp.float32)] * 2,
        compiler_params=pltpu.CompilerParams(vmem_limit_bytes=SMALL_VMEM),
        cost_estimate=micros(5),
        name="pack",
    )(info, wavefunction, wavefunction, diagonal)


def mixing_kernel(sizes, *refs):
    sources, outs = refs[:2], refs[2:]
    spread = (
        lax.broadcasted_iota(jnp.int32, (PHYS, LANES), 1) // SUB
        == lax.broadcasted_iota(jnp.int32, (PHYS, LANES), 0)
    ).astype(jnp.bfloat16)
    row = lax.broadcasted_iota(jnp.int32, (LANES, LANES), 0) // PHYS
    column = lax.broadcasted_iota(jnp.int32, (LANES, LANES), 1) % SUB
    same = row == column
    for n, source in enumerate(sources):
        start = 0
        for group, size in enumerate(sizes):
            out_ref = outs[n * len(sizes) + group]
            for at in range(size):
                for place, term in enumerate(split_two(source[start + at, 0:PHYS].T)):
                    wide = jnp.dot(term, spread, preferred_element_type=jnp.float32)
                    tall = jnp.concatenate([wide] * SUB, axis=0)
                    tall = jnp.where(same, tall, 0.0).astype(jnp.bfloat16)
                    rows = slice(place * LANES, (place + 1) * LANES)
                    out_ref[at, rows] = jnp.concatenate([tall, tall], axis=1)
            start += size


def mixing_operands(sources, sizes):
    out = pl.pallas_call(
        functools.partial(mixing_kernel, sizes),
        out_shape=[
            jax.ShapeDtypeStruct((size, 2 * LANES, 2 * LANES), jnp.bfloat16)
            for _ in sources
            for size in sizes
        ],
        compiler_params=pltpu.CompilerParams(vmem_limit_bytes=SMALL_VMEM),
        cost_estimate=micros(2),
        name="mixing",
    )(*sources)
    return [out[: len(sizes)], out[len(sizes) :]]


def own_operands_kernel(info_ref, *refs):
    pieces, (left_high, left_low, right_out, send, blocks_ref, upright_ref) = refs[:4], refs[4:]
    per, blocks, half, lanes = left_high.shape
    rows = half // 4
    wide = half // 2
    first = lane_is_first(half)
    first_wide = lane_is_first(wide)
    first_rows = lane_is_first(rows)
    mine_at = pl.multiple_of(half + info_ref[6] * wide, wide)
    theirs_at = pl.multiple_of(lanes - wide - info_ref[6] * wide, wide)
    for j in range(blocks):
        for w in range(per):
            for z in range(4):
                row = pl.multiple_of((info_ref[4] ^ z) * rows, rows)
                blocks_ref[w, j, pl.ds(row, rows), :] = pieces[z][w, j]
        for w in range(per):
            block = blocks_ref[w, j]
            upright_ref[w, j] = jnp.concatenate([block, block], axis=0).T
            turned = pltpu.roll(block, half, 1)
            high, low = split_two(jnp.where(first, block, turned))
            left_high[w, j] = high
            left_low[w, j] = low
            send[w, j, 0:wide] = jnp.where(first_wide, block[:wide], turned[wide:])
        for w in range(per):
            high, low = split_two(upright_ref[w, j, pl.ds(mine_at, wide), :])
            right_out[j, wide * w : wide * (w + 1), 0:lanes] = high
            right_out[j, wide * w : wide * (w + 1), lanes:] = low
            upper = upright_ref[w, j, pl.ds(theirs_at, rows), :]
            lower = upright_ref[w, j, pl.ds(theirs_at + rows, rows), :]
            send[w, j, wide : wide + rows] = jnp.where(first_rows, upper, lower)


def other_operands(sent, left_high, left_low, right_out, j):
    per, blocks, half, lanes = left_high.shape
    rows = half // 4
    wide = half // 2
    first = lane_is_first(wide)
    first_rows = lane_is_first(rows)
    for w in range(per):
        both = sent[w, j, 0:wide]
        turned = pltpu.roll(both, half, 1)
        full = jnp.concatenate(
            [jnp.where(first, both, turned), jnp.where(first, turned, both)], axis=0
        )
        high, low = split_two(full)
        left_high[w, j] = high
        left_low[w, j] = low
        both = sent[w, j, wide : wide + rows]
        turned = pltpu.roll(both, half, 1)
        full = jnp.concatenate(
            [jnp.where(first_rows, both, turned), jnp.where(first_rows, turned, both)], axis=0
        )
        high, low = split_two(full)
        right_out[j, wide * w : wide * (w + 1), 0:lanes] = high
        right_out[j, wide * w : wide * (w + 1), lanes:] = low


def operand_specs(per, step, half, lanes, at=0):
    return [
        pl.BlockSpec((per, step, half, lanes), lambda i, *_: (0, at + i, 0, 0)),
        pl.BlockSpec((per, step, half, lanes), lambda i, *_: (0, at + i, 0, 0)),
        pl.BlockSpec((step, per * 32, 2 * lanes), lambda i, *_: (at + i, 0, 0)),
    ]


def operand_shapes(per, blocks, half, lanes):
    return [
        jax.ShapeDtypeStruct((per, blocks, half, lanes), jnp.bfloat16),
        jax.ShapeDtypeStruct((per, blocks, half, lanes), jnp.bfloat16),
        jax.ShapeDtypeStruct((blocks, per * 32, 2 * lanes), jnp.bfloat16),
    ]


def cut_kernel(first, info_ref, source, *refs):
    outs, sems = refs[:4], refs[4]
    per = outs[0].shape[0]
    copies = []
    for k in range(4):
        part = source.at[pl.ds(first, per), info_ref[4] ^ k]
        copies.append(pltpu.make_async_copy(part, outs[k], sems.at[k]))
    for copy in copies:
        copy.start()
    for copy in copies:
        copy.wait()


def cut_pieces(info, by_owner, first, per):
    shape = jax.ShapeDtypeStruct((per,) + by_owner.shape[2:], jnp.float32)
    return pl.pallas_call(
        functools.partial(cut_kernel, first),
        grid_spec=pltpu.PrefetchScalarGridSpec(
            num_scalar_prefetch=1,
            grid=(1,),
            in_specs=[pl.BlockSpec(memory_space=pl.ANY)],
            out_specs=[pl.BlockSpec(memory_space=pl.ANY)] * 4,
            scratch_shapes=[pltpu.SemaphoreType.DMA((4,))],
        ),
        out_shape=[shape] * 4,
        compiler_params=pltpu.CompilerParams(vmem_limit_bytes=SMALL_VMEM),
        cost_estimate=micros(1),
        name="cut_pieces",
    )(info, *(in_hbm(by_owner) if first == 0 else [by_owner]))


def own_operands(info, pieces):
    per, blocks, rows, lanes = pieces[0].shape
    half = lanes // 2
    step = 4
    return pl.pallas_call(
        own_operands_kernel,
        grid_spec=pltpu.PrefetchScalarGridSpec(
            num_scalar_prefetch=1,
            grid=(blocks // step,),
            in_specs=[pl.BlockSpec((per, step, rows, lanes), lambda i, *_: (0, i, 0, 0))] * 4,
            out_specs=operand_specs(per, step, half, lanes)
            + [pl.BlockSpec((per, step, 3 * rows, lanes), lambda i, *_: (0, i, 0, 0))],
            scratch_shapes=[
                pltpu.VMEM((per, step, half, lanes), jnp.float32),
                pltpu.VMEM((per, step, lanes, lanes), jnp.float32),
            ],
        ),
        out_shape=operand_shapes(per, blocks, half, lanes)
        + [jax.ShapeDtypeStruct((per, blocks, 3 * rows, lanes), jnp.float32)],
        compiler_params=pltpu.CompilerParams(vmem_limit_bytes=SMALL_VMEM),
        cost_estimate=micros(12),
        name="own_operands",
    )(info, *pieces)


def apply_kernel(plan, info_ref, *refs):
    chunks, first_block, parts_given, sent_given, before_given, pieces = plan
    refs = list(refs)
    take = lambda n: [refs.pop(0) for _ in range(n)]
    slots = take(2)
    vector = take(4 if parts_given else 1)
    operands = [take(3) for _ in chunks[: -1 if sent_given else None]]
    sent = take(1)[0] if sent_given else None
    mixes = take(len(chunks))
    before = take(1)[0] if before_given else None
    outs = take(2 if pieces else 1)
    made = take(3) if sent_given else []
    scratch = take(2)
    vec, mid = scratch
    total_ref = take(1)[0] if pieces else outs[0]
    kept = []
    if sent_given:
        operands.append(take(3))
        sems = take(1)[0]
        kept = [
            pltpu.make_async_copy(operands[-1][i], made[i], sems.at[i]) for i in range(3)
        ]
    step = mid.shape[0]
    lanes, half = LANES, LANES // 2
    first = lane_is_first(SUB)
    first_half = lane_is_first(half)
    keep_first = jnp.where(first_half, 1.0, 0.0).astype(jnp.bfloat16)
    keep_second = jnp.where(first_half, 0.0, 1.0).astype(jnp.bfloat16)
    me = info_ref[4]

    if not before_given:
        total_ref[...] = jnp.zeros_like(total_ref)
    else:
        total_ref[...] = before[...]

    def right_side(j):
        if sent_given:
            other_operands(sent, *operands[-1], first_block + j)
        if parts_given:

            def put(row, pair, high, low):
                columns = slice(pair * lanes, (pair + 1) * lanes)
                vec[j, pl.ds(row, 16), columns] = high
                vec[j, pl.ds(row + half, 16), columns] = low

            rows_of = [pl.multiple_of(info_ref[g] * 16, 16) for g in range(4)]
            store_vector([x.at[pl.ds(j * lanes, lanes)] for x in vector], rows_of, put)
            source = vec[j]
        else:
            source = vector[0][first_block + j]
        source = jnp.concatenate([source, source], axis=0)
        at = 0
        for left_high, left_low, right in operands:
            count = right.shape[1]
            mid[j, at : at + count, :] = jnp.dot(
                right[first_block + j], source, preferred_element_type=jnp.float32
            )
            at += count

    def prepared(j, refs_of, w, row_of):
        left_high, left_low, right = refs_of
        tiles = []
        for part in range(2):
            row = row_of + part * 16
            for pair in range(PHYS // 2):
                columns = slice(pair * lanes, (pair + 1) * lanes)
                upper = mid[j, row : row + SUB, columns]
                lower = mid[j, row + SUB : row + 2 * SUB, columns]
                tiles.append(jnp.where(first, upper, pltpu.roll(lower, half, 1)))
                tiles.append(jnp.where(first, pltpu.roll(upper, half, 1), lower))
        t_high, t_low = split_two(jnp.concatenate(tiles, axis=0))
        lh, ll = left_high[w, first_block + j], left_low[w, first_block + j]
        wide_high = jnp.concatenate([lh * keep_first, lh * keep_second], axis=0)
        wide_low = jnp.concatenate([ll * keep_first, ll * keep_second], axis=0)
        weights = jnp.concatenate([wide_high, wide_low], axis=1)
        weights = jnp.concatenate([weights, weights], axis=0)
        return jnp.concatenate([t_high, t_low], axis=1), weights

    def mix_unit(mixing, w, z):
        z_high, z_low = [jnp.concatenate([x[:lanes], x[lanes:]], axis=1) for x in z]
        return jnp.dot(
            mixing[w],
            jnp.concatenate([z_high, z_low], axis=0),
            preferred_element_type=jnp.float32,
        )

    def add_up(j, table, bond, mixed):
        slot = table[bond, first_block + j]
        slot = ((slot >> 1) ^ me) * 2 + (slot & 1)
        for part in range(2):
            columns = slice(part * lanes, (part + 1) * lanes)
            total_ref[part, slot] += mixed[:lanes, columns] + mixed[lanes:, columns]

    bonds = []
    for (source, start), refs_of, mix in zip(chunks, operands, mixes):
        for w in range(mix.shape[0]):
            bonds.append((refs_of, mix, w, slots[source], start + w))
    right_side(0)
    units = [(j, at) for j in range(step) for at in range(len(bonds))]

    def prepare_unit(n):
        j, at = units[n]
        refs_of, mixing, w, table, bond = bonds[at]
        return prepared(j, refs_of, w, at * 32)

    ready = prepare_unit(0)
    waiting = None
    for n, (j, at) in enumerate(units):
        refs_of, mixing, w, table, bond = bonds[at]
        z = jnp.dot(*ready, preferred_element_type=jnp.float32)
        if j + 1 < step and at == len(bonds) // 3:
            right_side(j + 1)
            if j + 2 == step:
                for copy in kept:
                    copy.start()
        if n + 1 < len(units):
            ready = prepare_unit(n + 1)
        if waiting is not None:
            before_j, before_mixing, before_w, before_table, before_bond, before_z = waiting
            mixed = mix_unit(before_mixing, before_w, before_z)
        z = split_two(z[:, :lanes] + z[:, lanes:])
        if waiting is not None:
            add_up(before_j, before_table, before_bond, mixed)
        waiting = (j, mixing, w, table, bond, z)
    j, mixing, w, table, bond, z = waiting
    add_up(j, table, bond, mix_unit(mixing, w, z))
    for copy in kept:
        copy.wait()

    if pieces:
        stats = jnp.zeros((SUB, lanes), jnp.float32)
        if parts_given:
            tail = vector[0].shape[0] - SUB
            stats = stacked_rows(*merged([x[tail:] for x in vector]))
        for out, part in ((outs[0], info_ref[5]), (outs[1], 1 - info_ref[5])):
            for k in range(4):
                for i in range(2):
                    out[k, i * lanes : (i + 1) * lanes] = total_ref[part, 2 * k + i]
                out[k, 2 * lanes :] = stats
            stats = jnp.zeros((SUB, lanes), jnp.float32)


def apply_bonds(info, slots, vector, chunks, operands, sent, mixes, before, pieces, half_of=None):
    blocks, half, lanes = operands[0][0].shape[1:]
    parts_given = half_of is not None
    step = 4 if parts_given else blocks
    arguments = list(vector) if parts_given else [vector]
    for made in operands:
        arguments += made
    if sent is not None:
        arguments.append(sent)
    arguments += mixes
    aliases = {}
    if before is not None:
        if not pieces:
            aliases[3 + len(arguments)] = 0
        arguments.append(before)
    counts = [mix.shape[0] for mix in mixes]
    shapes = [(4, 2 * lanes + SUB, lanes)] * 2 if pieces else [(2, 8, lanes, lanes)]
    out_shape = [jax.ShapeDtypeStruct(shape, jnp.float32) for shape in shapes]
    if sent is not None:
        out_shape += operand_shapes(counts[-1], blocks, half, lanes)
    scratch = [
        pltpu.VMEM((step if parts_given else 1, lanes, PHYS * half), jnp.bfloat16),
        pltpu.VMEM((step, sum(counts) * 32, PHYS * half), jnp.float32),
    ]
    if pieces:
        scratch.append(pltpu.VMEM((2, 8, lanes, lanes), jnp.float32))
    out_specs = [pl.BlockSpec(memory_space=pltpu.VMEM)] * len(shapes)
    if sent is not None:
        out_specs += [pl.BlockSpec(memory_space=pltpu.HBM)] * 3
        scratch += [pltpu.VMEM(x.shape, x.dtype) for x in out_shape[len(shapes) :]]
        scratch.append(pltpu.SemaphoreType.DMA((3,)))
    plan = (
        tuple(chunks), (half_of or 0) * step, parts_given, sent is not None, before is not None,
        pieces,
    )
    out = pl.pallas_call(
        functools.partial(apply_kernel, plan),
        in_specs=[pl.BlockSpec(memory_space=pltpu.SMEM)] * 3
        + [pl.BlockSpec(memory_space=pltpu.VMEM)] * len(arguments),
        out_specs=out_specs,
        scratch_shapes=scratch,
        out_shape=out_shape,
        input_output_aliases=aliases,
        compiler_params=pltpu.CompilerParams(vmem_limit_bytes=APPLY_VMEM),
        cost_estimate=micros(10 if parts_given else 1),
        name="apply_bonds",
    )(info, *slots, *arguments)
    return out[: len(shapes)], out[len(shapes) :]


def add_arrived(info_ref, owner_ref, arrived, total):
    for k in range(4):
        for i in range(2):
            rows = slice(i * LANES, (i + 1) * LANES)
            total[owner_ref[info_ref[4] ^ k, i]] += arrived[k][rows]


def stacked_rows(*rows):
    at = lax.broadcasted_iota(jnp.int32, (SUB, LANES), 0)
    tile = jnp.zeros((SUB, LANES), jnp.float32)
    for i, row in enumerate(rows):
        tile = jnp.where(at == i, row, tile)
    return tile


def merged(tiles):
    rows = [[tile[i : i + 1] for i in range(3)] for tile in tiles]
    cross = sum(row[0] for row in rows)
    square = sum(row[1] for row in rows)
    ratio = cross / jnp.maximum(square, TINY)
    apart = [
        (row[0] / jnp.maximum(row[1], TINY) - ratio) * jnp.sqrt(row[1]) for row in rows
    ]
    rest = sum(row[2] for row in rows) + sum(x * x for x in apart)
    return cross, square, rest


def image_kernel(info_ref, owner_ref, a3, a2, a1, a0, start_ref, lower_ref, upper_ref, total):
    total[...] = start_ref[...]
    add_arrived(info_ref, owner_ref, (a0, a1, a2, a3), total)
    blocks = total.shape[0]
    for k in range(blocks):
        half = lower_ref if k < blocks // 2 else upper_ref
        at = k % (blocks // 2) * LANES
        half[at : at + LANES] = total[k]


def owner_image(info, owners, arrived, start):
    blocks = start.shape[0]
    shape = jax.ShapeDtypeStruct((blocks // 2 * LANES, LANES), jnp.float32)
    return pl.pallas_call(
        image_kernel,
        in_specs=[pl.BlockSpec(memory_space=pltpu.SMEM)] * 2
        + [pl.BlockSpec(memory_space=pltpu.VMEM)] * 5,
        out_specs=[pl.BlockSpec(memory_space=pltpu.VMEM)] * 2,
        scratch_shapes=[pltpu.VMEM(start.shape, jnp.float32)],
        out_shape=[shape, shape],
        compiler_params=pltpu.CompilerParams(vmem_limit_bytes=SMALL_VMEM),
        cost_estimate=micros(1),
        name="owner_image",
    )(info, owners, *arrived[::-1], start)


def statistics_kernel(own_hbm, lower_ref, upper_ref, out_ref, own_ref, sem):
    copy = pltpu.make_async_copy(own_hbm, own_ref, sem)
    copy.start()
    rows = upper_ref.shape[0]
    out_ref[0:rows] = upper_ref[...]
    copy.wait()
    blocks = own_ref.shape[0]
    images = []
    for half in (lower_ref, upper_ref):
        images += [half.at[pl.ds(k * LANES, LANES)] for k in range(blocks // 2)]
    cross = jnp.zeros((LANES, LANES), jnp.float32)
    square = jnp.zeros((LANES, LANES), jnp.float32)
    for k in range(blocks):
        own = own_ref[k]
        cross += own * images[k][...]
        square += own * own
    cross = jnp.sum(cross, keepdims=True)
    square = jnp.sum(square, keepdims=True)
    ratio = cross / jnp.maximum(square, TINY)
    rest = jnp.zeros((LANES, LANES), jnp.float32)
    for k in range(blocks):
        apart = images[k][...] - ratio * own_ref[k]
        rest += apart * apart
    out_ref[rows:] = stacked_rows(cross, square, jnp.sum(rest, keepdims=True))


def with_statistics(own, lower, upper):
    return pl.pallas_call(
        statistics_kernel,
        in_specs=[pl.BlockSpec(memory_space=pl.ANY)]
        + [pl.BlockSpec(memory_space=pltpu.VMEM)] * 2,
        out_specs=pl.BlockSpec(memory_space=pltpu.VMEM),
        scratch_shapes=[pltpu.VMEM(own.shape, jnp.float32), pltpu.SemaphoreType.DMA],
        out_shape=jax.ShapeDtypeStruct((upper.shape[0] + SUB, LANES), jnp.float32),
        compiler_params=pltpu.CompilerParams(vmem_limit_bytes=SMALL_VMEM),
        cost_estimate=micros(3),
        name="statistics",
    )(*in_hbm(own), lower, upper)


def final_kernel(
    entries, info_ref, owner_ref, a3, a2, a1, a0, diag_ref, own_ref, lower_ref, upper_ref,
    first_ref, vector_ref, second_ref, total,
):
    arrived = (a0, a1, a2, a3)
    cross, square, rest = merged([ref[2 * LANES :] for ref in arrived])
    scale = lax.rsqrt(square / entries + 1e-06)
    rayleigh = scale * scale * (cross / entries)
    apart = (cross / jnp.maximum(square, TINY) - rayleigh) * jnp.sqrt(square)
    mean = scale * scale * ((rest + apart * apart) / entries)
    second_scale = scale * lax.rsqrt(mean + 1e-06)
    for k in range(total.shape[0]):
        at = k % (total.shape[0] // 2) * LANES
        image = (lower_ref if k < total.shape[0] // 2 else upper_ref)[at : at + LANES]
        total[k] = (diag_ref[k] - rayleigh) * image
        first_ref[k] = unpack_tile(scale * image)
        vector_ref[k] = unpack_tile(second_scale * (image - rayleigh * own_ref[k]))
    add_arrived(info_ref, owner_ref, arrived, total)
    for k in range(total.shape[0]):
        second_ref[k] = unpack_tile(second_scale * total[k])


def outputs(info, owners, arrived, diagonal, own, images, entries):
    blocks = diagonal.shape[0]
    shape = (blocks, LANES // 2, 2 * LANES)
    return pl.pallas_call(
        functools.partial(final_kernel, entries),
        grid_spec=pltpu.PrefetchScalarGridSpec(
            num_scalar_prefetch=2,
            grid=(1,),
            in_specs=[whole(*x.shape) for x in (*arrived, diagonal, own)]
            + [whole(blocks // 2 * LANES, LANES)] * 2,
            out_specs=[whole(*shape)] * 3,
            scratch_shapes=[pltpu.VMEM(diagonal.shape, jnp.float32)],
        ),
        out_shape=[jax.ShapeDtypeStruct(shape, jnp.float32)] * 3,
        compiler_params=pltpu.CompilerParams(vmem_limit_bytes=SMALL_VMEM),
        cost_estimate=micros(4),
        name="outputs",
    )(info, owners, *arrived[::-1], diagonal, own, *images)


def in_hbm(*arrays):
    return [pltpu.with_memory_space_constraint(x, pltpu.HBM) for x in arrays]


def partner(x, axis, k):
    size = lax.axis_size(axis)
    return lax.ppermute(x, axis, [(i, i ^ k) for i in range(size)])


def after(x, *others):
    return lax.optimization_barrier((x, *others))[0]


def gathered(x):
    across = partner(x, "mpo", 1)
    return [x, across, partner(x, "rep", 1), partner(across, "rep", 1)]


def everyone_of(pieces, axis):
    return [pieces[0]] + [partner(pieces[k], axis, k) for k in range(1, 4)]


def to_owners(mine, theirs):
    other = partner(theirs, "rep", 1)
    pieces = [mine[k] + other[k] for k in range(4)]
    return everyone_of(pieces, "blk")


def per_device(wavefunction, environment, bond_terms, diagonal, term_slot, slot_block):
    blocks, rows, width = wavefunction.shape
    zs = lax.axis_size("blk")
    mpo, rep, blk = lax.axis_index("mpo"), lax.axis_index("rep"), lax.axis_index("blk")
    place = 2 * mpo + rep
    info = jnp.stack([place, place ^ 2, place ^ 1, place ^ 3, blk, rep, mpo]).astype(jnp.int32)
    bonds = environment.shape[0]
    sizes = tuple(bonds * part // 6 for part in (2, 2, 2))
    firsts = tuple(sum(sizes[:group]) for group in range(len(sizes)))
    entries = float(blocks * zs * rows * width)

    vector, own, diagonal_packed = pack(info, wavefunction, diagonal)

    by_owner = environment.reshape(bonds, zs, blocks, rows // zs, 2 * rows)
    pieces = []
    for group in range(len(sizes)):
        cuts = list(cut_pieces(info, by_owner, firsts[group], sizes[group]))
        if group:
            cuts[1:] = [after(x, y) for x, y in zip(cuts[1:], pieces[-1][1:])]
        pieces.append(cuts[:1] + [partner(cuts[k], "blk", k) for k in range(1, 4)])
    pieces[0][1] = after(pieces[0][1], vector)
    phys = bond_terms.shape[-1]
    table = jnp.pad(term_slot.astype(jnp.float32), ((0, 0), (0, phys - blocks)))
    tables = jnp.pad(table[:, None], ((0, 0), (0, SUB - 1), (0, 0)))
    both = jnp.concatenate([bond_terms, tables], axis=1)
    other_terms = partner(after(both, pieces[0][1]), "mpo", 1)
    mixing = mixing_operands([bond_terms, other_terms], sizes)
    slots = [term_slot, other_terms[:, phys, :blocks].astype(jnp.int32)]

    made, sent = [], []
    total = None
    operands = []
    done = 0

    def apply_group(group, vector):
        out, other = apply_bonds(
            info, slots, vector, [(0, firsts[group]), (1, firsts[group])], [made[group]],
            partner(sent[group], "mpo", 1), [terms[group] for terms in mixing], total,
            group == len(sizes) - 1,
        )
        operands.extend([made[group], other])
        return out

    for group in range(len(sizes)):
        if group >= 2:
            total = apply_group(group - 2, after(vector, sent[group - 1]))[0]
            pieces[group][3] = after(pieces[group][3], total)
        if group < 1:
            pieces[group][1] = after(pieces[group][1], pieces[group + 1][1])
        *own_set, send = own_operands(info, pieces[group])
        made.append(own_set)
        sent.append(send)
    total = apply_group(len(sizes) - 2, after(vector, sent[-1]))[0]
    out = apply_group(len(sizes) - 1, vector)
    arrived = to_owners(*out)
    start = after(diagonal_packed, arrived[0]) * own
    lower, upper = owner_image(info, slot_block, arrived, start)
    upper = with_statistics(own, lower, upper)

    chunks = [(source, first) for first in firsts for source in range(2)]
    mixes = [mixing[source][group] for group in range(len(sizes)) for source in range(2)]
    lower_parts = [lower, partner(lower, "mpo", 1), partner(lower, "rep", 1)]
    lower_parts.append(partner(after(lower_parts[1], upper), "rep", 1))
    across = partner(after(upper, lower_parts[1]), "mpo", 1)
    out, _ = apply_bonds(
        info, slots, lower_parts, chunks, operands, None, mixes, None, False, 0
    )
    upper_parts = [upper, across, partner(upper, "rep", 1)]
    upper_parts.append(partner(after(across, out[0]), "rep", 1))
    out, _ = apply_bonds(
        info, slots, upper_parts, chunks, operands, None, mixes, out[0], True, 1
    )
    return tuple(
        outputs(
            info, slot_block, to_owners(*out), diagonal_packed, own, (lower, upper), entries
        )
    )


def solution(mesh):
    packed = mesh.shape["mpo"] == 2 and mesh.shape["rep"] == 2 and mesh.shape["blk"] == 4
    return jax.shard_map(
        per_device if packed else plain_device,
        mesh=mesh,
        in_specs=(
            P(("grp", "blk"), None, None),
            P(("grp", "mpo", "rep"), None, "blk", None),
            P(("grp", "mpo", "rep"), None, None),
            P(("grp", "blk"), None, ("mpo", "rep")),
            P(("grp", "mpo", "rep"), "blk"),
            P("grp", "blk"),
        ),
        out_specs=(
            P(("grp", "blk"), None, ("mpo", "rep")),
            P(("grp", "blk"), None, ("mpo", "rep")),
            P(("grp", "blk"), None, ("mpo", "rep")),
        ),
        check_vma=False,
    )
```

```python
import functools

import jax
import jax.numpy as jnp
from jax import lax
from jax.experimental import pallas as pl
from jax.experimental.pallas import tpu as pltpu
from jax.sharding import PartitionSpec as P

LANES = 128
SUB = 8
PHYS = 16
TINY = 1e-30
SMALL_VMEM = 16 * 1024 * 1024
APPLY_VMEM = 16 * 1024 * 1024


def plain_apply(vector_full, environment, bond_terms, term_slot, slot_block, diagonal):
    block_count, block_rows, block_width = vector_full.shape
    phys_size = bond_terms.shape[-1]
    right_rows = block_width // phys_size
    slot_count = slot_block.shape[0] * slot_block.shape[1]
    blocks = vector_full.reshape(block_count, block_rows, right_rows, phys_size)
    ordered = jnp.transpose(blocks, (0, 3, 1, 2))
    left_env = environment[:, :, :, :block_rows]
    right_env = environment[:, :, :, block_rows:]
    left_done = jnp.einsum("wjab,jsac->wjsbc", left_env, ordered, precision=lax.Precision.HIGHEST)
    right_done = jnp.einsum(
        "wjsbc,wjcd->wjsbd", left_done, right_env, precision=lax.Precision.HIGHEST
    )
    right_done = right_done.reshape(
        environment.shape[0], block_count, phys_size, block_rows * right_rows
    )
    bond_term = jnp.einsum(
        "wjsx,wst->wjtx", right_done, bond_terms, precision=lax.Precision.HIGHEST
    )
    bond_term = bond_term.reshape(environment.shape[0], block_count, block_rows * block_width)
    slot_table = (
        term_slot[:, None, :] == jnp.arange(slot_count, dtype=jnp.int32)[None, :, None]
    ).astype(jnp.float32)
    slot_buffer = jnp.einsum("wsj,wjx->sx", slot_table, bond_term, precision=lax.Precision.HIGHEST)
    slot_buffer = slot_buffer.reshape(slot_count, phys_size, block_rows, right_rows)
    slot_buffer = jnp.transpose(slot_buffer, (0, 2, 3, 1)).reshape(
        slot_count, block_rows, block_width
    )
    owners = slot_block.reshape(-1)
    selector = (owners[None, :] == jnp.arange(block_count, dtype=jnp.int32)[:, None]).astype(
        jnp.float32
    )
    column_width = block_width // lax.axis_size(("mpo", "rep"))
    column_start = lax.axis_index(("mpo", "rep")) * column_width
    own_part = lax.dynamic_slice_in_dim(vector_full, column_start, column_width, 2)
    shares = lax.psum_scatter(slot_buffer, ("mpo", "rep"), scatter_dimension=2, tiled=True)
    arrived = lax.all_to_all(shares, "blk", split_axis=0, concat_axis=0, tiled=True)
    result = jnp.einsum("ks,sbc->kbc", selector, arrived, precision=lax.Precision.HIGHEST)
    return (result + diagonal * own_part, own_part)


def plain_device(wavefunction, environment, bond_terms, diagonal, term_slot, slot_block):
    arranged = lax.all_to_all(environment, "blk", split_axis=1, concat_axis=2, tiled=True)
    entries = float(
        wavefunction.shape[0] * lax.axis_size("blk") * wavefunction.shape[1] * wavefunction.shape[2]
    )
    square_sum = lax.psum(jnp.sum(wavefunction * wavefunction), "blk")
    first_vector = wavefunction * lax.rsqrt(square_sum / entries + 1e-06)
    first_image, first_part = plain_apply(
        first_vector, arranged, bond_terms, term_slot, slot_block, diagonal
    )
    rayleigh = lax.psum(jnp.sum(first_part * first_image), ("blk", "mpo", "rep")) / entries
    residual = first_image - rayleigh * first_part
    resid_sum = lax.psum(jnp.sum(residual * residual), ("blk", "mpo", "rep"))
    second_vector = residual * lax.rsqrt(resid_sum / entries + 1e-06)
    second_full = lax.all_gather(second_vector, ("mpo", "rep"), axis=2, tiled=True)
    second_image, unused = plain_apply(
        second_full, arranged, bond_terms, term_slot, slot_block, diagonal
    )
    return (first_image, second_vector, second_image)


def split_two(x):
    high = x.astype(jnp.bfloat16)
    low = (x - high.astype(jnp.float32)).astype(jnp.bfloat16)
    return high, low


def lane_is_first(rows):
    return lax.broadcasted_iota(jnp.int32, (rows, LANES), 1) < LANES // 2


def micros(count):
    return pl.CostEstimate(flops=count * 1100000000, bytes_accessed=1 << 20, transcendentals=0)


def whole(*shape):
    return pl.BlockSpec(shape, lambda i, *_: (0,) * len(shape))


def pack_tile(x):
    return jnp.concatenate([x[:, :LANES], x[:, LANES:]], axis=0).T


def unpack_tile(x):
    upright = x.T
    return jnp.concatenate([upright[: LANES // 2], upright[LANES // 2 :]], axis=1)


def store_vector(parts, rows_of, put):
    first = lane_is_first(SUB)
    for pair in range(PHYS // 2):
        for part, row in zip(parts, rows_of):
            even = part[pl.ds(2 * pair, SUB, stride=PHYS), :]
            odd = part[pl.ds(2 * pair + 1, SUB, stride=PHYS), :]
            upper = jnp.where(first, even, pltpu.roll(odd, LANES // 2, 1))
            lower = jnp.where(first, pltpu.roll(even, LANES // 2, 1), odd)
            high, low = split_two(jnp.concatenate([upper, lower], axis=0))
            put(row, pair, high, low)


def pack_kernel(info_ref, wave_ref, own_wave_ref, diag_ref, vec_ref, own_ref, diag_out, tiles):
    half = LANES // 2
    for j in range(wave_ref.shape[0]):
        own_ref[j] = pack_tile(own_wave_ref[j])
        diag_out[j] = pack_tile(diag_ref[j])
        for q in range(4):
            tiles[q, j] = pack_tile(wave_ref[j, :, 2 * LANES * q : 2 * LANES * (q + 1)])

        def put(row, pair, high, low):
            columns = slice(pair * LANES, (pair + 1) * LANES)
            vec_ref[j, row : row + 16, columns] = high
            vec_ref[j, row + half : row + half + 16, columns] = low

        store_vector([tiles.at[q, j] for q in range(4)], [16 * q for q in range(4)], put)


def pack(info, wavefunction, diagonal):
    blocks, rows, width = wavefunction.shape
    step = 2
    tile = pl.BlockSpec((step, LANES, LANES), lambda i, *_: (i, 0, 0))
    return pl.pallas_call(
        pack_kernel,
        grid_spec=pltpu.PrefetchScalarGridSpec(
            num_scalar_prefetch=1,
            grid=(blocks // step,),
            in_specs=[
                pl.BlockSpec((step, rows, width), lambda i, *_: (i, 0, 0)),
                pl.BlockSpec((step, rows, width // 4), lambda i, info: (i, 0, info[0])),
                pl.BlockSpec((step, rows, width // 4), lambda i, *_: (i, 0, 0)),
            ],
            out_specs=[pl.BlockSpec((step, LANES, width), lambda i, *_: (i, 0, 0))] + [tile] * 2,
            scratch_shapes=[pltpu.VMEM((4, step, LANES, LANES), jnp.float32)],
        ),
        out_shape=[
            jax.ShapeDtypeStruct((blocks, LANES, width), jnp.bfloat16),
        ]
        + [jax.ShapeDtypeStruct((blocks, LANES, LANES), jnp.float32)] * 2,
        compiler_params=pltpu.CompilerParams(vmem_limit_bytes=SMALL_VMEM),
        cost_estimate=micros(5),
        name="pack",
    )(info, wavefunction, wavefunction, diagonal)


def mixing_kernel(sizes, *refs):
    sources, outs = refs[:2], refs[2:]
    spread = (
        lax.broadcasted_iota(jnp.int32, (PHYS, LANES), 1) // SUB
        == lax.broadcasted_iota(jnp.int32, (PHYS, LANES), 0)
    ).astype(jnp.bfloat16)
    row = lax.broadcasted_iota(jnp.int32, (LANES, LANES), 0) // PHYS
    column = lax.broadcasted_iota(jnp.int32, (LANES, LANES), 1) % SUB
    same = row == column
    for n, source in enumerate(sources):
        start = 0
        for group, size in enumerate(sizes):
            out_ref = outs[n * len(sizes) + group]
            for at in range(size):
                for place, term in enumerate(split_two(source[start + at, 0:PHYS].T)):
                    wide = jnp.dot(term, spread, preferred_element_type=jnp.float32)
                    tall = jnp.concatenate([wide] * SUB, axis=0)
                    tall = jnp.where(same, tall, 0.0).astype(jnp.bfloat16)
                    rows = slice(place * LANES, (place + 1) * LANES)
                    out_ref[at, rows] = jnp.concatenate([tall, tall], axis=1)
            start += size


def mixing_operands(sources, sizes):
    out = pl.pallas_call(
        functools.partial(mixing_kernel, sizes),
        out_shape=[
            jax.ShapeDtypeStruct((size, 2 * LANES, 2 * LANES), jnp.bfloat16)
            for _ in sources
            for size in sizes
        ],
        compiler_params=pltpu.CompilerParams(vmem_limit_bytes=SMALL_VMEM),
        cost_estimate=micros(2),
        name="mixing",
    )(*sources)
    return [out[: len(sizes)], out[len(sizes) :]]


def own_operands_kernel(info_ref, *refs):
    pieces, (left_high, left_low, right_out, send, blocks_ref, upright_ref) = refs[:4], refs[4:]
    per, blocks, half, lanes = left_high.shape
    rows = half // 4
    wide = half // 2
    first = lane_is_first(half)
    first_wide = lane_is_first(wide)
    first_rows = lane_is_first(rows)
    mine_at = pl.multiple_of(half + info_ref[6] * wide, wide)
    theirs_at = pl.multiple_of(lanes - wide - info_ref[6] * wide, wide)
    for j in range(blocks):
        for w in range(per):
            for z in range(4):
                row = pl.multiple_of((info_ref[4] ^ z) * rows, rows)
                blocks_ref[w, j, pl.ds(row, rows), :] = pieces[z][w, j]
        for w in range(per):
            block = blocks_ref[w, j]
            upright_ref[w, j] = jnp.concatenate([block, block], axis=0).T
            turned = pltpu.roll(block, half, 1)
            high, low = split_two(jnp.where(first, block, turned))
            left_high[w, j] = high
            left_low[w, j] = low
            send[w, j, 0:wide] = jnp.where(first_wide, block[:wide], turned[wide:])
        for w in range(per):
            high, low = split_two(upright_ref[w, j, pl.ds(mine_at, wide), :])
            right_out[j, wide * w : wide * (w + 1), 0:lanes] = high
            right_out[j, wide * w : wide * (w + 1), lanes:] = low
            upper = upright_ref[w, j, pl.ds(theirs_at, rows), :]
            lower = upright_ref[w, j, pl.ds(theirs_at + rows, rows), :]
            send[w, j, wide : wide + rows] = jnp.where(first_rows, upper, lower)


def other_operands(sent, left_high, left_low, right_out, j):
    per, blocks, half, lanes = left_high.shape
    rows = half // 4
    wide = half // 2
    first = lane_is_first(wide)
    first_rows = lane_is_first(rows)
    for w in range(per):
        both = sent[w, j, 0:wide]
        turned = pltpu.roll(both, half, 1)
        full = jnp.concatenate(
            [jnp.where(first, both, turned), jnp.where(first, turned, both)], axis=0
        )
        high, low = split_two(full)
        left_high[w, j] = high
        left_low[w, j] = low
        both = sent[w, j, wide : wide + rows]
        turned = pltpu.roll(both, half, 1)
        full = jnp.concatenate(
            [jnp.where(first_rows, both, turned), jnp.where(first_rows, turned, both)], axis=0
        )
        high, low = split_two(full)
        right_out[j, wide * w : wide * (w + 1), 0:lanes] = high
        right_out[j, wide * w : wide * (w + 1), lanes:] = low


def operand_specs(per, step, half, lanes, at=0):
    return [
        pl.BlockSpec((per, step, half, lanes), lambda i, *_: (0, at + i, 0, 0)),
        pl.BlockSpec((per, step, half, lanes), lambda i, *_: (0, at + i, 0, 0)),
        pl.BlockSpec((step, per * 32, 2 * lanes), lambda i, *_: (at + i, 0, 0)),
    ]


def operand_shapes(per, blocks, half, lanes):
    return [
        jax.ShapeDtypeStruct((per, blocks, half, lanes), jnp.bfloat16),
        jax.ShapeDtypeStruct((per, blocks, half, lanes), jnp.bfloat16),
        jax.ShapeDtypeStruct((blocks, per * 32, 2 * lanes), jnp.bfloat16),
    ]


def cut_kernel(first, info_ref, source, *refs):
    outs, sems = refs[:4], refs[4]
    per = outs[0].shape[0]
    copies = []
    for k in range(4):
        part = source.at[pl.ds(first, per), info_ref[4] ^ k]
        copies.append(pltpu.make_async_copy(part, outs[k], sems.at[k]))
    for copy in copies:
        copy.start()
    for copy in copies:
        copy.wait()


def cut_pieces(info, by_owner, first, per):
    shape = jax.ShapeDtypeStruct((per,) + by_owner.shape[2:], jnp.float32)
    return pl.pallas_call(
        functools.partial(cut_kernel, first),
        grid_spec=pltpu.PrefetchScalarGridSpec(
            num_scalar_prefetch=1,
            grid=(1,),
            in_specs=[pl.BlockSpec(memory_space=pl.ANY)],
            out_specs=[pl.BlockSpec(memory_space=pl.ANY)] * 4,
            scratch_shapes=[pltpu.SemaphoreType.DMA((4,))],
        ),
        out_shape=[shape] * 4,
        compiler_params=pltpu.CompilerParams(vmem_limit_bytes=SMALL_VMEM),
        cost_estimate=micros(1),
        name="cut_pieces",
    )(info, *(in_hbm(by_owner) if first == 0 else [by_owner]))


def own_operands(info, pieces):
    per, blocks, rows, lanes = pieces[0].shape
    half = lanes // 2
    step = 4
    return pl.pallas_call(
        own_operands_kernel,
        grid_spec=pltpu.PrefetchScalarGridSpec(
            num_scalar_prefetch=1,
            grid=(blocks // step,),
            in_specs=[pl.BlockSpec((per, step, rows, lanes), lambda i, *_: (0, i, 0, 0))] * 4,
            out_specs=operand_specs(per, step, half, lanes)
            + [pl.BlockSpec((per, step, 3 * rows, lanes), lambda i, *_: (0, i, 0, 0))],
            scratch_shapes=[
                pltpu.VMEM((per, step, half, lanes), jnp.float32),
                pltpu.VMEM((per, step, lanes, lanes), jnp.float32),
            ],
        ),
        out_shape=operand_shapes(per, blocks, half, lanes)
        + [jax.ShapeDtypeStruct((per, blocks, 3 * rows, lanes), jnp.float32)],
        compiler_params=pltpu.CompilerParams(vmem_limit_bytes=SMALL_VMEM),
        cost_estimate=micros(12),
        name="own_operands",
    )(info, *pieces)


def apply_kernel(plan, info_ref, *refs):
    chunks, first_block, parts_given, sent_given, before_given, pieces = plan
    refs = list(refs)
    take = lambda n: [refs.pop(0) for _ in range(n)]
    slots = take(2)
    vector = take(4 if parts_given else 1)
    operands = [take(3) for _ in chunks[: -1 if sent_given else None]]
    sent = take(1)[0] if sent_given else None
    mixes = take(len(chunks))
    before = take(1)[0] if before_given else None
    outs = take(2 if pieces else 1)
    made = take(3) if sent_given else []
    scratch = take(2)
    vec, mid = scratch
    total_ref = take(1)[0] if pieces else outs[0]
    kept = []
    if sent_given:
        operands.append(take(3))
        sems = take(1)[0]
        kept = [
            pltpu.make_async_copy(operands[-1][i], made[i], sems.at[i]) for i in range(3)
        ]
    step = mid.shape[0]
    lanes, half = LANES, LANES // 2
    first = lane_is_first(SUB)
    first_half = lane_is_first(half)
    keep_first = jnp.where(first_half, 1.0, 0.0).astype(jnp.bfloat16)
    keep_second = jnp.where(first_half, 0.0, 1.0).astype(jnp.bfloat16)
    me = info_ref[4]

    if not before_given:
        total_ref[...] = jnp.zeros_like(total_ref)
    else:
        total_ref[...] = before[...]

    def right_side(j):
        if sent_given:
            other_operands(sent, *operands[-1], first_block + j)
        if parts_given:

            def put(row, pair, high, low):
                columns = slice(pair * lanes, (pair + 1) * lanes)
                vec[j, pl.ds(row, 16), columns] = high
                vec[j, pl.ds(row + half, 16), columns] = low

            rows_of = [pl.multiple_of(info_ref[g] * 16, 16) for g in range(4)]
            store_vector([x.at[pl.ds(j * lanes, lanes)] for x in vector], rows_of, put)
            source = vec[j]
        else:
            source = vector[0][first_block + j]
        source = jnp.concatenate([source, source], axis=0)
        at = 0
        for left_high, left_low, right in operands:
            count = right.shape[1]
            mid[j, at : at + count, :] = jnp.dot(
                right[first_block + j], source, preferred_element_type=jnp.float32
            )
            at += count

    def prepared(j, refs_of, w, row_of):
        left_high, left_low, right = refs_of
        tiles = []
        for part in range(2):
            row = row_of + part * 16
            for pair in range(PHYS // 2):
                columns = slice(pair * lanes, (pair + 1) * lanes)
                upper = mid[j, row : row + SUB, columns]
                lower = mid[j, row + SUB : row + 2 * SUB, columns]
                tiles.append(jnp.where(first, upper, pltpu.roll(lower, half, 1)))
                tiles.append(jnp.where(first, pltpu.roll(upper, half, 1), lower))
        t_high, t_low = split_two(jnp.concatenate(tiles, axis=0))
        lh, ll = left_high[w, first_block + j], left_low[w, first_block + j]
        wide_high = jnp.concatenate([lh * keep_first, lh * keep_second], axis=0)
        wide_low = jnp.concatenate([ll * keep_first, ll * keep_second], axis=0)
        weights = jnp.concatenate([wide_high, wide_low], axis=1)
        weights = jnp.concatenate([weights, weights], axis=0)
        return jnp.concatenate([t_high, t_low], axis=1), weights

    def mix_unit(mixing, w, z):
        z_high, z_low = [jnp.concatenate([x[:lanes], x[lanes:]], axis=1) for x in z]
        return jnp.dot(
            mixing[w],
            jnp.concatenate([z_high, z_low], axis=0),
            preferred_element_type=jnp.float32,
        )

    def add_up(j, table, bond, mixed):
        slot = table[bond, first_block + j]
        slot = ((slot >> 1) ^ me) * 2 + (slot & 1)
        for part in range(2):
            columns = slice(part * lanes, (part + 1) * lanes)
            total_ref[part, slot] += mixed[:lanes, columns] + mixed[lanes:, columns]

    bonds = []
    for (source, start), refs_of, mix in zip(chunks, operands, mixes):
        for w in range(mix.shape[0]):
            bonds.append((refs_of, mix, w, slots[source], start + w))
    right_side(0)
    units = [(j, at) for j in range(step) for at in range(len(bonds))]

    def prepare_unit(n):
        j, at = units[n]
        refs_of, mixing, w, table, bond = bonds[at]
        return prepared(j, refs_of, w, at * 32)

    ready = prepare_unit(0)
    waiting = None
    for n, (j, at) in enumerate(units):
        refs_of, mixing, w, table, bond = bonds[at]
        z = jnp.dot(*ready, preferred_element_type=jnp.float32)
        if j + 1 < step and at == len(bonds) // 3:
            right_side(j + 1)
            if j + 2 == step:
                for copy in kept:
                    copy.start()
        if n + 1 < len(units):
            ready = prepare_unit(n + 1)
        if waiting is not None:
            before_j, before_mixing, before_w, before_table, before_bond, before_z = waiting
            mixed = mix_unit(before_mixing, before_w, before_z)
        z = split_two(z[:, :lanes] + z[:, lanes:])
        if waiting is not None:
            add_up(before_j, before_table, before_bond, mixed)
        waiting = (j, mixing, w, table, bond, z)
    j, mixing, w, table, bond, z = waiting
    add_up(j, table, bond, mix_unit(mixing, w, z))
    for copy in kept:
        copy.wait()

    if pieces:
        stats = jnp.zeros((SUB, lanes), jnp.float32)
        if parts_given:
            tail = vector[0].shape[0] - SUB
            stats = stacked_rows(*merged([x[tail:] for x in vector]))
        for out, part in ((outs[0], info_ref[5]), (outs[1], 1 - info_ref[5])):
            for k in range(4):
                for i in range(2):
                    out[k, i * lanes : (i + 1) * lanes] = total_ref[part, 2 * k + i]
                out[k, 2 * lanes :] = stats
            stats = jnp.zeros((SUB, lanes), jnp.float32)


def apply_bonds(info, slots, vector, chunks, operands, sent, mixes, before, pieces, half_of=None):
    blocks, half, lanes = operands[0][0].shape[1:]
    parts_given = half_of is not None
    step = 4 if parts_given else blocks
    arguments = list(vector) if parts_given else [vector]
    for made in operands:
        arguments += made
    if sent is not None:
        arguments.append(sent)
    arguments += mixes
    aliases = {}
    if before is not None:
        if not pieces:
            aliases[3 + len(arguments)] = 0
        arguments.append(before)
    counts = [mix.shape[0] for mix in mixes]
    shapes = [(4, 2 * lanes + SUB, lanes)] * 2 if pieces else [(2, 8, lanes, lanes)]
    out_shape = [jax.ShapeDtypeStruct(shape, jnp.float32) for shape in shapes]
    if sent is not None:
        out_shape += operand_shapes(counts[-1], blocks, half, lanes)
    scratch = [
        pltpu.VMEM((step if parts_given else 1, lanes, PHYS * half), jnp.bfloat16),
        pltpu.VMEM((step, sum(counts) * 32, PHYS * half), jnp.float32),
    ]
    if pieces:
        scratch.append(pltpu.VMEM((2, 8, lanes, lanes), jnp.float32))
    out_specs = [pl.BlockSpec(memory_space=pltpu.VMEM)] * len(shapes)
    if sent is not None:
        out_specs += [pl.BlockSpec(memory_space=pltpu.HBM)] * 3
        scratch += [pltpu.VMEM(x.shape, x.dtype) for x in out_shape[len(shapes) :]]
        scratch.append(pltpu.SemaphoreType.DMA((3,)))
    plan = (
        tuple(chunks), (half_of or 0) * step, parts_given, sent is not None, before is not None,
        pieces,
    )
    out = pl.pallas_call(
        functools.partial(apply_kernel, plan),
        in_specs=[pl.BlockSpec(memory_space=pltpu.SMEM)] * 3
        + [pl.BlockSpec(memory_space=pltpu.VMEM)] * len(arguments),
        out_specs=out_specs,
        scratch_shapes=scratch,
        out_shape=out_shape,
        input_output_aliases=aliases,
        compiler_params=pltpu.CompilerParams(vmem_limit_bytes=APPLY_VMEM),
        cost_estimate=micros(10 if parts_given else 1),
        name="apply_bonds",
    )(info, *slots, *arguments)
    return out[: len(shapes)], out[len(shapes) :]


def add_arrived(info_ref, owner_ref, arrived, total):
    for k in range(4):
        for i in range(2):
            rows = slice(i * LANES, (i + 1) * LANES)
            total[owner_ref[info_ref[4] ^ k, i]] += arrived[k][rows]


def stacked_rows(*rows):
    at = lax.broadcasted_iota(jnp.int32, (SUB, LANES), 0)
    tile = jnp.zeros((SUB, LANES), jnp.float32)
    for i, row in enumerate(rows):
        tile = jnp.where(at == i, row, tile)
    return tile


def merged(tiles):
    rows = [[tile[i : i + 1] for i in range(3)] for tile in tiles]
    cross = sum(row[0] for row in rows)
    square = sum(row[1] for row in rows)
    ratio = cross / jnp.maximum(square, TINY)
    apart = [
        (row[0] / jnp.maximum(row[1], TINY) - ratio) * jnp.sqrt(row[1]) for row in rows
    ]
    rest = sum(row[2] for row in rows) + sum(x * x for x in apart)
    return cross, square, rest


def image_kernel(info_ref, owner_ref, a3, a2, a1, a0, start_ref, lower_ref, upper_ref, total):
    total[...] = start_ref[...]
    add_arrived(info_ref, owner_ref, (a0, a1, a2, a3), total)
    blocks = total.shape[0]
    for k in range(blocks):
        half = lower_ref if k < blocks // 2 else upper_ref
        at = k % (blocks // 2) * LANES
        half[at : at + LANES] = total[k]


def owner_image(info, owners, arrived, start):
    blocks = start.shape[0]
    shape = jax.ShapeDtypeStruct((blocks // 2 * LANES, LANES), jnp.float32)
    return pl.pallas_call(
        image_kernel,
        in_specs=[pl.BlockSpec(memory_space=pltpu.SMEM)] * 2
        + [pl.BlockSpec(memory_space=pltpu.VMEM)] * 5,
        out_specs=[pl.BlockSpec(memory_space=pltpu.VMEM)] * 2,
        scratch_shapes=[pltpu.VMEM(start.shape, jnp.float32)],
        out_shape=[shape, shape],
        compiler_params=pltpu.CompilerParams(vmem_limit_bytes=SMALL_VMEM),
        cost_estimate=micros(1),
        name="owner_image",
    )(info, owners, *arrived[::-1], start)


def statistics_kernel(own_hbm, lower_ref, upper_ref, out_ref, own_ref, sem):
    copy = pltpu.make_async_copy(own_hbm, own_ref, sem)
    copy.start()
    rows = upper_ref.shape[0]
    out_ref[0:rows] = upper_ref[...]
    copy.wait()
    blocks = own_ref.shape[0]
    images = []
    for half in (lower_ref, upper_ref):
        images += [half.at[pl.ds(k * LANES, LANES)] for k in range(blocks // 2)]
    cross = jnp.zeros((LANES, LANES), jnp.float32)
    square = jnp.zeros((LANES, LANES), jnp.float32)
    for k in range(blocks):
        own = own_ref[k]
        cross += own * images[k][...]
        square += own * own
    cross = jnp.sum(cross, keepdims=True)
    square = jnp.sum(square, keepdims=True)
    ratio = cross / jnp.maximum(square, TINY)
    rest = jnp.zeros((LANES, LANES), jnp.float32)
    for k in range(blocks):
        apart = images[k][...] - ratio * own_ref[k]
        rest += apart * apart
    out_ref[rows:] = stacked_rows(cross, square, jnp.sum(rest, keepdims=True))


def with_statistics(own, lower, upper):
    return pl.pallas_call(
        statistics_kernel,
        in_specs=[pl.BlockSpec(memory_space=pl.ANY)]
        + [pl.BlockSpec(memory_space=pltpu.VMEM)] * 2,
        out_specs=pl.BlockSpec(memory_space=pltpu.VMEM),
        scratch_shapes=[pltpu.VMEM(own.shape, jnp.float32), pltpu.SemaphoreType.DMA],
        out_shape=jax.ShapeDtypeStruct((upper.shape[0] + SUB, LANES), jnp.float32),
        compiler_params=pltpu.CompilerParams(vmem_limit_bytes=SMALL_VMEM),
        cost_estimate=micros(3),
        name="statistics",
    )(*in_hbm(own), lower, upper)


def final_kernel(
    entries, info_ref, owner_ref, a3, a2, a1, a0, diag_ref, own_ref, lower_ref, upper_ref,
    first_ref, vector_ref, second_ref, total,
):
    arrived = (a0, a1, a2, a3)
    cross, square, rest = merged([ref[2 * LANES :] for ref in arrived])
    scale = lax.rsqrt(square / entries + 1e-06)
    rayleigh = scale * scale * (cross / entries)
    apart = (cross / jnp.maximum(square, TINY) - rayleigh) * jnp.sqrt(square)
    mean = scale * scale * ((rest + apart * apart) / entries)
    second_scale = scale * lax.rsqrt(mean + 1e-06)
    for k in range(total.shape[0]):
        at = k % (total.shape[0] // 2) * LANES
        image = (lower_ref if k < total.shape[0] // 2 else upper_ref)[at : at + LANES]
        total[k] = (diag_ref[k] - rayleigh) * image
        first_ref[k] = unpack_tile(scale * image)
        vector_ref[k] = unpack_tile(second_scale * (image - rayleigh * own_ref[k]))
    add_arrived(info_ref, owner_ref, arrived, total)
    for k in range(total.shape[0]):
        second_ref[k] = unpack_tile(second_scale * total[k])


def outputs(info, owners, arrived, diagonal, own, images, entries):
    blocks = diagonal.shape[0]
    shape = (blocks, LANES // 2, 2 * LANES)
    return pl.pallas_call(
        functools.partial(final_kernel, entries),
        grid_spec=pltpu.PrefetchScalarGridSpec(
            num_scalar_prefetch=2,
            grid=(1,),
            in_specs=[whole(*x.shape) for x in (*arrived, diagonal, own)]
            + [whole(blocks // 2 * LANES, LANES)] * 2,
            out_specs=[whole(*shape)] * 3,
            scratch_shapes=[pltpu.VMEM(diagonal.shape, jnp.float32)],
        ),
        out_shape=[jax.ShapeDtypeStruct(shape, jnp.float32)] * 3,
        compiler_params=pltpu.CompilerParams(vmem_limit_bytes=SMALL_VMEM),
        cost_estimate=micros(4),
        name="outputs",
    )(info, owners, *arrived[::-1], diagonal, own, *images)


def in_hbm(*arrays):
    return [pltpu.with_memory_space_constraint(x, pltpu.HBM) for x in arrays]


def partner(x, axis, k):
    size = lax.axis_size(axis)
    return lax.ppermute(x, axis, [(i, i ^ k) for i in range(size)])


def after(x, *others):
    return lax.optimization_barrier((x, *others))[0]


def gathered(x):
    across = partner(x, "mpo", 1)
    return [x, across, partner(x, "rep", 1), partner(across, "rep", 1)]


def everyone_of(pieces, axis):
    return [pieces[0]] + [partner(pieces[k], axis, k) for k in range(1, 4)]


def to_owners(mine, theirs):
    other = partner(theirs, "rep", 1)
    pieces = [mine[k] + other[k] for k in range(4)]
    return everyone_of(pieces, "blk")


def per_device(wavefunction, environment, bond_terms, diagonal, term_slot, slot_block):
    blocks, rows, width = wavefunction.shape
    zs = lax.axis_size("blk")
    mpo, rep, blk = lax.axis_index("mpo"), lax.axis_index("rep"), lax.axis_index("blk")
    place = 2 * mpo + rep
    info = jnp.stack([place, place ^ 2, place ^ 1, place ^ 3, blk, rep, mpo]).astype(jnp.int32)
    bonds = environment.shape[0]
    sizes = tuple(bonds * part // 6 for part in (3, 2, 1))
    firsts = tuple(sum(sizes[:group]) for group in range(len(sizes)))
    entries = float(blocks * zs * rows * width)

    vector, own, diagonal_packed = pack(info, wavefunction, diagonal)

    by_owner = environment.reshape(bonds, zs, blocks, rows // zs, 2 * rows)
    pieces = []
    for group in range(len(sizes)):
        cuts = list(cut_pieces(info, by_owner, firsts[group], sizes[group]))
        if group:
            cuts[1:] = [after(x, y) for x, y in zip(cuts[1:], pieces[-1][1:])]
        pieces.append(cuts[:1] + [partner(cuts[k], "blk", k) for k in range(1, 4)])
    pieces[0][1] = after(pieces[0][1], vector)
    phys = bond_terms.shape[-1]
    table = jnp.pad(term_slot.astype(jnp.float32), ((0, 0), (0, phys - blocks)))
    tables = jnp.pad(table[:, None], ((0, 0), (0, SUB - 1), (0, 0)))
    both = jnp.concatenate([bond_terms, tables], axis=1)
    other_terms = partner(after(both, pieces[0][1]), "mpo", 1)
    mixing = mixing_operands([bond_terms, other_terms], sizes)
    slots = [term_slot, other_terms[:, phys, :blocks].astype(jnp.int32)]

    made, sent = [], []
    total = None
    operands = []
    done = 0

    def apply_group(group, vector):
        out, other = apply_bonds(
            info, slots, vector, [(0, firsts[group]), (1, firsts[group])], [made[group]],
            partner(sent[group], "mpo", 1), [terms[group] for terms in mixing], total,
            group == len(sizes) - 1,
        )
        operands.extend([made[group], other])
        return out

    for group in range(len(sizes)):
        if group >= 2:
            total = apply_group(group - 2, after(vector, sent[group - 1]))[0]
            pieces[group][3] = after(pieces[group][3], total)
        if group < 2:
            pieces[group][1] = after(pieces[group][1], pieces[group + 1][1])
        *own_set, send = own_operands(info, pieces[group])
        made.append(own_set)
        sent.append(send)
    total = apply_group(len(sizes) - 2, after(vector, sent[-1]))[0]
    out = apply_group(len(sizes) - 1, vector)
    arrived = to_owners(*out)
    start = after(diagonal_packed, arrived[0]) * own
    lower, upper = owner_image(info, slot_block, arrived, start)
    upper = with_statistics(own, lower, upper)

    chunks = [(source, first) for first in firsts for source in range(2)]
    mixes = [mixing[source][group] for group in range(len(sizes)) for source in range(2)]
    lower_parts = [lower, partner(lower, "mpo", 1), partner(lower, "rep", 1)]
    lower_parts.append(partner(after(lower_parts[1], upper), "rep", 1))
    across = partner(after(upper, lower_parts[1]), "mpo", 1)
    out, _ = apply_bonds(
        info, slots, lower_parts, chunks, operands, None, mixes, None, False, 0
    )
    upper_parts = [upper, across, partner(upper, "rep", 1)]
    upper_parts.append(partner(after(across, out[0]), "rep", 1))
    out, _ = apply_bonds(
        info, slots, upper_parts, chunks, operands, None, mixes, out[0], True, 1
    )
    return tuple(
        outputs(
            info, slot_block, to_owners(*out), diagonal_packed, own, (lower, upper), entries
        )
    )


def solution(mesh):
    packed = mesh.shape["mpo"] == 2 and mesh.shape["rep"] == 2 and mesh.shape["blk"] == 4
    return jax.shard_map(
        per_device if packed else plain_device,
        mesh=mesh,
        in_specs=(
            P(("grp", "blk"), None, None),
            P(("grp", "mpo", "rep"), None, "blk", None),
            P(("grp", "mpo", "rep"), None, None),
            P(("grp", "blk"), None, ("mpo", "rep")),
            P(("grp", "mpo", "rep"), "blk"),
            P("grp", "blk"),
        ),
        out_specs=(
            P(("grp", "blk"), None, ("mpo", "rep")),
            P(("grp", "blk"), None, ("mpo", "rep")),
            P(("grp", "blk"), None, ("mpo", "rep")),
        ),
        check_vma=False,
    )
```

```python
import functools

import jax
import jax.numpy as jnp
from jax import lax
from jax.experimental import pallas as pl
from jax.experimental.pallas import tpu as pltpu
from jax.sharding import PartitionSpec as P

LANES = 128
SUB = 8
PHYS = 16
TINY = 1e-30
SMALL_VMEM = 16 * 1024 * 1024
APPLY_VMEM = 16 * 1024 * 1024


def plain_apply(vector_full, environment, bond_terms, term_slot, slot_block, diagonal):
    block_count, block_rows, block_width = vector_full.shape
    phys_size = bond_terms.shape[-1]
    right_rows = block_width // phys_size
    slot_count = slot_block.shape[0] * slot_block.shape[1]
    blocks = vector_full.reshape(block_count, block_rows, right_rows, phys_size)
    ordered = jnp.transpose(blocks, (0, 3, 1, 2))
    left_env = environment[:, :, :, :block_rows]
    right_env = environment[:, :, :, block_rows:]
    left_done = jnp.einsum("wjab,jsac->wjsbc", left_env, ordered, precision=lax.Precision.HIGHEST)
    right_done = jnp.einsum(
        "wjsbc,wjcd->wjsbd", left_done, right_env, precision=lax.Precision.HIGHEST
    )
    right_done = right_done.reshape(
        environment.shape[0], block_count, phys_size, block_rows * right_rows
    )
    bond_term = jnp.einsum(
        "wjsx,wst->wjtx", right_done, bond_terms, precision=lax.Precision.HIGHEST
    )
    bond_term = bond_term.reshape(environment.shape[0], block_count, block_rows * block_width)
    slot_table = (
        term_slot[:, None, :] == jnp.arange(slot_count, dtype=jnp.int32)[None, :, None]
    ).astype(jnp.float32)
    slot_buffer = jnp.einsum("wsj,wjx->sx", slot_table, bond_term, precision=lax.Precision.HIGHEST)
    slot_buffer = slot_buffer.reshape(slot_count, phys_size, block_rows, right_rows)
    slot_buffer = jnp.transpose(slot_buffer, (0, 2, 3, 1)).reshape(
        slot_count, block_rows, block_width
    )
    owners = slot_block.reshape(-1)
    selector = (owners[None, :] == jnp.arange(block_count, dtype=jnp.int32)[:, None]).astype(
        jnp.float32
    )
    column_width = block_width // lax.axis_size(("mpo", "rep"))
    column_start = lax.axis_index(("mpo", "rep")) * column_width
    own_part = lax.dynamic_slice_in_dim(vector_full, column_start, column_width, 2)
    shares = lax.psum_scatter(slot_buffer, ("mpo", "rep"), scatter_dimension=2, tiled=True)
    arrived = lax.all_to_all(shares, "blk", split_axis=0, concat_axis=0, tiled=True)
    result = jnp.einsum("ks,sbc->kbc", selector, arrived, precision=lax.Precision.HIGHEST)
    return (result + diagonal * own_part, own_part)


def plain_device(wavefunction, environment, bond_terms, diagonal, term_slot, slot_block):
    arranged = lax.all_to_all(environment, "blk", split_axis=1, concat_axis=2, tiled=True)
    entries = float(
        wavefunction.shape[0] * lax.axis_size("blk") * wavefunction.shape[1] * wavefunction.shape[2]
    )
    square_sum = lax.psum(jnp.sum(wavefunction * wavefunction), "blk")
    first_vector = wavefunction * lax.rsqrt(square_sum / entries + 1e-06)
    first_image, first_part = plain_apply(
        first_vector, arranged, bond_terms, term_slot, slot_block, diagonal
    )
    rayleigh = lax.psum(jnp.sum(first_part * first_image), ("blk", "mpo", "rep")) / entries
    residual = first_image - rayleigh * first_part
    resid_sum = lax.psum(jnp.sum(residual * residual), ("blk", "mpo", "rep"))
    second_vector = residual * lax.rsqrt(resid_sum / entries + 1e-06)
    second_full = lax.all_gather(second_vector, ("mpo", "rep"), axis=2, tiled=True)
    second_image, unused = plain_apply(
        second_full, arranged, bond_terms, term_slot, slot_block, diagonal
    )
    return (first_image, second_vector, second_image)


def split_two(x):
    high = x.astype(jnp.bfloat16)
    low = (x - high.astype(jnp.float32)).astype(jnp.bfloat16)
    return high, low


def lane_is_first(rows):
    return lax.broadcasted_iota(jnp.int32, (rows, LANES), 1) < LANES // 2


def micros(count):
    return pl.CostEstimate(flops=count * 1100000000, bytes_accessed=1 << 20, transcendentals=0)


def whole(*shape):
    return pl.BlockSpec(shape, lambda i, *_: (0,) * len(shape))


def pack_tile(x):
    return jnp.concatenate([x[:, :LANES], x[:, LANES:]], axis=0).T


def unpack_tile(x):
    upright = x.T
    return jnp.concatenate([upright[: LANES // 2], upright[LANES // 2 :]], axis=1)


def store_vector(parts, rows_of, put):
    first = lane_is_first(SUB)
    for pair in range(PHYS // 2):
        for part, row in zip(parts, rows_of):
            even = part[pl.ds(2 * pair, SUB, stride=PHYS), :]
            odd = part[pl.ds(2 * pair + 1, SUB, stride=PHYS), :]
            upper = jnp.where(first, even, pltpu.roll(odd, LANES // 2, 1))
            lower = jnp.where(first, pltpu.roll(even, LANES // 2, 1), odd)
            high, low = split_two(jnp.concatenate([upper, lower], axis=0))
            put(row, pair, high, low)


def pack_kernel(info_ref, wave_ref, own_wave_ref, diag_ref, vec_ref, own_ref, diag_out, tiles):
    half = LANES // 2
    for j in range(wave_ref.shape[0]):
        own_ref[j] = pack_tile(own_wave_ref[j])
        diag_out[j] = pack_tile(diag_ref[j])
        for q in range(4):
            tiles[q, j] = pack_tile(wave_ref[j, :, 2 * LANES * q : 2 * LANES * (q + 1)])

        def put(row, pair, high, low):
            columns = slice(pair * LANES, (pair + 1) * LANES)
            vec_ref[j, row : row + 16, columns] = high
            vec_ref[j, row + half : row + half + 16, columns] = low

        store_vector([tiles.at[q, j] for q in range(4)], [16 * q for q in range(4)], put)


def pack(info, wavefunction, diagonal):
    blocks, rows, width = wavefunction.shape
    step = 2
    tile = pl.BlockSpec((step, LANES, LANES), lambda i, *_: (i, 0, 0))
    return pl.pallas_call(
        pack_kernel,
        grid_spec=pltpu.PrefetchScalarGridSpec(
            num_scalar_prefetch=1,
            grid=(blocks // step,),
            in_specs=[
                pl.BlockSpec((step, rows, width), lambda i, *_: (i, 0, 0)),
                pl.BlockSpec((step, rows, width // 4), lambda i, info: (i, 0, info[0])),
                pl.BlockSpec((step, rows, width // 4), lambda i, *_: (i, 0, 0)),
            ],
            out_specs=[pl.BlockSpec((step, LANES, width), lambda i, *_: (i, 0, 0))] + [tile] * 2,
            scratch_shapes=[pltpu.VMEM((4, step, LANES, LANES), jnp.float32)],
        ),
        out_shape=[
            jax.ShapeDtypeStruct((blocks, LANES, width), jnp.bfloat16),
        ]
        + [jax.ShapeDtypeStruct((blocks, LANES, LANES), jnp.float32)] * 2,
        compiler_params=pltpu.CompilerParams(vmem_limit_bytes=SMALL_VMEM),
        cost_estimate=micros(5),
        name="pack",
    )(info, wavefunction, wavefunction, diagonal)


def mixing_kernel(sizes, *refs):
    sources, outs = refs[:2], refs[2:]
    spread = (
        lax.broadcasted_iota(jnp.int32, (PHYS, LANES), 1) // SUB
        == lax.broadcasted_iota(jnp.int32, (PHYS, LANES), 0)
    ).astype(jnp.bfloat16)
    row = lax.broadcasted_iota(jnp.int32, (LANES, LANES), 0) // PHYS
    column = lax.broadcasted_iota(jnp.int32, (LANES, LANES), 1) % SUB
    same = row == column
    for n, source in enumerate(sources):
        start = 0
        for group, size in enumerate(sizes):
            out_ref = outs[n * len(sizes) + group]
            for at in range(size):
                for place, term in enumerate(split_two(source[start + at, 0:PHYS].T)):
                    wide = jnp.dot(term, spread, preferred_element_type=jnp.float32)
                    tall = jnp.concatenate([wide] * SUB, axis=0)
                    tall = jnp.where(same, tall, 0.0).astype(jnp.bfloat16)
                    rows = slice(place * LANES, (place + 1) * LANES)
                    out_ref[at, rows] = jnp.concatenate([tall, tall], axis=1)
            start += size


def mixing_operands(sources, sizes):
    out = pl.pallas_call(
        functools.partial(mixing_kernel, sizes),
        out_shape=[
            jax.ShapeDtypeStruct((size, 2 * LANES, 2 * LANES), jnp.bfloat16)
            for _ in sources
            for size in sizes
        ],
        compiler_params=pltpu.CompilerParams(vmem_limit_bytes=SMALL_VMEM),
        cost_estimate=micros(2),
        name="mixing",
    )(*sources)
    return [out[: len(sizes)], out[len(sizes) :]]


def own_operands_kernel(info_ref, *refs):
    pieces, (left_high, left_low, right_out, send, blocks_ref, upright_ref) = refs[:4], refs[4:]
    per, blocks, half, lanes = left_high.shape
    rows = half // 4
    wide = half // 2
    first = lane_is_first(half)
    first_wide = lane_is_first(wide)
    first_rows = lane_is_first(rows)
    mine_at = pl.multiple_of(half + info_ref[6] * wide, wide)
    theirs_at = pl.multiple_of(lanes - wide - info_ref[6] * wide, wide)
    for j in range(blocks):
        for w in range(per):
            for z in range(4):
                row = pl.multiple_of((info_ref[4] ^ z) * rows, rows)
                blocks_ref[w, j, pl.ds(row, rows), :] = pieces[z][w, j]
        for w in range(per):
            block = blocks_ref[w, j]
            upright_ref[w, j] = jnp.concatenate([block, block], axis=0).T
            turned = pltpu.roll(block, half, 1)
            high, low = split_two(jnp.where(first, block, turned))
            left_high[w, j] = high
            left_low[w, j] = low
            send[w, j, 0:wide] = jnp.where(first_wide, block[:wide], turned[wide:])
        for w in range(per):
            high, low = split_two(upright_ref[w, j, pl.ds(mine_at, wide), :])
            right_out[j, wide * w : wide * (w + 1), 0:lanes] = high
            right_out[j, wide * w : wide * (w + 1), lanes:] = low
            upper = upright_ref[w, j, pl.ds(theirs_at, rows), :]
            lower = upright_ref[w, j, pl.ds(theirs_at + rows, rows), :]
            send[w, j, wide : wide + rows] = jnp.where(first_rows, upper, lower)


def other_operands(sent, left_high, left_low, right_out, j):
    per, blocks, half, lanes = left_high.shape
    rows = half // 4
    wide = half // 2
    first = lane_is_first(wide)
    first_rows = lane_is_first(rows)
    for w in range(per):
        both = sent[w, j, 0:wide]
        turned = pltpu.roll(both, half, 1)
        full = jnp.concatenate(
            [jnp.where(first, both, turned), jnp.where(first, turned, both)], axis=0
        )
        high, low = split_two(full)
        left_high[w, j] = high
        left_low[w, j] = low
        both = sent[w, j, wide : wide + rows]
        turned = pltpu.roll(both, half, 1)
        full = jnp.concatenate(
            [jnp.where(first_rows, both, turned), jnp.where(first_rows, turned, both)], axis=0
        )
        high, low = split_two(full)
        right_out[j, wide * w : wide * (w + 1), 0:lanes] = high
        right_out[j, wide * w : wide * (w + 1), lanes:] = low


def operand_specs(per, step, half, lanes, at=0):
    return [
        pl.BlockSpec((per, step, half, lanes), lambda i, *_: (0, at + i, 0, 0)),
        pl.BlockSpec((per, step, half, lanes), lambda i, *_: (0, at + i, 0, 0)),
        pl.BlockSpec((step, per * 32, 2 * lanes), lambda i, *_: (at + i, 0, 0)),
    ]


def operand_shapes(per, blocks, half, lanes):
    return [
        jax.ShapeDtypeStruct((per, blocks, half, lanes), jnp.bfloat16),
        jax.ShapeDtypeStruct((per, blocks, half, lanes), jnp.bfloat16),
        jax.ShapeDtypeStruct((blocks, per * 32, 2 * lanes), jnp.bfloat16),
    ]


def cut_kernel(first, info_ref, source, *refs):
    outs, sems = refs[:4], refs[4]
    per = outs[0].shape[0]
    copies = []
    for k in range(4):
        part = source.at[pl.ds(first, per), info_ref[4] ^ k]
        copies.append(pltpu.make_async_copy(part, outs[k], sems.at[k]))
    for copy in copies:
        copy.start()
    for copy in copies:
        copy.wait()


def cut_pieces(info, by_owner, first, per):
    shape = jax.ShapeDtypeStruct((per,) + by_owner.shape[2:], jnp.float32)
    return pl.pallas_call(
        functools.partial(cut_kernel, first),
        grid_spec=pltpu.PrefetchScalarGridSpec(
            num_scalar_prefetch=1,
            grid=(1,),
            in_specs=[pl.BlockSpec(memory_space=pl.ANY)],
            out_specs=[pl.BlockSpec(memory_space=pl.ANY)] * 4,
            scratch_shapes=[pltpu.SemaphoreType.DMA((4,))],
        ),
        out_shape=[shape] * 4,
        compiler_params=pltpu.CompilerParams(vmem_limit_bytes=SMALL_VMEM),
        cost_estimate=micros(1),
        name="cut_pieces",
    )(info, *(in_hbm(by_owner) if first == 0 else [by_owner]))


def own_operands(info, pieces):
    per, blocks, rows, lanes = pieces[0].shape
    half = lanes // 2
    step = 4
    return pl.pallas_call(
        own_operands_kernel,
        grid_spec=pltpu.PrefetchScalarGridSpec(
            num_scalar_prefetch=1,
            grid=(blocks // step,),
            in_specs=[pl.BlockSpec((per, step, rows, lanes), lambda i, *_: (0, i, 0, 0))] * 4,
            out_specs=operand_specs(per, step, half, lanes)
            + [pl.BlockSpec((per, step, 3 * rows, lanes), lambda i, *_: (0, i, 0, 0))],
            scratch_shapes=[
                pltpu.VMEM((per, step, half, lanes), jnp.float32),
                pltpu.VMEM((per, step, lanes, lanes), jnp.float32),
            ],
        ),
        out_shape=operand_shapes(per, blocks, half, lanes)
        + [jax.ShapeDtypeStruct((per, blocks, 3 * rows, lanes), jnp.float32)],
        compiler_params=pltpu.CompilerParams(vmem_limit_bytes=SMALL_VMEM),
        cost_estimate=micros(12),
        name="own_operands",
    )(info, *pieces)


def apply_kernel(plan, info_ref, *refs):
    chunks, first_block, parts_given, sent_given, before_given, pieces = plan
    refs = list(refs)
    take = lambda n: [refs.pop(0) for _ in range(n)]
    slots = take(2)
    vector = take(4 if parts_given else 1)
    operands = [take(3) for _ in chunks[: -1 if sent_given else None]]
    sent = take(1)[0] if sent_given else None
    mixes = take(len(chunks))
    before = take(1)[0] if before_given else None
    outs = take(2 if pieces else 1)
    made = take(3) if sent_given else []
    scratch = take(2)
    vec, mid = scratch
    total_ref = take(1)[0] if pieces else outs[0]
    kept = []
    if sent_given:
        operands.append(take(3))
        sems = take(1)[0]
        kept = [
            pltpu.make_async_copy(operands[-1][i], made[i], sems.at[i]) for i in range(3)
        ]
    step = mid.shape[0]
    lanes, half = LANES, LANES // 2
    first = lane_is_first(SUB)
    first_half = lane_is_first(half)
    keep_first = jnp.where(first_half, 1.0, 0.0).astype(jnp.bfloat16)
    keep_second = jnp.where(first_half, 0.0, 1.0).astype(jnp.bfloat16)
    me = info_ref[4]

    if not before_given:
        total_ref[...] = jnp.zeros_like(total_ref)
    else:
        total_ref[...] = before[...]

    def right_side(j):
        if sent_given:
            other_operands(sent, *operands[-1], first_block + j)
        if parts_given:

            def put(row, pair, high, low):
                columns = slice(pair * lanes, (pair + 1) * lanes)
                vec[j, pl.ds(row, 16), columns] = high
                vec[j, pl.ds(row + half, 16), columns] = low

            rows_of = [pl.multiple_of(info_ref[g] * 16, 16) for g in range(4)]
            store_vector([x.at[pl.ds(j * lanes, lanes)] for x in vector], rows_of, put)
            source = vec[j]
        else:
            source = vector[0][first_block + j]
        source = jnp.concatenate([source, source], axis=0)
        at = 0
        for left_high, left_low, right in operands:
            count = right.shape[1]
            mid[j, at : at + count, :] = jnp.dot(
                right[first_block + j], source, preferred_element_type=jnp.float32
            )
            at += count

    def prepared(j, refs_of, w, row_of):
        left_high, left_low, right = refs_of
        tiles = []
        for part in range(2):
            row = row_of + part * 16
            for pair in range(PHYS // 2):
                columns = slice(pair * lanes, (pair + 1) * lanes)
                upper = mid[j, row : row + SUB, columns]
                lower = mid[j, row + SUB : row + 2 * SUB, columns]
                tiles.append(jnp.where(first, upper, pltpu.roll(lower, half, 1)))
                tiles.append(jnp.where(first, pltpu.roll(upper, half, 1), lower))
        t_high, t_low = split_two(jnp.concatenate(tiles, axis=0))
        lh, ll = left_high[w, first_block + j], left_low[w, first_block + j]
        wide_high = jnp.concatenate([lh * keep_first, lh * keep_second], axis=0)
        wide_low = jnp.concatenate([ll * keep_first, ll * keep_second], axis=0)
        weights = jnp.concatenate([wide_high, wide_low], axis=1)
        weights = jnp.concatenate([weights, weights], axis=0)
        return jnp.concatenate([t_high, t_low], axis=1), weights

    def mix_unit(mixing, w, z):
        z_high, z_low = [jnp.concatenate([x[:lanes], x[lanes:]], axis=1) for x in z]
        return jnp.dot(
            mixing[w],
            jnp.concatenate([z_high, z_low], axis=0),
            preferred_element_type=jnp.float32,
        )

    def add_up(j, table, bond, mixed):
        slot = table[bond, first_block + j]
        slot = ((slot >> 1) ^ me) * 2 + (slot & 1)
        for part in range(2):
            columns = slice(part * lanes, (part + 1) * lanes)
            total_ref[part, slot] += mixed[:lanes, columns] + mixed[lanes:, columns]

    bonds = []
    for (source, start), refs_of, mix in zip(chunks, operands, mixes):
        for w in range(mix.shape[0]):
            bonds.append((refs_of, mix, w, slots[source], start + w))
    right_side(0)
    units = [(j, at) for j in range(step) for at in range(len(bonds))]

    def prepare_unit(n):
        j, at = units[n]
        refs_of, mixing, w, table, bond = bonds[at]
        return prepared(j, refs_of, w, at * 32)

    ready = prepare_unit(0)
    waiting = None
    for n, (j, at) in enumerate(units):
        refs_of, mixing, w, table, bond = bonds[at]
        z = jnp.dot(*ready, preferred_element_type=jnp.float32)
        if j + 1 < step and at == len(bonds) // 3:
            right_side(j + 1)
            if j + 2 == step:
                for copy in kept:
                    copy.start()
        if n + 1 < len(units):
            ready = prepare_unit(n + 1)
        if waiting is not None:
            before_j, before_mixing, before_w, before_table, before_bond, before_z = waiting
            mixed = mix_unit(before_mixing, before_w, before_z)
        z = split_two(z[:, :lanes] + z[:, lanes:])
        if waiting is not None:
            add_up(before_j, before_table, before_bond, mixed)
        waiting = (j, mixing, w, table, bond, z)
    j, mixing, w, table, bond, z = waiting
    add_up(j, table, bond, mix_unit(mixing, w, z))
    for copy in kept:
        copy.wait()

    if pieces:
        stats = jnp.zeros((SUB, lanes), jnp.float32)
        if parts_given:
            tail = vector[0].shape[0] - SUB
            stats = stacked_rows(*merged([x[tail:] for x in vector]))
        for out, part in ((outs[0], info_ref[5]), (outs[1], 1 - info_ref[5])):
            for k in range(4):
                for i in range(2):
                    out[k, i * lanes : (i + 1) * lanes] = total_ref[part, 2 * k + i]
                out[k, 2 * lanes :] = stats
            stats = jnp.zeros((SUB, lanes), jnp.float32)


def apply_bonds(info, slots, vector, chunks, operands, sent, mixes, before, pieces, half_of=None):
    blocks, half, lanes = operands[0][0].shape[1:]
    parts_given = half_of is not None
    step = 4 if parts_given else blocks
    arguments = list(vector) if parts_given else [vector]
    for made in operands:
        arguments += made
    if sent is not None:
        arguments.append(sent)
    arguments += mixes
    aliases = {}
    if before is not None:
        if not pieces:
            aliases[3 + len(arguments)] = 0
        arguments.append(before)
    counts = [mix.shape[0] for mix in mixes]
    shapes = [(4, 2 * lanes + SUB, lanes)] * 2 if pieces else [(2, 8, lanes, lanes)]
    out_shape = [jax.ShapeDtypeStruct(shape, jnp.float32) for shape in shapes]
    if sent is not None:
        out_shape += operand_shapes(counts[-1], blocks, half, lanes)
    scratch = [
        pltpu.VMEM((step if parts_given else 1, lanes, PHYS * half), jnp.bfloat16),
        pltpu.VMEM((step, sum(counts) * 32, PHYS * half), jnp.float32),
    ]
    if pieces:
        scratch.append(pltpu.VMEM((2, 8, lanes, lanes), jnp.float32))
    out_specs = [pl.BlockSpec(memory_space=pltpu.VMEM)] * len(shapes)
    if sent is not None:
        out_specs += [pl.BlockSpec(memory_space=pltpu.HBM)] * 3
        scratch += [pltpu.VMEM(x.shape, x.dtype) for x in out_shape[len(shapes) :]]
        scratch.append(pltpu.SemaphoreType.DMA((3,)))
    plan = (
        tuple(chunks), (half_of or 0) * step, parts_given, sent is not None, before is not None,
        pieces,
    )
    out = pl.pallas_call(
        functools.partial(apply_kernel, plan),
        in_specs=[pl.BlockSpec(memory_space=pltpu.SMEM)] * 3
        + [pl.BlockSpec(memory_space=pltpu.VMEM)] * len(arguments),
        out_specs=out_specs,
        scratch_shapes=scratch,
        out_shape=out_shape,
        input_output_aliases=aliases,
        compiler_params=pltpu.CompilerParams(vmem_limit_bytes=APPLY_VMEM),
        cost_estimate=micros(10 if parts_given else 1),
        name="apply_bonds",
    )(info, *slots, *arguments)
    return out[: len(shapes)], out[len(shapes) :]


def add_arrived(info_ref, owner_ref, arrived, total):
    for k in range(4):
        for i in range(2):
            rows = slice(i * LANES, (i + 1) * LANES)
            total[owner_ref[info_ref[4] ^ k, i]] += arrived[k][rows]


def stacked_rows(*rows):
    at = lax.broadcasted_iota(jnp.int32, (SUB, LANES), 0)
    tile = jnp.zeros((SUB, LANES), jnp.float32)
    for i, row in enumerate(rows):
        tile = jnp.where(at == i, row, tile)
    return tile


def merged(tiles):
    rows = [[tile[i : i + 1] for i in range(3)] for tile in tiles]
    cross = sum(row[0] for row in rows)
    square = sum(row[1] for row in rows)
    ratio = cross / jnp.maximum(square, TINY)
    apart = [
        (row[0] / jnp.maximum(row[1], TINY) - ratio) * jnp.sqrt(row[1]) for row in rows
    ]
    rest = sum(row[2] for row in rows) + sum(x * x for x in apart)
    return cross, square, rest


def image_kernel(info_ref, owner_ref, a3, a2, a1, a0, start_ref, lower_ref, upper_ref, total):
    total[...] = start_ref[...]
    add_arrived(info_ref, owner_ref, (a0, a1, a2, a3), total)
    blocks = total.shape[0]
    for k in range(blocks):
        half = lower_ref if k < blocks // 2 else upper_ref
        at = k % (blocks // 2) * LANES
        half[at : at + LANES] = total[k]


def owner_image(info, owners, arrived, start):
    blocks = start.shape[0]
    shape = jax.ShapeDtypeStruct((blocks // 2 * LANES, LANES), jnp.float32)
    return pl.pallas_call(
        image_kernel,
        in_specs=[pl.BlockSpec(memory_space=pltpu.SMEM)] * 2
        + [pl.BlockSpec(memory_space=pltpu.VMEM)] * 5,
        out_specs=[pl.BlockSpec(memory_space=pltpu.VMEM)] * 2,
        scratch_shapes=[pltpu.VMEM(start.shape, jnp.float32)],
        out_shape=[shape, shape],
        compiler_params=pltpu.CompilerParams(vmem_limit_bytes=SMALL_VMEM),
        cost_estimate=micros(1),
        name="owner_image",
    )(info, owners, *arrived[::-1], start)


def statistics_kernel(own_hbm, lower_ref, upper_ref, out_ref, own_ref, sem):
    copy = pltpu.make_async_copy(own_hbm, own_ref, sem)
    copy.start()
    rows = upper_ref.shape[0]
    out_ref[0:rows] = upper_ref[...]
    copy.wait()
    blocks = own_ref.shape[0]
    images = []
    for half in (lower_ref, upper_ref):
        images += [half.at[pl.ds(k * LANES, LANES)] for k in range(blocks // 2)]
    cross = jnp.zeros((LANES, LANES), jnp.float32)
    square = jnp.zeros((LANES, LANES), jnp.float32)
    for k in range(blocks):
        own = own_ref[k]
        cross += own * images[k][...]
        square += own * own
    cross = jnp.sum(cross, keepdims=True)
    square = jnp.sum(square, keepdims=True)
    ratio = cross / jnp.maximum(square, TINY)
    rest = jnp.zeros((LANES, LANES), jnp.float32)
    for k in range(blocks):
        apart = images[k][...] - ratio * own_ref[k]
        rest += apart * apart
    out_ref[rows:] = stacked_rows(cross, square, jnp.sum(rest, keepdims=True))


def with_statistics(own, lower, upper):
    return pl.pallas_call(
        statistics_kernel,
        in_specs=[pl.BlockSpec(memory_space=pl.ANY)]
        + [pl.BlockSpec(memory_space=pltpu.VMEM)] * 2,
        out_specs=pl.BlockSpec(memory_space=pltpu.VMEM),
        scratch_shapes=[pltpu.VMEM(own.shape, jnp.float32), pltpu.SemaphoreType.DMA],
        out_shape=jax.ShapeDtypeStruct((upper.shape[0] + SUB, LANES), jnp.float32),
        compiler_params=pltpu.CompilerParams(vmem_limit_bytes=SMALL_VMEM),
        cost_estimate=micros(3),
        name="statistics",
    )(*in_hbm(own), lower, upper)


def final_kernel(
    entries, info_ref, owner_ref, a3, a2, a1, a0, diag_any, own_any, lower_any, upper_any,
    first_any, vector_any, second_any, total, diag_ref, own_ref, image_ref, first_ref, vector_ref,
    second_ref, fetched, stored,
):
    arrived = (a0, a1, a2, a3)
    blocks = total.shape[0]
    fetches = []
    for k in range(blocks):
        image = (lower_any if k < blocks // 2 else upper_any).at[
            pl.ds(k % (blocks // 2) * LANES, LANES)
        ]
        fetches.append(
            [
                pltpu.make_async_copy(source, target.at[k], fetched.at[i, k])
                for i, (source, target) in enumerate(
                    ((diag_any.at[k], diag_ref), (own_any.at[k], own_ref), (image, image_ref))
                )
            ]
        )
    for copies in fetches:
        for copy in copies:
            copy.start()
    cross, square, rest = merged([ref[2 * LANES :] for ref in arrived])
    scale = lax.rsqrt(square / entries + 1e-06)
    rayleigh = scale * scale * (cross / entries)
    apart = (cross / jnp.maximum(square, TINY) - rayleigh) * jnp.sqrt(square)
    mean = scale * scale * ((rest + apart * apart) / entries)
    second_scale = scale * lax.rsqrt(mean + 1e-06)
    total[...] = jnp.zeros_like(total)
    add_arrived(info_ref, owner_ref, arrived, total)
    stores = []
    for k in range(blocks):
        for copy in fetches[k]:
            copy.wait()
        image = image_ref[k]
        first_ref[k] = unpack_tile(scale * image)
        vector_ref[k] = unpack_tile(second_scale * (image - rayleigh * own_ref[k]))
        image = (diag_ref[k] - rayleigh) * image + total[k]
        second_ref[k] = unpack_tile(second_scale * image)
        for i, (source, target) in enumerate(
            ((first_ref, first_any), (vector_ref, vector_any), (second_ref, second_any))
        ):
            copy = pltpu.make_async_copy(source.at[k], target.at[k], stored.at[i, k])
            copy.start()
            stores.append(copy)
    for copy in stores:
        copy.wait()


def outputs(info, owners, arrived, diagonal, own, images, entries):
    blocks = diagonal.shape[0]
    shape = (blocks, LANES // 2, 2 * LANES)
    return pl.pallas_call(
        functools.partial(final_kernel, entries),
        in_specs=[pl.BlockSpec(memory_space=pltpu.SMEM)] * 2
        + [pl.BlockSpec(memory_space=pltpu.VMEM)] * 4
        + [pl.BlockSpec(memory_space=pl.ANY)] * 4,
        out_specs=[pl.BlockSpec(memory_space=pl.ANY)] * 3,
        scratch_shapes=[pltpu.VMEM(diagonal.shape, jnp.float32)] * 4
        + [pltpu.VMEM(shape, jnp.float32)] * 3
        + [pltpu.SemaphoreType.DMA((3, blocks))] * 2,
        out_shape=[jax.ShapeDtypeStruct(shape, jnp.float32)] * 3,
        compiler_params=pltpu.CompilerParams(vmem_limit_bytes=SMALL_VMEM),
        cost_estimate=micros(4),
        name="outputs",
    )(info, owners, *arrived[::-1], diagonal, own, *images)


def in_hbm(*arrays):
    return [pltpu.with_memory_space_constraint(x, pltpu.HBM) for x in arrays]


def partner(x, axis, k):
    size = lax.axis_size(axis)
    return lax.ppermute(x, axis, [(i, i ^ k) for i in range(size)])


def after(x, *others):
    return lax.optimization_barrier((x, *others))[0]


def gathered(x):
    across = partner(x, "mpo", 1)
    return [x, across, partner(x, "rep", 1), partner(across, "rep", 1)]


def everyone_of(pieces, axis):
    return [pieces[0]] + [partner(pieces[k], axis, k) for k in range(1, 4)]


def to_owners(mine, theirs):
    other = partner(theirs, "rep", 1)
    pieces = [mine[k] + other[k] for k in range(4)]
    return everyone_of(pieces, "blk")


def per_device(wavefunction, environment, bond_terms, diagonal, term_slot, slot_block):
    blocks, rows, width = wavefunction.shape
    zs = lax.axis_size("blk")
    mpo, rep, blk = lax.axis_index("mpo"), lax.axis_index("rep"), lax.axis_index("blk")
    place = 2 * mpo + rep
    info = jnp.stack([place, place ^ 2, place ^ 1, place ^ 3, blk, rep, mpo]).astype(jnp.int32)
    bonds = environment.shape[0]
    sizes = tuple(bonds * part // 6 for part in (2, 2, 2))
    firsts = tuple(sum(sizes[:group]) for group in range(len(sizes)))
    entries = float(blocks * zs * rows * width)

    vector, own, diagonal_packed = pack(info, wavefunction, diagonal)

    by_owner = environment.reshape(bonds, zs, blocks, rows // zs, 2 * rows)
    pieces = []
    for group in range(len(sizes)):
        cuts = list(cut_pieces(info, by_owner, firsts[group], sizes[group]))
        if group:
            cuts[1:] = [after(x, y) for x, y in zip(cuts[1:], pieces[-1][1:])]
        pieces.append(cuts[:1] + [partner(cuts[k], "blk", k) for k in range(1, 4)])
    pieces[0][1] = after(pieces[0][1], vector)
    phys = bond_terms.shape[-1]
    table = jnp.pad(term_slot.astype(jnp.float32), ((0, 0), (0, phys - blocks)))
    tables = jnp.pad(table[:, None], ((0, 0), (0, SUB - 1), (0, 0)))
    both = jnp.concatenate([bond_terms, tables], axis=1)
    other_terms = partner(after(both, pieces[0][1]), "mpo", 1)
    mixing = mixing_operands([bond_terms, other_terms], sizes)
    slots = [term_slot, other_terms[:, phys, :blocks].astype(jnp.int32)]

    made, sent = [], []
    total = None
    operands = []
    done = 0

    def apply_group(group, vector):
        out, other = apply_bonds(
            info, slots, vector, [(0, firsts[group]), (1, firsts[group])], [made[group]],
            partner(sent[group], "mpo", 1), [terms[group] for terms in mixing], total,
            group == len(sizes) - 1,
        )
        operands.extend([made[group], other])
        return out

    for group in range(len(sizes)):
        if group >= 2:
            total = apply_group(group - 2, after(vector, sent[group - 1]))[0]
            pieces[group][3] = after(pieces[group][3], total)
        if group < 1:
            pieces[group][1] = after(pieces[group][1], pieces[group + 1][1])
        *own_set, send = own_operands(info, pieces[group])
        made.append(own_set)
        sent.append(send)
    total = apply_group(len(sizes) - 2, after(vector, sent[-1]))[0]
    out = apply_group(len(sizes) - 1, vector)
    arrived = to_owners(*out)
    start = after(diagonal_packed, arrived[0]) * own
    lower, upper = owner_image(info, slot_block, arrived, start)
    upper = with_statistics(own, lower, upper)

    chunks = [(source, first) for first in firsts for source in range(2)]
    mixes = [mixing[source][group] for group in range(len(sizes)) for source in range(2)]
    lower_parts = [lower, partner(lower, "mpo", 1), partner(lower, "rep", 1)]
    lower_parts.append(partner(after(lower_parts[1], upper), "rep", 1))
    across = partner(after(upper, lower_parts[1]), "mpo", 1)
    out, _ = apply_bonds(
        info, slots, lower_parts, chunks, operands, None, mixes, None, False, 0
    )
    upper_parts = [upper, across, partner(upper, "rep", 1)]
    upper_parts.append(partner(after(across, out[0]), "rep", 1))
    out, _ = apply_bonds(
        info, slots, upper_parts, chunks, operands, None, mixes, out[0], True, 1
    )
    return tuple(
        outputs(
            info, slot_block, to_owners(*out), diagonal_packed, own, (lower, upper), entries
        )
    )


def solution(mesh):
    packed = mesh.shape["mpo"] == 2 and mesh.shape["rep"] == 2 and mesh.shape["blk"] == 4
    return jax.shard_map(
        per_device if packed else plain_device,
        mesh=mesh,
        in_specs=(
            P(("grp", "blk"), None, None),
            P(("grp", "mpo", "rep"), None, "blk", None),
            P(("grp", "mpo", "rep"), None, None),
            P(("grp", "blk"), None, ("mpo", "rep")),
            P(("grp", "mpo", "rep"), "blk"),
            P("grp", "blk"),
        ),
        out_specs=(
            P(("grp", "blk"), None, ("mpo", "rep")),
            P(("grp", "blk"), None, ("mpo", "rep")),
            P(("grp", "blk"), None, ("mpo", "rep")),
        ),
        check_vma=False,
    )
```

```python
import functools

import jax
import jax.numpy as jnp
from jax import lax
from jax.experimental import pallas as pl
from jax.experimental.pallas import tpu as pltpu
from jax.sharding import PartitionSpec as P

LANES = 128
SUB = 8
PHYS = 16
TINY = 1e-30
SMALL_VMEM = 16 * 1024 * 1024
APPLY_VMEM = 16 * 1024 * 1024


def plain_apply(vector_full, environment, bond_terms, term_slot, slot_block, diagonal):
    block_count, block_rows, block_width = vector_full.shape
    phys_size = bond_terms.shape[-1]
    right_rows = block_width // phys_size
    slot_count = slot_block.shape[0] * slot_block.shape[1]
    blocks = vector_full.reshape(block_count, block_rows, right_rows, phys_size)
    ordered = jnp.transpose(blocks, (0, 3, 1, 2))
    left_env = environment[:, :, :, :block_rows]
    right_env = environment[:, :, :, block_rows:]
    left_done = jnp.einsum("wjab,jsac->wjsbc", left_env, ordered, precision=lax.Precision.HIGHEST)
    right_done = jnp.einsum(
        "wjsbc,wjcd->wjsbd", left_done, right_env, precision=lax.Precision.HIGHEST
    )
    right_done = right_done.reshape(
        environment.shape[0], block_count, phys_size, block_rows * right_rows
    )
    bond_term = jnp.einsum(
        "wjsx,wst->wjtx", right_done, bond_terms, precision=lax.Precision.HIGHEST
    )
    bond_term = bond_term.reshape(environment.shape[0], block_count, block_rows * block_width)
    slot_table = (
        term_slot[:, None, :] == jnp.arange(slot_count, dtype=jnp.int32)[None, :, None]
    ).astype(jnp.float32)
    slot_buffer = jnp.einsum("wsj,wjx->sx", slot_table, bond_term, precision=lax.Precision.HIGHEST)
    slot_buffer = slot_buffer.reshape(slot_count, phys_size, block_rows, right_rows)
    slot_buffer = jnp.transpose(slot_buffer, (0, 2, 3, 1)).reshape(
        slot_count, block_rows, block_width
    )
    owners = slot_block.reshape(-1)
    selector = (owners[None, :] == jnp.arange(block_count, dtype=jnp.int32)[:, None]).astype(
        jnp.float32
    )
    column_width = block_width // lax.axis_size(("mpo", "rep"))
    column_start = lax.axis_index(("mpo", "rep")) * column_width
    own_part = lax.dynamic_slice_in_dim(vector_full, column_start, column_width, 2)
    shares = lax.psum_scatter(slot_buffer, ("mpo", "rep"), scatter_dimension=2, tiled=True)
    arrived = lax.all_to_all(shares, "blk", split_axis=0, concat_axis=0, tiled=True)
    result = jnp.einsum("ks,sbc->kbc", selector, arrived, precision=lax.Precision.HIGHEST)
    return (result + diagonal * own_part, own_part)


def plain_device(wavefunction, environment, bond_terms, diagonal, term_slot, slot_block):
    arranged = lax.all_to_all(environment, "blk", split_axis=1, concat_axis=2, tiled=True)
    entries = float(
        wavefunction.shape[0] * lax.axis_size("blk") * wavefunction.shape[1] * wavefunction.shape[2]
    )
    square_sum = lax.psum(jnp.sum(wavefunction * wavefunction), "blk")
    first_vector = wavefunction * lax.rsqrt(square_sum / entries + 1e-06)
    first_image, first_part = plain_apply(
        first_vector, arranged, bond_terms, term_slot, slot_block, diagonal
    )
    rayleigh = lax.psum(jnp.sum(first_part * first_image), ("blk", "mpo", "rep")) / entries
    residual = first_image - rayleigh * first_part
    resid_sum = lax.psum(jnp.sum(residual * residual), ("blk", "mpo", "rep"))
    second_vector = residual * lax.rsqrt(resid_sum / entries + 1e-06)
    second_full = lax.all_gather(second_vector, ("mpo", "rep"), axis=2, tiled=True)
    second_image, unused = plain_apply(
        second_full, arranged, bond_terms, term_slot, slot_block, diagonal
    )
    return (first_image, second_vector, second_image)


def split_two(x):
    high = x.astype(jnp.bfloat16)
    low = (x - high.astype(jnp.float32)).astype(jnp.bfloat16)
    return high, low


def lane_is_first(rows):
    return lax.broadcasted_iota(jnp.int32, (rows, LANES), 1) < LANES // 2


def micros(count):
    return pl.CostEstimate(flops=count * 1100000000, bytes_accessed=1 << 20, transcendentals=0)


def whole(*shape):
    return pl.BlockSpec(shape, lambda i, *_: (0,) * len(shape))


def pack_tile(x):
    return jnp.concatenate([x[:, :LANES], x[:, LANES:]], axis=0).T


def unpack_tile(x):
    upright = x.T
    return jnp.concatenate([upright[: LANES // 2], upright[LANES // 2 :]], axis=1)


def store_vector(parts, rows_of, put):
    first = lane_is_first(SUB)
    for pair in range(PHYS // 2):
        for part, row in zip(parts, rows_of):
            even = part[pl.ds(2 * pair, SUB, stride=PHYS), :]
            odd = part[pl.ds(2 * pair + 1, SUB, stride=PHYS), :]
            upper = jnp.where(first, even, pltpu.roll(odd, LANES // 2, 1))
            lower = jnp.where(first, pltpu.roll(even, LANES // 2, 1), odd)
            high, low = split_two(jnp.concatenate([upper, lower], axis=0))
            put(row, pair, high, low)


def pack_kernel(info_ref, wave_ref, own_wave_ref, diag_ref, vec_ref, own_ref, diag_out, tiles):
    half = LANES // 2
    for j in range(wave_ref.shape[0]):
        own_ref[j] = pack_tile(own_wave_ref[j])
        diag_out[j] = pack_tile(diag_ref[j])
        for q in range(4):
            tiles[q, j] = pack_tile(wave_ref[j, :, 2 * LANES * q : 2 * LANES * (q + 1)])

        def put(row, pair, high, low):
            columns = slice(pair * LANES, (pair + 1) * LANES)
            vec_ref[j, row : row + 16, columns] = high
            vec_ref[j, row + half : row + half + 16, columns] = low

        store_vector([tiles.at[q, j] for q in range(4)], [16 * q for q in range(4)], put)


def pack(info, wavefunction, diagonal):
    blocks, rows, width = wavefunction.shape
    step = 2
    tile = pl.BlockSpec((step, LANES, LANES), lambda i, *_: (i, 0, 0))
    return pl.pallas_call(
        pack_kernel,
        grid_spec=pltpu.PrefetchScalarGridSpec(
            num_scalar_prefetch=1,
            grid=(blocks // step,),
            in_specs=[
                pl.BlockSpec((step, rows, width), lambda i, *_: (i, 0, 0)),
                pl.BlockSpec((step, rows, width // 4), lambda i, info: (i, 0, info[0])),
                pl.BlockSpec((step, rows, width // 4), lambda i, *_: (i, 0, 0)),
            ],
            out_specs=[pl.BlockSpec((step, LANES, width), lambda i, *_: (i, 0, 0))] + [tile] * 2,
            scratch_shapes=[pltpu.VMEM((4, step, LANES, LANES), jnp.float32)],
        ),
        out_shape=[
            jax.ShapeDtypeStruct((blocks, LANES, width), jnp.bfloat16),
        ]
        + [jax.ShapeDtypeStruct((blocks, LANES, LANES), jnp.float32)] * 2,
        compiler_params=pltpu.CompilerParams(vmem_limit_bytes=SMALL_VMEM),
        cost_estimate=micros(5),
        name="pack",
    )(info, wavefunction, wavefunction, diagonal)


def mixing_kernel(sizes, *refs):
    sources, outs = refs[:2], refs[2:]
    spread = (
        lax.broadcasted_iota(jnp.int32, (PHYS, LANES), 1) // SUB
        == lax.broadcasted_iota(jnp.int32, (PHYS, LANES), 0)
    ).astype(jnp.bfloat16)
    row = lax.broadcasted_iota(jnp.int32, (LANES, LANES), 0) // PHYS
    column = lax.broadcasted_iota(jnp.int32, (LANES, LANES), 1) % SUB
    same = row == column
    for n, source in enumerate(sources):
        start = 0
        for group, size in enumerate(sizes):
            out_ref = outs[n * len(sizes) + group]
            for at in range(size):
                for place, term in enumerate(split_two(source[start + at].T)):
                    wide = jnp.dot(term, spread, preferred_element_type=jnp.float32)
                    tall = jnp.concatenate([wide] * SUB, axis=0)
                    tall = jnp.where(same, tall, 0.0).astype(jnp.bfloat16)
                    rows = slice(place * LANES, (place + 1) * LANES)
                    out_ref[at, rows] = jnp.concatenate([tall, tall], axis=1)
            start += size


def mixing_operands(sources, sizes):
    out = pl.pallas_call(
        functools.partial(mixing_kernel, sizes),
        out_shape=[
            jax.ShapeDtypeStruct((size, 2 * LANES, 2 * LANES), jnp.bfloat16)
            for _ in sources
            for size in sizes
        ],
        compiler_params=pltpu.CompilerParams(vmem_limit_bytes=SMALL_VMEM),
        cost_estimate=micros(2),
        name="mixing",
    )(*sources)
    return [out[: len(sizes)], out[len(sizes) :]]


def own_operands_kernel(info_ref, *refs):
    pieces, (left_high, left_low, right_out, send, blocks_ref, upright_ref) = refs[:4], refs[4:]
    per, blocks, half, lanes = left_high.shape
    rows = half // 4
    wide = half // 2
    first = lane_is_first(half)
    first_wide = lane_is_first(wide)
    first_rows = lane_is_first(rows)
    mine_at = pl.multiple_of(half + info_ref[6] * wide, wide)
    theirs_at = pl.multiple_of(lanes - wide - info_ref[6] * wide, wide)
    for j in range(blocks):
        for w in range(per):
            for z in range(4):
                row = pl.multiple_of((info_ref[4] ^ z) * rows, rows)
                blocks_ref[w, j, pl.ds(row, rows), :] = pieces[z][w, j]
        for w in range(per):
            block = blocks_ref[w, j]
            upright_ref[w, j] = jnp.concatenate([block, block], axis=0).T
            turned = pltpu.roll(block, half, 1)
            high, low = split_two(jnp.where(first, block, turned))
            left_high[w, j] = high
            left_low[w, j] = low
            send[w, j, 0:wide] = jnp.where(first_wide, block[:wide], turned[wide:])
        for w in range(per):
            high, low = split_two(upright_ref[w, j, pl.ds(mine_at, wide), :])
            right_out[j, wide * w : wide * (w + 1), 0:lanes] = high
            right_out[j, wide * w : wide * (w + 1), lanes:] = low
            upper = upright_ref[w, j, pl.ds(theirs_at, rows), :]
            lower = upright_ref[w, j, pl.ds(theirs_at + rows, rows), :]
            send[w, j, wide : wide + rows] = jnp.where(first_rows, upper, lower)


def other_operands(sent, left_high, left_low, right_out, j):
    per, blocks, half, lanes = left_high.shape
    rows = half // 4
    wide = half // 2
    first = lane_is_first(wide)
    first_rows = lane_is_first(rows)
    for w in range(per):
        both = sent[w, j, 0:wide]
        turned = pltpu.roll(both, half, 1)
        full = jnp.concatenate(
            [jnp.where(first, both, turned), jnp.where(first, turned, both)], axis=0
        )
        high, low = split_two(full)
        left_high[w, j] = high
        left_low[w, j] = low
        both = sent[w, j, wide : wide + rows]
        turned = pltpu.roll(both, half, 1)
        full = jnp.concatenate(
            [jnp.where(first_rows, both, turned), jnp.where(first_rows, turned, both)], axis=0
        )
        high, low = split_two(full)
        right_out[j, wide * w : wide * (w + 1), 0:lanes] = high
        right_out[j, wide * w : wide * (w + 1), lanes:] = low


def operand_specs(per, step, half, lanes, at=0):
    return [
        pl.BlockSpec((per, step, half, lanes), lambda i, *_: (0, at + i, 0, 0)),
        pl.BlockSpec((per, step, half, lanes), lambda i, *_: (0, at + i, 0, 0)),
        pl.BlockSpec((step, per * 32, 2 * lanes), lambda i, *_: (at + i, 0, 0)),
    ]


def operand_shapes(per, blocks, half, lanes):
    return [
        jax.ShapeDtypeStruct((per, blocks, half, lanes), jnp.bfloat16),
        jax.ShapeDtypeStruct((per, blocks, half, lanes), jnp.bfloat16),
        jax.ShapeDtypeStruct((blocks, per * 32, 2 * lanes), jnp.bfloat16),
    ]


def cut_kernel(first, info_ref, source, *refs):
    outs, sems = refs[:4], refs[4]
    per = outs[0].shape[0]
    copies = []
    for k in range(4):
        part = source.at[pl.ds(first, per), info_ref[4] ^ k]
        copies.append(pltpu.make_async_copy(part, outs[k], sems.at[k]))
    for copy in copies:
        copy.start()
    for copy in copies:
        copy.wait()


def cut_pieces(info, by_owner, first, per):
    shape = jax.ShapeDtypeStruct((per,) + by_owner.shape[2:], jnp.float32)
    return pl.pallas_call(
        functools.partial(cut_kernel, first),
        grid_spec=pltpu.PrefetchScalarGridSpec(
            num_scalar_prefetch=1,
            grid=(1,),
            in_specs=[pl.BlockSpec(memory_space=pl.ANY)],
            out_specs=[pl.BlockSpec(memory_space=pl.ANY)] * 4,
            scratch_shapes=[pltpu.SemaphoreType.DMA((4,))],
        ),
        out_shape=[shape] * 4,
        compiler_params=pltpu.CompilerParams(vmem_limit_bytes=SMALL_VMEM),
        cost_estimate=micros(1),
        name="cut_pieces",
    )(info, *(in_hbm(by_owner) if first == 0 else [by_owner]))


def own_operands(info, pieces):
    per, blocks, rows, lanes = pieces[0].shape
    half = lanes // 2
    step = 4
    return pl.pallas_call(
        own_operands_kernel,
        grid_spec=pltpu.PrefetchScalarGridSpec(
            num_scalar_prefetch=1,
            grid=(blocks // step,),
            in_specs=[pl.BlockSpec((per, step, rows, lanes), lambda i, *_: (0, i, 0, 0))] * 4,
            out_specs=operand_specs(per, step, half, lanes)
            + [pl.BlockSpec((per, step, 3 * rows, lanes), lambda i, *_: (0, i, 0, 0))],
            scratch_shapes=[
                pltpu.VMEM((per, step, half, lanes), jnp.float32),
                pltpu.VMEM((per, step, lanes, lanes), jnp.float32),
            ],
        ),
        out_shape=operand_shapes(per, blocks, half, lanes)
        + [jax.ShapeDtypeStruct((per, blocks, 3 * rows, lanes), jnp.float32)],
        compiler_params=pltpu.CompilerParams(vmem_limit_bytes=SMALL_VMEM),
        cost_estimate=micros(12),
        name="own_operands",
    )(info, *pieces)


def apply_kernel(plan, info_ref, *refs):
    chunks, first_block, parts_given, sent_given, before_given, pieces = plan
    refs = list(refs)
    take = lambda n: [refs.pop(0) for _ in range(n)]
    slots = take(2)
    vector = take(4 if parts_given else 1)
    operands = [take(3) for _ in chunks[: -1 if sent_given else None]]
    sent = take(1)[0] if sent_given else None
    mixes = take(len(chunks))
    before = take(1)[0] if before_given else None
    outs = take(2 if pieces else 1)
    made = take(3) if sent_given else []
    scratch = take(2)
    vec, mid = scratch
    total_ref = take(1)[0] if pieces else outs[0]
    kept = []
    if sent_given:
        operands.append(take(3))
        sems = take(1)[0]
        kept = [
            pltpu.make_async_copy(operands[-1][i], made[i], sems.at[i]) for i in range(3)
        ]
    step = mid.shape[0]
    lanes, half = LANES, LANES // 2
    first = lane_is_first(SUB)
    first_half = lane_is_first(half)
    keep_first = jnp.where(first_half, 1.0, 0.0).astype(jnp.bfloat16)
    keep_second = jnp.where(first_half, 0.0, 1.0).astype(jnp.bfloat16)
    me = info_ref[4]

    if not before_given:
        total_ref[...] = jnp.zeros_like(total_ref)
    else:
        total_ref[...] = before[...]

    def right_side(j):
        if sent_given:
            other_operands(sent, *operands[-1], first_block + j)
        if parts_given:

            def put(row, pair, high, low):
                columns = slice(pair * lanes, (pair + 1) * lanes)
                vec[j, pl.ds(row, 16), columns] = high
                vec[j, pl.ds(row + half, 16), columns] = low

            rows_of = [pl.multiple_of(info_ref[g] * 16, 16) for g in range(4)]
            store_vector([x.at[pl.ds(j * lanes, lanes)] for x in vector], rows_of, put)
            source = vec[j]
        else:
            source = vector[0][first_block + j]
        source = jnp.concatenate([source, source], axis=0)
        at = 0
        for left_high, left_low, right in operands:
            count = right.shape[1]
            mid[j, at : at + count, :] = jnp.dot(
                right[first_block + j], source, preferred_element_type=jnp.float32
            )
            at += count

    def prepared(j, refs_of, w, row_of):
        left_high, left_low, right = refs_of
        tiles = []
        for part in range(2):
            row = row_of + part * 16
            for pair in range(PHYS // 2):
                columns = slice(pair * lanes, (pair + 1) * lanes)
                upper = mid[j, row : row + SUB, columns]
                lower = mid[j, row + SUB : row + 2 * SUB, columns]
                tiles.append(jnp.where(first, upper, pltpu.roll(lower, half, 1)))
                tiles.append(jnp.where(first, pltpu.roll(upper, half, 1), lower))
        t_high, t_low = split_two(jnp.concatenate(tiles, axis=0))
        lh, ll = left_high[w, first_block + j], left_low[w, first_block + j]
        wide_high = jnp.concatenate([lh * keep_first, lh * keep_second], axis=0)
        wide_low = jnp.concatenate([ll * keep_first, ll * keep_second], axis=0)
        weights = jnp.concatenate([wide_high, wide_low], axis=1)
        weights = jnp.concatenate([weights, weights], axis=0)
        return jnp.concatenate([t_high, t_low], axis=1), weights

    def mix_unit(mixing, w, z):
        z_high, z_low = [jnp.concatenate([x[:lanes], x[lanes:]], axis=1) for x in z]
        return jnp.dot(
            mixing[w],
            jnp.concatenate([z_high, z_low], axis=0),
            preferred_element_type=jnp.float32,
        )

    def add_up(j, table, bond, mixed):
        slot = table[bond, first_block + j]
        slot = ((slot >> 1) ^ me) * 2 + (slot & 1)
        for part in range(2):
            columns = slice(part * lanes, (part + 1) * lanes)
            total_ref[part, slot] += mixed[:lanes, columns] + mixed[lanes:, columns]

    bonds = []
    for (source, start), refs_of, mix in zip(chunks, operands, mixes):
        for w in range(mix.shape[0]):
            bonds.append((refs_of, mix, w, slots[source], start + w))
    right_side(0)
    units = [(j, at) for j in range(step) for at in range(len(bonds))]

    def prepare_unit(n):
        j, at = units[n]
        refs_of, mixing, w, table, bond = bonds[at]
        return prepared(j, refs_of, w, at * 32)

    ready = prepare_unit(0)
    waiting = None
    for n, (j, at) in enumerate(units):
        refs_of, mixing, w, table, bond = bonds[at]
        z = jnp.dot(*ready, preferred_element_type=jnp.float32)
        if j + 1 < step and at == len(bonds) // 3:
            right_side(j + 1)
            if j + 2 == step:
                for copy in kept:
                    copy.start()
        if n + 1 < len(units):
            ready = prepare_unit(n + 1)
        if waiting is not None:
            before_j, before_mixing, before_w, before_table, before_bond, before_z = waiting
            mixed = mix_unit(before_mixing, before_w, before_z)
        z = split_two(z[:, :lanes] + z[:, lanes:])
        if waiting is not None:
            add_up(before_j, before_table, before_bond, mixed)
        waiting = (j, mixing, w, table, bond, z)
    j, mixing, w, table, bond, z = waiting
    add_up(j, table, bond, mix_unit(mixing, w, z))
    for copy in kept:
        copy.wait()

    if pieces:
        stats = jnp.zeros((SUB, lanes), jnp.float32)
        if parts_given:
            tail = vector[0].shape[0] - SUB
            stats = stacked_rows(*merged([x[tail:] for x in vector]))
        for out, part in ((outs[0], info_ref[5]), (outs[1], 1 - info_ref[5])):
            for k in range(4):
                for i in range(2):
                    out[k, i * lanes : (i + 1) * lanes] = total_ref[part, 2 * k + i]
                out[k, 2 * lanes :] = stats
            stats = jnp.zeros((SUB, lanes), jnp.float32)


def apply_bonds(info, slots, vector, chunks, operands, sent, mixes, before, pieces, half_of=None):
    blocks, half, lanes = operands[0][0].shape[1:]
    parts_given = half_of is not None
    step = 4 if parts_given else blocks
    arguments = list(vector) if parts_given else [vector]
    for made in operands:
        arguments += made
    if sent is not None:
        arguments.append(sent)
    arguments += mixes
    aliases = {}
    if before is not None:
        if not pieces:
            aliases[3 + len(arguments)] = 0
        arguments.append(before)
    counts = [mix.shape[0] for mix in mixes]
    shapes = [(4, 2 * lanes + SUB, lanes)] * 2 if pieces else [(2, 8, lanes, lanes)]
    out_shape = [jax.ShapeDtypeStruct(shape, jnp.float32) for shape in shapes]
    if sent is not None:
        out_shape += operand_shapes(counts[-1], blocks, half, lanes)
    scratch = [
        pltpu.VMEM((step if parts_given else 1, lanes, PHYS * half), jnp.bfloat16),
        pltpu.VMEM((step, sum(counts) * 32, PHYS * half), jnp.float32),
    ]
    if pieces:
        scratch.append(pltpu.VMEM((2, 8, lanes, lanes), jnp.float32))
    out_specs = [pl.BlockSpec(memory_space=pltpu.VMEM)] * len(shapes)
    if sent is not None:
        out_specs += [pl.BlockSpec(memory_space=pltpu.HBM)] * 3
        scratch += [pltpu.VMEM(x.shape, x.dtype) for x in out_shape[len(shapes) :]]
        scratch.append(pltpu.SemaphoreType.DMA((3,)))
    plan = (
        tuple(chunks), (half_of or 0) * step, parts_given, sent is not None, before is not None,
        pieces,
    )
    out = pl.pallas_call(
        functools.partial(apply_kernel, plan),
        in_specs=[pl.BlockSpec(memory_space=pltpu.SMEM)] * 3
        + [pl.BlockSpec(memory_space=pltpu.VMEM)] * len(arguments),
        out_specs=out_specs,
        scratch_shapes=scratch,
        out_shape=out_shape,
        input_output_aliases=aliases,
        compiler_params=pltpu.CompilerParams(vmem_limit_bytes=APPLY_VMEM),
        cost_estimate=micros(10 if parts_given else 1),
        name="apply_bonds",
    )(info, *slots, *arguments)
    return out[: len(shapes)], out[len(shapes) :]


def add_arrived(info_ref, owner_ref, arrived, total):
    for k in range(4):
        for i in range(2):
            rows = slice(i * LANES, (i + 1) * LANES)
            total[owner_ref[info_ref[4] ^ k, i]] += arrived[k][rows]


def stacked_rows(*rows):
    at = lax.broadcasted_iota(jnp.int32, (SUB, LANES), 0)
    tile = jnp.zeros((SUB, LANES), jnp.float32)
    for i, row in enumerate(rows):
        tile = jnp.where(at == i, row, tile)
    return tile


def merged(tiles):
    rows = [[tile[i : i + 1] for i in range(3)] for tile in tiles]
    cross = sum(row[0] for row in rows)
    square = sum(row[1] for row in rows)
    ratio = cross / jnp.maximum(square, TINY)
    apart = [
        (row[0] / jnp.maximum(row[1], TINY) - ratio) * jnp.sqrt(row[1]) for row in rows
    ]
    rest = sum(row[2] for row in rows) + sum(x * x for x in apart)
    return cross, square, rest


def image_kernel(info_ref, owner_ref, a3, a2, a1, a0, start_ref, lower_ref, upper_ref, total):
    total[...] = start_ref[...]
    add_arrived(info_ref, owner_ref, (a0, a1, a2, a3), total)
    blocks = total.shape[0]
    for k in range(blocks):
        half = lower_ref if k < blocks // 2 else upper_ref
        at = k % (blocks // 2) * LANES
        half[at : at + LANES] = total[k]


def owner_image(info, owners, arrived, start):
    blocks = start.shape[0]
    shape = jax.ShapeDtypeStruct((blocks // 2 * LANES, LANES), jnp.float32)
    return pl.pallas_call(
        image_kernel,
        in_specs=[pl.BlockSpec(memory_space=pltpu.SMEM)] * 2
        + [pl.BlockSpec(memory_space=pltpu.VMEM)] * 5,
        out_specs=[pl.BlockSpec(memory_space=pltpu.VMEM)] * 2,
        scratch_shapes=[pltpu.VMEM(start.shape, jnp.float32)],
        out_shape=[shape, shape],
        compiler_params=pltpu.CompilerParams(vmem_limit_bytes=SMALL_VMEM),
        cost_estimate=micros(1),
        name="owner_image",
    )(info, owners, *arrived[::-1], start)


def statistics_kernel(own_hbm, lower_ref, upper_ref, out_ref, own_ref, sem):
    copy = pltpu.make_async_copy(own_hbm, own_ref, sem)
    copy.start()
    rows = upper_ref.shape[0]
    out_ref[0:rows] = upper_ref[...]
    copy.wait()
    blocks = own_ref.shape[0]
    images = []
    for half in (lower_ref, upper_ref):
        images += [half.at[pl.ds(k * LANES, LANES)] for k in range(blocks // 2)]
    cross = jnp.zeros((LANES, LANES), jnp.float32)
    square = jnp.zeros((LANES, LANES), jnp.float32)
    for k in range(blocks):
        own = own_ref[k]
        cross += own * images[k][...]
        square += own * own
    cross = jnp.sum(cross, keepdims=True)
    square = jnp.sum(square, keepdims=True)
    ratio = cross / jnp.maximum(square, TINY)
    rest = jnp.zeros((LANES, LANES), jnp.float32)
    for k in range(blocks):
        apart = images[k][...] - ratio * own_ref[k]
        rest += apart * apart
    out_ref[rows:] = stacked_rows(cross, square, jnp.sum(rest, keepdims=True))


def with_statistics(own, lower, upper):
    return pl.pallas_call(
        statistics_kernel,
        in_specs=[pl.BlockSpec(memory_space=pl.ANY)]
        + [pl.BlockSpec(memory_space=pltpu.VMEM)] * 2,
        out_specs=pl.BlockSpec(memory_space=pltpu.VMEM),
        scratch_shapes=[pltpu.VMEM(own.shape, jnp.float32), pltpu.SemaphoreType.DMA],
        out_shape=jax.ShapeDtypeStruct((upper.shape[0] + SUB, LANES), jnp.float32),
        compiler_params=pltpu.CompilerParams(vmem_limit_bytes=SMALL_VMEM),
        cost_estimate=micros(3),
        name="statistics",
    )(*in_hbm(own), lower, upper)


def final_kernel(
    entries, info_ref, owner_ref, a3, a2, a1, a0, diag_ref, own_ref, lower_ref, upper_ref,
    first_ref, vector_ref, second_ref, total,
):
    arrived = (a0, a1, a2, a3)
    cross, square, rest = merged([ref[2 * LANES :] for ref in arrived])
    scale = lax.rsqrt(square / entries + 1e-06)
    rayleigh = scale * scale * (cross / entries)
    apart = (cross / jnp.maximum(square, TINY) - rayleigh) * jnp.sqrt(square)
    mean = scale * scale * ((rest + apart * apart) / entries)
    second_scale = scale * lax.rsqrt(mean + 1e-06)
    for k in range(total.shape[0]):
        at = k % (total.shape[0] // 2) * LANES
        image = (lower_ref if k < total.shape[0] // 2 else upper_ref)[at : at + LANES]
        total[k] = (diag_ref[k] - rayleigh) * image
        first_ref[k] = unpack_tile(scale * image)
        vector_ref[k] = unpack_tile(second_scale * (image - rayleigh * own_ref[k]))
    add_arrived(info_ref, owner_ref, arrived, total)
    for k in range(total.shape[0]):
        second_ref[k] = unpack_tile(second_scale * total[k])


def outputs(info, owners, arrived, diagonal, own, images, entries):
    blocks = diagonal.shape[0]
    shape = (blocks, LANES // 2, 2 * LANES)
    return pl.pallas_call(
        functools.partial(final_kernel, entries),
        grid_spec=pltpu.PrefetchScalarGridSpec(
            num_scalar_prefetch=2,
            grid=(1,),
            in_specs=[whole(*x.shape) for x in (*arrived, diagonal, own)]
            + [whole(blocks // 2 * LANES, LANES)] * 2,
            out_specs=[whole(*shape)] * 3,
            scratch_shapes=[pltpu.VMEM(diagonal.shape, jnp.float32)],
        ),
        out_shape=[jax.ShapeDtypeStruct(shape, jnp.float32)] * 3,
        compiler_params=pltpu.CompilerParams(vmem_limit_bytes=SMALL_VMEM),
        cost_estimate=micros(4),
        name="outputs",
    )(info, owners, *arrived[::-1], diagonal, own, *images)


def in_hbm(*arrays):
    return [pltpu.with_memory_space_constraint(x, pltpu.HBM) for x in arrays]


def partner(x, axis, k):
    size = lax.axis_size(axis)
    return lax.ppermute(x, axis, [(i, i ^ k) for i in range(size)])


def after(x, *others):
    return lax.optimization_barrier((x, *others))[0]


def gathered(x):
    across = partner(x, "mpo", 1)
    return [x, across, partner(x, "rep", 1), partner(across, "rep", 1)]


def everyone_of(pieces, axis):
    return [pieces[0]] + [partner(pieces[k], axis, k) for k in range(1, 4)]


def to_owners(mine, theirs):
    other = partner(theirs, "rep", 1)
    pieces = [mine[k] + other[k] for k in range(4)]
    return everyone_of(pieces, "blk")


def per_device(wavefunction, environment, bond_terms, diagonal, term_slot, slot_block):
    blocks, rows, width = wavefunction.shape
    zs = lax.axis_size("blk")
    mpo, rep, blk = lax.axis_index("mpo"), lax.axis_index("rep"), lax.axis_index("blk")
    place = 2 * mpo + rep
    info = jnp.stack([place, place ^ 2, place ^ 1, place ^ 3, blk, rep, mpo]).astype(jnp.int32)
    bonds = environment.shape[0]
    sizes = tuple(bonds * part // 6 for part in (2, 2, 2))
    firsts = tuple(sum(sizes[:group]) for group in range(len(sizes)))
    entries = float(blocks * zs * rows * width)

    vector, own, diagonal_packed = pack(info, wavefunction, diagonal)

    by_owner = environment.reshape(bonds, zs, blocks, rows // zs, 2 * rows)
    pieces = []
    for group in range(len(sizes)):
        cuts = list(cut_pieces(info, by_owner, firsts[group], sizes[group]))
        if group:
            cuts[1:] = [after(x, y) for x, y in zip(cuts[1:], pieces[-1][1:])]
        pieces.append(cuts[:1] + [partner(cuts[k], "blk", k) for k in range(1, 4)])
    pieces[0][1] = after(pieces[0][1], vector)
    other_terms = partner(after(bond_terms, pieces[0][1]), "mpo", 1)
    mixing = mixing_operands([bond_terms, other_terms], sizes)
    slots = [term_slot, partner(after(term_slot, pieces[0][1]), "mpo", 1)]

    made, sent = [], []
    total = None
    operands = []
    done = 0

    def apply_group(group, vector):
        out, other = apply_bonds(
            info, slots, vector, [(0, firsts[group]), (1, firsts[group])], [made[group]],
            partner(sent[group], "mpo", 1), [terms[group] for terms in mixing], total,
            group == len(sizes) - 1,
        )
        operands.extend([made[group], other])
        return out

    for group in range(len(sizes)):
        if group >= 2:
            total = apply_group(group - 2, after(vector, sent[group - 1]))[0]
            pieces[group][3] = after(pieces[group][3], total)
        if group < 1:
            pieces[group][1] = after(pieces[group][1], pieces[group + 1][1])
        *own_set, send = own_operands(info, pieces[group])
        made.append(own_set)
        sent.append(send)
    total = apply_group(len(sizes) - 2, after(vector, sent[-1]))[0]
    out = apply_group(len(sizes) - 1, vector)
    arrived = to_owners(*out)
    start = after(diagonal_packed, arrived[0]) * own
    lower, upper = owner_image(info, slot_block, arrived, start)
    upper = with_statistics(own, lower, upper)

    chunks = [(source, first) for first in firsts for source in range(2)]
    mixes = [mixing[source][group] for group in range(len(sizes)) for source in range(2)]
    lower_parts = [lower, partner(lower, "mpo", 1), partner(lower, "rep", 1)]
    lower_parts.append(partner(after(lower_parts[1], upper), "rep", 1))
    across = partner(after(upper, lower_parts[1]), "mpo", 1)
    out, _ = apply_bonds(
        info, slots, lower_parts, chunks, operands, None, mixes, None, False, 0
    )
    upper_parts = [upper, across, partner(upper, "rep", 1)]
    upper_parts.append(partner(after(across, out[0]), "rep", 1))
    out, _ = apply_bonds(
        info, slots, upper_parts, chunks, operands, None, mixes, out[0], True, 1
    )
    return tuple(
        outputs(
            info, slot_block, to_owners(*out), diagonal_packed, own, (lower, upper), entries
        )
    )


def solution(mesh):
    packed = mesh.shape["mpo"] == 2 and mesh.shape["rep"] == 2 and mesh.shape["blk"] == 4
    return jax.shard_map(
        per_device if packed else plain_device,
        mesh=mesh,
        in_specs=(
            P(("grp", "blk"), None, None),
            P(("grp", "mpo", "rep"), None, "blk", None),
            P(("grp", "mpo", "rep"), None, None),
            P(("grp", "blk"), None, ("mpo", "rep")),
            P(("grp", "mpo", "rep"), "blk"),
            P("grp", "blk"),
        ),
        out_specs=(
            P(("grp", "blk"), None, ("mpo", "rep")),
            P(("grp", "blk"), None, ("mpo", "rep")),
            P(("grp", "blk"), None, ("mpo", "rep")),
        ),
        check_vma=False,
    )
```
